512 devices in a mesh: step: 4 (over x), blk: 16 (over z_hi, y), head: 8 (over z_lo, core).
Axes of the slice: x: 4, y: 4, z: 16 (z_hi: 4, z_lo: 4; z = z_hi * 4 + z_lo), core: 2. Of those that a mesh axis runs over, the one named last changes fastest.
Arguments:
- states: bfloat16 [4, 2048, 3072], P('step', 'blk', 'head'), may hold values from -6 to 6
- modulation: float32 [4, 3, 3072], P('step'), may hold values from -2.5 to 2.5
- cotangent: float32 [2048, 3072], P('blk', 'head'), may hold values from -6 to 6
- w_qkv: bfloat16 [3072, 3, 3072], P(('step', 'blk'), None, 'head'), may hold values from -0.109375 to 0.109375
- q_gain: float32 [128], replicated, may hold values from 0.25 to 1.75
- k_gain: float32 [128], replicated, may hold values from 0.25 to 1.75
- step_ids: int32 [4], replicated, may hold values from 0 to 49
- coeffs: float32 [50, 2], replicated, may hold values from 0.2 to 1.2, as said below
- neighbours: int32 [16, 3], replicated, may hold values from 0 to 15, as said below
Outputs:
- adjoint: float32 [4, 2048, 3072], P('step', 'blk', 'head')
- moments_out: float32 [4, 2, 2048], P('step', None, 'blk')
The draws below stay inside these ranges and needn't reach their ends.
Inputs may be any that keep to these rules, and one draw needn't show every extreme that they name: `coeffs`: column 0 holds decays, column 1 weights; all positive. `neighbours`: row i starts with i itself, followed by the two tiles beside i on a closed cycle through all 16 tiles, so tile j is in row i exactly when i is in row j.
All inputs are finite; a program needn't handle non-finite values.
Results may differ from the reference program's by a relative error of at most 0.024.
Values may be sent and summed in bfloat16 or wider, within the bound.
No kernel may reach another device: no remote copies, remote signals or barrier semaphores. Data moves between devices by JAX's collectives and lax.ppermute only.
A program may use at most 64 MiB of HBM per device.

```python
import jax
import jax.numpy as jnp
from jax import lax

D = 3072
HEADS = 24
HEAD_DIM = 128
NEIGH = 3
SWEEPS = 2
NSCHED = 50
NSTEP = 4
TILE = 128
TILES = 16
TOKENS = 2048
N_HEAD = 8


def draw_coeffs(key, part):
    key = jax.random.fold_in(key, 11)
    first_key, second_key = jax.random.split(key)
    decay = 0.4 + 0.6 * jax.random.uniform(first_key, (NSCHED,), jnp.float32)
    weight = 0.3 + 0.7 * jax.random.uniform(second_key, (NSCHED,), jnp.float32)
    return jnp.stack([decay, weight], axis=1)


def draw_neighbours(key, part):
    key = jax.random.fold_in(key, 23)
    order = jax.random.permutation(key, TILES).astype(jnp.int32)
    before = jnp.roll(order, 1)
    after = jnp.roll(order, -1)
    rows_all = jnp.stack([order, before, after], axis=1).astype(jnp.int32)
    return jnp.zeros((TILES, NEIGH), jnp.int32).at[order].set(rows_all)


def with_ends(result, stream_key, low, top_value):
    longest = result.shape.index(max(result.shape))
    spots = []
    for shift in (0, 1):
        where = [jax.random.randint(jax.random.fold_in(stream_key, axis), (), 0, length) for axis, length in enumerate(result.shape)]
        where[longest] = (where[longest] + shift) % result.shape[longest]
        spots.append(tuple(where))
    return result.at[spots[0]].set(low).at[spots[1]].set(top_value)


def level_of(rng, shape, shards, low, top_value):
    def one(position, parts):
        draws = jax.random.uniform(jax.random.fold_in(jax.random.fold_in(rng, 6), position), (parts,), jnp.float32, low / len(shards), top_value / len(shards))
        return jnp.repeat(jnp.exp(draws), shape[position] // parts).reshape((-1,) + (1,) * (len(shape) - position - 1))

    factor_of = one(*shards[0])
    for cut in shards[1:]:
        factor_of = factor_of * one(*cut)
    return factor_of


def centred(key, dims, deviation, bound, cuts=(), dtype=jnp.bfloat16):
    factor_of = level_of(key, dims, cuts, -0.22, 0.18) if cuts else 1.0
    drawn = jax.random.normal(key, dims, jnp.float32) * deviation * factor_of
    return jnp.minimum(jnp.maximum(drawn, -bound), bound).astype(dtype)


def setup_inputs(seed: int = 0) -> dict:
    seeds = jax.random.split(jax.random.key(seed), 10)
    return {
        "states": centred(seeds[0], (NSTEP, TOKENS, D), 1.0, 6.0, ((0, 4), (1, 16), (2, 8))),
        "modulation": centred(seeds[1], (NSTEP, 3, D), 0.5, 2.5, ((0, 4),), jnp.float32),
        "cotangent": centred(seeds[2], (TOKENS, D), 1.0, 6.0, ((0, 16), (1, 8)), jnp.float32),
        "w_qkv": centred(seeds[3], (D, 3, D), D ** -0.5, 0.109375, ((0, 64), (2, 8))),
        "q_gain": jnp.clip(1.0 + 0.15 * jax.random.normal(seeds[4], (HEAD_DIM,), jnp.float32), 0.25, 1.75),
        "k_gain": jnp.clip(1.0 + 0.15 * jax.random.normal(seeds[5], (HEAD_DIM,), jnp.float32), 0.25, 1.75),
        "step_ids": with_ends(jax.random.randint(seeds[6], (NSTEP,), 0, NSCHED), jax.random.fold_in(seeds[6], 1), 0, NSCHED - 1).astype(jnp.int32),
        "coeffs": draw_coeffs(jax.random.fold_in(seeds[9], 71), 0),
        "neighbours": draw_neighbours(jax.random.fold_in(seeds[9], 71), 0),
    }


def head_norm(raw_in, gain_vec):
    inverse = lax.rsqrt(lax.optimization_barrier(jnp.mean(raw_in * raw_in, axis=-1, keepdims=True)) + 1e-06)
    return raw_in * inverse * gain_vec

def rounded(value):
    return lax.optimization_barrier(value.astype(jnp.bfloat16)).astype(jnp.float32)

def reference(states, modulation, cotangent, w_qkv, q_gain, k_gain, step_ids, coeffs, neighbours):
    rates = jnp.take(coeffs, step_ids, axis=0)
    decay = rates[:, 0]
    weight = rates[:, 1]
    width = HEADS * HEAD_DIM
    group_width = width // N_HEAD
    group_heads = HEADS // N_HEAD
    flat_w = w_qkv.reshape(D, 3 * width)
    q_scale = q_gain / jnp.sqrt(jnp.float32(HEAD_DIM))
    root_width = jnp.sqrt(jnp.float32(D))
    tile_shape = (TILES, TILE, HEADS, HEAD_DIM)
    prepared = []
    for step_no in range(NSTEP):
        x_full = states[step_no].astype(jnp.float32)
        row_mean = lax.optimization_barrier(jnp.mean(x_full, axis=-1, keepdims=True))
        centered = x_full - row_mean
        inv_std = lax.rsqrt(lax.optimization_barrier(jnp.mean(centered * centered, axis=-1, keepdims=True)) + 1e-06)
        normed = centered * inv_std
        shift_mod = modulation[step_no, 0]
        scale_mod = modulation[step_no, 1]
        gate_mod = modulation[step_no, 2]
        hmod = (normed * (1.0 + scale_mod) + shift_mod).astype(jnp.bfloat16)
        proj = jnp.dot(hmod, flat_w, preferred_element_type=jnp.float32).reshape(TOKENS, 3, HEADS, HEAD_DIM)
        q_raw = proj[:, 0]
        k_raw = proj[:, 1]
        v_raw = proj[:, 2]
        q_tiles = rounded(head_norm(q_raw, q_scale)).reshape(tile_shape)
        k_tiles = rounded(head_norm(k_raw, k_gain)).reshape(tile_shape)
        v_tiles = rounded(v_raw).reshape(tile_shape)
        k_keys = k_tiles[neighbours].reshape(TILES, NEIGH * TILE, HEADS, HEAD_DIM)
        v_keys = v_tiles[neighbours].reshape(TILES, NEIGH * TILE, HEADS, HEAD_DIM)
        scores = jnp.einsum('bqhd,bkhd->bhqk', q_tiles, k_keys)
        expo = jnp.exp(scores)
        prob = expo / lax.optimization_barrier(jnp.sum(expo, axis=-1, keepdims=True))
        prob_r = rounded(prob)
        out = jnp.einsum('bhqk,bkhd->bqhd', prob_r, v_keys)
        prepared.append((inv_std, normed, scale_mod, gate_mod, q_raw, k_raw, q_tiles, k_keys, v_keys, prob, prob_r, out))

    def adjoint_term(step_no, lam_next):
        inv_std, normed, scale_mod, gate_mod, q_raw, k_raw, q_tiles, k_keys, v_keys, prob, prob_r, out = prepared[step_no]
        upstream = rounded(gate_mod * weight[step_no] * lam_next).reshape(tile_shape)
        delta = lax.optimization_barrier(jnp.sum(upstream * out, axis=-1))
        dprob = jnp.einsum('bqhd,bkhd->bhqk', upstream, v_keys)
        dscore = rounded(prob * (dprob - jnp.transpose(delta, (0, 2, 1))[..., None]))
        query_grad = jnp.einsum('bhqk,bkhd->bqhd', dscore, k_keys).reshape(TOKENS, HEADS, HEAD_DIM)
        key_part = jnp.einsum('bhqk,bqhd->bkhd', dscore, q_tiles).reshape(TILES, NEIGH, TILE, HEADS, HEAD_DIM)
        value_part = jnp.einsum('bhqk,bqhd->bkhd', prob_r, upstream).reshape(TILES, NEIGH, TILE, HEADS, HEAD_DIM)
        key_grad = jnp.zeros(tile_shape, jnp.float32).at[neighbours].add(key_part).reshape(TOKENS, HEADS, HEAD_DIM)
        value_grad = jnp.zeros(tile_shape, jnp.float32).at[neighbours].add(value_part).reshape(TOKENS, HEADS, HEAD_DIM)
        q_back = jax.vjp(lambda raw_in: head_norm(raw_in, q_scale), q_raw)[1]
        k_back = jax.vjp(lambda raw_in: head_norm(raw_in, k_gain), k_raw)[1]
        dq_raw = q_back(query_grad)[0]
        dk_raw = k_back(key_grad)[0]
        dproj = jnp.stack([dq_raw, dk_raw, value_grad], axis=1).astype(jnp.bfloat16)
        feature_grad = jnp.zeros((TOKENS, D), jnp.float32)
        for group_no in range(N_HEAD):
            cols = dproj[:, :, group_no * group_heads:(group_no + 1) * group_heads].reshape(TOKENS, 3 * group_width)
            w_cols = w_qkv[:, :, group_no * group_width:(group_no + 1) * group_width].reshape(D, 3 * group_width)
            part_sum = lax.dot_general(cols, w_cols, (((1,), (1,)), ((), ())), preferred_element_type=jnp.float32)
            feature_grad = feature_grad + rounded(part_sum)
        dnorm = feature_grad * (1.0 + scale_mod)
        first_mean = lax.optimization_barrier(jnp.mean(dnorm, axis=-1, keepdims=True))
        second_mean = lax.optimization_barrier(jnp.mean(dnorm * normed, axis=-1, keepdims=True))
        stats = jnp.stack([first_mean[:, 0], second_mean[:, 0]], axis=0) * root_width
        return (inv_std * (dnorm - first_mean - normed * second_mean), stats)
    lam_list = [None] * NSTEP
    carry = cotangent
    for step_no in reversed(range(NSTEP)):
        lam_list[step_no] = carry
        carry = decay[step_no] * carry
    terms = None
    stats_list = None
    for sweep_no in range(SWEEPS):
        results = [adjoint_term(step_no, lam_list[step_no]) for step_no in range(NSTEP)]
        terms = [item[0] for item in results]
        stats_list = [item[1] for item in results]
        fresh = [None] * NSTEP
        carry = cotangent
        for step_no in reversed(range(NSTEP)):
            fresh[step_no] = carry
            carry = decay[step_no] * carry + terms[step_no]
        lam_list = fresh
    adjoint = jnp.stack([decay[step_no] * lam_list[step_no] + terms[step_no] for step_no in range(NSTEP)], axis=0)
    return (adjoint, jnp.stack(stats_list, axis=0))
```

```python
import jax
import jax.numpy as jnp
from jax import lax
from jax.experimental import pallas as pl
from jax.experimental.pallas import tpu as pltpu
from jax.sharding import Mesh
from jax.sharding import PartitionSpec as P

HD = 128
TILE = 128
WIDTH = 384
FEATS = 3072
SWEEPS = 2
EPS = 1e-06
BF = jnp.bfloat16
F32 = jnp.float32
VMEM_LIMIT = 48 * 1024 * 1024
PLACES = (0, -1, 1, 2)

VM = pl.BlockSpec(memory_space=pltpu.VMEM)
SM = pl.BlockSpec(memory_space=pltpu.SMEM)


def call(body, outs, args, smem, scratch=(), flops=0):
    specs = [SM if i < smem else VM for i in range(len(args))]
    moved = sum(a.size * a.dtype.itemsize for a in args) + sum(
        o.size * o.dtype.itemsize for o in outs
    )
    return pl.pallas_call(
        body,
        out_shape=tuple(outs),
        in_specs=specs,
        out_specs=tuple([VM] * len(outs)),
        scratch_shapes=list(scratch),
        compiler_params=pltpu.CompilerParams(vmem_limit_bytes=VMEM_LIMIT),
        cost_estimate=pl.CostEstimate(flops=flops, bytes_accessed=moved, transcendentals=0),
    )(*args)


def sds(shape, dtype):
    return jax.ShapeDtypeStruct(shape, dtype)


def nt(a, b):
    return lax.dot_general(a, b, (((1,), (1,)), ((), ())), preferred_element_type=F32)


def tn(a, b):
    return lax.dot_general(a, b, (((0,), (0,)), ((), ())), preferred_element_type=F32)


def nn(a, b):
    return jnp.dot(a, b, preferred_element_type=F32)


def hi_lo(value):
    hi = value.astype(BF)
    return hi, (value - hi.astype(F32)).astype(BF)


def mod4(value):
    return lax.rem(value + 8, 4)


def prep_kernel(
    meta, xa0, xa1, xa2, xa3, xb0, xb1, xb2, xb3,
    wa0, wa1, wa2, wa3, wb0, wb1, wb2, wb3, mod, q_gain, k_gain,
    qkv, proj, wk, ws, vec, normed_own, inv_own, nscr, wc,
):
    step, zhi, y, zlo, core = meta[0], meta[1], meta[2], meta[3], meta[4]
    for sy, ref in enumerate((wa0, wa1, wa2, wa3)):
        for sx in range(4):
            for dd in range(2):
                zh = mod4(zhi - dd)
                wc[mod4(step + PLACES[sx]) * 2 + zh // 2, lax.rem(zh, 2) * 4 + mod4(y + PLACES[sy])] = ref[sx, dd]
    for sx, ref in enumerate((wb0, wb1, wb2, wb3)):
        for sy in range(4):
            for dd in range(2):
                zh = mod4(zhi - 2 - dd)
                wc[mod4(step + PLACES[sx]) * 2 + zh // 2, lax.rem(zh, 2) * 4 + mod4(y + PLACES[sy])] = ref[sy, dd]
    for r in range(4):
        wk[r] = wc[2 * r + core]
        ws[r] = wc[2 * r + 1 - core]

    place = zhi * 4 + zlo
    own_far = jnp.where(core == 0, -2, 2)
    sources = []
    for refs, side, far in (
        ((xa0, xa1, xa2, xa3), core, own_far),
        ((xb0, xb1, xb2, xb3), 1 - core, -own_far),
    ):
        for ref, offset in zip(refs, (0, -1, 1, far)):
            at = lax.rem(place + offset + 16, 16)
            sources.append((ref, at // 4, lax.rem(at, 4) * 2 + side))

    rows = 32

    def chunk(turn, carry):
        t = turn // (TILE // rows)
        start = pl.multiple_of(lax.rem(turn, TILE // rows) * rows, rows)
        span = pl.ds(start, rows)
        parts = [(ref, mod4(z - t), g) for ref, z, g in sources]
        total = jnp.zeros((rows, WIDTH), F32)
        for ref, d, g in parts:
            total = total + ref[d, span, :].astype(F32)
        mean = jnp.sum(total, axis=1, keepdims=True) * (1.0 / FEATS)
        square = jnp.zeros((rows, WIDTH), F32)
        for ref, d, g in parts:
            centred = ref[d, span, :].astype(F32) - mean
            square = square + centred * centred
        inv = lax.rsqrt(jnp.sum(square, axis=1, keepdims=True) * (1.0 / FEATS) + EPS)
        for ref, d, g in parts:
            normed = (ref[d, span, :].astype(F32) - mean) * inv
            nscr[g, t, span, :] = (normed * (1.0 + mod[1, g])).astype(BF)

        @pl.when(t == zhi)
        def _():
            ref, d, g = parts[0]
            normed_own[span, :] = (ref[d, span, :].astype(F32) - mean) * inv
            inv_own[span, :] = jnp.broadcast_to(inv, (rows, HD))

        return carry

    lax.fori_loop(0, 4 * (TILE // rows), chunk, 0)

    acc = jnp.zeros((4 * TILE, WIDTH), F32)
    flat = jnp.zeros((16, WIDTH), F32)
    for g in range(8):
        w_g = wc[g].reshape(WIDTH, WIDTH)
        acc = acc + nn(nscr[g].reshape(4 * TILE, WIDTH), w_g)
        scale_hi, scale_lo = hi_lo(1.0 + mod[1, g])
        shift_hi, shift_lo = hi_lo(mod[0, g])
        four = jnp.concatenate([scale_hi, scale_lo, shift_hi, shift_lo], axis=0)
        lhs = jnp.concatenate([four, jnp.zeros((12, WIDTH), BF)], axis=0)
        flat = flat + nn(lhs, w_g)
    vec[...] = flat
    proj[...] = acc + (flat[2:3] + flat[3:4])
    for t in range(4):
        span = slice(t * TILE, (t + 1) * TILE)
        q = proj[span, 0:HD]
        k = proj[span, HD : 2 * HD]
        q_inv = lax.rsqrt(jnp.mean(q * q, axis=1, keepdims=True) + EPS)
        k_inv = lax.rsqrt(jnp.mean(k * k, axis=1, keepdims=True) + EPS)
        qkv[t, :, 0:HD] = (q * q_inv * q_gain[...]).astype(BF)
        qkv[t, :, HD : 2 * HD] = (k * k_inv * k_gain[...]).astype(BF)
        qkv[t, :, 2 * HD : 3 * HD] = proj[span, 2 * HD : 3 * HD].astype(BF)


def norm_back(raw, gain, grad):
    inv = lax.rsqrt(jnp.mean(raw * raw, axis=1, keepdims=True) + EPS)
    scaled = grad * gain
    dot = jnp.mean(scaled * raw, axis=1, keepdims=True)
    return inv * (scaled - raw * (inv * inv * dot))


def sweep_kernel(
    meta, nb, k0, k1, k2, k3, u0, u1, u2, u3, proj, vec, q_gain, k_gain,
    out, tiles, ups,
):
    zhi, y = meta[1], meta[2]
    for ref, uref, offset in zip((k0, k1, k2, k3), (u0, u1, u2, u3), PLACES):
        yy = mod4(y + offset)
        for z in range(4):
            tiles[z * 4 + yy] = ref[z]
            ups[mod4(zhi - z) * 4 + yy] = uref[z]

    m1_hi, m1_lo = hi_lo(vec[0:1] + vec[1:2])
    m1 = jnp.concatenate([m1_hi, m1_lo, jnp.zeros((14, WIDTH), BF)], axis=0)
    ones = jnp.ones((16, WIDTH), BF)
    s0 = vec[2:3] + vec[3:4]

    def k_of(t):
        return tiles[t, :, HD : 2 * HD]

    def v_of(t):
        return tiles[t, :, 2 * HD : 3 * HD]

    def own(jz, carry):
        j = jz * 4 + y
        near = (nb[j, 1], nb[j, 2])
        d_k = jnp.zeros((TILE, HD), F32)
        d_v = jnp.zeros((TILE, HD), F32)
        d_q = None
        for slot in range(3):
            if slot == 0:
                i = j
                keys = (j, near[0], near[1])
            else:
                i = near[slot - 1]
                keys = (j, i, nb[i, 1] + nb[i, 2] - j)
            q = tiles[i, :, 0:HD]
            up = ups[i]
            k_all = jnp.concatenate([k_of(t) for t in keys], axis=0)
            v_all = jnp.concatenate([v_of(t) for t in keys], axis=0)
            expo = jnp.exp(nt(q, k_all))
            prob = expo * (1.0 / jnp.sum(expo, axis=1, keepdims=True))
            prob_b = prob.astype(BF)
            dprob = nt(up, v_all)
            delta = jnp.sum(prob_b.astype(F32) * dprob, axis=1, keepdims=True)
            if slot == 0:
                dscore = (prob * (dprob - delta)).astype(BF)
                d_q = nn(dscore, k_all)
                dscore = dscore[:, 0:TILE]
            else:
                dscore = (prob[:, 0:TILE] * (dprob[:, 0:TILE] - delta)).astype(BF)
            d_k = d_k + tn(dscore, q)
            d_v = d_v + tn(prob_b[:, 0:TILE], up)
        start = pl.multiple_of(jz * TILE, TILE)
        raw = proj[pl.ds(start, TILE), :]
        d_q = norm_back(raw[:, 0:HD], q_gain[...], d_q)
        d_k = norm_back(raw[:, HD : 2 * HD], k_gain[...], d_k)
        d_all = jnp.concatenate([d_q, d_k, d_v], axis=1).astype(BF)
        out[pl.ds(start, TILE), :] = d_all
        first = nt(m1, d_all)
        prod_hi, prod_lo = hi_lo(d_all.astype(F32) * (raw - s0))
        second = nt(ones, prod_hi) + nt(ones, prod_lo)
        row = jnp.concatenate(
            [first[0:1] + first[1:2], second[0:1], jnp.zeros((1, TILE), F32)], axis=1
        )
        at = lax.broadcasted_iota(jnp.int32, (8, WIDTH), 0)
        return carry + jnp.where(at == jz, row, 0.0)

    stats = lax.fori_loop(0, 4, own, jnp.zeros((8, WIDTH), F32))
    out[4 * TILE : 4 * TILE + 16, :] = jnp.concatenate(hi_lo(stats), axis=0)


def stats_of(ref, start):
    both = ref[start : start + 16, :].astype(F32)
    return both[0:8] + both[8:16]


def feature_kernel(meta, own, other, wk, wr, o0, o1, o2, o3):
    zlo = meta[3]
    stats = jnp.concatenate(hi_lo(stats_of(own, 4 * TILE) + stats_of(other, 4 * TILE)), axis=0)
    for offset, o in enumerate((o0, o1, o2, o3)):
        r = mod4(zlo + offset)
        value = nt(own[0 : 4 * TILE, :], wk[r].reshape(WIDTH, WIDTH))
        value = value + nt(other[0 : 4 * TILE, :], wr[r].reshape(WIDTH, WIDTH))
        o[0 : 4 * TILE, :] = value.astype(BF)
        o[4 * TILE : 4 * TILE + 16, :] = stats


def window_kernel(meta, a0, a1, a2, a3, o0, o1, o2, o3):
    zhi = meta[1]
    refs = (a0, a1, a2, a3)
    stats = stats_of(a0, 4 * TILE)
    for a in refs[1:]:
        stats = stats + stats_of(a, 4 * TILE)
    at = lax.broadcasted_iota(jnp.int32, (8, WIDTH), 0)
    for d, o in enumerate((o0, o1, o2, o3)):
        t = mod4(zhi + d)
        span = pl.ds(pl.multiple_of(t * TILE, TILE), TILE)
        value = a0[span, :].astype(F32)
        for a in refs[1:]:
            value = value + a[span, :].astype(F32)
        o[0:TILE, :] = value.astype(BF)
        row = jnp.sum(jnp.where(at == t, stats, 0.0), axis=0, keepdims=True)
        o[TILE : TILE + 16, :] = jnp.concatenate(
            hi_lo(jnp.broadcast_to(row, (8, WIDTH))), axis=0
        )


def term_kernel(meta, a0, a1, a2, a3, normed, inv, mod, term, sent, moments):
    group = meta[3] * 2 + meta[4]
    grad = a0[0:TILE, :].astype(F32)
    stats = stats_of(a0, TILE)
    for a in (a1, a2, a3):
        grad = grad + a[0:TILE, :].astype(F32)
        stats = stats + stats_of(a, TILE)
    first = stats[0:1, 0:TILE]
    second = stats[0:1, TILE : 2 * TILE]
    moments[...] = jnp.concatenate([first, second], axis=0) * (FEATS**-0.5)

    def column(row):
        turned = jnp.transpose(jnp.broadcast_to(row * (1.0 / FEATS), (TILE, TILE)))
        return jnp.concatenate([turned] * 3, axis=1)

    du = grad * (1.0 + mod[1, group])
    inv_wide = jnp.concatenate([inv[...]] * 3, axis=1)
    value = inv_wide * (du - column(first) - normed[...] * column(second))
    term[...] = value
    sent[...] = value.astype(BF)


def decays(meta, ids, coeffs):
    step = meta[0]
    after = []
    for ahead in (1, 2, 3):
        at = jnp.minimum(step + ahead, 3)
        after.append(jnp.where(step + ahead <= 3, coeffs[ids[at], 0], 1.0))
    return after, coeffs[ids[step], 0], coeffs[ids[step], 1]


def lam_of(meta, ids, coeffs, cot, terms):
    after, decay, weight = decays(meta, ids, coeffs)
    lam = cot[...] * (after[0] * after[1] * after[2])
    for ref, factor in zip(terms, (1.0, after[0], after[0] * after[1])):
        lam = lam + ref[...].astype(F32) * factor
    return lam, decay, weight


def upstream_kernel(meta, ids, coeffs, cot, mod, *refs):
    terms, outs = refs[:-4], refs[-4:]
    zhi = meta[1]
    group = meta[3] * 2 + meta[4]
    lam, decay, weight = lam_of(meta, ids, coeffs, cot, terms)
    up = (mod[2, group] * weight * lam).astype(BF).astype(F32)
    pieces = [up[:, i * HD : (i + 1) * HD] for i in range(3)]
    for d, o in enumerate(outs):
        at = mod4(zhi + d)
        value = jnp.zeros((TILE, HD), F32)
        for i in range(3):
            value = jnp.where(at == i, pieces[i], value)
        o[...] = value.astype(BF)


def adjoint_kernel(meta, ids, coeffs, cot, term, t1, t2, t3, out):
    lam, decay, weight = lam_of(meta, ids, coeffs, cot, (t1, t2, t3))
    out[...] = decay * lam + term[...]


def turn(value, axis, offset):
    return lax.ppermute(value, axis, [(i, (i + offset) % 4) for i in range(4)])


def ring4(value, axis):
    return [value] + [turn(value, axis, -offset) for offset in PLACES[1:]]


def to_heads(pieces):
    got = [pieces[0]]
    for d in (1, 2, 3):
        pairs = [(i, (i + d) % 4) for i in range(4) if (i + d) % 4 != 3]
        got.append(lax.ppermute(pieces[d], "zhi", pairs))
    return got


def along_z(value, offset):
    return lax.ppermute(value, ("zhi", "zlo"), [(i, (i + offset) % 16) for i in range(16)])


def far_z(value):
    pairs = []
    for i in range(16):
        pairs.append((2 * i, 2 * ((i + 2) % 16)))
        pairs.append((2 * i + 1, 2 * ((i - 2) % 16) + 1))
    return lax.ppermute(value, ("zhi", "zlo", "core"), pairs)


def other_core(value):
    return lax.ppermute(value, "core", [(0, 1), (1, 0)])


def shards(states, modulation, cotangent, w_qkv, q_gain, k_gain, step_ids, coeffs, neighbours):
    zhi = lax.axis_index("zhi")
    meta = jnp.stack([lax.axis_index(a) for a in ("step", "zhi", "y", "zlo", "core")]).astype(jnp.int32)
    mod = modulation.reshape(3, 8, 1, WIDTH)
    gq = (q_gain / jnp.sqrt(jnp.float32(HD))).reshape(1, HD)
    gk = k_gain.reshape(1, HD)

    ups = call(upstream_kernel, [sds((TILE, HD), BF)] * 4, (meta, step_ids, coeffs, cotangent, mod), 3)

    x = states[0]
    x_tiles = jnp.stack([x] + [turn(x, "zhi", d) for d in (1, 2, 3)])
    xa = [x_tiles, along_z(x_tiles, 1), along_z(x_tiles, -1), far_z(x_tiles)]
    xb = [other_core(a) for a in xa]

    w_pad = jnp.pad(w_qkv, ((0, 0), (0, 0), (0, HD)))
    w_cut = [
        lax.dynamic_slice_in_dim(w_pad, ((zhi + d) % 4) * HD, HD, 2).reshape(48, WIDTH) for d in range(4)
    ]
    w_got = to_heads(w_cut)
    wa = ring4(jnp.stack(ring4(jnp.stack(w_got[0:2]), "step")), "y")
    wb = ring4(jnp.stack(ring4(jnp.stack(w_got[2:4]), "y")), "step")

    tokens = 4 * TILE
    qkv, proj, wk, ws, vec, normed, inv = call(
        prep_kernel,
        [
            sds((4, TILE, WIDTH), BF),
            sds((tokens, WIDTH), F32),
            sds((4, 8, 48, WIDTH), BF),
            sds((4, 8, 48, WIDTH), BF),
            sds((16, WIDTH), F32),
            sds((TILE, WIDTH), F32),
            sds((TILE, HD), F32),
        ],
        (meta, *xa, *xb, *wa, *wb, mod, gq, gk),
        1,
        [pltpu.VMEM((8, 4, TILE, WIDTH), BF), pltpu.VMEM((8, 8, 48, WIDTH), BF)],
        2 * tokens * FEATS * WIDTH,
    )
    wr = other_core(ws)
    all_qkv = ring4(qkv, "y")

    for sweep in range(SWEEPS):
        all_up = ring4(jnp.stack(to_heads(ups)), "y")
        (dproj,) = call(
            sweep_kernel,
            [sds((tokens + 16, WIDTH), BF)],
            (meta, neighbours, *all_qkv, *all_up, proj, vec, gq, gk),
            2,
            [pltpu.VMEM((16, TILE, WIDTH), BF), pltpu.VMEM((16, TILE, HD), BF)],
            400 * 1000 * 1000,
        )
        parts = call(
            feature_kernel,
            [sds((tokens + 16, WIDTH), BF)] * 4,
            (meta, dproj, other_core(dproj), wk, wr),
            1,
            (),
            2 * tokens * FEATS * WIDTH,
        )
        near = [parts[0], along_z(parts[1], 1), far_z(parts[2]), along_z(parts[3], -1)]
        blocks = call(window_kernel, [sds((TILE + 16, WIDTH), BF)] * 4, (meta, *near), 1)
        got = [blocks[0]] + [turn(blocks[d], "zhi", d) for d in (1, 2, 3)]
        term, sent, moments = call(
            term_kernel,
            [sds((TILE, WIDTH), F32), sds((TILE, WIDTH), BF), sds((2, TILE), F32)],
            (meta, *got, normed, inv, mod),
            1,
        )
        later = [lax.ppermute(sent, "step", [(j, j - d) for j in range(d, 4)]) for d in (1, 2, 3)]
        if sweep + 1 < SWEEPS:
            ups = call(
                upstream_kernel,
                [sds((TILE, HD), BF)] * 4,
                (meta, step_ids, coeffs, cotangent, mod, *later),
                3,
            )
    (adjoint,) = call(
        adjoint_kernel,
        [sds((TILE, WIDTH), F32)],
        (meta, step_ids, coeffs, cotangent, term, *later),
        3,
    )
    return adjoint[None], moments[None]


def solution(mesh):
    fine = Mesh(mesh.devices.reshape(4, 4, 4, 4, 2), ("step", "zhi", "y", "zlo", "core"))
    blk, head = ("zhi", "y"), ("zlo", "core")
    in_specs = (
        P("step", blk, head),
        P("step", None, None),
        P(blk, head),
        P(("step",) + blk, None, head),
        P(),
        P(),
        P(),
        P(),
        P(),
    )
    out_specs = (P("step", blk, head), P("step", None, blk))
    return jax.shard_map(shards, mesh=fine, in_specs=in_specs, out_specs=out_specs, check_vma=False)
```

```python
import jax
import jax.numpy as jnp
from jax import lax
from jax.experimental import pallas as pl
from jax.experimental.pallas import tpu as pltpu
from jax.sharding import Mesh
from jax.sharding import PartitionSpec as P

HD = 128
TILE = 128
WIDTH = 384
FEATS = 3072
SWEEPS = 2
EPS = 1e-06
BF = jnp.bfloat16
F32 = jnp.float32
VMEM_LIMIT = 48 * 1024 * 1024
PLACES = (0, -1, 1, 2)

VM = pl.BlockSpec(memory_space=pltpu.VMEM)
SM = pl.BlockSpec(memory_space=pltpu.SMEM)


def call(body, outs, args, smem, scratch=(), flops=0):
    specs = [SM if i < smem else VM for i in range(len(args))]
    moved = sum(a.size * a.dtype.itemsize for a in args) + sum(
        o.size * o.dtype.itemsize for o in outs
    )
    return pl.pallas_call(
        body,
        out_shape=tuple(outs),
        in_specs=specs,
        out_specs=tuple([VM] * len(outs)),
        scratch_shapes=list(scratch),
        compiler_params=pltpu.CompilerParams(vmem_limit_bytes=VMEM_LIMIT),
        cost_estimate=pl.CostEstimate(flops=flops, bytes_accessed=moved, transcendentals=0),
    )(*args)


def sds(shape, dtype):
    return jax.ShapeDtypeStruct(shape, dtype)


def nt(a, b):
    return lax.dot_general(a, b, (((1,), (1,)), ((), ())), preferred_element_type=F32)


def tn(a, b):
    return lax.dot_general(a, b, (((0,), (0,)), ((), ())), preferred_element_type=F32)


def nn(a, b):
    return jnp.dot(a, b, preferred_element_type=F32)


def hi_lo(value):
    hi = value.astype(BF)
    return hi, (value - hi.astype(F32)).astype(BF)


def mod4(value):
    return lax.rem(value + 8, 4)


def lane_piece(value, at):
    out = jnp.zeros(value.shape[:-1] + (HD,), value.dtype)
    for i in range(3):
        out = jnp.where(at == i, value[..., i * HD : (i + 1) * HD], out)
    return out


def prep_kernel(
    meta, xa0, xa1, xa2, xa3, xb0, xb1, xb2, xb3, wg, p0, p1, p2, p3, mod, q_gain, k_gain,
    qkvu, proj, wk, ws, vec, normed_own, inv_own, normed_piece, inv_all, nscr, wc,
):
    zhi, zlo, core = meta[1], meta[3], meta[4]
    for d, piece in enumerate((p0, p1, p2, p3)):
        zh = mod4(zhi - d)
        qkvu[zh, :, WIDTH : WIDTH + HD] = piece[144:272, :]
        for sy in range(16):
            for part in range(3):
                wc[(sy // 4) * 2 + zh // 2, lax.rem(zh, 2) * 4 + sy % 4, :, part * HD : (part + 1) * HD] = (
                    wg[sy, d, part * 48 : (part + 1) * 48, :]
                )
    for r in range(4):
        wk[r] = wc[2 * r + core]
        ws[r] = wc[2 * r + 1 - core]

    place = zhi * 4 + zlo
    own_far = jnp.where(core == 0, -2, 2)
    sources = []
    for refs, side, far in (
        ((xa0, xa1, xa2, xa3), core, own_far),
        ((xb0, xb1, xb2, xb3), 1 - core, -own_far),
    ):
        for ref, offset in zip(refs, (0, -1, 1, far)):
            at = lax.rem(place + offset + 16, 16)
            sources.append((ref, at // 4, lax.rem(at, 4) * 2 + side))

    rows = 32

    def chunk(turn, carry):
        t = turn // (TILE // rows)
        start = pl.multiple_of(lax.rem(turn, TILE // rows) * rows, rows)
        span = pl.ds(start, rows)
        parts = [(ref, mod4(z - t), g) for ref, z, g in sources]
        total = jnp.zeros((rows, WIDTH), F32)
        for ref, d, g in parts:
            total = total + ref[d, span, :].astype(F32)
        mean = jnp.sum(total, axis=1, keepdims=True) * (1.0 / FEATS)
        square = jnp.zeros((rows, WIDTH), F32)
        for ref, d, g in parts:
            centred = ref[d, span, :].astype(F32) - mean
            square = square + centred * centred
        inv = lax.rsqrt(jnp.sum(square, axis=1, keepdims=True) * (1.0 / FEATS) + EPS)
        for ref, d, g in parts:
            normed = (ref[d, span, :].astype(F32) - mean) * inv
            nscr[g, t, span, :] = (normed * (1.0 + mod[1, g])).astype(BF)

        ref, d, g = parts[0]
        normed = (ref[d, span, :].astype(F32) - mean) * inv
        normed_piece[t, span, :] = lane_piece(normed, zhi)
        inv_all[t, span, :] = jnp.broadcast_to(inv, (rows, HD))

        @pl.when(t == zhi)
        def _():
            normed_own[span, :] = normed
            inv_own[span, :] = jnp.broadcast_to(inv, (rows, HD))

        return carry

    lax.fori_loop(0, 4 * (TILE // rows), chunk, 0)

    acc = jnp.zeros((4 * TILE, WIDTH), F32)
    flat = jnp.zeros((16, WIDTH), F32)
    for g in range(8):
        w_g = wc[g].reshape(WIDTH, WIDTH)
        acc = acc + nn(nscr[g].reshape(4 * TILE, WIDTH), w_g)
        scale_hi, scale_lo = hi_lo(1.0 + mod[1, g])
        shift_hi, shift_lo = hi_lo(mod[0, g])
        four = jnp.concatenate([scale_hi, scale_lo, shift_hi, shift_lo], axis=0)
        lhs = jnp.concatenate([four, jnp.zeros((12, WIDTH), BF)], axis=0)
        flat = flat + nn(lhs, w_g)
    vec[...] = flat
    proj[...] = acc + (flat[2:3] + flat[3:4])
    for t in range(4):
        span = slice(t * TILE, (t + 1) * TILE)
        q = proj[span, 0:HD]
        k = proj[span, HD : 2 * HD]
        q_inv = lax.rsqrt(jnp.mean(q * q, axis=1, keepdims=True) + EPS)
        k_inv = lax.rsqrt(jnp.mean(k * k, axis=1, keepdims=True) + EPS)
        qkvu[t, :, 0:HD] = (q * q_inv * q_gain[...]).astype(BF)
        qkvu[t, :, HD : 2 * HD] = (k * k_inv * k_gain[...]).astype(BF)
        qkvu[t, :, 2 * HD : 3 * HD] = proj[span, 2 * HD : 3 * HD].astype(BF)


def norm_back(raw, gain, grad):
    inv = lax.rsqrt(jnp.mean(raw * raw, axis=1, keepdims=True) + EPS)
    scaled = grad * gain
    dot = jnp.mean(scaled * raw, axis=1, keepdims=True)
    return inv * (scaled - raw * (inv * inv * dot))


def sweep_kernel(
    meta, nb, k0, k1, k2, k3, proj, vec, q_gain, k_gain, *rest
):
    out, tiles, ups = rest[-3:]
    y = meta[2]
    for ref, offset in zip((k0, k1, k2, k3), PLACES):
        yy = mod4(y + offset)
        for z in range(4):
            tiles[z * 4 + yy] = ref[z, :, 0:WIDTH]
            if len(rest) == 3:
                ups[z * 4 + yy] = ref[z, :, WIDTH : WIDTH + HD]
    if len(rest) > 3:
        for yy in range(4):
            for z in range(4):
                ups[z * 4 + yy] = rest[0][yy, z]

    m1_hi, m1_lo = hi_lo(vec[0:1] + vec[1:2])
    m1 = jnp.concatenate([m1_hi, m1_lo, jnp.zeros((14, WIDTH), BF)], axis=0)
    ones = jnp.ones((16, WIDTH), BF)
    s0 = vec[2:3] + vec[3:4]

    def k_of(t):
        return tiles[t, :, HD : 2 * HD]

    def v_of(t):
        return tiles[t, :, 2 * HD : 3 * HD]

    def own(jz, carry):
        j = jz * 4 + y
        near = (nb[j, 1], nb[j, 2])
        d_k = jnp.zeros((TILE, HD), F32)
        d_v = jnp.zeros((TILE, HD), F32)
        d_q = None
        for slot in range(3):
            if slot == 0:
                i = j
                keys = (j, near[0], near[1])
            else:
                i = near[slot - 1]
                keys = (j, i, nb[i, 1] + nb[i, 2] - j)
            q = tiles[i, :, 0:HD]
            up = ups[i]
            k_all = jnp.concatenate([k_of(t) for t in keys], axis=0)
            v_all = jnp.concatenate([v_of(t) for t in keys], axis=0)
            expo = jnp.exp(nt(q, k_all))
            prob = expo * (1.0 / jnp.sum(expo, axis=1, keepdims=True))
            prob_b = prob.astype(BF)
            dprob = nt(up, v_all)
            delta = jnp.sum(prob_b.astype(F32) * dprob, axis=1, keepdims=True)
            if slot == 0:
                dscore = (prob * (dprob - delta)).astype(BF)
                d_q = nn(dscore, k_all)
                dscore = dscore[:, 0:TILE]
            else:
                dscore = (prob[:, 0:TILE] * (dprob[:, 0:TILE] - delta)).astype(BF)
            d_k = d_k + tn(dscore, q)
            d_v = d_v + tn(prob_b[:, 0:TILE], up)
        start = pl.multiple_of(jz * TILE, TILE)
        raw = proj[pl.ds(start, TILE), :]
        d_q = norm_back(raw[:, 0:HD], q_gain[...], d_q)
        d_k = norm_back(raw[:, HD : 2 * HD], k_gain[...], d_k)
        d_all = jnp.concatenate([d_q, d_k, d_v], axis=1).astype(BF)
        out[pl.ds(start, TILE), :] = d_all
        first = nt(m1, d_all)
        prod_hi, prod_lo = hi_lo(d_all.astype(F32) * (raw - s0))
        second = nt(ones, prod_hi) + nt(ones, prod_lo)
        row = jnp.concatenate(
            [first[0:1] + first[1:2], second[0:1], jnp.zeros((1, TILE), F32)], axis=1
        )
        at = lax.broadcasted_iota(jnp.int32, (8, WIDTH), 0)
        return carry + jnp.where(at == jz, row, 0.0)

    stats = lax.fori_loop(0, 4, own, jnp.zeros((8, WIDTH), F32))
    out[4 * TILE : 4 * TILE + 16, :] = jnp.concatenate(hi_lo(stats), axis=0)


def stats_of(ref, start):
    both = ref[start : start + 16, :].astype(F32)
    return both[0:8] + both[8:16]


def feature_kernel(meta, own, other, wk, wr, o0, o1, o2, o3):
    zlo = meta[3]
    stats = jnp.concatenate(hi_lo(stats_of(own, 4 * TILE) + stats_of(other, 4 * TILE)), axis=0)
    for offset, o in enumerate((o0, o1, o2, o3)):
        r = mod4(zlo + offset)
        value = nt(own[0 : 4 * TILE, :], wk[r].reshape(WIDTH, WIDTH))
        value = value + nt(other[0 : 4 * TILE, :], wr[r].reshape(WIDTH, WIDTH))
        o[0 : 4 * TILE, :] = value.astype(BF)
        o[4 * TILE : 4 * TILE + 16, :] = stats


def window_kernel(meta, a0, a1, a2, a3, o0, o1, o2, o3):
    zhi = meta[1]
    refs = (a0, a1, a2, a3)
    stats = stats_of(a0, 4 * TILE)
    for a in refs[1:]:
        stats = stats + stats_of(a, 4 * TILE)
    at = lax.broadcasted_iota(jnp.int32, (8, WIDTH), 0)
    for d, o in enumerate((o0, o1, o2, o3)):
        t = mod4(zhi + d)
        span = pl.ds(pl.multiple_of(t * TILE, TILE), TILE)
        value = a0[span, :].astype(F32)
        for a in refs[1:]:
            value = value + a[span, :].astype(F32)
        o[0:TILE, :] = value.astype(BF)
        row = jnp.sum(jnp.where(at == t, stats, 0.0), axis=0, keepdims=True)
        o[TILE : TILE + 16, :] = jnp.concatenate(
            hi_lo(jnp.broadcast_to(row, (8, WIDTH))), axis=0
        )


def window_piece_kernel(meta, a0, a1, a2, a3, o0, o1, o2, o3):
    zhi = meta[1]
    refs = (a0, a1, a2, a3)
    stats = stats_of(a0, 4 * TILE)
    for a in refs[1:]:
        stats = stats + stats_of(a, 4 * TILE)
    stats = jnp.concatenate(hi_lo(jnp.concatenate([stats[0:4, 0:TILE], stats[0:4, TILE : 2 * TILE]], axis=0)), axis=0)
    for t in range(4):
        span = slice(t * TILE, (t + 1) * TILE)
        value = a0[span, :].astype(F32)
        for a in refs[1:]:
            value = value + a[span, :].astype(F32)
        for d, o in enumerate((o0, o1, o2, o3)):
            o[span, :] = lane_piece(value, mod4(zhi + d)).astype(BF)
    for d, o in enumerate((o0, o1, o2, o3)):
        keep = jnp.where(mod4(zhi + d) == 3, 0.0, 1.0)
        o[4 * TILE : 4 * TILE + 16, :] = (stats.astype(F32) * keep).astype(BF)


def term_piece_kernel(meta, a0, a1, a2, a3, normed, inv, mod, sent):
    group = meta[3] * 2 + meta[4]
    stats = stats_of(a0, 4 * TILE)
    for a in (a1, a2, a3):
        stats = stats + stats_of(a, 4 * TILE)
    scale = 1.0 + lane_piece(mod[1, group], meta[1])
    for t in range(4):
        span = slice(t * TILE, (t + 1) * TILE)
        grad = a0[span, :].astype(F32)
        for a in (a1, a2, a3):
            grad = grad + a[span, :].astype(F32)
        value = inv[t] * (grad * scale - column(stats[t : t + 1]) - normed[t] * column(stats[4 + t : 5 + t]))
        sent[t] = value.astype(BF)


def upstream_piece_kernel(meta, ids, coeffs, qkvu, mod, t1, t2, t3, out):
    group = meta[3] * 2 + meta[4]
    after, decay, weight = decays(meta, ids, coeffs)
    gate = lane_piece(mod[2, group], meta[1]) * weight
    for t in range(4):
        later = t1[t].astype(F32) + t2[t].astype(F32) * after[0] + t3[t].astype(F32) * (after[0] * after[1])
        out[t] = (qkvu[t, :, WIDTH : WIDTH + HD].astype(F32) + gate * later).astype(BF)


def column(row):
    return jnp.transpose(jnp.broadcast_to(row * (1.0 / FEATS), (TILE, TILE)))


def term_kernel(meta, a0, a1, a2, a3, normed, inv, mod, term, sent, moments):
    group = meta[3] * 2 + meta[4]
    grad = a0[0:TILE, :].astype(F32)
    stats = stats_of(a0, TILE)
    for a in (a1, a2, a3):
        grad = grad + a[0:TILE, :].astype(F32)
        stats = stats + stats_of(a, TILE)
    first = stats[0:1, 0:TILE]
    second = stats[0:1, TILE : 2 * TILE]
    moments[...] = jnp.concatenate([first, second], axis=0) * (FEATS**-0.5)

    def wide(value):
        return jnp.concatenate([value] * 3, axis=1)

    du = grad * (1.0 + mod[1, group])
    value = wide(inv[...]) * (du - wide(column(first)) - normed[...] * wide(column(second)))
    term[...] = value
    sent[...] = value.astype(BF)


def decays(meta, ids, coeffs):
    step = meta[0]
    after = []
    for ahead in (1, 2, 3):
        at = jnp.minimum(step + ahead, 3)
        after.append(jnp.where(step + ahead <= 3, coeffs[ids[at], 0], 1.0))
    return after, coeffs[ids[step], 0], coeffs[ids[step], 1]


def lam_of(meta, ids, coeffs, cot, terms):
    after, decay, weight = decays(meta, ids, coeffs)
    lam = cot[...] * (after[0] * after[1] * after[2])
    for ref, factor in zip(terms, (1.0, after[0], after[0] * after[1])):
        lam = lam + ref[...].astype(F32) * factor
    return lam, decay, weight


def cut_kernel(meta, ids, coeffs, cot, mod, w, o0, o1, o2, o3):
    zhi = meta[1]
    group = meta[3] * 2 + meta[4]
    lam, decay, weight = lam_of(meta, ids, coeffs, cot, ())
    up = mod[2, group] * weight * lam
    for d, o in enumerate((o0, o1, o2, o3)):
        at = mod4(zhi + d)
        for part in range(3):
            o[part * 48 : (part + 1) * 48, :] = lane_piece(w[part].astype(F32), at).astype(BF)
        o[144:272, :] = lane_piece(up, at).astype(BF)


def adjoint_kernel(meta, ids, coeffs, cot, term, t1, t2, t3, out):
    lam, decay, weight = lam_of(meta, ids, coeffs, cot, (t1, t2, t3))
    out[...] = decay * lam + term[...]


def turn(value, axis, offset):
    return lax.ppermute(value, axis, [(i, (i + offset) % 4) for i in range(4)])


def ring4(value, axis):
    return [value] + [turn(value, axis, -offset) for offset in PLACES[1:]]


def relayed(value, axis):
    before, after = turn(value, axis, 1), turn(value, axis, -1)
    pairs = []
    for i in range(4):
        pairs.append((2 * i, 2 * ((i - 1) % 4)))
        pairs.append((2 * i + 1, 2 * ((i + 1) % 4) + 1))
    far = lax.ppermute(jnp.where(lax.axis_index("core") == 0, after, before), (axis, "core"), pairs)
    return [value, before, after, far]


def to_heads(pieces):
    got = [pieces[0]]
    for d in (1, 2, 3):
        pairs = [(i, (i + d) % 4) for i in range(4) if (i + d) % 4 != 3]
        got.append(lax.ppermute(pieces[d], "zhi", pairs))
    return got


def to_earlier(value):
    return [lax.ppermute(value, "step", [(j, j - d) for j in range(d, 4)]) for d in (1, 2, 3)]


def along_z(value, offset):
    return lax.ppermute(value, ("zhi", "zlo"), [(i, (i + offset) % 16) for i in range(16)])


def far_z(value):
    pairs = []
    for i in range(16):
        pairs.append((2 * i, 2 * ((i + 2) % 16)))
        pairs.append((2 * i + 1, 2 * ((i - 2) % 16) + 1))
    return lax.ppermute(value, ("zhi", "zlo", "core"), pairs)


def other_core(value):
    return lax.ppermute(value, "core", [(0, 1), (1, 0)])


def shards(states, modulation, cotangent, w_qkv, q_gain, k_gain, step_ids, coeffs, neighbours):
    zhi = lax.axis_index("zhi")
    meta = jnp.stack([lax.axis_index(a) for a in ("step", "zhi", "y", "zlo", "core")]).astype(jnp.int32)
    mod = modulation.reshape(3, 8, 1, WIDTH)
    gq = (q_gain / jnp.sqrt(jnp.float32(HD))).reshape(1, HD)
    gk = k_gain.reshape(1, HD)

    pieces = call(
        cut_kernel,
        [sds((272, HD), BF)] * 4,
        (meta, step_ids, coeffs, cotangent, mod, jnp.transpose(w_qkv, (1, 0, 2))),
        3,
    )
    pieces = to_heads(pieces)
    wg = lax.all_gather(jnp.stack([p[0:144] for p in pieces]), ("step", "y"))

    x = states[0]
    got = relayed(x, "zhi")
    x_tiles = jnp.stack([x, got[1], got[3], got[2]])
    xa = [x_tiles, along_z(x_tiles, 1), along_z(x_tiles, -1), far_z(x_tiles)]
    xb = [other_core(a) for a in xa]

    tokens = 4 * TILE
    qkvu, proj, wk, ws, vec, normed, inv, normed_piece, inv_all = call(
        prep_kernel,
        [
            sds((4, TILE, WIDTH + HD), BF),
            sds((tokens, WIDTH), F32),
            sds((4, 8, 48, WIDTH), BF),
            sds((4, 8, 48, WIDTH), BF),
            sds((16, WIDTH), F32),
            sds((TILE, WIDTH), F32),
            sds((TILE, HD), F32),
            sds((4, TILE, HD), F32),
            sds((4, TILE, HD), F32),
        ],
        (meta, *xa, *xb, wg, *pieces, mod, gq, gk),
        1,
        [pltpu.VMEM((8, 4, TILE, WIDTH), BF), pltpu.VMEM((8, 8, 48, WIDTH), BF)],
        2 * tokens * FEATS * WIDTH,
    )
    wr = other_core(ws)
    all_qkvu = relayed(qkvu, "y")

    all_up = ()
    for sweep in range(SWEEPS):
        (dproj,) = call(
            sweep_kernel,
            [sds((tokens + 16, WIDTH), BF)],
            (meta, neighbours, *all_qkvu, proj, vec, gq, gk, *all_up),
            2,
            [pltpu.VMEM((16, TILE, WIDTH), BF), pltpu.VMEM((16, TILE, HD), BF)],
            400 * 1000 * 1000,
        )
        parts = call(
            feature_kernel,
            [sds((tokens + 16, WIDTH), BF)] * 4,
            (meta, dproj, other_core(dproj), wk, wr),
            1,
            (),
            2 * tokens * FEATS * WIDTH,
        )
        near = [parts[0], along_z(parts[1], 1), far_z(parts[2]), along_z(parts[3], -1)]
        if sweep + 1 < SWEEPS:
            blocks = call(window_piece_kernel, [sds((tokens + 16, HD), BF)] * 4, (meta, *near), 1)
            (sent,) = call(
                term_piece_kernel,
                [sds((4, TILE, HD), BF)],
                (meta, *to_heads(blocks), normed_piece, inv_all, mod),
                1,
            )
            (up,) = call(
                upstream_piece_kernel,
                [sds((4, TILE, HD), BF)],
                (meta, step_ids, coeffs, qkvu, mod, *to_earlier(sent)),
                3,
            )
            all_up = (lax.all_gather(up, "y"),)
    blocks = call(window_kernel, [sds((TILE + 16, WIDTH), BF)] * 4, (meta, *near), 1)
    got = [blocks[0]] + [turn(blocks[d], "zhi", d) for d in (1, 2, 3)]
    term, sent, moments = call(
        term_kernel,
        [sds((TILE, WIDTH), F32), sds((TILE, WIDTH), BF), sds((2, TILE), F32)],
        (meta, *got, normed, inv, mod),
        1,
    )
    (adjoint,) = call(
        adjoint_kernel,
        [sds((TILE, WIDTH), F32)],
        (meta, step_ids, coeffs, cotangent, term, *to_earlier(sent)),
        3,
    )
    return adjoint[None], moments[None]


def solution(mesh):
    fine = Mesh(mesh.devices.reshape(4, 4, 4, 4, 2), ("step", "zhi", "y", "zlo", "core"))
    blk, head = ("zhi", "y"), ("zlo", "core")
    in_specs = (
        P("step", blk, head),
        P("step", None, None),
        P(blk, head),
        P(("step",) + blk, None, head),
        P(),
        P(),
        P(),
        P(),
        P(),
    )
    out_specs = (P("step", blk, head), P("step", None, blk))
    return jax.shard_map(shards, mesh=fine, in_specs=in_specs, out_specs=out_specs, check_vma=False)
```

```python
import jax
import jax.numpy as jnp
from jax import lax
from jax.experimental import pallas as pl
from jax.experimental.pallas import tpu as pltpu
from jax.sharding import Mesh
from jax.sharding import PartitionSpec as P

HD = 128
TILE = 128
WIDTH = 384
FEATS = 3072
SWEEPS = 2
EPS = 1e-06
BF = jnp.bfloat16
F32 = jnp.float32
MIB = 1024 * 1024
PLACES = (0, -1, 1, 2)

VM = pl.BlockSpec(memory_space=pltpu.VMEM)
SM = pl.BlockSpec(memory_space=pltpu.SMEM)


def call(body, outs, args, smem, scratch=(), flops=0, grant=8):
    specs = [SM if i < smem else VM for i in range(len(args))]
    moved = sum(a.size * a.dtype.itemsize for a in args) + sum(
        o.size * o.dtype.itemsize for o in outs
    )
    return pl.pallas_call(
        body,
        out_shape=tuple(outs),
        in_specs=specs,
        out_specs=tuple([VM] * len(outs)),
        scratch_shapes=list(scratch),
        compiler_params=pltpu.CompilerParams(vmem_limit_bytes=grant * MIB),
        cost_estimate=pl.CostEstimate(flops=flops, bytes_accessed=moved, transcendentals=0),
    )(*args)


def sds(shape, dtype):
    return jax.ShapeDtypeStruct(shape, dtype)


def nt(a, b):
    return lax.dot_general(a, b, (((1,), (1,)), ((), ())), preferred_element_type=F32)


def tn(a, b):
    return lax.dot_general(a, b, (((0,), (0,)), ((), ())), preferred_element_type=F32)


def nn(a, b):
    return jnp.dot(a, b, preferred_element_type=F32)


def hi_lo(value):
    hi = value.astype(BF)
    return hi, (value - hi.astype(F32)).astype(BF)


def mod4(value):
    return lax.rem(value + 8, 4)


def lane_piece(value, at):
    out = jnp.zeros(value.shape[:-1] + (HD,), value.dtype)
    for i in range(3):
        out = jnp.where(at == i, value[..., i * HD : (i + 1) * HD], out)
    return out


def prep_kernel(
    meta, xa0, xa1, xa2, xa3, xb0, xb1, xb2, xb3, wg, p0, p1, p2, p3, mod, q_gain, k_gain,
    qkvu, proj, wk, ws, vec, normed_own, inv_own, normed_piece, inv_all, nscr, wc,
):
    zhi, zlo, core = meta[1], meta[3], meta[4]
    for d, piece in enumerate((p0, p1, p2, p3)):
        zh = mod4(zhi - d)
        qkvu[zh, :, WIDTH : WIDTH + HD] = piece[144:272, :]
        for sy in range(16):
            for part in range(3):
                wc[(sy // 4) * 2 + zh // 2, lax.rem(zh, 2) * 4 + sy % 4, :, part * HD : (part + 1) * HD] = (
                    wg[sy, d, part * 48 : (part + 1) * 48, :]
                )
    for r in range(4):
        wk[r] = wc[2 * r + core]
        ws[r] = wc[2 * r + 1 - core]

    place = zhi * 4 + zlo
    own_far = jnp.where(core == 0, -2, 2)
    sources = []
    for refs, side, far in (
        ((xa0, xa1, xa2, xa3), core, own_far),
        ((xb0, xb1, xb2, xb3), 1 - core, -own_far),
    ):
        for ref, offset in zip(refs, (0, -1, 1, far)):
            at = lax.rem(place + offset + 16, 16)
            sources.append((ref, at // 4, lax.rem(at, 4) * 2 + side))

    rows = 32

    def chunk(turn, carry):
        t = turn // (TILE // rows)
        start = pl.multiple_of(lax.rem(turn, TILE // rows) * rows, rows)
        span = pl.ds(start, rows)
        parts = [(ref, mod4(z - t), g) for ref, z, g in sources]
        total = jnp.zeros((rows, WIDTH), F32)
        for ref, d, g in parts:
            total = total + ref[d, span, :].astype(F32)
        mean = jnp.sum(total, axis=1, keepdims=True) * (1.0 / FEATS)
        square = jnp.zeros((rows, WIDTH), F32)
        for ref, d, g in parts:
            centred = ref[d, span, :].astype(F32) - mean
            square = square + centred * centred
        inv = lax.rsqrt(jnp.sum(square, axis=1, keepdims=True) * (1.0 / FEATS) + EPS)
        for ref, d, g in parts:
            normed = (ref[d, span, :].astype(F32) - mean) * inv
            nscr[g, t, span, :] = (normed * (1.0 + mod[1, g])).astype(BF)

        ref, d, g = parts[0]
        normed = (ref[d, span, :].astype(F32) - mean) * inv
        normed_piece[t, span, :] = lane_piece(normed, zhi)
        inv_all[t, span, :] = jnp.broadcast_to(inv, (rows, HD))

        @pl.when(t == zhi)
        def _():
            normed_own[span, :] = normed
            inv_own[span, :] = jnp.broadcast_to(inv, (rows, HD))

        return carry

    lax.fori_loop(0, 4 * (TILE // rows), chunk, 0)

    acc = jnp.zeros((4 * TILE, WIDTH), F32)
    flat = jnp.zeros((16, WIDTH), F32)
    for g in range(8):
        w_g = wc[g].reshape(WIDTH, WIDTH)
        acc = acc + nn(nscr[g].reshape(4 * TILE, WIDTH), w_g)
        scale_hi, scale_lo = hi_lo(1.0 + mod[1, g])
        shift_hi, shift_lo = hi_lo(mod[0, g])
        four = jnp.concatenate([scale_hi, scale_lo, shift_hi, shift_lo], axis=0)
        lhs = jnp.concatenate([four, jnp.zeros((12, WIDTH), BF)], axis=0)
        flat = flat + nn(lhs, w_g)
    vec[...] = flat
    proj[...] = acc + (flat[2:3] + flat[3:4])
    for t in range(4):
        span = slice(t * TILE, (t + 1) * TILE)
        q = proj[span, 0:HD]
        k = proj[span, HD : 2 * HD]
        q_inv = lax.rsqrt(jnp.mean(q * q, axis=1, keepdims=True) + EPS)
        k_inv = lax.rsqrt(jnp.mean(k * k, axis=1, keepdims=True) + EPS)
        qkvu[t, :, 0:HD] = (q * q_inv * q_gain[...]).astype(BF)
        qkvu[t, :, HD : 2 * HD] = (k * k_inv * k_gain[...]).astype(BF)
        qkvu[t, :, 2 * HD : 3 * HD] = proj[span, 2 * HD : 3 * HD].astype(BF)


def norm_back(raw, gain, grad):
    inv = lax.rsqrt(jnp.mean(raw * raw, axis=1, keepdims=True) + EPS)
    scaled = grad * gain
    dot = jnp.mean(scaled * raw, axis=1, keepdims=True)
    return inv * (scaled - raw * (inv * inv * dot))


def sweep_kernel(
    meta, nb, k0, k1, k2, k3, proj, vec, q_gain, k_gain, *rest
):
    out, tiles, ups = rest[-3:]
    y = meta[2]
    for ref, offset in zip((k0, k1, k2, k3), PLACES):
        yy = mod4(y + offset)
        for z in range(4):
            tiles[z * 4 + yy] = ref[z, :, 0:WIDTH]
            if len(rest) == 3:
                ups[z * 4 + yy] = ref[z, :, WIDTH : WIDTH + HD]
    if len(rest) > 3:
        for yy in range(4):
            for z in range(4):
                ups[z * 4 + yy] = rest[0][yy, z]

    m1_hi, m1_lo = hi_lo(vec[0:1] + vec[1:2])
    m1 = jnp.concatenate([m1_hi, m1_lo, jnp.zeros((14, WIDTH), BF)], axis=0)
    ones = jnp.ones((16, WIDTH), BF)
    s0 = vec[2:3] + vec[3:4]

    def k_of(t):
        return tiles[t, :, HD : 2 * HD]

    def v_of(t):
        return tiles[t, :, 2 * HD : 3 * HD]

    def own(jz, carry):
        j = jz * 4 + y
        near = (nb[1, j], nb[2, j])
        d_k = jnp.zeros((TILE, HD), F32)
        d_v = jnp.zeros((TILE, HD), F32)
        d_q = None
        for slot in range(3):
            if slot == 0:
                i = j
                keys = (j, near[0], near[1])
            else:
                i = near[slot - 1]
                keys = (j, i, nb[1, i] + nb[2, i] - j)
            q = tiles[i, :, 0:HD]
            up = ups[i]
            k_all = jnp.concatenate([k_of(t) for t in keys], axis=0)
            v_all = jnp.concatenate([v_of(t) for t in keys], axis=0)
            expo = jnp.exp(nt(q, k_all))
            prob = expo * (1.0 / jnp.sum(expo, axis=1, keepdims=True))
            prob_b = prob.astype(BF)
            dprob = nt(up, v_all)
            delta = jnp.sum(prob_b.astype(F32) * dprob, axis=1, keepdims=True)
            if slot == 0:
                dscore = (prob * (dprob - delta)).astype(BF)
                d_q = nn(dscore, k_all)
                dscore = dscore[:, 0:TILE]
            else:
                dscore = (prob[:, 0:TILE] * (dprob[:, 0:TILE] - delta)).astype(BF)
            d_k = d_k + tn(dscore, q)
            d_v = d_v + tn(prob_b[:, 0:TILE], up)
        start = pl.multiple_of(jz * TILE, TILE)
        raw = proj[pl.ds(start, TILE), :]
        d_q = norm_back(raw[:, 0:HD], q_gain[...], d_q)
        d_k = norm_back(raw[:, HD : 2 * HD], k_gain[...], d_k)
        d_all = jnp.concatenate([d_q, d_k, d_v], axis=1).astype(BF)
        out[pl.ds(start, TILE), :] = d_all
        first = nt(m1, d_all)
        prod_hi, prod_lo = hi_lo(d_all.astype(F32) * (raw - s0))
        second = nt(ones, prod_hi) + nt(ones, prod_lo)
        row = jnp.concatenate(
            [first[0:1] + first[1:2], second[0:1], jnp.zeros((1, TILE), F32)], axis=1
        )
        at = lax.broadcasted_iota(jnp.int32, (8, WIDTH), 0)
        return carry + jnp.where(at == jz, row, 0.0)

    stats = lax.fori_loop(0, 4, own, jnp.zeros((8, WIDTH), F32))
    out[4 * TILE : 4 * TILE + 16, :] = jnp.concatenate(hi_lo(stats), axis=0)


def stats_of(ref, start):
    both = ref[start : start + 16, :].astype(F32)
    return both[0:8] + both[8:16]


def feature_kernel(meta, own, other, wk, wr, o0, o1, o2, o3):
    zlo = meta[3]
    stats = jnp.concatenate(hi_lo(stats_of(own, 4 * TILE) + stats_of(other, 4 * TILE)), axis=0)
    for offset, o in enumerate((o0, o1, o2, o3)):
        r = mod4(zlo + offset)
        value = nt(own[0 : 4 * TILE, :], wk[r].reshape(WIDTH, WIDTH))
        value = value + nt(other[0 : 4 * TILE, :], wr[r].reshape(WIDTH, WIDTH))
        o[0 : 4 * TILE, :] = value.astype(BF)
        o[4 * TILE : 4 * TILE + 16, :] = stats


def window_kernel(meta, a0, a1, a2, a3, o0, o1, o2, o3):
    zhi = meta[1]
    refs = (a0, a1, a2, a3)
    stats = stats_of(a0, 4 * TILE)
    for a in refs[1:]:
        stats = stats + stats_of(a, 4 * TILE)
    at = lax.broadcasted_iota(jnp.int32, (8, WIDTH), 0)
    for d, o in enumerate((o0, o1, o2, o3)):
        t = mod4(zhi + d)
        span = pl.ds(pl.multiple_of(t * TILE, TILE), TILE)
        value = a0[span, :].astype(F32)
        for a in refs[1:]:
            value = value + a[span, :].astype(F32)
        o[0:TILE, :] = value.astype(BF)
        row = jnp.sum(jnp.where(at == t, stats, 0.0), axis=0, keepdims=True)
        o[TILE : TILE + 16, :] = jnp.concatenate(
            hi_lo(jnp.broadcast_to(row, (8, WIDTH))), axis=0
        )


def window_piece_kernel(meta, a0, a1, a2, a3, o0, o1, o2, o3):
    zhi = meta[1]
    refs = (a0, a1, a2, a3)
    stats = stats_of(a0, 4 * TILE)
    for a in refs[1:]:
        stats = stats + stats_of(a, 4 * TILE)
    stats = jnp.concatenate(hi_lo(jnp.concatenate([stats[0:4, 0:TILE], stats[0:4, TILE : 2 * TILE]], axis=0)), axis=0)
    for t in range(4):
        span = slice(t * TILE, (t + 1) * TILE)
        value = a0[span, :].astype(F32)
        for a in refs[1:]:
            value = value + a[span, :].astype(F32)
        for d, o in enumerate((o0, o1, o2, o3)):
            o[span, :] = lane_piece(value, mod4(zhi + d)).astype(BF)
    for d, o in enumerate((o0, o1, o2, o3)):
        keep = jnp.where(mod4(zhi + d) == 3, 0.0, 1.0)
        o[4 * TILE : 4 * TILE + 16, :] = (stats.astype(F32) * keep).astype(BF)


def term_piece_kernel(meta, a0, a1, a2, a3, normed, inv, mod, sent):
    group = meta[3] * 2 + meta[4]
    stats = stats_of(a0, 4 * TILE)
    for a in (a1, a2, a3):
        stats = stats + stats_of(a, 4 * TILE)
    scale = 1.0 + lane_piece(mod[1, group], meta[1])
    for t in range(4):
        span = slice(t * TILE, (t + 1) * TILE)
        grad = a0[span, :].astype(F32)
        for a in (a1, a2, a3):
            grad = grad + a[span, :].astype(F32)
        value = inv[t] * (grad * scale - column(stats[t : t + 1]) - normed[t] * column(stats[4 + t : 5 + t]))
        sent[t] = value.astype(BF)


def upstream_piece_kernel(meta, ids, coeffs, qkvu, mod, t1, t2, t3, out):
    group = meta[3] * 2 + meta[4]
    after, decay, weight = decays(meta, ids, coeffs)
    gate = lane_piece(mod[2, group], meta[1]) * weight
    for t in range(4):
        later = t1[t].astype(F32) + t2[t].astype(F32) * after[0] + t3[t].astype(F32) * (after[0] * after[1])
        out[t] = (qkvu[t, :, WIDTH : WIDTH + HD].astype(F32) + gate * later).astype(BF)


def column(row):
    return jnp.transpose(jnp.broadcast_to(row * (1.0 / FEATS), (TILE, TILE)))


def term_kernel(meta, a0, a1, a2, a3, normed, inv, mod, term, sent, moments):
    group = meta[3] * 2 + meta[4]
    grad = a0[0:TILE, :].astype(F32)
    stats = stats_of(a0, TILE)
    for a in (a1, a2, a3):
        grad = grad + a[0:TILE, :].astype(F32)
        stats = stats + stats_of(a, TILE)
    first = stats[0:1, 0:TILE]
    second = stats[0:1, TILE : 2 * TILE]
    moments[...] = jnp.concatenate([first, second], axis=0) * (FEATS**-0.5)

    def wide(value):
        return jnp.concatenate([value] * 3, axis=1)

    du = grad * (1.0 + mod[1, group])
    value = wide(inv[...]) * (du - wide(column(first)) - normed[...] * wide(column(second)))
    term[...] = value
    sent[...] = value.astype(BF)


def decays(meta, ids, coeffs):
    step = meta[0]
    after = []
    for ahead in (1, 2, 3):
        at = jnp.minimum(step + ahead, 3)
        after.append(jnp.where(step + ahead <= 3, coeffs[0, ids[at]], 1.0))
    return after, coeffs[0, ids[step]], coeffs[1, ids[step]]


def lam_of(meta, ids, coeffs, cot, terms):
    after, decay, weight = decays(meta, ids, coeffs)
    lam = cot[...] * (after[0] * after[1] * after[2])
    for ref, factor in zip(terms, (1.0, after[0], after[0] * after[1])):
        lam = lam + ref[...].astype(F32) * factor
    return lam, decay, weight


def cut_kernel(meta, ids, coeffs, cot, mod, w, o0, o1, o2, o3):
    zhi = meta[1]
    group = meta[3] * 2 + meta[4]
    lam, decay, weight = lam_of(meta, ids, coeffs, cot, ())
    up = mod[2, group] * weight * lam
    for d, o in enumerate((o0, o1, o2, o3)):
        at = mod4(zhi + d)
        for part in range(3):
            o[part * 48 : (part + 1) * 48, :] = lane_piece(w[part].astype(F32), at).astype(BF)
        o[144:272, :] = lane_piece(up, at).astype(BF)


def adjoint_kernel(meta, ids, coeffs, cot, term, t1, t2, t3, out):
    lam, decay, weight = lam_of(meta, ids, coeffs, cot, (t1, t2, t3))
    out[...] = decay * lam + term[...]


def turn(value, axis, offset):
    return lax.ppermute(value, axis, [(i, (i + offset) % 4) for i in range(4)])


def ring4(value, axis):
    return [value] + [turn(value, axis, -offset) for offset in PLACES[1:]]


def hand_on(before, after, axis):
    pairs = []
    for i in range(4):
        pairs.append((2 * i, 2 * ((i - 1) % 4)))
        pairs.append((2 * i + 1, 2 * ((i + 1) % 4) + 1))
    return lax.ppermute(jnp.where(lax.axis_index("core") == 0, after, before), (axis, "core"), pairs)


def relayed(value, axis):
    before, after = turn(value, axis, 1), turn(value, axis, -1)
    return [value, before, after, hand_on(before, after, axis)]


def to_heads(pieces):
    got = [pieces[0]]
    for d in (1, 2, 3):
        pairs = [(i, (i + d) % 4) for i in range(4) if (i + d) % 4 != 3]
        got.append(lax.ppermute(pieces[d], "zhi", pairs))
    return got


def to_earlier(value):
    return [lax.ppermute(value, "step", [(j, j - d) for j in range(d, 4)]) for d in (1, 2, 3)]


def relay_hop(value):
    pairs = []
    for i in range(4):
        pairs.append((2 * i, 2 * ((i + 1) % 4)))
        pairs.append((2 * i + 1, 2 * ((i - 1) % 4) + 1))
    return lax.ppermute(value, ("zhi", "core"), pairs)


def exchange_zhi(blocks):
    half_way = relay_hop(blocks[2])
    one, three = turn(blocks[1], "zhi", 1), turn(blocks[3], "zhi", 3)
    return [blocks[0], one, relay_hop(half_way), three]


def along_z(value, offset):
    return lax.ppermute(value, ("zhi", "zlo"), [(i, (i + offset) % 16) for i in range(16)])


def far_z(value):
    pairs = []
    for i in range(16):
        pairs.append((2 * i, 2 * ((i + 2) % 16)))
        pairs.append((2 * i + 1, 2 * ((i - 2) % 16) + 1))
    return lax.ppermute(value, ("zhi", "zlo", "core"), pairs)


def other_core(value):
    return lax.ppermute(value, "core", [(0, 1), (1, 0)])


def shards(states, modulation, cotangent, w_qkv, q_gain, k_gain, step_ids, coeffs, neighbours):
    zhi = lax.axis_index("zhi")
    meta = jnp.stack([lax.axis_index(a) for a in ("step", "zhi", "y", "zlo", "core")]).astype(jnp.int32)
    coeffs, neighbours = coeffs.T, neighbours.T
    mod = modulation.reshape(3, 8, 1, WIDTH)
    gq = (q_gain / jnp.sqrt(jnp.float32(HD))).reshape(1, HD)
    gk = k_gain.reshape(1, HD)

    pieces = call(
        cut_kernel,
        [sds((272, HD), BF)] * 4,
        (meta, step_ids, coeffs, cotangent, mod, jnp.transpose(w_qkv, (1, 0, 2))),
        3,
    )
    x = states[0]
    before, after = turn(x, "zhi", 1), turn(x, "zhi", -1)
    pieces = to_heads(pieces)
    own_rows = jnp.stack([p[0:144] for p in pieces])
    own_rows, before, after = lax.optimization_barrier((own_rows, before, after))
    y_rows = lax.all_gather(own_rows, "y")
    far = hand_on(before, after, "zhi")
    y_rows, far = lax.optimization_barrier((y_rows, far))
    wg = lax.all_gather(y_rows, "step").reshape(16, 4, 144, HD)

    x_tiles = jnp.stack([x, before, far, after])
    xa = [x_tiles, along_z(x_tiles, 1), along_z(x_tiles, -1), far_z(x_tiles)]
    xb = [other_core(a) for a in xa]

    tokens = 4 * TILE
    qkvu, proj, wk, ws, vec, normed, inv, normed_piece, inv_all = call(
        prep_kernel,
        [
            sds((4, TILE, WIDTH + HD), BF),
            sds((tokens, WIDTH), F32),
            sds((4, 8, 48, WIDTH), BF),
            sds((4, 8, 48, WIDTH), BF),
            sds((16, WIDTH), F32),
            sds((TILE, WIDTH), F32),
            sds((TILE, HD), F32),
            sds((4, TILE, HD), F32),
            sds((4, TILE, HD), F32),
        ],
        (meta, *xa, *xb, wg, *pieces, mod, gq, gk),
        1,
        [pltpu.VMEM((8, 4, TILE, WIDTH), BF), pltpu.VMEM((8, 8, 48, WIDTH), BF)],
        2 * tokens * FEATS * WIDTH,
        24,
    )
    wr = other_core(ws)
    all_qkvu = relayed(qkvu, "y")

    all_up = ()
    for sweep in range(SWEEPS):
        (dproj,) = call(
            sweep_kernel,
            [sds((tokens + 16, WIDTH), BF)],
            (meta, neighbours, *all_qkvu, proj, vec, gq, gk, *all_up),
            2,
            [pltpu.VMEM((16, TILE, WIDTH), BF), pltpu.VMEM((16, TILE, HD), BF)],
            400 * 1000 * 1000,
            16,
        )
        parts = call(
            feature_kernel,
            [sds((tokens + 16, WIDTH), BF)] * 4,
            (meta, dproj, other_core(dproj), wk, wr),
            1,
            (),
            2 * tokens * FEATS * WIDTH,
            16,
        )
        near = [parts[0], along_z(parts[1], 1), far_z(parts[2]), along_z(parts[3], -1)]
        if sweep + 1 < SWEEPS:
            blocks = call(window_piece_kernel, [sds((tokens + 16, HD), BF)] * 4, (meta, *near), 1)
            (sent,) = call(
                term_piece_kernel,
                [sds((4, TILE, HD), BF)],
                (meta, *exchange_zhi(blocks), normed_piece, inv_all, mod),
                1,
            )
            (up,) = call(
                upstream_piece_kernel,
                [sds((4, TILE, HD), BF)],
                (meta, step_ids, coeffs, qkvu, mod, *to_earlier(sent)),
                3,
            )
            all_up = (lax.all_gather(up, "y"),)
    blocks = call(window_kernel, [sds((TILE + 16, WIDTH), BF)] * 4, (meta, *near), 1)
    got = exchange_zhi(blocks)
    term, sent, moments = call(
        term_kernel,
        [sds((TILE, WIDTH), F32), sds((TILE, WIDTH), BF), sds((2, TILE), F32)],
        (meta, *got, normed, inv, mod),
        1,
    )
    (adjoint,) = call(
        adjoint_kernel,
        [sds((TILE, WIDTH), F32)],
        (meta, step_ids, coeffs, cotangent, term, *to_earlier(sent)),
        3,
    )
    return adjoint[None], moments[None]


def solution(mesh):
    fine = Mesh(mesh.devices.reshape(4, 4, 4, 4, 2), ("step", "zhi", "y", "zlo", "core"))
    blk, head = ("zhi", "y"), ("zlo", "core")
    in_specs = (
        P("step", blk, head),
        P("step", None, None),
        P(blk, head),
        P(("step",) + blk, None, head),
        P(),
        P(),
        P(),
        P(),
        P(),
    )
    out_specs = (P("step", blk, head), P("step", None, blk))
    return jax.shard_map(shards, mesh=fine, in_specs=in_specs, out_specs=out_specs, check_vma=False)
```

```python
import jax
import jax.numpy as jnp
from jax import lax
from jax.experimental import pallas as pl
from jax.experimental.pallas import tpu as pltpu
from jax.sharding import Mesh
from jax.sharding import PartitionSpec as P

HD = 128
TILE = 128
WIDTH = 384
FEATS = 3072
SWEEPS = 2
EPS = 1e-06
BF = jnp.bfloat16
F32 = jnp.float32
MIB = 1024 * 1024
PLACES = (0, -1, 1, 2)

VM = pl.BlockSpec(memory_space=pltpu.VMEM)
SM = pl.BlockSpec(memory_space=pltpu.SMEM)


def call(body, outs, args, smem, scratch=(), flops=0, grant=8):
    specs = [SM if i < smem else VM for i in range(len(args))]
    moved = sum(a.size * a.dtype.itemsize for a in args) + sum(
        o.size * o.dtype.itemsize for o in outs
    )
    return pl.pallas_call(
        body,
        out_shape=tuple(outs),
        in_specs=specs,
        out_specs=tuple([VM] * len(outs)),
        scratch_shapes=list(scratch),
        compiler_params=pltpu.CompilerParams(vmem_limit_bytes=grant * MIB),
        cost_estimate=pl.CostEstimate(flops=flops, bytes_accessed=moved, transcendentals=0),
    )(*args)


def sds(shape, dtype):
    return jax.ShapeDtypeStruct(shape, dtype)


def nt(a, b):
    return lax.dot_general(a, b, (((1,), (1,)), ((), ())), preferred_element_type=F32)


def tn(a, b):
    return lax.dot_general(a, b, (((0,), (0,)), ((), ())), preferred_element_type=F32)


def nn(a, b):
    return jnp.dot(a, b, preferred_element_type=F32)


def hi_lo(value):
    hi = value.astype(BF)
    return hi, (value - hi.astype(F32)).astype(BF)


def mod4(value):
    return lax.rem(value + 8, 4)


def lane_piece(value, at):
    out = jnp.zeros(value.shape[:-1] + (HD,), value.dtype)
    for i in range(3):
        out = jnp.where(at == i, value[..., i * HD : (i + 1) * HD], out)
    return out


def norm_kernel(
    meta, xa0, xa1, xa2, xa3, xb0, xb1, xb2, xb3, mod,
    scaled, normed_own, inv_own, normed_piece, inv_all,
):
    zhi, zlo, core = meta[1], meta[3], meta[4]
    place = zhi * 4 + zlo
    own_far = jnp.where(core == 0, -2, 2)
    sources = []
    for refs, side, far in (
        ((xa0, xa1, xa2, xa3), core, own_far),
        ((xb0, xb1, xb2, xb3), 1 - core, -own_far),
    ):
        for ref, offset in zip(refs, (0, -1, 1, far)):
            at = lax.rem(place + offset + 16, 16)
            sources.append((ref, at // 4, lax.rem(at, 4) * 2 + side))

    rows = 32

    def chunk(turn, carry):
        t = turn // (TILE // rows)
        start = lax.rem(turn, TILE // rows) * rows
        span = pl.ds(pl.multiple_of(start, rows), rows)

        def load(source):
            ref, z, g = source
            d = mod4(z - t)
            spans = [pl.ds(pl.multiple_of(start + i * TILE, rows), rows) for i in range(3)]
            return jnp.concatenate([ref[d, at, :] for at in spans], axis=1).astype(F32)

        total = jnp.zeros((rows, WIDTH), F32)
        for source in sources:
            total = total + load(source)
        mean = jnp.sum(total, axis=1, keepdims=True) * (1.0 / FEATS)
        square = jnp.zeros((rows, WIDTH), F32)
        for source in sources:
            centred = load(source) - mean
            square = square + centred * centred
        inv = lax.rsqrt(jnp.sum(square, axis=1, keepdims=True) * (1.0 / FEATS) + EPS)
        for source in sources:
            normed = (load(source) - mean) * inv
            scaled[source[2], t, span, :] = (normed * (1.0 + mod[1, source[2]])).astype(BF)
        normed = (load(sources[0]) - mean) * inv
        normed_piece[t, span, :] = lane_piece(normed, zhi)
        inv_all[t, span, :] = jnp.broadcast_to(inv, (rows, HD))

        @pl.when(t == zhi)
        def _():
            normed_own[span, :] = normed
            inv_own[span, :] = jnp.broadcast_to(inv, (rows, HD))

        return carry

    lax.fori_loop(0, 4 * (TILE // rows), chunk, 0)


def proj_kernel(
    meta, nscr, w0, w1, w2, w3, mod, q_gain, k_gain,
    qkv, proj, wk, ws, vec, wc,
):
    step, zhi, y, core = meta[0], meta[1], meta[2], meta[4]
    for ref, at_step in zip((w0, w1, w2, w3), PLACES):
        s = mod4(step + at_step)
        for sy, at_y in enumerate(PLACES):
            yy = mod4(y + at_y)
            for d in range(4):
                zh = mod4(zhi - d)
                for part in range(3):
                    wc[s * 2 + zh // 2, lax.rem(zh, 2) * 4 + yy, :, part * HD : (part + 1) * HD] = (
                        ref[sy, d, part * 48 : (part + 1) * 48, :]
                    )
    for r in range(4):
        wk[r] = wc[2 * r + core]
        ws[r] = wc[2 * r + 1 - core]

    acc = jnp.zeros((4 * TILE, WIDTH), F32)
    flat = jnp.zeros((16, WIDTH), F32)
    for g in range(8):
        w_g = wc[g].reshape(WIDTH, WIDTH)
        acc = acc + nn(nscr[g].reshape(4 * TILE, WIDTH), w_g)
        scale_hi, scale_lo = hi_lo(1.0 + mod[1, g])
        shift_hi, shift_lo = hi_lo(mod[0, g])
        four = jnp.concatenate([scale_hi, scale_lo, shift_hi, shift_lo], axis=0)
        lhs = jnp.concatenate([four, jnp.zeros((12, WIDTH), BF)], axis=0)
        flat = flat + nn(lhs, w_g)
    vec[...] = flat
    proj[...] = acc + (flat[2:3] + flat[3:4])
    for t in range(4):
        span = slice(t * TILE, (t + 1) * TILE)
        q = proj[span, 0:HD]
        k = proj[span, HD : 2 * HD]
        q_inv = lax.rsqrt(jnp.mean(q * q, axis=1, keepdims=True) + EPS)
        k_inv = lax.rsqrt(jnp.mean(k * k, axis=1, keepdims=True) + EPS)
        qkv[t, :, 0:HD] = (q * q_inv * q_gain[...]).astype(BF)
        qkv[t, :, HD : 2 * HD] = (k * k_inv * k_gain[...]).astype(BF)
        qkv[t, :, 2 * HD : 3 * HD] = proj[span, 2 * HD : 3 * HD].astype(BF)


def norm_back(raw, gain, grad):
    inv = lax.rsqrt(jnp.mean(raw * raw, axis=1, keepdims=True) + EPS)
    scaled = grad * gain
    dot = jnp.mean(scaled * raw, axis=1, keepdims=True)
    return inv * (scaled - raw * (inv * inv * dot))


def sweep_kernel(
    meta, nb, k0, k1, k2, k3, proj, vec, q_gain, k_gain, *rest
):
    out, tiles, ups = rest[-3:]
    zhi, y = meta[1], meta[2]
    for ref, offset in zip((k0, k1, k2, k3), PLACES):
        yy = mod4(y + offset)
        for z in range(4):
            tiles[z * 4 + yy] = ref[z]
    if len(rest) > 4:
        for ref, offset in zip(rest[:4], PLACES):
            for d in range(4):
                ups[mod4(zhi - d) * 4 + mod4(y + offset)] = ref[d, 144:272, :]
    else:
        for yy in range(4):
            for z in range(4):
                ups[z * 4 + yy] = rest[0][yy, z]

    m1_hi, m1_lo = hi_lo(vec[0:1] + vec[1:2])
    m1 = jnp.concatenate([m1_hi, m1_lo, jnp.zeros((14, WIDTH), BF)], axis=0)
    ones = jnp.ones((16, WIDTH), BF)
    s0 = vec[2:3] + vec[3:4]

    def k_of(t):
        return tiles[t, :, HD : 2 * HD]

    def v_of(t):
        return tiles[t, :, 2 * HD : 3 * HD]

    def own(jz, carry):
        j = jz * 4 + y
        near = (nb[1, j], nb[2, j])
        d_k = jnp.zeros((TILE, HD), F32)
        d_v = jnp.zeros((TILE, HD), F32)
        d_q = None
        for slot in range(3):
            if slot == 0:
                i = j
                keys = (j, near[0], near[1])
            else:
                i = near[slot - 1]
                keys = (j, i, nb[1, i] + nb[2, i] - j)
            q = tiles[i, :, 0:HD]
            up = ups[i]
            k_all = jnp.concatenate([k_of(t) for t in keys], axis=0)
            v_all = jnp.concatenate([v_of(t) for t in keys], axis=0)
            expo = jnp.exp(nt(q, k_all))
            prob = expo * (1.0 / jnp.sum(expo, axis=1, keepdims=True))
            prob_b = prob.astype(BF)
            dprob = nt(up, v_all)
            delta = jnp.sum(prob_b.astype(F32) * dprob, axis=1, keepdims=True)
            if slot == 0:
                dscore = (prob * (dprob - delta)).astype(BF)
                d_q = nn(dscore, k_all)
                dscore = dscore[:, 0:TILE]
            else:
                dscore = (prob[:, 0:TILE] * (dprob[:, 0:TILE] - delta)).astype(BF)
            d_k = d_k + tn(dscore, q)
            d_v = d_v + tn(prob_b[:, 0:TILE], up)
        start = pl.multiple_of(jz * TILE, TILE)
        raw = proj[pl.ds(start, TILE), :]
        d_q = norm_back(raw[:, 0:HD], q_gain[...], d_q)
        d_k = norm_back(raw[:, HD : 2 * HD], k_gain[...], d_k)
        d_all = jnp.concatenate([d_q, d_k, d_v], axis=1).astype(BF)
        out[pl.ds(start, TILE), :] = d_all
        first = nt(m1, d_all)
        prod_hi, prod_lo = hi_lo(d_all.astype(F32) * (raw - s0))
        second = nt(ones, prod_hi) + nt(ones, prod_lo)
        row = jnp.concatenate(
            [first[0:1] + first[1:2], second[0:1], jnp.zeros((1, TILE), F32)], axis=1
        )
        at = lax.broadcasted_iota(jnp.int32, (8, WIDTH), 0)
        return carry + jnp.where(at == jz, row, 0.0)

    stats = lax.fori_loop(0, 4, own, jnp.zeros((8, WIDTH), F32))
    out[4 * TILE : 4 * TILE + 16, :] = jnp.concatenate(hi_lo(stats), axis=0)


def stats_of(ref, start):
    both = ref[start : start + 16, :].astype(F32)
    return both[0:8] + both[8:16]


def feature_kernel(meta, own, other, wk, wr, o0, o1, o2, o3):
    zlo = meta[3]
    stats = jnp.concatenate(hi_lo(stats_of(own, 4 * TILE) + stats_of(other, 4 * TILE)), axis=0)
    for offset, o in enumerate((o0, o1, o2, o3)):
        r = mod4(zlo + offset)
        value = nt(own[0 : 4 * TILE, :], wk[r].reshape(WIDTH, WIDTH))
        value = value + nt(other[0 : 4 * TILE, :], wr[r].reshape(WIDTH, WIDTH))
        o[0 : 4 * TILE, :] = value.astype(BF)
        o[4 * TILE : 4 * TILE + 16, :] = stats


def window_kernel(meta, a0, a1, a2, a3, out):
    refs = (a0, a1, a2, a3)
    stats = stats_of(a0, 4 * TILE)
    for a in refs[1:]:
        stats = stats + stats_of(a, 4 * TILE)
    at = lax.broadcasted_iota(jnp.int32, (8, WIDTH), 0)
    for t in range(4):
        span = slice(t * TILE, (t + 1) * TILE)
        value = a0[span, :].astype(F32)
        for a in refs[1:]:
            value = value + a[span, :].astype(F32)
        out[t, 0:TILE, :] = value.astype(BF)
        row = jnp.sum(jnp.where(at == t, stats, 0.0), axis=0, keepdims=True)
        out[t, TILE : TILE + 16, :] = jnp.concatenate(
            hi_lo(jnp.broadcast_to(row, (8, WIDTH))), axis=0
        )


def window_piece_kernel(meta, a0, a1, a2, a3, o0, o1, o2, o3):
    zhi = meta[1]
    refs = (a0, a1, a2, a3)
    stats = stats_of(a0, 4 * TILE)
    for a in refs[1:]:
        stats = stats + stats_of(a, 4 * TILE)
    stats = jnp.concatenate(hi_lo(jnp.concatenate([stats[0:4, 0:TILE], stats[0:4, TILE : 2 * TILE]], axis=0)), axis=0)
    for t in range(4):
        span = slice(t * TILE, (t + 1) * TILE)
        value = a0[span, :].astype(F32)
        for a in refs[1:]:
            value = value + a[span, :].astype(F32)
        for d, o in enumerate((o0, o1, o2, o3)):
            o[span, :] = lane_piece(value, mod4(zhi + d)).astype(BF)
    for d, o in enumerate((o0, o1, o2, o3)):
        keep = jnp.where(mod4(zhi + d) == 3, 0.0, 1.0)
        o[4 * TILE : 4 * TILE + 16, :] = (stats.astype(F32) * keep).astype(BF)


def term_piece_kernel(meta, a0, a1, a2, a3, normed, inv, mod, sent):
    group = meta[3] * 2 + meta[4]
    stats = stats_of(a0, 4 * TILE)
    for a in (a1, a2, a3):
        stats = stats + stats_of(a, 4 * TILE)
    scale = 1.0 + lane_piece(mod[1, group], meta[1])
    for t in range(4):
        span = slice(t * TILE, (t + 1) * TILE)
        grad = a0[span, :].astype(F32)
        for a in (a1, a2, a3):
            grad = grad + a[span, :].astype(F32)
        value = inv[t] * (grad * scale - column(stats[t : t + 1]) - normed[t] * column(stats[4 + t : 5 + t]))
        sent[t] = value.astype(BF)


def upstream_piece_kernel(meta, ids, coeffs, first, mod, t1, t2, t3, out):
    group = meta[3] * 2 + meta[4]
    after, decay, weight = decays(meta, ids, coeffs)
    gate = lane_piece(mod[2, group], meta[1]) * weight
    for t in range(4):
        later = t1[t].astype(F32) + t2[t].astype(F32) * after[0] + t3[t].astype(F32) * (after[0] * after[1])
        out[t] = (first[mod4(meta[1] - t), 144:272, :].astype(F32) + gate * later).astype(BF)


def column(row):
    return jnp.transpose(jnp.broadcast_to(row * (1.0 / FEATS), (TILE, TILE)))


def term_kernel(meta, got, normed, inv, mod, term, sent, moments):
    group = meta[3] * 2 + meta[4]
    grad = got[0, 0:TILE, :].astype(F32)
    stats = stats_of(got.at[0], TILE)
    for i in (1, 2, 3):
        grad = grad + got[i, 0:TILE, :].astype(F32)
        stats = stats + stats_of(got.at[i], TILE)
    first = stats[0:1, 0:TILE]
    second = stats[0:1, TILE : 2 * TILE]
    moments[...] = jnp.concatenate([first, second], axis=0) * (FEATS**-0.5)

    def wide(value):
        return jnp.concatenate([value] * 3, axis=1)

    du = grad * (1.0 + mod[1, group])
    value = wide(inv[...]) * (du - wide(column(first)) - normed[...] * wide(column(second)))
    term[...] = value
    sent[...] = value.astype(BF)


def decays(meta, ids, coeffs):
    step = meta[0]
    after = []
    for ahead in (1, 2, 3):
        at = jnp.minimum(step + ahead, 3)
        after.append(jnp.where(step + ahead <= 3, coeffs[0, ids[at]], 1.0))
    return after, coeffs[0, ids[step]], coeffs[1, ids[step]]


def lam_of(meta, ids, coeffs, cot, terms):
    after, decay, weight = decays(meta, ids, coeffs)
    lam = cot[...] * (after[0] * after[1] * after[2])
    for ref, factor in zip(terms, (1.0, after[0], after[0] * after[1])):
        lam = lam + ref[...].astype(F32) * factor
    return lam, decay, weight


def cut_kernel(meta, ids, coeffs, cot, mod, w, x, o0, o1, o2, o3):
    zhi = meta[1]
    group = meta[3] * 2 + meta[4]
    lam, decay, weight = lam_of(meta, ids, coeffs, cot, ())
    up = mod[2, group] * weight * lam
    for d, o in enumerate((o0, o1, o2, o3)):
        at = mod4(zhi + d)
        for part in range(3):
            o[part * 48 : (part + 1) * 48, :] = lane_piece(w[part].astype(F32), at).astype(BF)
        o[144:272, :] = lane_piece(up, at).astype(BF)
        if d != 2:
            for i in range(3):
                o[272 + i * TILE : 272 + (i + 1) * TILE, :] = x[:, i * HD : (i + 1) * HD]


def adjoint_kernel(meta, ids, coeffs, cot, term, t1, t2, t3, out):
    lam, decay, weight = lam_of(meta, ids, coeffs, cot, (t1, t2, t3))
    out[...] = decay * lam + term[...]


def turn(value, axis, offset):
    return lax.ppermute(value, axis, [(i, (i + offset) % 4) for i in range(4)])


def ring4(value, axis):
    return [value] + [turn(value, axis, -offset) for offset in PLACES[1:]]


def hand_on(before, after, axis):
    pairs = []
    for i in range(4):
        pairs.append((2 * i, 2 * ((i - 1) % 4)))
        pairs.append((2 * i + 1, 2 * ((i + 1) % 4) + 1))
    return lax.ppermute(jnp.where(lax.axis_index("core") == 0, after, before), (axis, "core"), pairs)


def relayed(value, axis):
    before, after = turn(value, axis, 1), turn(value, axis, -1)
    return [value, before, after, hand_on(before, after, axis)]


def to_earlier(value):
    return [lax.ppermute(value, "step", [(j, j - d) for j in range(d, 4)]) for d in (1, 2, 3)]


def relay_hop(value):
    pairs = []
    for i in range(4):
        pairs.append((2 * i, 2 * ((i + 1) % 4)))
        pairs.append((2 * i + 1, 2 * ((i - 1) % 4) + 1))
    return lax.ppermute(value, ("zhi", "core"), pairs)


def exchange_zhi(blocks):
    half_way = relay_hop(blocks[2])
    one, three = turn(blocks[1], "zhi", 1), turn(blocks[3], "zhi", 3)
    return [blocks[0], one, relay_hop(half_way), three]


def along_z(value, offset):
    return lax.ppermute(value, ("zhi", "zlo"), [(i, (i + offset) % 16) for i in range(16)])


def far_z(value):
    pairs = []
    for i in range(16):
        pairs.append((2 * i, 2 * ((i + 2) % 16)))
        pairs.append((2 * i + 1, 2 * ((i - 2) % 16) + 1))
    return lax.ppermute(value, ("zhi", "zlo", "core"), pairs)


def other_core(value):
    return lax.ppermute(value, "core", [(0, 1), (1, 0)])


def shards(states, modulation, cotangent, w_qkv, q_gain, k_gain, step_ids, coeffs, neighbours):
    zhi = lax.axis_index("zhi")
    meta = jnp.stack([lax.axis_index(a) for a in ("step", "zhi", "y", "zlo", "core")]).astype(jnp.int32)
    coeffs, neighbours = coeffs.T, neighbours.T
    mod = modulation.reshape(3, 8, 1, WIDTH)
    gq = (q_gain / jnp.sqrt(jnp.float32(HD))).reshape(1, HD)
    gk = k_gain.reshape(1, HD)

    tall = 272 + 3 * TILE
    own, ahead, across, back = call(
        cut_kernel,
        [sds((tall, HD), BF), sds((tall, HD), BF), sds((272, HD), BF), sds((tall, HD), BF)],
        (meta, step_ids, coeffs, cotangent, mod, jnp.transpose(w_qkv, (1, 0, 2)), states[0]),
        3,
    )
    half_way = relay_hop(across)
    before, after = turn(ahead, "zhi", 1), turn(back, "zhi", -1)
    passed = jnp.where(lax.axis_index("core") == 0, before[272:], after[272:])
    far = relay_hop(jnp.concatenate([half_way, passed], axis=0))
    got = [own, before, far, after]

    x_tiles = jnp.stack([g[272:] for g in got])
    xa = [x_tiles, along_z(x_tiles, 1), along_z(x_tiles, -1), far_z(x_tiles)]

    own_rows = jnp.stack([g[0:272] for g in got])
    before, after = turn(own_rows, "y", 1), turn(own_rows, "y", -1)
    before, after, xa[1] = lax.optimization_barrier((before, after, xa[1]))
    rows_y = [own_rows, before, after, hand_on(before, after, "y")]
    w_y = jnp.stack([r[:, 0:144] for r in rows_y])
    w_y, xa[2], xa[3] = lax.optimization_barrier((w_y, xa[2], xa[3]))
    before, after = turn(w_y, "step", 1), turn(w_y, "step", -1)
    xb = [other_core(a) for a in xa]

    tokens = 4 * TILE
    scaled, normed, inv, normed_piece, inv_all = call(
        norm_kernel,
        [
            sds((8, 4, TILE, WIDTH), BF),
            sds((TILE, WIDTH), F32),
            sds((TILE, HD), F32),
            sds((4, TILE, HD), F32),
            sds((4, TILE, HD), F32),
        ],
        (meta, *xa, *xb, mod),
        1,
        (),
        0,
        16,
    )
    before, after, scaled = lax.optimization_barrier((before, after, scaled))
    wg = [w_y, before, after, hand_on(before, after, "step")]
    qkv, proj, wk, ws, vec = call(
        proj_kernel,
        [
            sds((4, TILE, WIDTH), BF),
            sds((tokens, WIDTH), F32),
            sds((4, 8, 48, WIDTH), BF),
            sds((4, 8, 48, WIDTH), BF),
            sds((16, WIDTH), F32),
        ],
        (meta, scaled, *wg, mod, gq, gk),
        1,
        [pltpu.VMEM((8, 8, 48, WIDTH), BF)],
        2 * tokens * FEATS * WIDTH,
        24,
    )
    wr = other_core(ws)
    all_qkv = relayed(qkv, "y")

    all_up = rows_y
    for sweep in range(SWEEPS):
        (dproj,) = call(
            sweep_kernel,
            [sds((tokens + 16, WIDTH), BF)],
            (meta, neighbours, *all_qkv, proj, vec, gq, gk, *all_up),
            2,
            [pltpu.VMEM((16, TILE, WIDTH), BF), pltpu.VMEM((16, TILE, HD), BF)],
            400 * 1000 * 1000,
            16,
        )
        parts = call(
            feature_kernel,
            [sds((tokens + 16, WIDTH), BF)] * 4,
            (meta, dproj, other_core(dproj), wk, wr),
            1,
            (),
            2 * tokens * FEATS * WIDTH,
            16,
        )
        near = [parts[0], along_z(parts[1], 1), far_z(parts[2]), along_z(parts[3], -1)]
        if sweep + 1 < SWEEPS:
            blocks = call(window_piece_kernel, [sds((tokens + 16, HD), BF)] * 4, (meta, *near), 1)
            (sent,) = call(
                term_piece_kernel,
                [sds((4, TILE, HD), BF)],
                (meta, *exchange_zhi(blocks), normed_piece, inv_all, mod),
                1,
            )
            (up,) = call(
                upstream_piece_kernel,
                [sds((4, TILE, HD), BF)],
                (meta, step_ids, coeffs, rows_y[0], mod, *to_earlier(sent)),
                3,
            )
            all_up = (lax.all_gather(up, "y"),)
    (blocks,) = call(window_kernel, [sds((4, TILE + 16, WIDTH), BF)], (meta, *near), 1)
    got = lax.all_to_all(blocks, "zhi", 0, 0)
    term, sent, moments = call(
        term_kernel,
        [sds((TILE, WIDTH), F32), sds((TILE, WIDTH), BF), sds((2, TILE), F32)],
        (meta, got, normed, inv, mod),
        1,
    )
    (adjoint,) = call(
        adjoint_kernel,
        [sds((TILE, WIDTH), F32)],
        (meta, step_ids, coeffs, cotangent, term, *to_earlier(sent)),
        3,
    )
    return adjoint[None], moments[None]


def solution(mesh):
    fine = Mesh(mesh.devices.reshape(4, 4, 4, 4, 2), ("step", "zhi", "y", "zlo", "core"))
    blk, head = ("zhi", "y"), ("zlo", "core")
    in_specs = (
        P("step", blk, head),
        P("step", None, None),
        P(blk, head),
        P(("step",) + blk, None, head),
        P(),
        P(),
        P(),
        P(),
        P(),
    )
    out_specs = (P("step", blk, head), P("step", None, blk))
    return jax.shard_map(shards, mesh=fine, in_specs=in_specs, out_specs=out_specs, check_vma=False)
```

```python
import jax
import jax.numpy as jnp
from jax import lax
from jax.experimental import pallas as pl
from jax.experimental.pallas import tpu as pltpu
from jax.sharding import Mesh
from jax.sharding import PartitionSpec as P

HD = 128
TILE = 128
WIDTH = 384
FEATS = 3072
SWEEPS = 2
EPS = 1e-06
BF = jnp.bfloat16
F32 = jnp.float32
MIB = 1024 * 1024
PLACES = (0, -1, 1, 2)

VM = pl.BlockSpec(memory_space=pltpu.VMEM)
SM = pl.BlockSpec(memory_space=pltpu.SMEM)


def call(body, outs, args, smem, scratch=(), flops=0, grant=8, far=0):
    specs = [SM if i < smem else VM for i in range(len(args))]
    specs[smem : smem + far] = [pl.BlockSpec(memory_space=pl.ANY)] * far
    moved = sum(a.size * a.dtype.itemsize for a in args) + sum(
        o.size * o.dtype.itemsize for o in outs
    )
    return pl.pallas_call(
        body,
        out_shape=tuple(outs),
        in_specs=specs,
        out_specs=tuple([VM] * len(outs)),
        scratch_shapes=list(scratch),
        compiler_params=pltpu.CompilerParams(vmem_limit_bytes=grant * MIB),
        cost_estimate=pl.CostEstimate(flops=flops, bytes_accessed=moved, transcendentals=0),
    )(*args)


def sds(shape, dtype):
    return jax.ShapeDtypeStruct(shape, dtype)


def nt(a, b):
    return lax.dot_general(a, b, (((1,), (1,)), ((), ())), preferred_element_type=F32)


def tn(a, b):
    return lax.dot_general(a, b, (((0,), (0,)), ((), ())), preferred_element_type=F32)


def nn(a, b):
    return jnp.dot(a, b, preferred_element_type=F32)


def hi_lo(value):
    hi = value.astype(BF)
    return hi, (value - hi.astype(F32)).astype(BF)


def mod4(value):
    return lax.rem(value + 8, 4)


def lane_piece(value, at):
    out = jnp.zeros(value.shape[:-1] + (HD,), value.dtype)
    for i in range(3):
        out = jnp.where(at == i, value[..., i * HD : (i + 1) * HD], out)
    return out


def norm_kernel(
    meta, xa0, xa1, xa2, xa3, xb0, xb1, xb2, xb3, mod,
    scaled, normed_own, inv_own, normed_piece, inv_all,
):
    zhi, zlo, core = meta[1], meta[3], meta[4]
    place = zhi * 4 + zlo
    own_far = jnp.where(core == 0, -2, 2)
    sources = []
    for refs, side, far in (
        ((xa0, xa1, xa2, xa3), core, own_far),
        ((xb0, xb1, xb2, xb3), 1 - core, -own_far),
    ):
        for ref, offset in zip(refs, (0, -1, 1, far)):
            at = lax.rem(place + offset + 16, 16)
            sources.append((ref, at // 4, lax.rem(at, 4) * 2 + side))

    rows = 32

    def chunk(turn, carry):
        t = turn // (TILE // rows)
        start = lax.rem(turn, TILE // rows) * rows
        span = pl.ds(pl.multiple_of(start, rows), rows)

        def load(source):
            ref, z, g = source
            d = mod4(z - t)
            return ref[d, span, :].astype(F32)

        total = jnp.zeros((rows, WIDTH), F32)
        for source in sources:
            total = total + load(source)
        mean = jnp.sum(total, axis=1, keepdims=True) * (1.0 / FEATS)
        square = jnp.zeros((rows, WIDTH), F32)
        for source in sources:
            centred = load(source) - mean
            square = square + centred * centred
        inv = lax.rsqrt(jnp.sum(square, axis=1, keepdims=True) * (1.0 / FEATS) + EPS)
        for source in sources:
            normed = (load(source) - mean) * inv
            scaled[source[2], t, span, :] = (normed * (1.0 + mod[1, source[2]])).astype(BF)
        normed = (load(sources[0]) - mean) * inv
        normed_piece[t, span, :] = lane_piece(normed, zhi)
        inv_all[t, span, :] = jnp.broadcast_to(inv, (rows, HD))

        @pl.when(t == zhi)
        def _():
            normed_own[span, :] = normed
            inv_own[span, :] = jnp.broadcast_to(inv, (rows, HD))

        return carry

    lax.fori_loop(0, 4 * (TILE // rows), chunk, 0)


def proj_kernel(
    meta, nscr, wg, p0, p1, p2, p3, mod, q_gain, k_gain,
    qkvu, proj, wk, ws, vec, wc,
):
    zhi, core = meta[1], meta[4]
    for d, piece in enumerate((p0, p1, p2, p3)):
        zh = mod4(zhi - d)
        qkvu[zh, :, WIDTH : WIDTH + HD] = piece[144:272, :]
        for sy in range(16):
            for part in range(3):
                wc[(sy // 4) * 2 + zh // 2, lax.rem(zh, 2) * 4 + sy % 4, :, part * HD : (part + 1) * HD] = (
                    wg[sy, d, part * 48 : (part + 1) * 48, :]
                )
    for r in range(4):
        wk[r] = wc[2 * r + core]
        ws[r] = wc[2 * r + 1 - core]

    acc = jnp.zeros((4 * TILE, WIDTH), F32)
    flat = jnp.zeros((16, WIDTH), F32)
    for g in range(8):
        w_g = wc[g].reshape(WIDTH, WIDTH)
        acc = acc + nn(nscr[g].reshape(4 * TILE, WIDTH), w_g)
        scale_hi, scale_lo = hi_lo(1.0 + mod[1, g])
        shift_hi, shift_lo = hi_lo(mod[0, g])
        four = jnp.concatenate([scale_hi, scale_lo, shift_hi, shift_lo], axis=0)
        lhs = jnp.concatenate([four, jnp.zeros((12, WIDTH), BF)], axis=0)
        flat = flat + nn(lhs, w_g)
    vec[...] = flat
    proj[...] = acc + (flat[2:3] + flat[3:4])
    for t in range(4):
        span = slice(t * TILE, (t + 1) * TILE)
        q = proj[span, 0:HD]
        k = proj[span, HD : 2 * HD]
        q_inv = lax.rsqrt(jnp.mean(q * q, axis=1, keepdims=True) + EPS)
        k_inv = lax.rsqrt(jnp.mean(k * k, axis=1, keepdims=True) + EPS)
        qkvu[t, :, 0:HD] = (q * q_inv * q_gain[...]).astype(BF)
        qkvu[t, :, HD : 2 * HD] = (k * k_inv * k_gain[...]).astype(BF)
        qkvu[t, :, 2 * HD : 3 * HD] = proj[span, 2 * HD : 3 * HD].astype(BF)


def norm_back(raw, gain, grad):
    inv = lax.rsqrt(jnp.mean(raw * raw, axis=1, keepdims=True) + EPS)
    scaled = grad * gain
    dot = jnp.mean(scaled * raw, axis=1, keepdims=True)
    return inv * (scaled - raw * (inv * inv * dot))


def sweep_kernel(
    meta, nb, k0, k1, k2, k3, proj, vec, q_gain, k_gain, *rest
):
    first_sweep = len(rest) == 4
    probs = rest[1]
    out = rest[0] if first_sweep else rest[2]
    tiles, ups = rest[-2:]
    y = meta[2]
    for ref, offset in zip((k0, k1, k2, k3), PLACES):
        yy = mod4(y + offset)
        for z in range(4):
            tiles[z * 4 + yy] = ref[z, :, 0:WIDTH]
            if first_sweep:
                ups[z * 4 + yy] = ref[z, :, WIDTH : WIDTH + HD]
    if not first_sweep:
        for yy in range(4):
            for z in range(4):
                ups[z * 4 + yy] = rest[0][yy, z]

    m1_hi, m1_lo = hi_lo(vec[0:1] + vec[1:2])
    m1 = jnp.concatenate([m1_hi, m1_lo, jnp.zeros((14, WIDTH), BF)], axis=0)
    ones = jnp.ones((16, WIDTH), BF)
    s0 = vec[2:3] + vec[3:4]

    def k_of(t):
        return tiles[t, :, HD : 2 * HD]

    def v_of(t):
        return tiles[t, :, 2 * HD : 3 * HD]

    def own(jz, carry):
        j = jz * 4 + y
        near = (nb[1, j], nb[2, j])
        d_k = jnp.zeros((TILE, HD), F32)
        d_v = jnp.zeros((TILE, HD), F32)
        d_q = None
        for slot in range(3):
            if slot == 0:
                i = j
                keys = (j, near[0], near[1])
            else:
                i = near[slot - 1]
                keys = (j, i, nb[1, i] + nb[2, i] - j)
            q = tiles[i, :, 0:HD]
            up = ups[i]
            k_all = jnp.concatenate([k_of(t) for t in keys], axis=0)
            v_all = jnp.concatenate([v_of(t) for t in keys], axis=0)
            if first_sweep:
                expo = jnp.exp(nt(q, k_all))
                prob = expo * (1.0 / jnp.sum(expo, axis=1, keepdims=True))
                probs[jz, slot] = prob
            else:
                prob = probs[jz, slot]
            prob_b = prob.astype(BF)
            dprob = nt(up, v_all)
            delta = jnp.sum(prob_b.astype(F32) * dprob, axis=1, keepdims=True)
            if slot == 0:
                dscore = (prob * (dprob - delta)).astype(BF)
                d_q = nn(dscore, k_all)
                dscore = dscore[:, 0:TILE]
            else:
                dscore = (prob[:, 0:TILE] * (dprob[:, 0:TILE] - delta)).astype(BF)
            d_k = d_k + tn(dscore, q)
            d_v = d_v + tn(prob_b[:, 0:TILE], up)
        start = pl.multiple_of(jz * TILE, TILE)
        raw = proj[pl.ds(start, TILE), :]
        d_q = norm_back(raw[:, 0:HD], q_gain[...], d_q)
        d_k = norm_back(raw[:, HD : 2 * HD], k_gain[...], d_k)
        d_all = jnp.concatenate([d_q, d_k, d_v], axis=1).astype(BF)
        out[pl.ds(start, TILE), :] = d_all
        first = nt(m1, d_all)
        prod_hi, prod_lo = hi_lo(d_all.astype(F32) * (raw - s0))
        second = nt(ones, prod_hi) + nt(ones, prod_lo)
        row = jnp.concatenate(
            [first[0:1] + first[1:2], second[0:1], jnp.zeros((1, TILE), F32)], axis=1
        )
        at = lax.broadcasted_iota(jnp.int32, (8, WIDTH), 0)
        return carry + jnp.where(at == jz, row, 0.0)

    stats = lax.fori_loop(0, 4, own, jnp.zeros((8, WIDTH), F32))
    out[4 * TILE : 4 * TILE + 16, :] = jnp.concatenate(hi_lo(stats), axis=0)


def stats_of(ref, start):
    both = ref[start : start + 16, :].astype(F32)
    return both[0:8] + both[8:16]


def feature_kernel(meta, own, other, wk, wr, o0, o1, o2, o3):
    zlo = meta[3]
    stats = jnp.concatenate(hi_lo(stats_of(own, 4 * TILE) + stats_of(other, 4 * TILE)), axis=0)
    for offset, o in enumerate((o0, o1, o2, o3)):
        r = mod4(zlo + offset)
        value = nt(own[0 : 4 * TILE, :], wk[r].reshape(WIDTH, WIDTH))
        value = value + nt(other[0 : 4 * TILE, :], wr[r].reshape(WIDTH, WIDTH))
        o[0 : 4 * TILE, :] = value.astype(BF)
        o[4 * TILE : 4 * TILE + 16, :] = stats


def window_kernel(meta, a0, a1, a2, a3, o0, o1, o2, o3):
    zhi = meta[1]
    refs = (a0, a1, a2, a3)
    stats = stats_of(a0, 4 * TILE)
    for a in refs[1:]:
        stats = stats + stats_of(a, 4 * TILE)
    at = lax.broadcasted_iota(jnp.int32, (8, WIDTH), 0)
    for d, o in enumerate((o0, o1, o2, o3)):
        t = mod4(zhi + d)
        span = pl.ds(pl.multiple_of(t * TILE, TILE), TILE)
        value = a0[span, :].astype(F32)
        for a in refs[1:]:
            value = value + a[span, :].astype(F32)
        o[0:TILE, :] = value.astype(BF)
        row = jnp.sum(jnp.where(at == t, stats, 0.0), axis=0, keepdims=True)
        o[TILE : TILE + 16, :] = jnp.concatenate(
            hi_lo(jnp.broadcast_to(row, (8, WIDTH))), axis=0
        )


def window_piece_kernel(meta, a0, a1, a2, a3, o0, o1, o2, o3):
    zhi = meta[1]
    refs = (a0, a1, a2, a3)
    stats = stats_of(a0, 4 * TILE)
    for a in refs[1:]:
        stats = stats + stats_of(a, 4 * TILE)
    stats = jnp.concatenate(hi_lo(jnp.concatenate([stats[0:4, 0:TILE], stats[0:4, TILE : 2 * TILE]], axis=0)), axis=0)
    for t in range(4):
        span = slice(t * TILE, (t + 1) * TILE)
        value = a0[span, :].astype(F32)
        for a in refs[1:]:
            value = value + a[span, :].astype(F32)
        for d, o in enumerate((o0, o1, o2, o3)):
            o[span, :] = lane_piece(value, mod4(zhi + d)).astype(BF)
    for d, o in enumerate((o0, o1, o2, o3)):
        keep = jnp.where(mod4(zhi + d) == 3, 0.0, 1.0)
        o[4 * TILE : 4 * TILE + 16, :] = (stats.astype(F32) * keep).astype(BF)


def term_piece_kernel(meta, a0, a1, a2, a3, normed, inv, mod, sent):
    group = meta[3] * 2 + meta[4]
    stats = stats_of(a0, 4 * TILE)
    for a in (a1, a2, a3):
        stats = stats + stats_of(a, 4 * TILE)
    scale = 1.0 + lane_piece(mod[1, group], meta[1])
    for t in range(4):
        span = slice(t * TILE, (t + 1) * TILE)
        grad = a0[span, :].astype(F32)
        for a in (a1, a2, a3):
            grad = grad + a[span, :].astype(F32)
        value = inv[t] * (grad * scale - column(stats[t : t + 1]) - normed[t] * column(stats[4 + t : 5 + t]))
        sent[t] = value.astype(BF)


def upstream_piece_kernel(meta, ids, coeffs, qkvu, mod, t1, t2, t3, out):
    group = meta[3] * 2 + meta[4]
    after, decay, weight = decays(meta, ids, coeffs)
    gate = lane_piece(mod[2, group], meta[1]) * weight
    for t in range(4):
        later = t1[t].astype(F32) + t2[t].astype(F32) * after[0] + t3[t].astype(F32) * (after[0] * after[1])
        out[t] = (qkvu[t, :, WIDTH : WIDTH + HD].astype(F32) + gate * later).astype(BF)


def column(row):
    return jnp.transpose(jnp.broadcast_to(row * (1.0 / FEATS), (TILE, TILE)))


def term_kernel(meta, a0, a1, a2, a3, normed, inv, mod, term, sent, moments):
    group = meta[3] * 2 + meta[4]
    grad = a0[0:TILE, :].astype(F32)
    stats = stats_of(a0, TILE)
    for a in (a1, a2, a3):
        grad = grad + a[0:TILE, :].astype(F32)
        stats = stats + stats_of(a, TILE)
    first = stats[0:1, 0:TILE]
    second = stats[0:1, TILE : 2 * TILE]
    moments[...] = jnp.concatenate([first, second], axis=0) * (FEATS**-0.5)

    def wide(value):
        return jnp.concatenate([value] * 3, axis=1)

    du = grad * (1.0 + mod[1, group])
    value = wide(inv[...]) * (du - wide(column(first)) - normed[...] * wide(column(second)))
    term[...] = value
    sent[...] = value.astype(BF)


def decays(meta, ids, coeffs):
    step = meta[0]
    after = []
    for ahead in (1, 2, 3):
        at = jnp.minimum(step + ahead, 3)
        after.append(jnp.where(step + ahead <= 3, coeffs[0, ids[at]], 1.0))
    return after, coeffs[0, ids[step]], coeffs[1, ids[step]]


def lam_of(meta, ids, coeffs, cot, terms):
    after, decay, weight = decays(meta, ids, coeffs)
    lam = cot[...] * (after[0] * after[1] * after[2])
    for ref, factor in zip(terms, (1.0, after[0], after[0] * after[1])):
        lam = lam + ref[...].astype(F32) * factor
    return lam, decay, weight


def cut_kernel(meta, ids, coeffs, cot_far, mod_far, w_far, o0, o1, o2, o3, cot, mod, w, sems):
    copies = [
        pltpu.make_async_copy(src, dst, sems.at[i])
        for i, (src, dst) in enumerate(((cot_far, cot), (mod_far, mod), (w_far, w)))
    ]
    for copy in copies:
        copy.start()
    for copy in copies:
        copy.wait()
    zhi = meta[1]
    group = meta[3] * 2 + meta[4]
    lam, decay, weight = lam_of(meta, ids, coeffs, cot, ())
    up = mod[2, group] * weight * lam
    for d, o in enumerate((o0, o1, o2, o3)):
        at = mod4(zhi + d)
        for part in range(3):
            o[part * 48 : (part + 1) * 48, :] = lane_piece(w[part].astype(F32), at).astype(BF)
        o[144:272, :] = lane_piece(up, at).astype(BF)


def adjoint_kernel(meta, ids, coeffs, cot, term, t1, t2, t3, out):
    lam, decay, weight = lam_of(meta, ids, coeffs, cot, (t1, t2, t3))
    out[...] = decay * lam + term[...]


def turn(value, axis, offset):
    return lax.ppermute(value, axis, [(i, (i + offset) % 4) for i in range(4)])


def ring4(value, axis):
    return [value] + [turn(value, axis, -offset) for offset in PLACES[1:]]


def hand_on(before, after, axis):
    pairs = []
    for i in range(4):
        pairs.append((2 * i, 2 * ((i - 1) % 4)))
        pairs.append((2 * i + 1, 2 * ((i + 1) % 4) + 1))
    return lax.ppermute(jnp.where(lax.axis_index("core") == 0, after, before), (axis, "core"), pairs)


def relayed(value, axis):
    before, after = turn(value, axis, 1), turn(value, axis, -1)
    return [value, before, after, hand_on(before, after, axis)]


def to_heads(pieces):
    got = [pieces[0]]
    for d in (1, 2, 3):
        pairs = [(i, (i + d) % 4) for i in range(4) if (i + d) % 4 != 3]
        got.append(lax.ppermute(pieces[d], "zhi", pairs))
    return got


def to_earlier(value):
    return [lax.ppermute(value, "step", [(j, j - d) for j in range(d, 4)]) for d in (1, 2, 3)]


def relay_hop(value):
    pairs = []
    for i in range(4):
        pairs.append((2 * i, 2 * ((i + 1) % 4)))
        pairs.append((2 * i + 1, 2 * ((i - 1) % 4) + 1))
    return lax.ppermute(value, ("zhi", "core"), pairs)


def exchange_zhi(blocks):
    half_way = relay_hop(blocks[2])
    one, three = turn(blocks[1], "zhi", 1), turn(blocks[3], "zhi", 3)
    return [blocks[0], one, relay_hop(half_way), three]


def along_z(value, offset):
    return lax.ppermute(value, ("zhi", "zlo"), [(i, (i + offset) % 16) for i in range(16)])


def far_z(value):
    pairs = []
    for i in range(16):
        pairs.append((2 * i, 2 * ((i + 2) % 16)))
        pairs.append((2 * i + 1, 2 * ((i - 2) % 16) + 1))
    return lax.ppermute(value, ("zhi", "zlo", "core"), pairs)


def other_core(value):
    return lax.ppermute(value, "core", [(0, 1), (1, 0)])


def shards(states, modulation, cotangent, w_qkv, q_gain, k_gain, step_ids, coeffs, neighbours):
    zhi = lax.axis_index("zhi")
    meta = jnp.stack([lax.axis_index(a) for a in ("step", "zhi", "y", "zlo", "core")]).astype(jnp.int32)
    coeffs, neighbours = coeffs.T, neighbours.T
    mod = modulation.reshape(3, 8, 1, WIDTH)
    gq = (q_gain / jnp.sqrt(jnp.float32(HD))).reshape(1, HD)
    gk = k_gain.reshape(1, HD)

    pieces = call(
        cut_kernel,
        [sds((272, HD), BF)] * 4,
        (meta, step_ids, coeffs, cotangent, mod, jnp.transpose(w_qkv, (1, 0, 2))),
        3,
        [
            pltpu.VMEM((TILE, WIDTH), F32),
            pltpu.VMEM((3, 8, 1, WIDTH), F32),
            pltpu.VMEM((3, 48, WIDTH), BF),
            pltpu.SemaphoreType.DMA((3,)),
        ],
        grant=60,
        far=3,
    )
    *pieces, x = lax.optimization_barrier((*pieces, states[0]))
    pieces = to_heads(pieces)
    own_rows = jnp.stack([p[0:144] for p in pieces])

    before, after = turn(x, "zhi", 1), turn(x, "zhi", -1)
    own_rows, before, after = lax.optimization_barrier((own_rows, before, after))
    y_rows = lax.all_gather(own_rows, "y")
    y_rows, before, after = lax.optimization_barrier((y_rows, before, after))
    wg = lax.all_gather(y_rows, "step").reshape(16, 4, 144, HD)
    x_tiles = jnp.stack([x, before, hand_on(before, after, "zhi"), after])
    xa = [x_tiles, along_z(x_tiles, 1), along_z(x_tiles, -1), far_z(x_tiles)]
    xb = [other_core(a) for a in xa]

    tokens = 4 * TILE
    scaled, normed, inv, normed_piece, inv_all = call(
        norm_kernel,
        [
            sds((8, 4, TILE, WIDTH), BF),
            sds((TILE, WIDTH), F32),
            sds((TILE, HD), F32),
            sds((4, TILE, HD), F32),
            sds((4, TILE, HD), F32),
        ],
        (meta, *xa, *xb, mod),
        1,
        (),
        0,
        16,
    )
    scaled, wg = lax.optimization_barrier((scaled, wg))
    qkvu, proj, wk, ws, vec = call(
        proj_kernel,
        [
            sds((4, TILE, WIDTH + HD), BF),
            sds((tokens, WIDTH), F32),
            sds((4, 8, 48, WIDTH), BF),
            sds((4, 8, 48, WIDTH), BF),
            sds((16, WIDTH), F32),
        ],
        (meta, scaled, wg, *pieces, mod, gq, gk),
        1,
        [pltpu.VMEM((8, 8, 48, WIDTH), BF)],
        2 * tokens * FEATS * WIDTH,
        24,
    )
    wr = other_core(ws)
    all_qkvu = relayed(qkvu, "y")

    again = ()
    for sweep in range(SWEEPS):
        outs = [sds((tokens + 16, WIDTH), BF), sds((4, 3, TILE, WIDTH), F32)]
        dproj, *kept = call(
            sweep_kernel,
            outs[: 2 - sweep],
            (meta, neighbours, *all_qkvu, proj, vec, gq, gk, *again),
            2,
            [pltpu.VMEM((16, TILE, WIDTH), BF), pltpu.VMEM((16, TILE, HD), BF)],
            400 * 1000 * 1000,
            16,
        )
        parts = call(
            feature_kernel,
            [sds((tokens + 16, WIDTH), BF)] * 4,
            (meta, dproj, other_core(dproj), wk, wr),
            1,
            (),
            2 * tokens * FEATS * WIDTH,
            16,
        )
        near = [parts[0], along_z(parts[1], 1), far_z(parts[2]), along_z(parts[3], -1)]
        if sweep + 1 < SWEEPS:
            blocks = call(window_piece_kernel, [sds((tokens + 16, HD), BF)] * 4, (meta, *near), 1)
            (sent,) = call(
                term_piece_kernel,
                [sds((4, TILE, HD), BF)],
                (meta, *exchange_zhi(blocks), normed_piece, inv_all, mod),
                1,
            )
            (up,) = call(
                upstream_piece_kernel,
                [sds((4, TILE, HD), BF)],
                (meta, step_ids, coeffs, qkvu, mod, *to_earlier(sent)),
                3,
            )
            again = (lax.all_gather(up, "y"), *kept)
    blocks = call(window_kernel, [sds((TILE + 16, WIDTH), BF)] * 4, (meta, *near), 1)
    got = exchange_zhi(blocks)
    term, sent, moments = call(
        term_kernel,
        [sds((TILE, WIDTH), F32), sds((TILE, WIDTH), BF), sds((2, TILE), F32)],
        (meta, *got, normed, inv, mod),
        1,
    )
    (adjoint,) = call(
        adjoint_kernel,
        [sds((TILE, WIDTH), F32)],
        (meta, step_ids, coeffs, cotangent, term, *to_earlier(sent)),
        3,
    )
    return adjoint[None], moments[None]


def solution(mesh):
    fine = Mesh(mesh.devices.reshape(4, 4, 4, 4, 2), ("step", "zhi", "y", "zlo", "core"))
    blk, head = ("zhi", "y"), ("zlo", "core")
    in_specs = (
        P("step", blk, head),
        P("step", None, None),
        P(blk, head),
        P(("step",) + blk, None, head),
        P(),
        P(),
        P(),
        P(),
        P(),
    )
    out_specs = (P("step", blk, head), P("step", None, blk))
    return jax.shard_map(shards, mesh=fine, in_specs=in_specs, out_specs=out_specs, check_vma=False)
```

```python
import jax
import jax.numpy as jnp
from jax import lax
from jax.experimental import pallas as pl
from jax.experimental.pallas import tpu as pltpu
from jax.sharding import Mesh
from jax.sharding import PartitionSpec as P

HD = 128
TILE = 128
WIDTH = 384
FEATS = 3072
SWEEPS = 2
EPS = 1e-06
BF = jnp.bfloat16
F32 = jnp.float32
MIB = 1024 * 1024
PLACES = (0, -1, 1, 2)

VM = pl.BlockSpec(memory_space=pltpu.VMEM)
SM = pl.BlockSpec(memory_space=pltpu.SMEM)


def call(body, outs, args, smem, scratch=(), flops=0, grant=8, far=0):
    specs = [SM if i < smem else VM for i in range(len(args))]
    specs[smem : smem + far] = [pl.BlockSpec(memory_space=pl.ANY)] * far
    moved = sum(a.size * a.dtype.itemsize for a in args) + sum(
        o.size * o.dtype.itemsize for o in outs
    )
    return pl.pallas_call(
        body,
        out_shape=tuple(outs),
        in_specs=specs,
        out_specs=tuple([VM] * len(outs)),
        scratch_shapes=list(scratch),
        compiler_params=pltpu.CompilerParams(vmem_limit_bytes=grant * MIB),
        cost_estimate=pl.CostEstimate(flops=flops, bytes_accessed=moved, transcendentals=0),
    )(*args)


def sds(shape, dtype):
    return jax.ShapeDtypeStruct(shape, dtype)


def nt(a, b):
    return lax.dot_general(a, b, (((1,), (1,)), ((), ())), preferred_element_type=F32)


def tn(a, b):
    return lax.dot_general(a, b, (((0,), (0,)), ((), ())), preferred_element_type=F32)


def nn(a, b):
    return jnp.dot(a, b, preferred_element_type=F32)


def hi_lo(value):
    hi = value.astype(BF)
    return hi, (value - hi.astype(F32)).astype(BF)


def mod4(value):
    return lax.rem(value + 8, 4)


def lane_piece(value, at):
    out = jnp.zeros(value.shape[:-1] + (HD,), value.dtype)
    for i in range(3):
        out = jnp.where(at == i, value[..., i * HD : (i + 1) * HD], out)
    return out


def norm_kernel(
    meta, xa0, xa1, xa2, xa3, xb0, xb1, xb2, xb3, mod,
    scaled, normed_own, inv_own, normed_piece, inv_all,
):
    zhi, zlo, core = meta[1], meta[3], meta[4]
    place = zhi * 4 + zlo
    own_far = jnp.where(core == 0, -2, 2)
    sources = []
    for refs, side, far in (
        ((xa0, xa1, xa2, xa3), core, own_far),
        ((xb0, xb1, xb2, xb3), 1 - core, -own_far),
    ):
        for ref, offset in zip(refs, (0, -1, 1, far)):
            at = lax.rem(place + offset + 16, 16)
            sources.append((ref, at // 4, lax.rem(at, 4) * 2 + side))

    rows = 32

    def chunk(turn, carry):
        t = turn // (TILE // rows)
        start = lax.rem(turn, TILE // rows) * rows
        span = pl.ds(pl.multiple_of(start, rows), rows)

        def load(source):
            ref, z, g = source
            d = mod4(z - t)
            return ref[d, span, :].astype(F32)

        total = jnp.zeros((rows, WIDTH), F32)
        for source in sources:
            total = total + load(source)
        mean = jnp.sum(total, axis=1, keepdims=True) * (1.0 / FEATS)
        square = jnp.zeros((rows, WIDTH), F32)
        for source in sources:
            centred = load(source) - mean
            square = square + centred * centred
        inv = lax.rsqrt(jnp.sum(square, axis=1, keepdims=True) * (1.0 / FEATS) + EPS)
        for source in sources:
            normed = (load(source) - mean) * inv
            scaled[source[2], t, span, :] = (normed * (1.0 + mod[1, source[2]])).astype(BF)
        normed = (load(sources[0]) - mean) * inv
        normed_piece[t, span, :] = lane_piece(normed, zhi)
        inv_all[t, span, :] = jnp.broadcast_to(inv, (rows, HD))

        @pl.when(t == zhi)
        def _():
            normed_own[span, :] = normed
            inv_own[span, :] = jnp.broadcast_to(inv, (rows, HD))

        return carry

    lax.fori_loop(0, 4 * (TILE // rows), chunk, 0)


def proj_kernel(
    meta, nscr, wg, mod, q_gain, k_gain,
    qkv, proj, wk, ws, vec, wc,
):
    zhi, core = meta[1], meta[4]
    for d in range(4):
        zh = mod4(zhi - d)
        for sy in range(16):
            for part in range(3):
                wc[(sy // 4) * 2 + zh // 2, lax.rem(zh, 2) * 4 + sy % 4, :, part * HD : (part + 1) * HD] = (
                    wg[sy, d, part * 48 : (part + 1) * 48, :]
                )
    for r in range(4):
        wk[r] = wc[2 * r + core]
        ws[r] = wc[2 * r + 1 - core]

    acc = jnp.zeros((4 * TILE, WIDTH), F32)
    flat = jnp.zeros((16, WIDTH), F32)
    for g in range(8):
        w_g = wc[g].reshape(WIDTH, WIDTH)
        acc = acc + nn(nscr[g].reshape(4 * TILE, WIDTH), w_g)
        scale_hi, scale_lo = hi_lo(1.0 + mod[1, g])
        shift_hi, shift_lo = hi_lo(mod[0, g])
        four = jnp.concatenate([scale_hi, scale_lo, shift_hi, shift_lo], axis=0)
        lhs = jnp.concatenate([four, jnp.zeros((12, WIDTH), BF)], axis=0)
        flat = flat + nn(lhs, w_g)
    vec[...] = flat
    proj[...] = acc + (flat[2:3] + flat[3:4])
    for t in range(4):
        span = slice(t * TILE, (t + 1) * TILE)
        q = proj[span, 0:HD]
        k = proj[span, HD : 2 * HD]
        q_inv = lax.rsqrt(jnp.mean(q * q, axis=1, keepdims=True) + EPS)
        k_inv = lax.rsqrt(jnp.mean(k * k, axis=1, keepdims=True) + EPS)
        qkv[t, :, 0:HD] = (q * q_inv * q_gain[...]).astype(BF)
        qkv[t, :, HD : 2 * HD] = (k * k_inv * k_gain[...]).astype(BF)
        qkv[t, :, 2 * HD : 3 * HD] = proj[span, 2 * HD : 3 * HD].astype(BF)


def norm_back(raw, gain, grad):
    inv = lax.rsqrt(jnp.mean(raw * raw, axis=1, keepdims=True) + EPS)
    scaled = grad * gain
    dot = jnp.mean(scaled * raw, axis=1, keepdims=True)
    return inv * (scaled - raw * (inv * inv * dot))


def sweep_kernel(
    meta, nb, k0, k1, k2, k3, proj, vec, q_gain, k_gain, *rest
):
    ups_all, tiles, ups = rest[0], rest[-2], rest[-1]
    first_sweep = len(ups_all.shape) == 4 and ups_all.shape[2] == 272
    probs, out = (rest[2], rest[1]) if first_sweep else (rest[1], rest[2])
    zhi, y = meta[1], meta[2]
    for ref, offset in zip((k0, k1, k2, k3), PLACES):
        yy = mod4(y + offset)
        for z in range(4):
            tiles[z * 4 + yy] = ref[z]
    for yy in range(4):
        for d in range(4):
            if first_sweep:
                ups[mod4(zhi - d) * 4 + yy] = ups_all[yy, d, 144:272, :]
            else:
                ups[d * 4 + yy] = ups_all[yy, d]

    m1_hi, m1_lo = hi_lo(vec[0:1] + vec[1:2])
    m1 = jnp.concatenate([m1_hi, m1_lo, jnp.zeros((14, WIDTH), BF)], axis=0)
    ones = jnp.ones((16, WIDTH), BF)
    s0 = vec[2:3] + vec[3:4]

    def k_of(t):
        return tiles[t, :, HD : 2 * HD]

    def v_of(t):
        return tiles[t, :, 2 * HD : 3 * HD]

    def own(jz, carry):
        j = jz * 4 + y
        near = (nb[1, j], nb[2, j])
        d_k = jnp.zeros((TILE, HD), F32)
        d_v = jnp.zeros((TILE, HD), F32)
        d_q = None
        for slot in range(3):
            if slot == 0:
                i = j
                keys = (j, near[0], near[1])
            else:
                i = near[slot - 1]
                keys = (j, i, nb[1, i] + nb[2, i] - j)
            q = tiles[i, :, 0:HD]
            up = ups[i]
            k_all = jnp.concatenate([k_of(t) for t in keys], axis=0)
            v_all = jnp.concatenate([v_of(t) for t in keys], axis=0)
            if first_sweep:
                expo = jnp.exp(nt(k_all, q))
                prob = expo * (1.0 / jnp.sum(expo, axis=0, keepdims=True))
                probs[jz, slot] = prob
            else:
                prob = probs[jz, slot]
            prob_b = prob.astype(BF)
            dprob = nt(v_all, up)
            delta = jnp.sum(prob_b.astype(F32) * dprob, axis=0, keepdims=True)
            if slot == 0:
                dscore = (prob * (dprob - delta)).astype(BF)
                d_q = tn(dscore, k_all)
                dscore = dscore[0:TILE]
            else:
                dscore = (prob[0:TILE] * (dprob[0:TILE] - delta)).astype(BF)
            d_k = d_k + nn(dscore, q)
            d_v = d_v + nn(prob_b[0:TILE], up)
        start = pl.multiple_of(jz * TILE, TILE)
        raw = proj[pl.ds(start, TILE), :]
        d_q = norm_back(raw[:, 0:HD], q_gain[...], d_q)
        d_k = norm_back(raw[:, HD : 2 * HD], k_gain[...], d_k)
        d_all = jnp.concatenate([d_q, d_k, d_v], axis=1).astype(BF)
        out[pl.ds(start, TILE), :] = d_all
        first = nt(m1, d_all)
        prod_hi, prod_lo = hi_lo(d_all.astype(F32) * (raw - s0))
        second = nt(ones, prod_hi) + nt(ones, prod_lo)
        row = jnp.concatenate(
            [first[0:1] + first[1:2], second[0:1], jnp.zeros((1, TILE), F32)], axis=1
        )
        at = lax.broadcasted_iota(jnp.int32, (8, WIDTH), 0)
        return carry + jnp.where(at == jz, row, 0.0)

    stats = lax.fori_loop(0, 4, own, jnp.zeros((8, WIDTH), F32))
    out[4 * TILE : 4 * TILE + 16, :] = jnp.concatenate(hi_lo(stats), axis=0)


def stats_of(ref, start):
    both = ref[start : start + 16, :].astype(F32)
    return both[0:8] + both[8:16]


def feature_kernel(meta, own, other, wk, wr, o0, o1, o2, o3):
    zlo = meta[3]
    stats = jnp.concatenate(hi_lo(stats_of(own, 4 * TILE) + stats_of(other, 4 * TILE)), axis=0)
    for offset, o in enumerate((o0, o1, o2, o3)):
        r = mod4(zlo + offset)
        value = nt(own[0 : 4 * TILE, :], wk[r].reshape(WIDTH, WIDTH))
        value = value + nt(other[0 : 4 * TILE, :], wr[r].reshape(WIDTH, WIDTH))
        o[0 : 4 * TILE, :] = value.astype(BF)
        o[4 * TILE : 4 * TILE + 16, :] = stats


def window_kernel(meta, a0, a1, a2, a3, o0, o1, o2, o3):
    zhi = meta[1]
    refs = (a0, a1, a2, a3)
    stats = stats_of(a0, 4 * TILE)
    for a in refs[1:]:
        stats = stats + stats_of(a, 4 * TILE)
    at = lax.broadcasted_iota(jnp.int32, (8, WIDTH), 0)
    for d, o in enumerate((o0, o1, o2, o3)):
        t = mod4(zhi + d)
        span = pl.ds(pl.multiple_of(t * TILE, TILE), TILE)
        value = a0[span, :].astype(F32)
        for a in refs[1:]:
            value = value + a[span, :].astype(F32)
        o[0:TILE, :] = value.astype(BF)
        row = jnp.sum(jnp.where(at == t, stats, 0.0), axis=0, keepdims=True)
        o[TILE : TILE + 16, :] = jnp.concatenate(
            hi_lo(jnp.broadcast_to(row, (8, WIDTH))), axis=0
        )


def window_piece_kernel(meta, a0, a1, a2, a3, o0, o1, o2, o3):
    zhi = meta[1]
    refs = (a0, a1, a2, a3)
    stats = stats_of(a0, 4 * TILE)
    for a in refs[1:]:
        stats = stats + stats_of(a, 4 * TILE)
    stats = jnp.concatenate(hi_lo(jnp.concatenate([stats[0:4, 0:TILE], stats[0:4, TILE : 2 * TILE]], axis=0)), axis=0)
    for t in range(4):
        span = slice(t * TILE, (t + 1) * TILE)
        value = a0[span, :].astype(F32)
        for a in refs[1:]:
            value = value + a[span, :].astype(F32)
        for d, o in enumerate((o0, o1, o2, o3)):
            o[span, :] = lane_piece(value, mod4(zhi + d)).astype(BF)
    for d, o in enumerate((o0, o1, o2, o3)):
        keep = jnp.where(mod4(zhi + d) == 3, 0.0, 1.0)
        o[4 * TILE : 4 * TILE + 16, :] = (stats.astype(F32) * keep).astype(BF)


def term_piece_kernel(meta, a0, a1, a2, a3, normed, inv, mod, sent):
    group = meta[3] * 2 + meta[4]
    stats = stats_of(a0, 4 * TILE)
    for a in (a1, a2, a3):
        stats = stats + stats_of(a, 4 * TILE)
    scale = 1.0 + lane_piece(mod[1, group], meta[1])
    for t in range(4):
        span = slice(t * TILE, (t + 1) * TILE)
        grad = a0[span, :].astype(F32)
        for a in (a1, a2, a3):
            grad = grad + a[span, :].astype(F32)
        value = inv[t] * (grad * scale - column(stats[t : t + 1]) - normed[t] * column(stats[4 + t : 5 + t]))
        sent[t] = value.astype(BF)


def upstream_piece_kernel(meta, ids, coeffs, first, mod, t1, t2, t3, out):
    group = meta[3] * 2 + meta[4]
    after, decay, weight = decays(meta, ids, coeffs)
    gate = lane_piece(mod[2, group], meta[1]) * weight
    for t in range(4):
        later = t1[t].astype(F32) + t2[t].astype(F32) * after[0] + t3[t].astype(F32) * (after[0] * after[1])
        out[t] = (first[mod4(meta[1] - t), 144:272, :].astype(F32) + gate * later).astype(BF)


def column(row):
    return jnp.transpose(jnp.broadcast_to(row * (1.0 / FEATS), (TILE, TILE)))


def term_kernel(meta, a0, a1, a2, a3, normed, inv, mod, term, sent, moments):
    group = meta[3] * 2 + meta[4]
    grad = a0[0:TILE, :].astype(F32)
    stats = stats_of(a0, TILE)
    for a in (a1, a2, a3):
        grad = grad + a[0:TILE, :].astype(F32)
        stats = stats + stats_of(a, TILE)
    first = stats[0:1, 0:TILE]
    second = stats[0:1, TILE : 2 * TILE]
    moments[...] = jnp.concatenate([first, second], axis=0) * (FEATS**-0.5)

    def wide(value):
        return jnp.concatenate([value] * 3, axis=1)

    du = grad * (1.0 + mod[1, group])
    value = wide(inv[...]) * (du - wide(column(first)) - normed[...] * wide(column(second)))
    term[...] = value
    sent[...] = value.astype(BF)


def decays(meta, ids, coeffs):
    step = meta[0]
    after = []
    for ahead in (1, 2, 3):
        at = jnp.minimum(step + ahead, 3)
        after.append(jnp.where(step + ahead <= 3, coeffs[0, ids[at]], 1.0))
    return after, coeffs[0, ids[step]], coeffs[1, ids[step]]


def lam_of(meta, ids, coeffs, cot, terms):
    after, decay, weight = decays(meta, ids, coeffs)
    lam = cot[...] * (after[0] * after[1] * after[2])
    for ref, factor in zip(terms, (1.0, after[0], after[0] * after[1])):
        lam = lam + ref[...].astype(F32) * factor
    return lam, decay, weight


def cut_kernel(meta, ids, coeffs, cot_far, mod_far, w_far, o0, o1, o2, o3, cot, mod, w, sems):
    copies = [
        pltpu.make_async_copy(src, dst, sems.at[i])
        for i, (src, dst) in enumerate(((cot_far, cot), (mod_far, mod), (w_far, w)))
    ]
    for copy in copies:
        copy.start()
    for copy in copies:
        copy.wait()
    zhi = meta[1]
    group = meta[3] * 2 + meta[4]
    lam, decay, weight = lam_of(meta, ids, coeffs, cot, ())
    up = mod[2, group] * weight * lam
    for d, o in enumerate((o0, o1, o2, o3)):
        at = mod4(zhi + d)
        for part in range(3):
            o[part * 48 : (part + 1) * 48, :] = lane_piece(w[part].astype(F32), at).astype(BF)
        o[144:272, :] = lane_piece(up, at).astype(BF)


def adjoint_kernel(meta, ids, coeffs, cot, term, t1, t2, t3, out):
    lam, decay, weight = lam_of(meta, ids, coeffs, cot, (t1, t2, t3))
    out[...] = decay * lam + term[...]


def turn(value, axis, offset):
    return lax.ppermute(value, axis, [(i, (i + offset) % 4) for i in range(4)])


def ring4(value, axis):
    return [value] + [turn(value, axis, -offset) for offset in PLACES[1:]]


def hand_on(before, after, axis):
    pairs = []
    for i in range(4):
        pairs.append((2 * i, 2 * ((i - 1) % 4)))
        pairs.append((2 * i + 1, 2 * ((i + 1) % 4) + 1))
    return lax.ppermute(jnp.where(lax.axis_index("core") == 0, after, before), (axis, "core"), pairs)


def relayed(value, axis):
    before, after = turn(value, axis, 1), turn(value, axis, -1)
    return [value, before, after, hand_on(before, after, axis)]


def to_heads(pieces):
    got = [pieces[0]]
    for d in (1, 2, 3):
        pairs = [(i, (i + d) % 4) for i in range(4) if (i + d) % 4 != 3]
        got.append(lax.ppermute(pieces[d], "zhi", pairs))
    return got


def to_earlier(value):
    return [lax.ppermute(value, "step", [(j, j - d) for j in range(d, 4)]) for d in (1, 2, 3)]


def relay_hop(value):
    pairs = []
    for i in range(4):
        pairs.append((2 * i, 2 * ((i + 1) % 4)))
        pairs.append((2 * i + 1, 2 * ((i - 1) % 4) + 1))
    return lax.ppermute(value, ("zhi", "core"), pairs)


def exchange_zhi(blocks):
    half_way = relay_hop(blocks[2])
    one, three = turn(blocks[1], "zhi", 1), turn(blocks[3], "zhi", 3)
    return [blocks[0], one, relay_hop(half_way), three]


def along_z(value, offset):
    return lax.ppermute(value, ("zhi", "zlo"), [(i, (i + offset) % 16) for i in range(16)])


def far_z(value):
    pairs = []
    for i in range(16):
        pairs.append((2 * i, 2 * ((i + 2) % 16)))
        pairs.append((2 * i + 1, 2 * ((i - 2) % 16) + 1))
    return lax.ppermute(value, ("zhi", "zlo", "core"), pairs)


def other_core(value):
    return lax.ppermute(value, "core", [(0, 1), (1, 0)])


def shards(states, modulation, cotangent, w_qkv, q_gain, k_gain, step_ids, coeffs, neighbours):
    zhi = lax.axis_index("zhi")
    meta = jnp.stack([lax.axis_index(a) for a in ("step", "zhi", "y", "zlo", "core")]).astype(jnp.int32)
    coeffs, neighbours = coeffs.T, neighbours.T
    mod = modulation.reshape(3, 8, 1, WIDTH)
    gq = (q_gain / jnp.sqrt(jnp.float32(HD))).reshape(1, HD)
    gk = k_gain.reshape(1, HD)

    pieces = call(
        cut_kernel,
        [sds((272, HD), BF)] * 4,
        (meta, step_ids, coeffs, cotangent, mod, jnp.transpose(w_qkv, (1, 0, 2))),
        3,
        [
            pltpu.VMEM((TILE, WIDTH), F32),
            pltpu.VMEM((3, 8, 1, WIDTH), F32),
            pltpu.VMEM((3, 48, WIDTH), BF),
            pltpu.SemaphoreType.DMA((3,)),
        ],
        grant=12,
        far=3,
    )
    pieces = to_heads(pieces)
    pieces[1], x = lax.optimization_barrier((pieces[1], states[0]))

    before, after = turn(x, "zhi", 1), turn(x, "zhi", -1)
    y_rows = lax.all_gather(jnp.stack(pieces), "y")
    y_rows, before, after = lax.optimization_barrier((y_rows, before, after))
    wg = lax.all_gather(y_rows[:, :, 0:144], "step").reshape(16, 4, 144, HD)
    x_tiles = jnp.stack([x, before, hand_on(before, after, "zhi"), after])
    xa = [x_tiles, along_z(x_tiles, 1), along_z(x_tiles, -1), far_z(x_tiles)]
    xb = [other_core(a) for a in xa]

    tokens = 4 * TILE
    scaled, normed, inv, normed_piece, inv_all = call(
        norm_kernel,
        [
            sds((8, 4, TILE, WIDTH), BF),
            sds((TILE, WIDTH), F32),
            sds((TILE, HD), F32),
            sds((4, TILE, HD), F32),
            sds((4, TILE, HD), F32),
        ],
        (meta, *xa, *xb, mod),
        1,
        (),
        0,
        16,
    )
    scaled, wg = lax.optimization_barrier((scaled, wg))
    qkv, proj, wk, ws, vec = call(
        proj_kernel,
        [
            sds((4, TILE, WIDTH), BF),
            sds((tokens, WIDTH), F32),
            sds((4, 8, 48, WIDTH), BF),
            sds((4, 8, 48, WIDTH), BF),
            sds((16, WIDTH), F32),
        ],
        (meta, scaled, wg, mod, gq, gk),
        1,
        [pltpu.VMEM((8, 8, 48, WIDTH), BF)],
        2 * tokens * FEATS * WIDTH,
        24,
    )
    wr = other_core(ws)
    all_qkv = relayed(qkv, "y")

    again = (y_rows,)
    for sweep in range(SWEEPS):
        outs = [sds((tokens + 16, WIDTH), BF), sds((4, 3, WIDTH, TILE), F32)]
        dproj, *kept = call(
            sweep_kernel,
            outs[: 2 - sweep],
            (meta, neighbours, *all_qkv, proj, vec, gq, gk, *again),
            2,
            [pltpu.VMEM((16, TILE, WIDTH), BF), pltpu.VMEM((16, TILE, HD), BF)],
            400 * 1000 * 1000,
            16,
        )
        parts = call(
            feature_kernel,
            [sds((tokens + 16, WIDTH), BF)] * 4,
            (meta, dproj, other_core(dproj), wk, wr),
            1,
            (),
            2 * tokens * FEATS * WIDTH,
            16,
        )
        near = [parts[0], along_z(parts[1], 1), far_z(parts[2]), along_z(parts[3], -1)]
        if sweep + 1 < SWEEPS:
            blocks = call(window_piece_kernel, [sds((tokens + 16, HD), BF)] * 4, (meta, *near), 1)
            (sent,) = call(
                term_piece_kernel,
                [sds((4, TILE, HD), BF)],
                (meta, *exchange_zhi(blocks), normed_piece, inv_all, mod),
                1,
            )
            (up,) = call(
                upstream_piece_kernel,
                [sds((4, TILE, HD), BF)],
                (meta, step_ids, coeffs, jnp.stack(pieces), mod, *to_earlier(sent)),
                3,
            )
            again = (lax.all_gather(up, "y"), *kept)
    blocks = call(window_kernel, [sds((TILE + 16, WIDTH), BF)] * 4, (meta, *near), 1)
    got = exchange_zhi(blocks)
    term, sent, moments = call(
        term_kernel,
        [sds((TILE, WIDTH), F32), sds((TILE, WIDTH), BF), sds((2, TILE), F32)],
        (meta, *got, normed, inv, mod),
        1,
    )
    (adjoint,) = call(
        adjoint_kernel,
        [sds((TILE, WIDTH), F32)],
        (meta, step_ids, coeffs, cotangent, term, *to_earlier(sent)),
        3,
    )
    return adjoint[None], moments[None]


def solution(mesh):
    fine = Mesh(mesh.devices.reshape(4, 4, 4, 4, 2), ("step", "zhi", "y", "zlo", "core"))
    blk, head = ("zhi", "y"), ("zlo", "core")
    in_specs = (
        P("step", blk, head),
        P("step", None, None),
        P(blk, head),
        P(("step",) + blk, None, head),
        P(),
        P(),
        P(),
        P(),
        P(),
    )
    out_specs = (P("step", blk, head), P("step", None, blk))
    return jax.shard_map(shards, mesh=fine, in_specs=in_specs, out_specs=out_specs, check_vma=False)
```

```python
import jax
import jax.numpy as jnp
from jax import lax
from jax.experimental import pallas as pl
from jax.experimental.pallas import tpu as pltpu
from jax.sharding import Mesh
from jax.sharding import PartitionSpec as P

HD = 128
TILE = 128
WIDTH = 384
FEATS = 3072
SWEEPS = 2
EPS = 1e-06
BF = jnp.bfloat16
F32 = jnp.float32
MIB = 1024 * 1024
PLACES = (0, -1, 1, 2)

VM = pl.BlockSpec(memory_space=pltpu.VMEM)
SM = pl.BlockSpec(memory_space=pltpu.SMEM)


def call(body, outs, args, smem, scratch=(), flops=0, grant=8, far=0):
    specs = [SM if i < smem else VM for i in range(len(args))]
    specs[smem : smem + far] = [pl.BlockSpec(memory_space=pl.ANY)] * far
    moved = sum(a.size * a.dtype.itemsize for a in args) + sum(
        o.size * o.dtype.itemsize for o in outs
    )
    return pl.pallas_call(
        body,
        out_shape=tuple(outs),
        in_specs=specs,
        out_specs=tuple([VM] * len(outs)),
        scratch_shapes=list(scratch),
        compiler_params=pltpu.CompilerParams(vmem_limit_bytes=grant * MIB),
        cost_estimate=pl.CostEstimate(flops=flops, bytes_accessed=moved, transcendentals=0),
    )(*args)


def sds(shape, dtype):
    return jax.ShapeDtypeStruct(shape, dtype)


def nt(a, b):
    return lax.dot_general(a, b, (((1,), (1,)), ((), ())), preferred_element_type=F32)


def tn(a, b):
    return lax.dot_general(a, b, (((0,), (0,)), ((), ())), preferred_element_type=F32)


def nn(a, b):
    return jnp.dot(a, b, preferred_element_type=F32)


def hi_lo(value):
    hi = value.astype(BF)
    return hi, (value - hi.astype(F32)).astype(BF)


def mod4(value):
    return lax.rem(value + 8, 4)


def lane_piece(value, at):
    out = jnp.zeros(value.shape[:-1] + (HD,), value.dtype)
    for i in range(3):
        out = jnp.where(at == i, value[..., i * HD : (i + 1) * HD], out)
    return out


def norm_kernel(
    meta, xa0, xa1, xa2, xa3, xb0, xb1, xb2, xb3, mod,
    scaled, normed_own, inv_own, normed_piece, inv_all,
):
    zhi, zlo, core = meta[1], meta[3], meta[4]
    place = zhi * 4 + zlo
    own_far = jnp.where(core == 0, -2, 2)
    sources = []
    for refs, side, far in (
        ((xa0, xa1, xa2, xa3), core, own_far),
        ((xb0, xb1, xb2, xb3), 1 - core, -own_far),
    ):
        for ref, offset in zip(refs, (0, -1, 1, far)):
            at = lax.rem(place + offset + 16, 16)
            sources.append((ref, at // 4, lax.rem(at, 4) * 2 + side))

    rows = 32

    def chunk(turn, carry):
        t = turn // (TILE // rows)
        start = lax.rem(turn, TILE // rows) * rows
        span = pl.ds(pl.multiple_of(start, rows), rows)

        def load(source):
            ref, z, g = source
            d = mod4(z - t)
            return ref[d, span, :].astype(F32)

        total = jnp.zeros((rows, WIDTH), F32)
        for source in sources:
            total = total + load(source)
        mean = jnp.sum(total, axis=1, keepdims=True) * (1.0 / FEATS)
        square = jnp.zeros((rows, WIDTH), F32)
        for source in sources:
            centred = load(source) - mean
            square = square + centred * centred
        inv = lax.rsqrt(jnp.sum(square, axis=1, keepdims=True) * (1.0 / FEATS) + EPS)
        for source in sources:
            normed = (load(source) - mean) * inv
            scaled[source[2], t, span, :] = (normed * (1.0 + mod[1, source[2]])).astype(BF)
        normed = (load(sources[0]) - mean) * inv
        normed_piece[t, span, :] = lane_piece(normed, zhi)
        inv_all[t, span, :] = jnp.broadcast_to(inv, (rows, HD))

        @pl.when(t == zhi)
        def _():
            normed_own[span, :] = normed
            inv_own[span, :] = jnp.broadcast_to(inv, (rows, HD))

        return carry

    lax.fori_loop(0, 4 * (TILE // rows), chunk, 0)


def proj_kernel(
    meta, nscr, wg, mod, q_gain, k_gain,
    qkv, proj, wk, ws, vec, wc,
):
    zhi, core = meta[1], meta[4]
    for d in range(4):
        zh = mod4(zhi - d)
        for sy in range(16):
            for part in range(3):
                wc[(sy // 4) * 2 + zh // 2, lax.rem(zh, 2) * 4 + sy % 4, :, part * HD : (part + 1) * HD] = (
                    wg[sy, d, part * 48 : (part + 1) * 48, :]
                )
    for r in range(4):
        wk[r] = wc[2 * r + core]
        ws[r] = wc[2 * r + 1 - core]

    acc = jnp.zeros((4 * TILE, WIDTH), F32)
    flat = jnp.zeros((16, WIDTH), F32)
    for g in range(8):
        w_g = wc[g].reshape(WIDTH, WIDTH)
        acc = acc + nn(nscr[g].reshape(4 * TILE, WIDTH), w_g)
        scale_hi, scale_lo = hi_lo(1.0 + mod[1, g])
        shift_hi, shift_lo = hi_lo(mod[0, g])
        four = jnp.concatenate([scale_hi, scale_lo, shift_hi, shift_lo], axis=0)
        lhs = jnp.concatenate([four, jnp.zeros((12, WIDTH), BF)], axis=0)
        flat = flat + nn(lhs, w_g)
    vec[...] = flat
    proj[...] = acc + (flat[2:3] + flat[3:4])
    for t in range(4):
        span = slice(t * TILE, (t + 1) * TILE)
        q = proj[span, 0:HD]
        k = proj[span, HD : 2 * HD]
        q_inv = lax.rsqrt(jnp.mean(q * q, axis=1, keepdims=True) + EPS)
        k_inv = lax.rsqrt(jnp.mean(k * k, axis=1, keepdims=True) + EPS)
        qkv[t, :, 0:HD] = (q * q_inv * q_gain[...]).astype(BF)
        qkv[t, :, HD : 2 * HD] = (k * k_inv * k_gain[...]).astype(BF)
        qkv[t, :, 2 * HD : 3 * HD] = proj[span, 2 * HD : 3 * HD].astype(BF)


def norm_back(raw, gain, grad):
    inv = lax.rsqrt(jnp.mean(raw * raw, axis=1, keepdims=True) + EPS)
    scaled = grad * gain
    dot = jnp.mean(scaled * raw, axis=1, keepdims=True)
    return inv * (scaled - raw * (inv * inv * dot))


def sweep_kernel(
    meta, nb, k0, k1, k2, k3, proj, vec, q_gain, k_gain, *rest
):
    tiles, ups = rest[-2:]
    first_sweep = len(rest) == 8
    probs, out = (rest[5], rest[4]) if first_sweep else (rest[1], rest[2])
    zhi, y = meta[1], meta[2]
    for ref, offset in zip((k0, k1, k2, k3), PLACES):
        yy = mod4(y + offset)
        for z in range(4):
            tiles[z * 4 + yy] = ref[z]
    for i, offset in enumerate(PLACES):
        for z in range(4):
            if first_sweep:
                ups[mod4(zhi - z) * 4 + mod4(y + offset)] = rest[i][z]
            else:
                ups[z * 4 + i] = rest[0][i, z]

    m1_hi, m1_lo = hi_lo(vec[0:1] + vec[1:2])
    m1 = jnp.concatenate([m1_hi, m1_lo, jnp.zeros((14, WIDTH), BF)], axis=0)
    ones = jnp.ones((16, WIDTH), BF)
    s0 = vec[2:3] + vec[3:4]

    def k_of(t):
        return tiles[t, :, HD : 2 * HD]

    def v_of(t):
        return tiles[t, :, 2 * HD : 3 * HD]

    def own(jz, carry):
        j = jz * 4 + y
        near = (nb[1, j], nb[2, j])
        d_k = jnp.zeros((TILE, HD), F32)
        d_v = jnp.zeros((TILE, HD), F32)
        d_q = None
        for slot in range(3):
            if slot == 0:
                i = j
                keys = (j, near[0], near[1])
            else:
                i = near[slot - 1]
                keys = (j, i, nb[1, i] + nb[2, i] - j)
            q = tiles[i, :, 0:HD]
            up = ups[i]
            k_all = jnp.concatenate([k_of(t) for t in keys], axis=0)
            v_all = jnp.concatenate([v_of(t) for t in keys], axis=0)
            if first_sweep:
                expo = jnp.exp(nt(k_all, q))
                prob = expo * (1.0 / jnp.sum(expo, axis=0, keepdims=True))
                probs[jz, slot] = prob
            else:
                prob = probs[jz, slot]
            prob_b = prob.astype(BF)
            dprob = nt(v_all, up)
            delta = jnp.sum(prob_b.astype(F32) * dprob, axis=0, keepdims=True)
            if slot == 0:
                dscore = (prob * (dprob - delta)).astype(BF)
                d_q = tn(dscore, k_all)
                dscore = dscore[0:TILE]
            else:
                dscore = (prob[0:TILE] * (dprob[0:TILE] - delta)).astype(BF)
            d_k = d_k + nn(dscore, q)
            d_v = d_v + nn(prob_b[0:TILE], up)
        start = pl.multiple_of(jz * TILE, TILE)
        raw = proj[pl.ds(start, TILE), :]
        d_q = norm_back(raw[:, 0:HD], q_gain[...], d_q)
        d_k = norm_back(raw[:, HD : 2 * HD], k_gain[...], d_k)
        d_all = jnp.concatenate([d_q, d_k, d_v], axis=1).astype(BF)
        out[pl.ds(start, TILE), :] = d_all
        first = nt(m1, d_all)
        prod_hi, prod_lo = hi_lo(d_all.astype(F32) * (raw - s0))
        second = nt(ones, prod_hi) + nt(ones, prod_lo)
        row = jnp.concatenate(
            [first[0:1] + first[1:2], second[0:1], jnp.zeros((1, TILE), F32)], axis=1
        )
        at = lax.broadcasted_iota(jnp.int32, (8, WIDTH), 0)
        return carry + jnp.where(at == jz, row, 0.0)

    stats = lax.fori_loop(0, 4, own, jnp.zeros((8, WIDTH), F32))
    out[4 * TILE : 4 * TILE + 16, :] = jnp.concatenate(hi_lo(stats), axis=0)


def stats_of(ref, start):
    both = ref[start : start + 16, :].astype(F32)
    return both[0:8] + both[8:16]


def feature_kernel(meta, own, other, wk, wr, o0, o1, o2, o3):
    zlo = meta[3]
    stats = jnp.concatenate(hi_lo(stats_of(own, 4 * TILE) + stats_of(other, 4 * TILE)), axis=0)
    for offset, o in enumerate((o0, o1, o2, o3)):
        r = mod4(zlo + offset)
        value = nt(own[0 : 4 * TILE, :], wk[r].reshape(WIDTH, WIDTH))
        value = value + nt(other[0 : 4 * TILE, :], wr[r].reshape(WIDTH, WIDTH))
        o[0 : 4 * TILE, :] = value.astype(BF)
        o[4 * TILE : 4 * TILE + 16, :] = stats


def window_kernel(meta, a0, a1, a2, a3, o0, o1, o2, o3):
    zhi = meta[1]
    refs = (a0, a1, a2, a3)
    stats = stats_of(a0, 4 * TILE)
    for a in refs[1:]:
        stats = stats + stats_of(a, 4 * TILE)
    at = lax.broadcasted_iota(jnp.int32, (8, WIDTH), 0)
    for d, o in enumerate((o0, o1, o2, o3)):
        t = mod4(zhi + d)
        span = pl.ds(pl.multiple_of(t * TILE, TILE), TILE)
        value = a0[span, :].astype(F32)
        for a in refs[1:]:
            value = value + a[span, :].astype(F32)
        o[0:TILE, :] = value.astype(BF)
        row = jnp.sum(jnp.where(at == t, stats, 0.0), axis=0, keepdims=True)
        o[TILE : TILE + 16, :] = jnp.concatenate(
            hi_lo(jnp.broadcast_to(row, (8, WIDTH))), axis=0
        )


def window_piece_kernel(meta, a0, a1, a2, a3, o0, o1, o2, o3):
    zhi = meta[1]
    refs = (a0, a1, a2, a3)
    stats = stats_of(a0, 4 * TILE)
    for a in refs[1:]:
        stats = stats + stats_of(a, 4 * TILE)
    stats = jnp.concatenate(hi_lo(jnp.concatenate([stats[0:4, 0:TILE], stats[0:4, TILE : 2 * TILE]], axis=0)), axis=0)
    for t in range(4):
        span = slice(t * TILE, (t + 1) * TILE)
        value = a0[span, :].astype(F32)
        for a in refs[1:]:
            value = value + a[span, :].astype(F32)
        for d, o in enumerate((o0, o1, o2, o3)):
            o[span, :] = lane_piece(value, mod4(zhi + d)).astype(BF)
    for d, o in enumerate((o0, o1, o2, o3)):
        keep = jnp.where(mod4(zhi + d) == 3, 0.0, 1.0)
        o[4 * TILE : 4 * TILE + 16, :] = (stats.astype(F32) * keep).astype(BF)


def term_piece_kernel(meta, a0, a1, a2, a3, normed, inv, mod, sent):
    group = meta[3] * 2 + meta[4]
    stats = stats_of(a0, 4 * TILE)
    for a in (a1, a2, a3):
        stats = stats + stats_of(a, 4 * TILE)
    scale = 1.0 + lane_piece(mod[1, group], meta[1])
    for t in range(4):
        span = slice(t * TILE, (t + 1) * TILE)
        grad = a0[span, :].astype(F32)
        for a in (a1, a2, a3):
            grad = grad + a[span, :].astype(F32)
        value = inv[t] * (grad * scale - column(stats[t : t + 1]) - normed[t] * column(stats[4 + t : 5 + t]))
        sent[t] = value.astype(BF)


def upstream_piece_kernel(meta, ids, coeffs, first, mod, t1, t2, t3, out):
    group = meta[3] * 2 + meta[4]
    after, decay, weight = decays(meta, ids, coeffs)
    gate = lane_piece(mod[2, group], meta[1]) * weight
    for t in range(4):
        later = t1[t].astype(F32) + t2[t].astype(F32) * after[0] + t3[t].astype(F32) * (after[0] * after[1])
        out[t] = (first[mod4(meta[1] - t)].astype(F32) + gate * later).astype(BF)


def column(row):
    return jnp.transpose(jnp.broadcast_to(row * (1.0 / FEATS), (TILE, TILE)))


def term_kernel(meta, a0, a1, a2, a3, normed, inv, mod, term, sent, moments):
    group = meta[3] * 2 + meta[4]
    grad = a0[0:TILE, :].astype(F32)
    stats = stats_of(a0, TILE)
    for a in (a1, a2, a3):
        grad = grad + a[0:TILE, :].astype(F32)
        stats = stats + stats_of(a, TILE)
    first = stats[0:1, 0:TILE]
    second = stats[0:1, TILE : 2 * TILE]
    moments[...] = jnp.concatenate([first, second], axis=0) * (FEATS**-0.5)

    def wide(value):
        return jnp.concatenate([value] * 3, axis=1)

    du = grad * (1.0 + mod[1, group])
    value = wide(inv[...]) * (du - wide(column(first)) - normed[...] * wide(column(second)))
    term[...] = value
    sent[...] = value.astype(BF)


def decays(meta, ids, coeffs):
    step = meta[0]
    after = []
    for ahead in (1, 2, 3):
        at = jnp.minimum(step + ahead, 3)
        after.append(jnp.where(step + ahead <= 3, coeffs[0, ids[at]], 1.0))
    return after, coeffs[0, ids[step]], coeffs[1, ids[step]]


def lam_of(meta, ids, coeffs, cot, terms):
    after, decay, weight = decays(meta, ids, coeffs)
    lam = cot[...] * (after[0] * after[1] * after[2])
    for ref, factor in zip(terms, (1.0, after[0], after[0] * after[1])):
        lam = lam + ref[...].astype(F32) * factor
    return lam, decay, weight


def cut_kernel(meta, ids, coeffs, cot_far, mod_far, w_far, o0, o1, o2, o3, cot, mod, w, sems):
    copies = [
        pltpu.make_async_copy(src, dst, sems.at[i])
        for i, (src, dst) in enumerate(((cot_far, cot), (mod_far, mod), (w_far, w)))
    ]
    for copy in copies:
        copy.start()
    for copy in copies:
        copy.wait()
    zhi = meta[1]
    group = meta[3] * 2 + meta[4]
    lam, decay, weight = lam_of(meta, ids, coeffs, cot, ())
    up = mod[2, group] * weight * lam
    for d, o in enumerate((o0, o1, o2, o3)):
        at = mod4(zhi + d)
        for part in range(3):
            o[part * 48 : (part + 1) * 48, :] = lane_piece(w[part].astype(F32), at).astype(BF)
        o[144:272, :] = lane_piece(up, at).astype(BF)


def adjoint_kernel(meta, ids, coeffs, cot, term, t1, t2, t3, out):
    lam, decay, weight = lam_of(meta, ids, coeffs, cot, (t1, t2, t3))
    out[...] = decay * lam + term[...]


def turn(value, axis, offset):
    return lax.ppermute(value, axis, [(i, (i + offset) % 4) for i in range(4)])


def ring4(value, axis):
    return [value] + [turn(value, axis, -offset) for offset in PLACES[1:]]


def hand_on(before, after, axis):
    pairs = []
    for i in range(4):
        pairs.append((2 * i, 2 * ((i - 1) % 4)))
        pairs.append((2 * i + 1, 2 * ((i + 1) % 4) + 1))
    return lax.ppermute(jnp.where(lax.axis_index("core") == 0, after, before), (axis, "core"), pairs)


def relayed(value, axis):
    before, after = turn(value, axis, 1), turn(value, axis, -1)
    return [value, before, after, hand_on(before, after, axis)]


def to_heads(pieces):
    got = [pieces[0]]
    for d in (1, 2, 3):
        pairs = [(i, (i + d) % 4) for i in range(4) if (i + d) % 4 != 3]
        got.append(lax.ppermute(pieces[d], "zhi", pairs))
    return got


def to_earlier(value):
    return [lax.ppermute(value, "step", [(j, j - d) for j in range(d, 4)]) for d in (1, 2, 3)]


def relay_hop(value):
    pairs = []
    for i in range(4):
        pairs.append((2 * i, 2 * ((i + 1) % 4)))
        pairs.append((2 * i + 1, 2 * ((i - 1) % 4) + 1))
    return lax.ppermute(value, ("zhi", "core"), pairs)


def exchange_zhi(blocks):
    half_way = relay_hop(blocks[2])
    one, three = turn(blocks[1], "zhi", 1), turn(blocks[3], "zhi", 3)
    return [blocks[0], one, relay_hop(half_way), three]


def along_z(value, offset):
    return lax.ppermute(value, ("zhi", "zlo"), [(i, (i + offset) % 16) for i in range(16)])


def far_z(value):
    pairs = []
    for i in range(16):
        pairs.append((2 * i, 2 * ((i + 2) % 16)))
        pairs.append((2 * i + 1, 2 * ((i - 2) % 16) + 1))
    return lax.ppermute(value, ("zhi", "zlo", "core"), pairs)


def other_core(value):
    return lax.ppermute(value, "core", [(0, 1), (1, 0)])


def shards(states, modulation, cotangent, w_qkv, q_gain, k_gain, step_ids, coeffs, neighbours):
    zhi = lax.axis_index("zhi")
    meta = jnp.stack([lax.axis_index(a) for a in ("step", "zhi", "y", "zlo", "core")]).astype(jnp.int32)
    coeffs, neighbours = coeffs.T, neighbours.T
    mod = modulation.reshape(3, 8, 1, WIDTH)
    gq = (q_gain / jnp.sqrt(jnp.float32(HD))).reshape(1, HD)
    gk = k_gain.reshape(1, HD)

    pieces = call(
        cut_kernel,
        [sds((272, HD), BF)] * 4,
        (meta, step_ids, coeffs, cotangent, mod, jnp.transpose(w_qkv, (1, 0, 2))),
        3,
        [
            pltpu.VMEM((TILE, WIDTH), F32),
            pltpu.VMEM((3, 8, 1, WIDTH), F32),
            pltpu.VMEM((3, 48, WIDTH), BF),
            pltpu.SemaphoreType.DMA((3,)),
        ],
        grant=12,
        far=3,
    )
    *pieces, x = lax.optimization_barrier((*pieces, states[0]))

    before, after = turn(x, "zhi", 1), turn(x, "zhi", -1)
    pieces = to_heads(pieces)
    own_rows = jnp.stack([p[0:144] for p in pieces])
    own_up = jnp.stack([p[144:272] for p in pieces])
    own_rows, before, after = lax.optimization_barrier((own_rows, before, after))
    far = hand_on(before, after, "zhi")
    y_rows = lax.all_gather(own_rows, "y")
    y_rows, far = lax.optimization_barrier((y_rows, far))
    wg = lax.all_gather(y_rows, "step").reshape(16, 4, 144, HD)
    x_tiles = jnp.stack([x, before, far, after])
    xa = [x_tiles, along_z(x_tiles, 1), along_z(x_tiles, -1), far_z(x_tiles)]
    own_up, xa[3] = lax.optimization_barrier((own_up, xa[3]))
    first_ups = relayed(own_up, "y")
    xb = [other_core(a) for a in xa]

    tokens = 4 * TILE
    scaled, normed, inv, normed_piece, inv_all = call(
        norm_kernel,
        [
            sds((8, 4, TILE, WIDTH), BF),
            sds((TILE, WIDTH), F32),
            sds((TILE, HD), F32),
            sds((4, TILE, HD), F32),
            sds((4, TILE, HD), F32),
        ],
        (meta, *xa, *xb, mod),
        1,
        (),
        0,
        16,
    )
    scaled, wg, *first_ups = lax.optimization_barrier((scaled, wg, *first_ups))
    qkv, proj, wk, ws, vec = call(
        proj_kernel,
        [
            sds((4, TILE, WIDTH), BF),
            sds((tokens, WIDTH), F32),
            sds((4, 8, 48, WIDTH), BF),
            sds((4, 8, 48, WIDTH), BF),
            sds((16, WIDTH), F32),
        ],
        (meta, scaled, wg, mod, gq, gk),
        1,
        [pltpu.VMEM((8, 8, 48, WIDTH), BF)],
        2 * tokens * FEATS * WIDTH,
        24,
    )
    wr = other_core(ws)
    all_qkv = relayed(qkv, "y")

    again = first_ups
    for sweep in range(SWEEPS):
        outs = [sds((tokens + 16, WIDTH), BF), sds((4, 3, WIDTH, TILE), F32)]
        dproj, *kept = call(
            sweep_kernel,
            outs[: 2 - sweep],
            (meta, neighbours, *all_qkv, proj, vec, gq, gk, *again),
            2,
            [pltpu.VMEM((16, TILE, WIDTH), BF), pltpu.VMEM((16, TILE, HD), BF)],
            400 * 1000 * 1000,
            16,
        )
        parts = call(
            feature_kernel,
            [sds((tokens + 16, WIDTH), BF)] * 4,
            (meta, dproj, other_core(dproj), wk, wr),
            1,
            (),
            2 * tokens * FEATS * WIDTH,
            16,
        )
        near = [parts[0], along_z(parts[1], 1), far_z(parts[2]), along_z(parts[3], -1)]
        if sweep + 1 < SWEEPS:
            blocks = call(window_piece_kernel, [sds((tokens + 16, HD), BF)] * 4, (meta, *near), 1)
            (sent,) = call(
                term_piece_kernel,
                [sds((4, TILE, HD), BF)],
                (meta, *exchange_zhi(blocks), normed_piece, inv_all, mod),
                1,
            )
            (up,) = call(
                upstream_piece_kernel,
                [sds((4, TILE, HD), BF)],
                (meta, step_ids, coeffs, first_ups[0], mod, *to_earlier(sent)),
                3,
            )
            again = (lax.all_gather(up, "y"), *kept)
    blocks = call(window_kernel, [sds((TILE + 16, WIDTH), BF)] * 4, (meta, *near), 1)
    got = exchange_zhi(blocks)
    term, sent, moments = call(
        term_kernel,
        [sds((TILE, WIDTH), F32), sds((TILE, WIDTH), BF), sds((2, TILE), F32)],
        (meta, *got, normed, inv, mod),
        1,
    )
    (adjoint,) = call(
        adjoint_kernel,
        [sds((TILE, WIDTH), F32)],
        (meta, step_ids, coeffs, cotangent, term, *to_earlier(sent)),
        3,
    )
    return adjoint[None], moments[None]


def solution(mesh):
    fine = Mesh(mesh.devices.reshape(4, 4, 4, 4, 2), ("step", "zhi", "y", "zlo", "core"))
    blk, head = ("zhi", "y"), ("zlo", "core")
    in_specs = (
        P("step", blk, head),
        P("step", None, None),
        P(blk, head),
        P(("step",) + blk, None, head),
        P(),
        P(),
        P(),
        P(),
        P(),
    )
    out_specs = (P("step", blk, head), P("step", None, blk))
    return jax.shard_map(shards, mesh=fine, in_specs=in_specs, out_specs=out_specs, check_vma=False)
```

```python
import jax
import jax.numpy as jnp
from jax import lax
from jax.experimental import pallas as pl
from jax.experimental.pallas import tpu as pltpu
from jax.sharding import Mesh
from jax.sharding import PartitionSpec as P

HD = 128
TILE = 128
WIDTH = 384
FEATS = 3072
SWEEPS = 2
EPS = 1e-06
BF = jnp.bfloat16
F32 = jnp.float32
MIB = 1024 * 1024
PLACES = (0, -1, 1, 2)

VM = pl.BlockSpec(memory_space=pltpu.VMEM)
SM = pl.BlockSpec(memory_space=pltpu.SMEM)


def call(body, outs, args, smem, scratch=(), flops=0, grant=8, far=0):
    specs = [SM if i < smem else VM for i in range(len(args))]
    specs[smem : smem + far] = [pl.BlockSpec(memory_space=pl.ANY)] * far
    moved = sum(a.size * a.dtype.itemsize for a in args) + sum(
        o.size * o.dtype.itemsize for o in outs
    )
    return pl.pallas_call(
        body,
        out_shape=tuple(outs),
        in_specs=specs,
        out_specs=tuple([VM] * len(outs)),
        scratch_shapes=list(scratch),
        compiler_params=pltpu.CompilerParams(vmem_limit_bytes=grant * MIB),
        cost_estimate=pl.CostEstimate(flops=flops, bytes_accessed=moved, transcendentals=0),
    )(*args)


def sds(shape, dtype):
    return jax.ShapeDtypeStruct(shape, dtype)


def nt(a, b):
    return lax.dot_general(a, b, (((1,), (1,)), ((), ())), preferred_element_type=F32)


def tn(a, b):
    return lax.dot_general(a, b, (((0,), (0,)), ((), ())), preferred_element_type=F32)


def nn(a, b):
    return jnp.dot(a, b, preferred_element_type=F32)


def hi_lo(value):
    hi = value.astype(BF)
    return hi, (value - hi.astype(F32)).astype(BF)


def mod4(value):
    return lax.rem(value + 8, 4)


def lane_piece(value, at):
    out = jnp.zeros(value.shape[:-1] + (HD,), value.dtype)
    for i in range(3):
        out = jnp.where(at == i, value[..., i * HD : (i + 1) * HD], out)
    return out


def norm_kernel(
    meta, xa0, xa1, xa2, xa3, xb0, xb1, xb2, xb3, mod,
    scaled, normed_own, inv_own, normed_piece, inv_all,
):
    zhi, zlo, core = meta[1], meta[3], meta[4]
    place = zhi * 4 + zlo
    own_far = jnp.where(core == 0, -2, 2)
    sources = []
    for refs, side, far in (
        ((xa0, xa1, xa2, xa3), core, own_far),
        ((xb0, xb1, xb2, xb3), 1 - core, -own_far),
    ):
        for ref, offset in zip(refs, (0, -1, 1, far)):
            at = lax.rem(place + offset + 16, 16)
            sources.append((ref, at // 4, lax.rem(at, 4) * 2 + side))

    rows = 32

    def chunk(turn, carry):
        t = turn // (TILE // rows)
        start = lax.rem(turn, TILE // rows) * rows
        span = pl.ds(pl.multiple_of(start, rows), rows)

        def load(source):
            ref, z, g = source
            d = mod4(z - t)
            return ref[d, span, :].astype(F32)

        total = jnp.zeros((rows, WIDTH), F32)
        for source in sources:
            total = total + load(source)
        mean = jnp.sum(total, axis=1, keepdims=True) * (1.0 / FEATS)
        square = jnp.zeros((rows, WIDTH), F32)
        for source in sources:
            centred = load(source) - mean
            square = square + centred * centred
        inv = lax.rsqrt(jnp.sum(square, axis=1, keepdims=True) * (1.0 / FEATS) + EPS)
        for source in sources:
            normed = (load(source) - mean) * inv
            scaled[source[2], t, span, :] = (normed * (1.0 + mod[1, source[2]])).astype(BF)
        normed = (load(sources[0]) - mean) * inv
        normed_piece[t, span, :] = lane_piece(normed, zhi)
        inv_all[t, span, :] = jnp.broadcast_to(inv, (rows, HD))

        @pl.when(t == zhi)
        def _():
            normed_own[span, :] = normed
            inv_own[span, :] = jnp.broadcast_to(inv, (rows, HD))

        return carry

    lax.fori_loop(0, 4 * (TILE // rows), chunk, 0)


def proj_kernel(
    meta, nscr, wg, mod, q_gain, k_gain,
    qkv, proj, wk, ws, vec, wc,
):
    zhi, core = meta[1], meta[4]
    for d in range(4):
        zh = mod4(zhi - d)
        for sy in range(16):
            for part in range(3):
                wc[(sy // 4) * 2 + zh // 2, lax.rem(zh, 2) * 4 + sy % 4, :, part * HD : (part + 1) * HD] = (
                    wg[sy, d, part * 48 : (part + 1) * 48, :]
                )
    for r in range(4):
        wk[r] = wc[2 * r + core]
        ws[r] = wc[2 * r + 1 - core]

    acc = jnp.zeros((4 * TILE, WIDTH), F32)
    flat = jnp.zeros((16, WIDTH), F32)
    for g in range(8):
        w_g = wc[g].reshape(WIDTH, WIDTH)
        acc = acc + nn(nscr[g].reshape(4 * TILE, WIDTH), w_g)
        scale_hi, scale_lo = hi_lo(1.0 + mod[1, g])
        shift_hi, shift_lo = hi_lo(mod[0, g])
        four = jnp.concatenate([scale_hi, scale_lo, shift_hi, shift_lo], axis=0)
        lhs = jnp.concatenate([four, jnp.zeros((12, WIDTH), BF)], axis=0)
        flat = flat + nn(lhs, w_g)
    vec[...] = flat
    proj[...] = acc + (flat[2:3] + flat[3:4])
    for t in range(4):
        span = slice(t * TILE, (t + 1) * TILE)
        q = proj[span, 0:HD]
        k = proj[span, HD : 2 * HD]
        q_inv = lax.rsqrt(jnp.mean(q * q, axis=1, keepdims=True) + EPS)
        k_inv = lax.rsqrt(jnp.mean(k * k, axis=1, keepdims=True) + EPS)
        qkv[t, :, 0:HD] = (q * q_inv * q_gain[...]).astype(BF)
        qkv[t, :, HD : 2 * HD] = (k * k_inv * k_gain[...]).astype(BF)
        qkv[t, :, 2 * HD : 3 * HD] = proj[span, 2 * HD : 3 * HD].astype(BF)


def norm_back(raw, gain, grad):
    inv = lax.rsqrt(jnp.mean(raw * raw, axis=1, keepdims=True) + EPS)
    scaled = grad * gain
    dot = jnp.mean(scaled * raw, axis=1, keepdims=True)
    return inv * (scaled - raw * (inv * inv * dot))


def sweep_kernel(
    meta, nb, k0, k1, k2, k3, proj, vec, q_gain, k_gain, *rest
):
    tiles, ups = rest[-2:]
    first_sweep = len(rest) == 8
    probs, out = (rest[5], rest[4]) if first_sweep else (rest[1], rest[2])
    zhi, y = meta[1], meta[2]
    for ref, offset in zip((k0, k1, k2, k3), PLACES):
        yy = mod4(y + offset)
        for z in range(4):
            tiles[z * 4 + yy] = ref[z]
    for i, offset in enumerate(PLACES):
        for z in range(4):
            if first_sweep:
                ups[mod4(zhi - z) * 4 + mod4(y + offset)] = rest[i][z]
            else:
                ups[z * 4 + i] = rest[0][i, z]

    m1_hi, m1_lo = hi_lo(vec[0:1] + vec[1:2])
    m1 = jnp.concatenate([m1_hi, m1_lo, jnp.zeros((14, WIDTH), BF)], axis=0)
    ones = jnp.ones((16, WIDTH), BF)
    s0 = vec[2:3] + vec[3:4]

    def k_of(t):
        return tiles[t, :, HD : 2 * HD]

    def v_of(t):
        return tiles[t, :, 2 * HD : 3 * HD]

    def own(jz, carry):
        j = jz * 4 + y
        near = (nb[1, j], nb[2, j])
        d_k = jnp.zeros((TILE, HD), F32)
        d_v = jnp.zeros((TILE, HD), F32)
        d_q = None
        for slot in range(3):
            if slot == 0:
                i = j
                keys = (j, near[0], near[1])
            else:
                i = near[slot - 1]
                keys = (j, i, nb[1, i] + nb[2, i] - j)
            q = tiles[i, :, 0:HD]
            up = ups[i]
            k_all = jnp.concatenate([k_of(t) for t in keys], axis=0)
            v_all = jnp.concatenate([v_of(t) for t in keys], axis=0)
            if first_sweep:
                expo = jnp.exp(nt(k_all, q))
                prob = expo * (1.0 / jnp.sum(expo, axis=0, keepdims=True))
                probs[jz, slot] = prob
            else:
                prob = probs[jz, slot]
            prob_b = prob.astype(BF)
            dprob = nt(v_all, up)
            delta = jnp.sum(prob_b.astype(F32) * dprob, axis=0, keepdims=True)
            if slot == 0:
                dscore = (prob * (dprob - delta)).astype(BF)
                d_q = tn(dscore, k_all)
                dscore = dscore[0:TILE]
            else:
                dscore = (prob[0:TILE] * (dprob[0:TILE] - delta)).astype(BF)
            d_k = d_k + nn(dscore, q)
            d_v = d_v + nn(prob_b[0:TILE], up)
        start = pl.multiple_of(jz * TILE, TILE)
        raw = proj[pl.ds(start, TILE), :]
        d_q = norm_back(raw[:, 0:HD], q_gain[...], d_q)
        d_k = norm_back(raw[:, HD : 2 * HD], k_gain[...], d_k)
        d_all = jnp.concatenate([d_q, d_k, d_v], axis=1).astype(BF)
        out[pl.ds(start, TILE), :] = d_all
        first = nt(m1, d_all)
        prod_hi, prod_lo = hi_lo(d_all.astype(F32) * (raw - s0))
        second = nt(ones, prod_hi) + nt(ones, prod_lo)
        row = jnp.concatenate(
            [first[0:1] + first[1:2], second[0:1], jnp.zeros((1, TILE), F32)], axis=1
        )
        at = lax.broadcasted_iota(jnp.int32, (8, WIDTH), 0)
        return carry + jnp.where(at == jz, row, 0.0)

    stats = lax.fori_loop(0, 4, own, jnp.zeros((8, WIDTH), F32))
    out[4 * TILE : 4 * TILE + 16, :] = jnp.concatenate(hi_lo(stats), axis=0)


def stats_of(ref, start):
    both = ref[start : start + 16, :].astype(F32)
    return both[0:8] + both[8:16]


def feature_kernel(meta, own, other, wk, wr, o0, o1, o2, o3):
    zlo = meta[3]
    stats = jnp.concatenate(hi_lo(stats_of(own, 4 * TILE) + stats_of(other, 4 * TILE)), axis=0)
    for offset, o in enumerate((o0, o1, o2, o3)):
        r = mod4(zlo + offset)
        value = nt(own[0 : 4 * TILE, :], wk[r].reshape(WIDTH, WIDTH))
        value = value + nt(other[0 : 4 * TILE, :], wr[r].reshape(WIDTH, WIDTH))
        o[0 : 4 * TILE, :] = value.astype(BF)
        o[4 * TILE : 4 * TILE + 16, :] = stats


def window_kernel(meta, a0, a1, a2, a3, o0, o1, o2, o3):
    zhi = meta[1]
    refs = (a0, a1, a2, a3)
    stats = stats_of(a0, 4 * TILE)
    for a in refs[1:]:
        stats = stats + stats_of(a, 4 * TILE)
    at = lax.broadcasted_iota(jnp.int32, (8, WIDTH), 0)
    for d, o in enumerate((o0, o1, o2, o3)):
        t = mod4(zhi + d)
        span = pl.ds(pl.multiple_of(t * TILE, TILE), TILE)
        value = a0[span, :].astype(F32)
        for a in refs[1:]:
            value = value + a[span, :].astype(F32)
        o[0:TILE, :] = value.astype(BF)
        row = jnp.sum(jnp.where(at == t, stats, 0.0), axis=0, keepdims=True)
        o[TILE : TILE + 16, :] = jnp.concatenate(
            hi_lo(jnp.broadcast_to(row, (8, WIDTH))), axis=0
        )


def window_piece_kernel(meta, a0, a1, a2, a3, o0, o1, o2, o3):
    zhi = meta[1]
    refs = (a0, a1, a2, a3)
    stats = stats_of(a0, 4 * TILE)
    for a in refs[1:]:
        stats = stats + stats_of(a, 4 * TILE)
    stats = jnp.concatenate(hi_lo(jnp.concatenate([stats[0:4, 0:TILE], stats[0:4, TILE : 2 * TILE]], axis=0)), axis=0)
    for t in range(4):
        span = slice(t * TILE, (t + 1) * TILE)
        value = a0[span, :].astype(F32)
        for a in refs[1:]:
            value = value + a[span, :].astype(F32)
        for d, o in enumerate((o0, o1, o2, o3)):
            o[span, :] = lane_piece(value, mod4(zhi + d)).astype(BF)
    for d, o in enumerate((o0, o1, o2, o3)):
        keep = jnp.where(mod4(zhi + d) == 3, 0.0, 1.0)
        o[4 * TILE : 4 * TILE + 16, :] = (stats.astype(F32) * keep).astype(BF)


def term_piece_kernel(meta, a0, a1, a2, a3, normed, inv, mod, sent):
    group = meta[3] * 2 + meta[4]
    stats = stats_of(a0, 4 * TILE)
    for a in (a1, a2, a3):
        stats = stats + stats_of(a, 4 * TILE)
    scale = 1.0 + lane_piece(mod[1, group], meta[1])
    for t in range(4):
        span = slice(t * TILE, (t + 1) * TILE)
        grad = a0[span, :].astype(F32)
        for a in (a1, a2, a3):
            grad = grad + a[span, :].astype(F32)
        value = inv[t] * (grad * scale - column(stats[t : t + 1]) - normed[t] * column(stats[4 + t : 5 + t]))
        sent[t] = value.astype(BF)


def upstream_piece_kernel(meta, ids, coeffs, first, mod, t1, t2, t3, out):
    group = meta[3] * 2 + meta[4]
    after, decay, weight = decays(meta, ids, coeffs)
    gate = lane_piece(mod[2, group], meta[1]) * weight
    for t in range(4):
        later = t1[t].astype(F32) + t2[t].astype(F32) * after[0] + t3[t].astype(F32) * (after[0] * after[1])
        out[t] = (first[mod4(meta[1] - t)].astype(F32) + gate * later).astype(BF)


def column(row):
    return jnp.transpose(jnp.broadcast_to(row * (1.0 / FEATS), (TILE, TILE)))


def term_kernel(meta, a0, a1, a2, a3, normed, inv, mod, term, sent, moments):
    group = meta[3] * 2 + meta[4]
    grad = a0[0:TILE, :].astype(F32)
    stats = stats_of(a0, TILE)
    for a in (a1, a2, a3):
        grad = grad + a[0:TILE, :].astype(F32)
        stats = stats + stats_of(a, TILE)
    first = stats[0:1, 0:TILE]
    second = stats[0:1, TILE : 2 * TILE]
    moments[...] = jnp.concatenate([first, second], axis=0) * (FEATS**-0.5)

    def wide(value):
        return jnp.concatenate([value] * 3, axis=1)

    du = grad * (1.0 + mod[1, group])
    value = wide(inv[...]) * (du - wide(column(first)) - normed[...] * wide(column(second)))
    term[...] = value
    sent[...] = value.astype(BF)


def decays(meta, ids, coeffs):
    step = meta[0]
    after = []
    for ahead in (1, 2, 3):
        at = jnp.minimum(step + ahead, 3)
        after.append(jnp.where(step + ahead <= 3, coeffs[0, ids[at]], 1.0))
    return after, coeffs[0, ids[step]], coeffs[1, ids[step]]


def lam_of(meta, ids, coeffs, cot, terms):
    after, decay, weight = decays(meta, ids, coeffs)
    lam = cot[...] * (after[0] * after[1] * after[2])
    for ref, factor in zip(terms, (1.0, after[0], after[0] * after[1])):
        lam = lam + ref[...].astype(F32) * factor
    return lam, decay, weight


def cut_kernel(meta, ids, coeffs, cot_far, mod_far, w_far, o0, o1, o2, o3, cot, mod, w, sems):
    copies = [
        pltpu.make_async_copy(src, dst, sems.at[i])
        for i, (src, dst) in enumerate(((cot_far, cot), (mod_far, mod), (w_far, w)))
    ]
    for copy in copies:
        copy.start()
    for copy in copies:
        copy.wait()
    zhi = meta[1]
    group = meta[3] * 2 + meta[4]
    lam, decay, weight = lam_of(meta, ids, coeffs, cot, ())
    up = mod[2, group] * weight * lam
    for d, o in enumerate((o0, o1, o2, o3)):
        at = mod4(zhi + d)
        for part in range(3):
            o[part * 48 : (part + 1) * 48, :] = lane_piece(w[part].astype(F32), at).astype(BF)
        o[144:272, :] = lane_piece(up, at).astype(BF)


def adjoint_kernel(meta, ids, coeffs, cot, term, t1, t2, t3, out):
    lam, decay, weight = lam_of(meta, ids, coeffs, cot, (t1, t2, t3))
    out[...] = decay * lam + term[...]


def turn(value, axis, offset):
    return lax.ppermute(value, axis, [(i, (i + offset) % 4) for i in range(4)])


def ring4(value, axis):
    return [value] + [turn(value, axis, -offset) for offset in PLACES[1:]]


def hand_on(before, after, axis):
    pairs = []
    for i in range(4):
        pairs.append((2 * i, 2 * ((i - 1) % 4)))
        pairs.append((2 * i + 1, 2 * ((i + 1) % 4) + 1))
    return lax.ppermute(jnp.where(lax.axis_index("core") == 0, after, before), (axis, "core"), pairs)


def relayed(value, axis):
    before, after = turn(value, axis, 1), turn(value, axis, -1)
    return [value, before, after, hand_on(before, after, axis)]


def to_heads(pieces):
    got = [pieces[0]]
    for d in (1, 2, 3):
        pairs = [(i, (i + d) % 4) for i in range(4) if (i + d) % 4 != 3]
        got.append(lax.ppermute(pieces[d], "zhi", pairs))
    return got


def to_earlier(value):
    return [lax.ppermute(value, "step", [(j, j - d) for j in range(d, 4)]) for d in (1, 2, 3)]


def relay_hop(value):
    pairs = []
    for i in range(4):
        pairs.append((2 * i, 2 * ((i + 1) % 4)))
        pairs.append((2 * i + 1, 2 * ((i - 1) % 4) + 1))
    return lax.ppermute(value, ("zhi", "core"), pairs)


def exchange_zhi(blocks):
    half_way = relay_hop(blocks[2])
    one, three = turn(blocks[1], "zhi", 1), turn(blocks[3], "zhi", 3)
    return [blocks[0], one, relay_hop(half_way), three]


def along_z(value, offset):
    return lax.ppermute(value, ("zhi", "zlo"), [(i, (i + offset) % 16) for i in range(16)])


def far_z(value):
    pairs = []
    for i in range(16):
        pairs.append((2 * i, 2 * ((i + 2) % 16)))
        pairs.append((2 * i + 1, 2 * ((i - 2) % 16) + 1))
    return lax.ppermute(value, ("zhi", "zlo", "core"), pairs)


def other_core(value):
    return lax.ppermute(value, "core", [(0, 1), (1, 0)])


def shards(states, modulation, cotangent, w_qkv, q_gain, k_gain, step_ids, coeffs, neighbours):
    zhi = lax.axis_index("zhi")
    meta = jnp.stack([lax.axis_index(a) for a in ("step", "zhi", "y", "zlo", "core")]).astype(jnp.int32)
    coeffs, neighbours = coeffs.T, neighbours.T
    mod = modulation.reshape(3, 8, 1, WIDTH)
    gq = (q_gain / jnp.sqrt(jnp.float32(HD))).reshape(1, HD)
    gk = k_gain.reshape(1, HD)

    pieces = call(
        cut_kernel,
        [sds((272, HD), BF)] * 4,
        (meta, step_ids, coeffs, cotangent, mod, jnp.transpose(w_qkv, (1, 0, 2))),
        3,
        [
            pltpu.VMEM((TILE, WIDTH), F32),
            pltpu.VMEM((3, 8, 1, WIDTH), F32),
            pltpu.VMEM((3, 48, WIDTH), BF),
            pltpu.SemaphoreType.DMA((3,)),
        ],
        grant=12,
        far=3,
    )
    *pieces, x = lax.optimization_barrier((*pieces, states[0]))

    before, after = turn(x, "zhi", 1), turn(x, "zhi", -1)
    pieces = to_heads(pieces)
    own_rows = jnp.stack([p[0:144] for p in pieces])
    own_up = jnp.stack([p[144:272] for p in pieces])
    own_rows, before, after = lax.optimization_barrier((own_rows, before, after))
    far = hand_on(before, after, "zhi")
    y_rows = lax.all_gather(own_rows, "y")
    y_rows, far, own_up = lax.optimization_barrier((y_rows, far, own_up))
    wg = lax.all_gather(y_rows, "step").reshape(16, 4, 144, HD)
    x_tiles = jnp.stack([x, before, far, after])
    xa = [x_tiles, along_z(x_tiles, 1), along_z(x_tiles, -1), far_z(x_tiles)]
    up_before, up_after = turn(own_up, "y", 1), turn(own_up, "y", -1)
    up_before, up_after, xa[3] = lax.optimization_barrier((up_before, up_after, xa[3]))
    first_ups = [own_up, up_before, up_after, hand_on(up_before, up_after, "y")]
    xb = [other_core(a) for a in xa]

    tokens = 4 * TILE
    scaled, normed, inv, normed_piece, inv_all = call(
        norm_kernel,
        [
            sds((8, 4, TILE, WIDTH), BF),
            sds((TILE, WIDTH), F32),
            sds((TILE, HD), F32),
            sds((4, TILE, HD), F32),
            sds((4, TILE, HD), F32),
        ],
        (meta, *xa, *xb, mod),
        1,
        (),
        0,
        16,
    )
    scaled, wg, *first_ups = lax.optimization_barrier((scaled, wg, *first_ups))
    qkv, proj, wk, ws, vec = call(
        proj_kernel,
        [
            sds((4, TILE, WIDTH), BF),
            sds((tokens, WIDTH), F32),
            sds((4, 8, 48, WIDTH), BF),
            sds((4, 8, 48, WIDTH), BF),
            sds((16, WIDTH), F32),
        ],
        (meta, scaled, wg, mod, gq, gk),
        1,
        [pltpu.VMEM((8, 8, 48, WIDTH), BF)],
        2 * tokens * FEATS * WIDTH,
        24,
    )
    all_qkv = relayed(qkv, "y")
    all_qkv[3], ws = lax.optimization_barrier((all_qkv[3], ws))
    wr = other_core(ws)

    again = first_ups
    for sweep in range(SWEEPS):
        outs = [sds((tokens + 16, WIDTH), BF), sds((4, 3, WIDTH, TILE), F32)]
        dproj, *kept = call(
            sweep_kernel,
            outs[: 2 - sweep],
            (meta, neighbours, *all_qkv, proj, vec, gq, gk, *again),
            2,
            [pltpu.VMEM((16, TILE, WIDTH), BF), pltpu.VMEM((16, TILE, HD), BF)],
            400 * 1000 * 1000,
            16,
        )
        parts = call(
            feature_kernel,
            [sds((tokens + 16, WIDTH), BF)] * 4,
            (meta, dproj, other_core(dproj), wk, wr),
            1,
            (),
            2 * tokens * FEATS * WIDTH,
            16,
        )
        near = [parts[0], along_z(parts[1], 1), far_z(parts[2]), along_z(parts[3], -1)]
        if sweep + 1 < SWEEPS:
            blocks = call(window_piece_kernel, [sds((tokens + 16, HD), BF)] * 4, (meta, *near), 1)
            (sent,) = call(
                term_piece_kernel,
                [sds((4, TILE, HD), BF)],
                (meta, *exchange_zhi(blocks), normed_piece, inv_all, mod),
                1,
            )
            (up,) = call(
                upstream_piece_kernel,
                [sds((4, TILE, HD), BF)],
                (meta, step_ids, coeffs, first_ups[0], mod, *to_earlier(sent)),
                3,
            )
            again = (lax.all_gather(up, "y"), *kept)
    blocks = call(window_kernel, [sds((TILE + 16, WIDTH), BF)] * 4, (meta, *near), 1)
    got = exchange_zhi(blocks)
    term, sent, moments = call(
        term_kernel,
        [sds((TILE, WIDTH), F32), sds((TILE, WIDTH), BF), sds((2, TILE), F32)],
        (meta, *got, normed, inv, mod),
        1,
    )
    (adjoint,) = call(
        adjoint_kernel,
        [sds((TILE, WIDTH), F32)],
        (meta, step_ids, coeffs, cotangent, term, *to_earlier(sent)),
        3,
    )
    return adjoint[None], moments[None]


def solution(mesh):
    fine = Mesh(mesh.devices.reshape(4, 4, 4, 4, 2), ("step", "zhi", "y", "zlo", "core"))
    blk, head = ("zhi", "y"), ("zlo", "core")
    in_specs = (
        P("step", blk, head),
        P("step", None, None),
        P(blk, head),
        P(("step",) + blk, None, head),
        P(),
        P(),
        P(),
        P(),
        P(),
    )
    out_specs = (P("step", blk, head), P("step", None, blk))
    return jax.shard_map(shards, mesh=fine, in_specs=in_specs, out_specs=out_specs, check_vma=False)
```

```python
import functools

import jax
import jax.numpy as jnp
from jax import lax
from jax.experimental import pallas as pl
from jax.experimental.pallas import tpu as pltpu
from jax.sharding import Mesh
from jax.sharding import PartitionSpec as P

HD = 128
TILE = 128
WIDTH = 384
FEATS = 3072
SWEEPS = 2
EPS = 1e-06
BF = jnp.bfloat16
F32 = jnp.float32
MIB = 1024 * 1024
PLACES = (0, -1, 1, 2)

VM = pl.BlockSpec(memory_space=pltpu.VMEM)
SM = pl.BlockSpec(memory_space=pltpu.SMEM)


def call(body, outs, args, smem, scratch=(), flops=0, grant=8, far=0):
    specs = [SM if i < smem else VM for i in range(len(args))]
    specs[smem : smem + far] = [pl.BlockSpec(memory_space=pl.ANY)] * far
    moved = sum(a.size * a.dtype.itemsize for a in args) + sum(
        o.size * o.dtype.itemsize for o in outs
    )
    return pl.pallas_call(
        body,
        out_shape=tuple(outs),
        in_specs=specs,
        out_specs=tuple([VM] * len(outs)),
        scratch_shapes=list(scratch),
        compiler_params=pltpu.CompilerParams(vmem_limit_bytes=grant * MIB),
        cost_estimate=pl.CostEstimate(flops=flops, bytes_accessed=moved, transcendentals=0),
    )(*args)


def sds(shape, dtype):
    return jax.ShapeDtypeStruct(shape, dtype)


def nt(a, b):
    return lax.dot_general(a, b, (((1,), (1,)), ((), ())), preferred_element_type=F32)


def tn(a, b):
    return lax.dot_general(a, b, (((0,), (0,)), ((), ())), preferred_element_type=F32)


def nn(a, b):
    return jnp.dot(a, b, preferred_element_type=F32)


def hi_lo(value):
    hi = value.astype(BF)
    return hi, (value - hi.astype(F32)).astype(BF)


def mod4(value):
    return lax.rem(value + 8, 4)


def lane_piece(value, at):
    out = jnp.zeros(value.shape[:-1] + (HD,), value.dtype)
    for i in range(3):
        out = jnp.where(at == i, value[..., i * HD : (i + 1) * HD], out)
    return out


def norm_kernel(
    meta, xa0, xa1, xa2, xa3, xb0, xb1, xb2, xb3, mod,
    scaled, normed_own, inv_own, normed_piece, inv_all,
):
    zhi, zlo, core = meta[1], meta[3], meta[4]
    place = zhi * 4 + zlo
    own_far = jnp.where(core == 0, -2, 2)
    sources = []
    for refs, side, far in (
        ((xa0, xa1, xa2, xa3), core, own_far),
        ((xb0, xb1, xb2, xb3), 1 - core, -own_far),
    ):
        for ref, offset in zip(refs, (0, -1, 1, far)):
            at = lax.rem(place + offset + 16, 16)
            sources.append((ref, at // 4, lax.rem(at, 4) * 2 + side))

    rows = 32

    def chunk(turn, carry):
        t = turn // (TILE // rows)
        start = lax.rem(turn, TILE // rows) * rows
        span = pl.ds(pl.multiple_of(start, rows), rows)

        def load(source):
            ref, z, g = source
            d = mod4(z - t)
            return ref[d, span, :].astype(F32)

        total = jnp.zeros((rows, WIDTH), F32)
        for source in sources:
            total = total + load(source)
        mean = jnp.sum(total, axis=1, keepdims=True) * (1.0 / FEATS)
        square = jnp.zeros((rows, WIDTH), F32)
        for source in sources:
            centred = load(source) - mean
            square = square + centred * centred
        inv = lax.rsqrt(jnp.sum(square, axis=1, keepdims=True) * (1.0 / FEATS) + EPS)
        for source in sources:
            normed = (load(source) - mean) * inv
            scaled[source[2], t, span, :] = (normed * (1.0 + mod[1, source[2]])).astype(BF)
        normed = (load(sources[0]) - mean) * inv
        normed_piece[t, span, :] = lane_piece(normed, zhi)
        inv_all[t, span, :] = jnp.broadcast_to(inv, (rows, HD))

        @pl.when(t == zhi)
        def _():
            normed_own[span, :] = normed
            inv_own[span, :] = jnp.broadcast_to(inv, (rows, HD))

        return carry

    lax.fori_loop(0, 4 * (TILE // rows), chunk, 0)


def proj_kernel(
    meta, nscr, wg, mod, q_gain, k_gain,
    qkv, proj, wk, ws, vec, wc,
):
    zhi, core = meta[1], meta[4]
    for d in range(4):
        zh = mod4(zhi - d)
        for sy in range(16):
            for part in range(3):
                wc[(sy // 4) * 2 + zh // 2, lax.rem(zh, 2) * 4 + sy % 4, :, part * HD : (part + 1) * HD] = (
                    wg[sy, d, part * 48 : (part + 1) * 48, :]
                )
    for r in range(4):
        wk[r] = wc[2 * r + core]
        ws[r] = wc[2 * r + 1 - core]

    acc = jnp.zeros((4 * TILE, WIDTH), F32)
    flat = jnp.zeros((16, WIDTH), F32)
    for g in range(8):
        w_g = wc[g].reshape(WIDTH, WIDTH)
        acc = acc + nn(nscr[g].reshape(4 * TILE, WIDTH), w_g)
        scale_hi, scale_lo = hi_lo(1.0 + mod[1, g])
        shift_hi, shift_lo = hi_lo(mod[0, g])
        four = jnp.concatenate([scale_hi, scale_lo, shift_hi, shift_lo], axis=0)
        lhs = jnp.concatenate([four, jnp.zeros((12, WIDTH), BF)], axis=0)
        flat = flat + nn(lhs, w_g)
    vec[...] = flat
    proj[...] = acc + (flat[2:3] + flat[3:4])
    for t in range(4):
        span = slice(t * TILE, (t + 1) * TILE)
        q = proj[span, 0:HD]
        k = proj[span, HD : 2 * HD]
        q_inv = lax.rsqrt(jnp.mean(q * q, axis=1, keepdims=True) + EPS)
        k_inv = lax.rsqrt(jnp.mean(k * k, axis=1, keepdims=True) + EPS)
        qkv[t, :, 0:HD] = (q * q_inv * q_gain[...]).astype(BF)
        qkv[t, :, HD : 2 * HD] = (k * k_inv * k_gain[...]).astype(BF)
        qkv[t, :, 2 * HD : 3 * HD] = proj[span, 2 * HD : 3 * HD].astype(BF)


def norm_back(raw, gain, grad):
    inv = lax.rsqrt(jnp.mean(raw * raw, axis=1, keepdims=True) + EPS)
    scaled = grad * gain
    dot = jnp.mean(scaled * raw, axis=1, keepdims=True)
    return inv * (scaled - raw * (inv * inv * dot))


def sweep_kernel(
    meta, nb, k0, k1, k2, k3, proj, vec, q_gain, k_gain, *rest
):
    tiles, ups = rest[-2:]
    first_sweep = len(rest) == 8
    probs, out = (rest[5], rest[4]) if first_sweep else (rest[1], rest[2])
    zhi, y = meta[1], meta[2]
    for ref, offset in zip((k0, k1, k2, k3), PLACES):
        yy = mod4(y + offset)
        for z in range(4):
            tiles[z * 4 + yy] = ref[z]
    for i, offset in enumerate(PLACES):
        for z in range(4):
            if first_sweep:
                ups[mod4(zhi - z) * 4 + mod4(y + offset)] = rest[i][z]
            else:
                ups[z * 4 + i] = rest[0][i, z]

    m1_hi, m1_lo = hi_lo(vec[0:1] + vec[1:2])
    m1 = jnp.concatenate([m1_hi, m1_lo, jnp.zeros((14, WIDTH), BF)], axis=0)
    ones = jnp.ones((16, WIDTH), BF)
    s0 = vec[2:3] + vec[3:4]

    def k_of(t):
        return tiles[t, :, HD : 2 * HD]

    def v_of(t):
        return tiles[t, :, 2 * HD : 3 * HD]

    def own(jz, carry):
        j = jz * 4 + y
        near = (nb[1, j], nb[2, j])
        d_k = jnp.zeros((TILE, HD), F32)
        d_v = jnp.zeros((TILE, HD), F32)
        d_q = None
        for slot in range(3):
            if slot == 0:
                i = j
                keys = (j, near[0], near[1])
            else:
                i = near[slot - 1]
                keys = (j, i, nb[1, i] + nb[2, i] - j)
            q = tiles[i, :, 0:HD]
            up = ups[i]
            k_all = jnp.concatenate([k_of(t) for t in keys], axis=0)
            v_all = jnp.concatenate([v_of(t) for t in keys], axis=0)
            if first_sweep:
                expo = jnp.exp(nt(k_all, q))
                prob = expo * (1.0 / jnp.sum(expo, axis=0, keepdims=True))
                probs[jz, slot] = prob
            else:
                prob = probs[jz, slot]
            prob_b = prob.astype(BF)
            dprob = nt(v_all, up)
            delta = jnp.sum(prob_b.astype(F32) * dprob, axis=0, keepdims=True)
            if slot == 0:
                dscore = (prob * (dprob - delta)).astype(BF)
                d_q = tn(dscore, k_all)
                dscore = dscore[0:TILE]
            else:
                dscore = (prob[0:TILE] * (dprob[0:TILE] - delta)).astype(BF)
            d_k = d_k + nn(dscore, q)
            d_v = d_v + nn(prob_b[0:TILE], up)
        start = pl.multiple_of(jz * TILE, TILE)
        raw = proj[pl.ds(start, TILE), :]
        d_q = norm_back(raw[:, 0:HD], q_gain[...], d_q)
        d_k = norm_back(raw[:, HD : 2 * HD], k_gain[...], d_k)
        d_all = jnp.concatenate([d_q, d_k, d_v], axis=1).astype(BF)
        out[pl.ds(start, TILE), :] = d_all
        first = nt(m1, d_all)
        prod_hi, prod_lo = hi_lo(d_all.astype(F32) * (raw - s0))
        second = nt(ones, prod_hi) + nt(ones, prod_lo)
        row = jnp.concatenate(
            [first[0:1] + first[1:2], second[0:1], jnp.zeros((1, TILE), F32)], axis=1
        )
        at = lax.broadcasted_iota(jnp.int32, (8, WIDTH), 0)
        return carry + jnp.where(at == jz, row, 0.0)

    stats = lax.fori_loop(0, 4, own, jnp.zeros((8, WIDTH), F32))
    out[4 * TILE : 4 * TILE + 16, :] = jnp.concatenate(hi_lo(stats), axis=0)


def stats_of(ref, start):
    both = ref[start : start + 16, :].astype(F32)
    return both[0:8] + both[8:16]


def feature_kernel(offsets, meta, own, other, wk, wr, *outs):
    zlo = meta[3]
    stats = jnp.concatenate(hi_lo(stats_of(own, 4 * TILE) + stats_of(other, 4 * TILE)), axis=0)
    for offset, o in zip(offsets, outs):
        r = mod4(zlo + offset)
        value = nt(own[0 : 4 * TILE, :], wk[r].reshape(WIDTH, WIDTH))
        value = value + nt(other[0 : 4 * TILE, :], wr[r].reshape(WIDTH, WIDTH))
        o[0 : 4 * TILE, :] = value.astype(BF)
        o[4 * TILE : 4 * TILE + 16, :] = stats


def features(offsets, args):
    return call(
        functools.partial(feature_kernel, offsets),
        [sds((4 * TILE + 16, WIDTH), BF)] * len(offsets),
        args,
        1,
        (),
        2 * 4 * TILE * FEATS * WIDTH * len(offsets) // 4,
        16,
    )


def window_kernel(meta, a0, a1, a2, a3, o0, o1, o2, o3):
    zhi = meta[1]
    refs = (a0, a1, a2, a3)
    stats = stats_of(a0, 4 * TILE)
    for a in refs[1:]:
        stats = stats + stats_of(a, 4 * TILE)
    at = lax.broadcasted_iota(jnp.int32, (8, WIDTH), 0)
    for d, o in enumerate((o0, o1, o2, o3)):
        t = mod4(zhi + d)
        span = pl.ds(pl.multiple_of(t * TILE, TILE), TILE)
        value = a0[span, :].astype(F32)
        for a in refs[1:]:
            value = value + a[span, :].astype(F32)
        o[0:TILE, :] = value.astype(BF)
        row = jnp.sum(jnp.where(at == t, stats, 0.0), axis=0, keepdims=True)
        o[TILE : TILE + 16, :] = jnp.concatenate(
            hi_lo(jnp.broadcast_to(row, (8, WIDTH))), axis=0
        )


def window_piece_kernel(meta, a0, a1, a2, a3, o0, o1, o2, o3):
    zhi = meta[1]
    refs = (a0, a1, a2, a3)
    stats = stats_of(a0, 4 * TILE)
    for a in refs[1:]:
        stats = stats + stats_of(a, 4 * TILE)
    stats = jnp.concatenate(hi_lo(jnp.concatenate([stats[0:4, 0:TILE], stats[0:4, TILE : 2 * TILE]], axis=0)), axis=0)
    for t in range(4):
        span = slice(t * TILE, (t + 1) * TILE)
        value = a0[span, :].astype(F32)
        for a in refs[1:]:
            value = value + a[span, :].astype(F32)
        for d, o in enumerate((o0, o1, o2, o3)):
            o[span, :] = lane_piece(value, mod4(zhi + d)).astype(BF)
    for d, o in enumerate((o0, o1, o2, o3)):
        keep = jnp.where(mod4(zhi + d) == 3, 0.0, 1.0)
        o[4 * TILE : 4 * TILE + 16, :] = (stats.astype(F32) * keep).astype(BF)


def term_piece_kernel(meta, a0, a1, a2, a3, normed, inv, mod, sent):
    group = meta[3] * 2 + meta[4]
    stats = stats_of(a0, 4 * TILE)
    for a in (a1, a2, a3):
        stats = stats + stats_of(a, 4 * TILE)
    scale = 1.0 + lane_piece(mod[1, group], meta[1])
    for t in range(4):
        span = slice(t * TILE, (t + 1) * TILE)
        grad = a0[span, :].astype(F32)
        for a in (a1, a2, a3):
            grad = grad + a[span, :].astype(F32)
        value = inv[t] * (grad * scale - column(stats[t : t + 1]) - normed[t] * column(stats[4 + t : 5 + t]))
        sent[t] = value.astype(BF)


def upstream_piece_kernel(meta, ids, coeffs, first, mod, t1, t2, t3, out):
    group = meta[3] * 2 + meta[4]
    after, decay, weight = decays(meta, ids, coeffs)
    gate = lane_piece(mod[2, group], meta[1]) * weight
    for t in range(4):
        later = t1[t].astype(F32) + t2[t].astype(F32) * after[0] + t3[t].astype(F32) * (after[0] * after[1])
        out[t] = (first[mod4(meta[1] - t)].astype(F32) + gate * later).astype(BF)


def column(row):
    return jnp.transpose(jnp.broadcast_to(row * (1.0 / FEATS), (TILE, TILE)))


def term_kernel(meta, a0, a1, a2, a3, normed, inv, mod, term, sent, moments):
    group = meta[3] * 2 + meta[4]
    grad = a0[0:TILE, :].astype(F32)
    stats = stats_of(a0, TILE)
    for a in (a1, a2, a3):
        grad = grad + a[0:TILE, :].astype(F32)
        stats = stats + stats_of(a, TILE)
    first = stats[0:1, 0:TILE]
    second = stats[0:1, TILE : 2 * TILE]
    moments[...] = jnp.concatenate([first, second], axis=0) * (FEATS**-0.5)

    def wide(value):
        return jnp.concatenate([value] * 3, axis=1)

    du = grad * (1.0 + mod[1, group])
    value = wide(inv[...]) * (du - wide(column(first)) - normed[...] * wide(column(second)))
    term[...] = value
    sent[...] = value.astype(BF)


def decays(meta, ids, coeffs):
    step = meta[0]
    after = []
    for ahead in (1, 2, 3):
        at = jnp.minimum(step + ahead, 3)
        after.append(jnp.where(step + ahead <= 3, coeffs[0, ids[at]], 1.0))
    return after, coeffs[0, ids[step]], coeffs[1, ids[step]]


def lam_of(meta, ids, coeffs, cot, terms):
    after, decay, weight = decays(meta, ids, coeffs)
    lam = cot[...] * (after[0] * after[1] * after[2])
    for ref, factor in zip(terms, (1.0, after[0], after[0] * after[1])):
        lam = lam + ref[...].astype(F32) * factor
    return lam, decay, weight


def cut_kernel(meta, ids, coeffs, cot_far, mod_far, w_far, o0, o1, o2, o3, cot, mod, w, sems):
    copies = [
        pltpu.make_async_copy(src, dst, sems.at[i])
        for i, (src, dst) in enumerate(((cot_far, cot), (mod_far, mod), (w_far, w)))
    ]
    for copy in copies:
        copy.start()
    for copy in copies:
        copy.wait()
    zhi = meta[1]
    group = meta[3] * 2 + meta[4]
    lam, decay, weight = lam_of(meta, ids, coeffs, cot, ())
    up = mod[2, group] * weight * lam
    for d, o in enumerate((o0, o1, o2, o3)):
        at = mod4(zhi + d)
        for part in range(3):
            o[part * 48 : (part + 1) * 48, :] = lane_piece(w[part].astype(F32), at).astype(BF)
        o[144:272, :] = lane_piece(up, at).astype(BF)


def adjoint_kernel(meta, ids, coeffs, cot, term, t1, t2, t3, out):
    lam, decay, weight = lam_of(meta, ids, coeffs, cot, (t1, t2, t3))
    out[...] = decay * lam + term[...]


def turn(value, axis, offset):
    return lax.ppermute(value, axis, [(i, (i + offset) % 4) for i in range(4)])


def ring4(value, axis):
    return [value] + [turn(value, axis, -offset) for offset in PLACES[1:]]


def hand_on(before, after, axis):
    pairs = []
    for i in range(4):
        pairs.append((2 * i, 2 * ((i - 1) % 4)))
        pairs.append((2 * i + 1, 2 * ((i + 1) % 4) + 1))
    return lax.ppermute(jnp.where(lax.axis_index("core") == 0, after, before), (axis, "core"), pairs)


def relayed(value, axis):
    before, after = turn(value, axis, 1), turn(value, axis, -1)
    return [value, before, after, hand_on(before, after, axis)]


def to_heads(pieces):
    got = [pieces[0]]
    for d in (1, 2, 3):
        pairs = [(i, (i + d) % 4) for i in range(4) if (i + d) % 4 != 3]
        got.append(lax.ppermute(pieces[d], "zhi", pairs))
    return got


def to_earlier(value):
    return [lax.ppermute(value, "step", [(j, j - d) for j in range(d, 4)]) for d in (1, 2, 3)]


def relay_hop(value):
    pairs = []
    for i in range(4):
        pairs.append((2 * i, 2 * ((i + 1) % 4)))
        pairs.append((2 * i + 1, 2 * ((i - 1) % 4) + 1))
    return lax.ppermute(value, ("zhi", "core"), pairs)


def exchange_zhi(blocks):
    half_way = relay_hop(blocks[2])
    one, three = turn(blocks[1], "zhi", 1), turn(blocks[3], "zhi", 3)
    return [blocks[0], one, relay_hop(half_way), three]


def along_z(value, offset):
    return lax.ppermute(value, ("zhi", "zlo"), [(i, (i + offset) % 16) for i in range(16)])


def far_z(value):
    pairs = []
    for i in range(16):
        pairs.append((2 * i, 2 * ((i + 2) % 16)))
        pairs.append((2 * i + 1, 2 * ((i - 2) % 16) + 1))
    return lax.ppermute(value, ("zhi", "zlo", "core"), pairs)


def other_core(value):
    return lax.ppermute(value, "core", [(0, 1), (1, 0)])


def shards(states, modulation, cotangent, w_qkv, q_gain, k_gain, step_ids, coeffs, neighbours):
    zhi = lax.axis_index("zhi")
    meta = jnp.stack([lax.axis_index(a) for a in ("step", "zhi", "y", "zlo", "core")]).astype(jnp.int32)
    coeffs, neighbours = coeffs.T, neighbours.T
    mod = modulation.reshape(3, 8, 1, WIDTH)
    gq = (q_gain / jnp.sqrt(jnp.float32(HD))).reshape(1, HD)
    gk = k_gain.reshape(1, HD)

    pieces = call(
        cut_kernel,
        [sds((272, HD), BF)] * 4,
        (meta, step_ids, coeffs, cotangent, mod, jnp.transpose(w_qkv, (1, 0, 2))),
        3,
        [
            pltpu.VMEM((TILE, WIDTH), F32),
            pltpu.VMEM((3, 8, 1, WIDTH), F32),
            pltpu.VMEM((3, 48, WIDTH), BF),
            pltpu.SemaphoreType.DMA((3,)),
        ],
        grant=12,
        far=3,
    )
    pieces = to_heads(pieces)
    own_rows = jnp.stack([p[0:144] for p in pieces])
    pieces[1], x = lax.optimization_barrier((pieces[1], states[0]))
    own_up = jnp.stack([p[144:272] for p in pieces])

    before, after = turn(x, "zhi", 1), turn(x, "zhi", -1)
    y_rows = lax.all_gather(own_rows, "y")
    y_rows, before, after, own_up = lax.optimization_barrier((y_rows, before, after, own_up))
    far = hand_on(before, after, "zhi")
    wg = lax.all_gather(y_rows, "step").reshape(16, 4, 144, HD)
    x_tiles = jnp.stack([x, before, far, after])
    xa = [x_tiles, along_z(x_tiles, 1), along_z(x_tiles, -1), far_z(x_tiles)]
    up_before, up_after = turn(own_up, "y", 1), turn(own_up, "y", -1)
    up_before, up_after, xa[3] = lax.optimization_barrier((up_before, up_after, xa[3]))
    first_ups = [own_up, up_before, up_after, hand_on(up_before, up_after, "y")]
    xb = [other_core(a) for a in xa]

    tokens = 4 * TILE
    scaled, normed, inv, normed_piece, inv_all = call(
        norm_kernel,
        [
            sds((8, 4, TILE, WIDTH), BF),
            sds((TILE, WIDTH), F32),
            sds((TILE, HD), F32),
            sds((4, TILE, HD), F32),
            sds((4, TILE, HD), F32),
        ],
        (meta, *xa, *xb, mod),
        1,
        (),
        0,
        16,
    )
    scaled, wg, *first_ups = lax.optimization_barrier((scaled, wg, *first_ups))
    qkv, proj, wk, ws, vec = call(
        proj_kernel,
        [
            sds((4, TILE, WIDTH), BF),
            sds((tokens, WIDTH), F32),
            sds((4, 8, 48, WIDTH), BF),
            sds((4, 8, 48, WIDTH), BF),
            sds((16, WIDTH), F32),
        ],
        (meta, scaled, wg, mod, gq, gk),
        1,
        [pltpu.VMEM((8, 8, 48, WIDTH), BF)],
        2 * tokens * FEATS * WIDTH,
        24,
    )
    all_qkv = relayed(qkv, "y")
    all_qkv[3], ws = lax.optimization_barrier((all_qkv[3], ws))
    wr = other_core(ws)

    again = first_ups
    for sweep in range(SWEEPS):
        outs = [sds((tokens + 16, WIDTH), BF), sds((4, 3, WIDTH, TILE), F32)]
        dproj, *kept = call(
            sweep_kernel,
            outs[: 2 - sweep],
            (meta, neighbours, *all_qkv, proj, vec, gq, gk, *again),
            2,
            [pltpu.VMEM((16, TILE, WIDTH), BF), pltpu.VMEM((16, TILE, HD), BF)],
            400 * 1000 * 1000,
            16,
        )
        pair = (meta, dproj, other_core(dproj), wk, wr)
        (far,) = features((2,), pair)
        here, above, below = features((0, 1, 3), pair)
        near = [here, along_z(above, 1), far_z(far), along_z(below, -1)]
        if sweep + 1 < SWEEPS:
            blocks = call(window_piece_kernel, [sds((tokens + 16, HD), BF)] * 4, (meta, *near), 1)
            (sent,) = call(
                term_piece_kernel,
                [sds((4, TILE, HD), BF)],
                (meta, *exchange_zhi(blocks), normed_piece, inv_all, mod),
                1,
            )
            (up,) = call(
                upstream_piece_kernel,
                [sds((4, TILE, HD), BF)],
                (meta, step_ids, coeffs, first_ups[0], mod, *to_earlier(sent)),
                3,
            )
            again = (lax.all_gather(up, "y"), *kept)
    blocks = call(window_kernel, [sds((TILE + 16, WIDTH), BF)] * 4, (meta, *near), 1)
    got = exchange_zhi(blocks)
    term, sent, moments = call(
        term_kernel,
        [sds((TILE, WIDTH), F32), sds((TILE, WIDTH), BF), sds((2, TILE), F32)],
        (meta, *got, normed, inv, mod),
        1,
    )
    (adjoint,) = call(
        adjoint_kernel,
        [sds((TILE, WIDTH), F32)],
        (meta, step_ids, coeffs, cotangent, term, *to_earlier(sent)),
        3,
    )
    return adjoint[None], moments[None]


def solution(mesh):
    fine = Mesh(mesh.devices.reshape(4, 4, 4, 4, 2), ("step", "zhi", "y", "zlo", "core"))
    blk, head = ("zhi", "y"), ("zlo", "core")
    in_specs = (
        P("step", blk, head),
        P("step", None, None),
        P(blk, head),
        P(("step",) + blk, None, head),
        P(),
        P(),
        P(),
        P(),
        P(),
    )
    out_specs = (P("step", blk, head), P("step", None, blk))
    return jax.shard_map(shards, mesh=fine, in_specs=in_specs, out_specs=out_specs, check_vma=False)
```

```python
import functools

import jax
import jax.numpy as jnp
from jax import lax
from jax.experimental import pallas as pl
from jax.experimental.pallas import tpu as pltpu
from jax.sharding import Mesh
from jax.sharding import PartitionSpec as P

HD = 128
TILE = 128
WIDTH = 384
FEATS = 3072
SWEEPS = 2
EPS = 1e-06
BF = jnp.bfloat16
F32 = jnp.float32
MIB = 1024 * 1024
PLACES = (0, -1, 1, 2)

VM = pl.BlockSpec(memory_space=pltpu.VMEM)
SM = pl.BlockSpec(memory_space=pltpu.SMEM)
HBM = pl.BlockSpec(memory_space=pltpu.HBM)


def call(body, outs, args, smem, scratch=(), flops=0, grant=8, far=0, far_outs=0):
    specs = [SM if i < smem else VM for i in range(len(args))]
    specs[smem : smem + far] = [HBM] * far
    moved = sum(a.size * a.dtype.itemsize for a in args) + sum(
        o.size * o.dtype.itemsize for o in outs
    )
    return pl.pallas_call(
        body,
        out_shape=tuple(outs),
        in_specs=specs,
        out_specs=tuple([VM] * (len(outs) - far_outs) + [HBM] * far_outs),
        scratch_shapes=list(scratch),
        compiler_params=pltpu.CompilerParams(vmem_limit_bytes=grant * MIB),
        cost_estimate=pl.CostEstimate(flops=flops, bytes_accessed=moved, transcendentals=0),
    )(*args)


def sds(shape, dtype):
    return jax.ShapeDtypeStruct(shape, dtype)


def nt(a, b):
    return lax.dot_general(a, b, (((1,), (1,)), ((), ())), preferred_element_type=F32)


def tn(a, b):
    return lax.dot_general(a, b, (((0,), (0,)), ((), ())), preferred_element_type=F32)


def nn(a, b):
    return jnp.dot(a, b, preferred_element_type=F32)


def hi_lo(value):
    hi = value.astype(BF)
    return hi, (value - hi.astype(F32)).astype(BF)


def mod4(value):
    return lax.rem(value + 8, 4)


def lane_piece(value, at):
    out = jnp.zeros(value.shape[:-1] + (HD,), value.dtype)
    for i in range(3):
        out = jnp.where(at == i, value[..., i * HD : (i + 1) * HD], out)
    return out


def norm_kernel(
    meta, xa0, xa1, xa2, xa3, xb0, xb1, xb2, xb3, mod,
    scaled, far_own, far_own_inv, far_piece, far_inv,
    normed_own, inv_own, normed_piece, inv_all, sems,
):
    zhi, zlo, core = meta[1], meta[3], meta[4]
    place = zhi * 4 + zlo
    own_far = jnp.where(core == 0, -2, 2)
    sources = []
    for refs, side, far in (
        ((xa0, xa1, xa2, xa3), core, own_far),
        ((xb0, xb1, xb2, xb3), 1 - core, -own_far),
    ):
        for ref, offset in zip(refs, (0, -1, 1, far)):
            at = lax.rem(place + offset + 16, 16)
            sources.append((ref, at // 4, lax.rem(at, 4) * 2 + side))

    rows = 32

    def chunk(turn, carry):
        t = turn // (TILE // rows)
        start = lax.rem(turn, TILE // rows) * rows
        span = pl.ds(pl.multiple_of(start, rows), rows)

        def load(source):
            ref, z, g = source
            d = mod4(z - t)
            return ref[d, span, :].astype(F32)

        total = jnp.zeros((rows, WIDTH), F32)
        for source in sources:
            total = total + load(source)
        mean = jnp.sum(total, axis=1, keepdims=True) * (1.0 / FEATS)
        square = jnp.zeros((rows, WIDTH), F32)
        for source in sources:
            centred = load(source) - mean
            square = square + centred * centred
        inv = lax.rsqrt(jnp.sum(square, axis=1, keepdims=True) * (1.0 / FEATS) + EPS)
        for source in sources:
            normed = (load(source) - mean) * inv
            scaled[source[2], t, span, :] = (normed * (1.0 + mod[1, source[2]])).astype(BF)
        normed = (load(sources[0]) - mean) * inv
        normed_piece[t, span, :] = lane_piece(normed, zhi)
        inv_all[t, span, :] = jnp.broadcast_to(inv, (rows, HD))

        @pl.when(t == zhi)
        def _():
            normed_own[span, :] = normed
            inv_own[span, :] = jnp.broadcast_to(inv, (rows, HD))

        return carry

    lax.fori_loop(0, 4 * (TILE // rows), chunk, 0)
    pairs = ((normed_own, far_own), (inv_own, far_own_inv), (normed_piece, far_piece), (inv_all, far_inv))
    copies = [pltpu.make_async_copy(src, dst, sems.at[i]) for i, (src, dst) in enumerate(pairs)]
    for copy in copies:
        copy.start()
    for copy in copies:
        copy.wait()


def proj_kernel(
    meta, wg_far, nscr, mod, q_gain, k_gain,
    qkv, proj, wk, ws, vec, wc, wg, sems,
):
    zhi, core = meta[1], meta[4]
    copies = [pltpu.make_async_copy(wg_far.at[i], wg.at[i], sems.at[i]) for i in range(16)]
    for copy in copies:
        copy.start()
    for sy in range(16):
        copies[sy].wait()
        for d in range(4):
            zh = mod4(zhi - d)
            for part in range(3):
                wc[(sy // 4) * 2 + zh // 2, lax.rem(zh, 2) * 4 + sy % 4, :, part * HD : (part + 1) * HD] = (
                    wg[sy, d, part * 48 : (part + 1) * 48, :]
                )
    for r in range(4):
        wk[r] = wc[2 * r + core]
        ws[r] = wc[2 * r + 1 - core]

    acc = jnp.zeros((4 * TILE, WIDTH), F32)
    flat = jnp.zeros((16, WIDTH), F32)
    for g in range(8):
        w_g = wc[g].reshape(WIDTH, WIDTH)
        acc = acc + nn(nscr[g].reshape(4 * TILE, WIDTH), w_g)
        scale_hi, scale_lo = hi_lo(1.0 + mod[1, g])
        shift_hi, shift_lo = hi_lo(mod[0, g])
        four = jnp.concatenate([scale_hi, scale_lo, shift_hi, shift_lo], axis=0)
        lhs = jnp.concatenate([four, jnp.zeros((12, WIDTH), BF)], axis=0)
        flat = flat + nn(lhs, w_g)
    vec[...] = flat
    proj[...] = acc + (flat[2:3] + flat[3:4])
    for t in range(4):
        span = slice(t * TILE, (t + 1) * TILE)
        q = proj[span, 0:HD]
        k = proj[span, HD : 2 * HD]
        q_inv = lax.rsqrt(jnp.mean(q * q, axis=1, keepdims=True) + EPS)
        k_inv = lax.rsqrt(jnp.mean(k * k, axis=1, keepdims=True) + EPS)
        qkv[t, :, 0:HD] = (q * q_inv * q_gain[...]).astype(BF)
        qkv[t, :, HD : 2 * HD] = (k * k_inv * k_gain[...]).astype(BF)
        qkv[t, :, 2 * HD : 3 * HD] = proj[span, 2 * HD : 3 * HD].astype(BF)


def norm_back(raw, gain, grad):
    inv = lax.rsqrt(jnp.mean(raw * raw, axis=1, keepdims=True) + EPS)
    scaled = grad * gain
    dot = jnp.mean(scaled * raw, axis=1, keepdims=True)
    return inv * (scaled - raw * (inv * inv * dot))


def sweep_kernel(
    meta, nb, k0, k1, k2, k3, proj, vec, q_gain, k_gain, *rest
):
    tiles, ups = rest[-2:]
    first_sweep = len(rest) == 8
    probs, out = (rest[5], rest[4]) if first_sweep else (rest[1], rest[2])
    zhi, y = meta[1], meta[2]
    for ref, offset in zip((k0, k1, k2, k3), PLACES):
        yy = mod4(y + offset)
        for z in range(4):
            tiles[z * 4 + yy] = ref[z]
    for i, offset in enumerate(PLACES):
        for z in range(4):
            if first_sweep:
                ups[mod4(zhi - z) * 4 + mod4(y + offset)] = rest[i][z]
            else:
                ups[z * 4 + i] = rest[0][i, z]

    m1_hi, m1_lo = hi_lo(vec[0:1] + vec[1:2])
    m1 = jnp.concatenate([m1_hi, m1_lo, jnp.zeros((14, WIDTH), BF)], axis=0)
    ones = jnp.ones((16, WIDTH), BF)
    s0 = vec[2:3] + vec[3:4]

    def k_of(t):
        return tiles[t, :, HD : 2 * HD]

    def v_of(t):
        return tiles[t, :, 2 * HD : 3 * HD]

    def own(jz, carry):
        j = jz * 4 + y
        near = (nb[1, j], nb[2, j])
        d_k = jnp.zeros((TILE, HD), F32)
        d_v = jnp.zeros((TILE, HD), F32)
        d_q = None
        for slot in range(3):
            if slot == 0:
                i = j
                keys = (j, near[0], near[1])
            else:
                i = near[slot - 1]
                keys = (j, i, nb[1, i] + nb[2, i] - j)
            q = tiles[i, :, 0:HD]
            up = ups[i]
            k_all = jnp.concatenate([k_of(t) for t in keys], axis=0)
            v_all = jnp.concatenate([v_of(t) for t in keys], axis=0)
            if first_sweep:
                expo = jnp.exp(nt(k_all, q))
                prob = expo * (1.0 / jnp.sum(expo, axis=0, keepdims=True))
                probs[jz, slot] = prob
            else:
                prob = probs[jz, slot]
            prob_b = prob.astype(BF)
            dprob = nt(v_all, up)
            delta = jnp.sum(prob_b.astype(F32) * dprob, axis=0, keepdims=True)
            if slot == 0:
                dscore = (prob * (dprob - delta)).astype(BF)
                d_q = tn(dscore, k_all)
                dscore = dscore[0:TILE]
            else:
                dscore = (prob[0:TILE] * (dprob[0:TILE] - delta)).astype(BF)
            d_k = d_k + nn(dscore, q)
            d_v = d_v + nn(prob_b[0:TILE], up)
        start = pl.multiple_of(jz * TILE, TILE)
        raw = proj[pl.ds(start, TILE), :]
        d_q = norm_back(raw[:, 0:HD], q_gain[...], d_q)
        d_k = norm_back(raw[:, HD : 2 * HD], k_gain[...], d_k)
        d_all = jnp.concatenate([d_q, d_k, d_v], axis=1).astype(BF)
        out[pl.ds(start, TILE), :] = d_all
        first = nt(m1, d_all)
        prod_hi, prod_lo = hi_lo(d_all.astype(F32) * (raw - s0))
        second = nt(ones, prod_hi) + nt(ones, prod_lo)
        row = jnp.concatenate(
            [first[0:1] + first[1:2], second[0:1], jnp.zeros((1, TILE), F32)], axis=1
        )
        at = lax.broadcasted_iota(jnp.int32, (8, WIDTH), 0)
        return carry + jnp.where(at == jz, row, 0.0)

    stats = lax.fori_loop(0, 4, own, jnp.zeros((8, WIDTH), F32))
    out[4 * TILE : 4 * TILE + 16, :] = jnp.concatenate(hi_lo(stats), axis=0)


def stats_of(ref, start):
    both = ref[start : start + 16, :].astype(F32)
    return both[0:8] + both[8:16]


def route(meta):
    forward = meta[4] == 0
    return jnp.where(forward, 3, 1), jnp.where(forward, 1, 3)


def feature_kernel(far_only, meta, own, other, wk, wr, *outs):
    zlo = meta[3]
    stats = jnp.concatenate(hi_lo(stats_of(own, 4 * TILE) + stats_of(other, 4 * TILE)), axis=0)
    for offset, o in zip((2,) if far_only else (0, *route(meta)), outs):
        r = mod4(zlo + offset)
        value = nt(own[0 : 4 * TILE, :], wk[r].reshape(WIDTH, WIDTH))
        value = value + nt(other[0 : 4 * TILE, :], wr[r].reshape(WIDTH, WIDTH))
        o[0 : 4 * TILE, :] = value.astype(BF)
        o[4 * TILE : 4 * TILE + 16, :] = stats


def features(far_only, args):
    count = 1 if far_only else 3
    return call(
        functools.partial(feature_kernel, far_only),
        [sds((4 * TILE + 16, WIDTH), BF)] * count,
        args,
        1,
        (),
        2 * 4 * TILE * FEATS * WIDTH * count // 4,
        16,
    )


def add_kernel(a, b, out):
    rows = out.shape[0] - 16
    out[0:rows, :] = (a[0:rows, :].astype(F32) + b[0:rows, :].astype(F32)).astype(BF)
    out[rows : rows + 16, :] = jnp.concatenate(hi_lo(stats_of(a, rows) + stats_of(b, rows)), axis=0)


def window_kernel(meta, a0, a1, a2, *outs):
    zhi = meta[1]
    stats = stats_of(a0, 4 * TILE) + stats_of(a1, 4 * TILE) + stats_of(a2, 4 * TILE)
    at = lax.broadcasted_iota(jnp.int32, (8, WIDTH), 0)
    for d, o in zip((0, 2, *route(meta)), outs):
        t = mod4(zhi + d)
        span = pl.ds(pl.multiple_of(t * TILE, TILE), TILE)
        o[0:TILE, :] = (a0[span, :].astype(F32) + a1[span, :].astype(F32) + a2[span, :].astype(F32)).astype(BF)
        row = jnp.sum(jnp.where(at == t, stats, 0.0), axis=0, keepdims=True)
        o[TILE : TILE + 16, :] = jnp.concatenate(hi_lo(jnp.broadcast_to(row, (8, WIDTH))), axis=0)


def window_piece_kernel(meta, a0, a1, a2, *outs):
    zhi = meta[1]
    places = [mod4(zhi + d) for d in (0, 2, *route(meta))]
    stats = stats_of(a0, 4 * TILE) + stats_of(a1, 4 * TILE) + stats_of(a2, 4 * TILE)
    stats = jnp.concatenate([stats[0:4, 0:TILE], stats[0:4, TILE : 2 * TILE]], axis=0)
    for t in range(4):
        span = slice(t * TILE, (t + 1) * TILE)
        value = a0[span, :].astype(F32) + a1[span, :].astype(F32) + a2[span, :].astype(F32)
        for at, o in zip(places, outs):
            o[span, :] = lane_piece(value, at).astype(BF)
    for at, o in zip(places, outs):
        o[4 * TILE : 4 * TILE + 16, :] = jnp.concatenate(hi_lo(stats * jnp.where(at == 3, 0.0, 1.0)), axis=0)


def term_piece_kernel(meta, a0, a1, a2, normed, inv, mod, sent):
    group = meta[3] * 2 + meta[4]
    stats = stats_of(a0, 4 * TILE)
    for a in (a1, a2):
        stats = stats + stats_of(a, 4 * TILE)
    scale = 1.0 + lane_piece(mod[1, group], meta[1])
    for t in range(4):
        span = slice(t * TILE, (t + 1) * TILE)
        grad = a0[span, :].astype(F32)
        for a in (a1, a2):
            grad = grad + a[span, :].astype(F32)
        value = inv[t] * (grad * scale - column(stats[t : t + 1]) - normed[t] * column(stats[4 + t : 5 + t]))
        sent[t] = value.astype(BF)


def upstream_piece_kernel(meta, ids, coeffs, first, mod, t1, t2, t3, out):
    group = meta[3] * 2 + meta[4]
    after, decay, weight = decays(meta, ids, coeffs)
    gate = lane_piece(mod[2, group], meta[1]) * weight
    for t in range(4):
        later = t1[t].astype(F32) + t2[t].astype(F32) * after[0] + t3[t].astype(F32) * (after[0] * after[1])
        out[t] = (first[mod4(meta[1] - t)].astype(F32) + gate * later).astype(BF)


def column(row):
    return jnp.transpose(jnp.broadcast_to(row * (1.0 / FEATS), (TILE, TILE)))


def term_kernel(meta, a0, a1, a2, normed, inv, mod, term, sent, moments):
    group = meta[3] * 2 + meta[4]
    grad = a0[0:TILE, :].astype(F32)
    stats = stats_of(a0, TILE)
    for a in (a1, a2):
        grad = grad + a[0:TILE, :].astype(F32)
        stats = stats + stats_of(a, TILE)
    first = stats[0:1, 0:TILE]
    second = stats[0:1, TILE : 2 * TILE]
    moments[...] = jnp.concatenate([first, second], axis=0) * (FEATS**-0.5)

    def wide(value):
        return jnp.concatenate([value] * 3, axis=1)

    du = grad * (1.0 + mod[1, group])
    value = wide(inv[...]) * (du - wide(column(first)) - normed[...] * wide(column(second)))
    term[...] = value
    sent[...] = value.astype(BF)


def decays(meta, ids, coeffs):
    step = meta[0]
    after = []
    for ahead in (1, 2, 3):
        at = jnp.minimum(step + ahead, 3)
        after.append(jnp.where(step + ahead <= 3, coeffs[0, ids[at]], 1.0))
    return after, coeffs[0, ids[step]], coeffs[1, ids[step]]


def lam_of(meta, ids, coeffs, cot, terms):
    after, decay, weight = decays(meta, ids, coeffs)
    lam = cot[...] * (after[0] * after[1] * after[2])
    for ref, factor in zip(terms, (1.0, after[0], after[0] * after[1])):
        lam = lam + ref[...].astype(F32) * factor
    return lam, decay, weight


def cut_kernel(meta, ids, coeffs, cot_far, mod_far, w_far, o0, o1, o2, o3, cot, mod, w, sems):
    copies = [
        pltpu.make_async_copy(src, dst, sems.at[i])
        for i, (src, dst) in enumerate(((cot_far, cot), (mod_far, mod), (w_far, w)))
    ]
    for copy in copies:
        copy.start()
    for copy in copies:
        copy.wait()
    zhi = meta[1]
    group = meta[3] * 2 + meta[4]
    lam, decay, weight = lam_of(meta, ids, coeffs, cot, ())
    up = mod[2, group] * weight * lam
    for d, o in enumerate((o0, o1, o2, o3)):
        at = mod4(zhi + d)
        for part in range(3):
            o[part * 48 : (part + 1) * 48, :] = lane_piece(w[part].astype(F32), at).astype(BF)
        o[144:272, :] = lane_piece(up, at).astype(BF)


def adjoint_kernel(meta, ids, coeffs, cot, term, t1, t2, t3, out):
    lam, decay, weight = lam_of(meta, ids, coeffs, cot, (t1, t2, t3))
    out[...] = decay * lam + term[...]


def turn(value, axis, offset):
    return lax.ppermute(value, axis, [(i, (i + offset) % 4) for i in range(4)])


def ring4(value, axis):
    return [value] + [turn(value, axis, -offset) for offset in PLACES[1:]]


def hand_on(before, after, axis):
    pairs = []
    for i in range(4):
        pairs.append((2 * i, 2 * ((i - 1) % 4)))
        pairs.append((2 * i + 1, 2 * ((i + 1) % 4) + 1))
    return lax.ppermute(jnp.where(lax.axis_index("core") == 0, after, before), (axis, "core"), pairs)


def relayed(value, axis):
    before, after = turn(value, axis, 1), turn(value, axis, -1)
    return [value, before, after, hand_on(before, after, axis)]


def to_heads(pieces):
    got = [pieces[0]]
    for d in (1, 2, 3):
        pairs = [(i, (i + d) % 4) for i in range(4) if (i + d) % 4 != 3]
        got.append(lax.ppermute(pieces[d], "zhi", pairs))
    return got


def to_earlier(value):
    return [lax.ppermute(value, "step", [(j, j - d) for j in range(d, 4)]) for d in (1, 2, 3)]


def swing(value, axes, count, forward):
    pairs = []
    for i in range(count):
        pairs.append((2 * i, 2 * ((i + forward) % count)))
        pairs.append((2 * i + 1, 2 * ((i - forward) % count) + 1))
    return lax.ppermute(value, (*axes, "core"), pairs)


def reduced(far, plain, waiting, axes, count):
    half_way = swing(far, axes, count, 1)
    got = swing(plain, axes, count, -1)
    (waiting,) = call(add_kernel, [sds(waiting.shape, BF)], (waiting, half_way), 0)
    return got, swing(waiting, axes, count, 1)


def along_z(value, offset):
    return lax.ppermute(value, ("zhi", "zlo"), [(i, (i + offset) % 16) for i in range(16)])


def far_z(value):
    pairs = []
    for i in range(16):
        pairs.append((2 * i, 2 * ((i + 2) % 16)))
        pairs.append((2 * i + 1, 2 * ((i - 2) % 16) + 1))
    return lax.ppermute(value, ("zhi", "zlo", "core"), pairs)


def other_core(value):
    return lax.ppermute(value, "core", [(0, 1), (1, 0)])


def shards(states, modulation, cotangent, w_qkv, q_gain, k_gain, step_ids, coeffs, neighbours):
    zhi = lax.axis_index("zhi")
    meta = jnp.stack([lax.axis_index(a) for a in ("step", "zhi", "y", "zlo", "core")]).astype(jnp.int32)
    coeffs, neighbours = coeffs.T, neighbours.T
    mod = modulation.reshape(3, 8, 1, WIDTH)
    gq = (q_gain / jnp.sqrt(jnp.float32(HD))).reshape(1, HD)
    gk = k_gain.reshape(1, HD)

    pieces = call(
        cut_kernel,
        [sds((272, HD), BF)] * 4,
        (meta, step_ids, coeffs, cotangent, mod, jnp.transpose(w_qkv, (1, 0, 2))),
        3,
        [
            pltpu.VMEM((TILE, WIDTH), F32),
            pltpu.VMEM((3, 8, 1, WIDTH), F32),
            pltpu.VMEM((3, 48, WIDTH), BF),
            pltpu.SemaphoreType.DMA((3,)),
        ],
        grant=12,
        far=3,
    )
    pieces = to_heads(pieces)
    own_rows = jnp.stack([p[0:144] for p in pieces])
    pieces[1], x = lax.optimization_barrier((pieces[1], states[0]))
    own_up = jnp.stack([p[144:272] for p in pieces])

    before, after = turn(x, "zhi", 1), turn(x, "zhi", -1)
    own_rows, before, after = lax.optimization_barrier((own_rows, before, after))
    far = hand_on(before, after, "zhi")
    y_rows = lax.all_gather(own_rows, "y")
    y_rows, far, own_up = lax.optimization_barrier((y_rows, far, own_up))
    wg = lax.all_gather(y_rows, "step").reshape(16, 4, 144, HD)
    x_tiles = jnp.stack([x, before, far, after])
    xa = [x_tiles, along_z(x_tiles, 1), along_z(x_tiles, -1), far_z(x_tiles)]
    up_before, up_after = turn(own_up, "y", 1), turn(own_up, "y", -1)
    up_before, up_after, xa[3] = lax.optimization_barrier((up_before, up_after, xa[3]))
    first_ups = [own_up, up_before, up_after, hand_on(up_before, up_after, "y")]
    xb = [other_core(a) for a in xa]

    tokens = 4 * TILE
    scaled, normed, inv, normed_piece, inv_all = call(
        norm_kernel,
        [
            sds((8, 4, TILE, WIDTH), BF),
            sds((TILE, WIDTH), F32),
            sds((TILE, HD), F32),
            sds((4, TILE, HD), F32),
            sds((4, TILE, HD), F32),
        ],
        (meta, *xa, *xb, mod),
        1,
        [
            pltpu.VMEM((TILE, WIDTH), F32),
            pltpu.VMEM((TILE, HD), F32),
            pltpu.VMEM((4, TILE, HD), F32),
            pltpu.VMEM((4, TILE, HD), F32),
            pltpu.SemaphoreType.DMA((4,)),
        ],
        0,
        16,
        far_outs=4,
    )
    scaled, wg, *first_ups = lax.optimization_barrier((scaled, wg, *first_ups))
    qkv, proj, wk, ws, vec = call(
        proj_kernel,
        [
            sds((4, TILE, WIDTH), BF),
            sds((tokens, WIDTH), F32),
            sds((4, 8, 48, WIDTH), BF),
            sds((4, 8, 48, WIDTH), BF),
            sds((16, WIDTH), F32),
        ],
        (meta, wg, scaled, mod, gq, gk),
        1,
        [
            pltpu.VMEM((8, 8, 48, WIDTH), BF),
            pltpu.VMEM((16, 4, 144, HD), BF),
            pltpu.SemaphoreType.DMA((16,)),
        ],
        2 * tokens * FEATS * WIDTH,
        24,
        far=1,
    )
    all_qkv = relayed(qkv, "y")
    all_qkv[3], ws = lax.optimization_barrier((all_qkv[3], ws))
    wr = other_core(ws)

    again = first_ups
    for sweep in range(SWEEPS):
        outs = [sds((tokens + 16, WIDTH), BF), sds((4, 3, WIDTH, TILE), F32)]
        dproj, *kept = call(
            sweep_kernel,
            outs[: 2 - sweep],
            (meta, neighbours, *all_qkv, proj, vec, gq, gk, *again),
            2,
            [pltpu.VMEM((16, TILE, WIDTH), BF), pltpu.VMEM((16, TILE, HD), BF)],
            400 * 1000 * 1000,
            16,
        )
        pair = (meta, dproj, other_core(dproj), wk, wr)
        (far,) = features(True, pair)
        here, plain, waiting = features(False, pair)
        near = (here, *reduced(far, plain, waiting, ("zhi", "zlo"), 16))
        if sweep + 1 < SWEEPS:
            own, *others = call(window_piece_kernel, [sds((tokens + 16, HD), BF)] * 4, (meta, *near), 1)
            (sent,) = call(
                term_piece_kernel,
                [sds((4, TILE, HD), BF)],
                (meta, own, *reduced(*others, ("zhi",), 4), normed_piece, inv_all, mod),
                1,
            )
            (up,) = call(
                upstream_piece_kernel,
                [sds((4, TILE, HD), BF)],
                (meta, step_ids, coeffs, first_ups[0], mod, *to_earlier(sent)),
                3,
            )
            again = (lax.all_gather(up, "y"), *kept)
    own, *others = call(window_kernel, [sds((TILE + 16, WIDTH), BF)] * 4, (meta, *near), 1)
    term, sent, moments = call(
        term_kernel,
        [sds((TILE, WIDTH), F32), sds((TILE, WIDTH), BF), sds((2, TILE), F32)],
        (meta, own, *reduced(*others, ("zhi",), 4), normed, inv, mod),
        1,
    )
    (adjoint,) = call(
        adjoint_kernel,
        [sds((TILE, WIDTH), F32)],
        (meta, step_ids, coeffs, cotangent, term, *to_earlier(sent)),
        3,
    )
    return adjoint[None], moments[None]


def solution(mesh):
    fine = Mesh(mesh.devices.reshape(4, 4, 4, 4, 2), ("step", "zhi", "y", "zlo", "core"))
    blk, head = ("zhi", "y"), ("zlo", "core")
    in_specs = (
        P("step", blk, head),
        P("step", None, None),
        P(blk, head),
        P(("step",) + blk, None, head),
        P(),
        P(),
        P(),
        P(),
        P(),
    )
    out_specs = (P("step", blk, head), P("step", None, blk))
    return jax.shard_map(shards, mesh=fine, in_specs=in_specs, out_specs=out_specs, check_vma=False)
```

```python
import functools

import jax
import jax.numpy as jnp
from jax import lax
from jax.experimental import pallas as pl
from jax.experimental.pallas import tpu as pltpu
from jax.sharding import Mesh
from jax.sharding import PartitionSpec as P

HD = 128
TILE = 128
WIDTH = 384
FEATS = 3072
SWEEPS = 2
EPS = 1e-06
BF = jnp.bfloat16
F32 = jnp.float32
MIB = 1024 * 1024
PLACES = (0, -1, 1, 2)

VM = pl.BlockSpec(memory_space=pltpu.VMEM)
SM = pl.BlockSpec(memory_space=pltpu.SMEM)
HBM = pl.BlockSpec(memory_space=pltpu.HBM)


def call(body, outs, args, smem, scratch=(), flops=0, grant=8, far=0, far_outs=0):
    specs = [SM if i < smem else VM for i in range(len(args))]
    specs[smem : smem + far] = [HBM] * far
    moved = sum(a.size * a.dtype.itemsize for a in args) + sum(
        o.size * o.dtype.itemsize for o in outs
    )
    return pl.pallas_call(
        body,
        out_shape=tuple(outs),
        in_specs=specs,
        out_specs=tuple([VM] * (len(outs) - far_outs) + [HBM] * far_outs),
        scratch_shapes=list(scratch),
        compiler_params=pltpu.CompilerParams(vmem_limit_bytes=grant * MIB),
        cost_estimate=pl.CostEstimate(flops=flops, bytes_accessed=moved, transcendentals=0),
    )(*args)


def sds(shape, dtype):
    return jax.ShapeDtypeStruct(shape, dtype)


def nt(a, b):
    return lax.dot_general(a, b, (((1,), (1,)), ((), ())), preferred_element_type=F32)


def tn(a, b):
    return lax.dot_general(a, b, (((0,), (0,)), ((), ())), preferred_element_type=F32)


def nn(a, b):
    return jnp.dot(a, b, preferred_element_type=F32)


def hi_lo(value):
    hi = value.astype(BF)
    return hi, (value - hi.astype(F32)).astype(BF)


def mod4(value):
    return lax.rem(value + 8, 4)


def lane_piece(value, at):
    out = jnp.zeros(value.shape[:-1] + (HD,), value.dtype)
    for i in range(3):
        out = jnp.where(at == i, value[..., i * HD : (i + 1) * HD], out)
    return out


def norm_kernel(
    meta, xa0, xa1, xa2, xa3, xb0, xb1, xb2, xb3, mod,
    scaled, packed,
):
    zhi, zlo, core = meta[1], meta[3], meta[4]
    place = zhi * 4 + zlo
    own_far = jnp.where(core == 0, -2, 2)
    sources = []
    for refs, side, far in (
        ((xa0, xa1, xa2, xa3), core, own_far),
        ((xb0, xb1, xb2, xb3), 1 - core, -own_far),
    ):
        for ref, offset in zip(refs, (0, -1, 1, far)):
            at = lax.rem(place + offset + 16, 16)
            sources.append((ref, at // 4, lax.rem(at, 4) * 2 + side))

    rows = 32

    def chunk(turn, carry):
        t = turn // (TILE // rows)
        start = lax.rem(turn, TILE // rows) * rows
        span = pl.ds(pl.multiple_of(start, rows), rows)

        def load(source):
            ref, z, g = source
            d = mod4(z - t)
            return ref[d, span, :].astype(F32)

        total = jnp.zeros((rows, WIDTH), F32)
        for source in sources:
            total = total + load(source)
        mean = jnp.sum(total, axis=1, keepdims=True) * (1.0 / FEATS)
        square = jnp.zeros((rows, WIDTH), F32)
        for source in sources:
            centred = load(source) - mean
            square = square + centred * centred
        inv = lax.rsqrt(jnp.sum(square, axis=1, keepdims=True) * (1.0 / FEATS) + EPS)
        for source in sources:
            normed = (load(source) - mean) * inv
            scaled[source[2], t, span, :] = (normed * (1.0 + mod[1, source[2]])).astype(BF)
        normed = (load(sources[0]) - mean) * inv
        inv_wide = jnp.broadcast_to(inv, (rows, HD))
        packed[t, span, :] = lane_piece(normed, zhi)
        packed[4 + t, span, :] = inv_wide

        @pl.when(t == zhi)
        def _():
            packed[8, span, :] = inv_wide
            for i in range(3):
                packed[9 + i, span, :] = normed[:, i * HD : (i + 1) * HD]

        return carry

    lax.fori_loop(0, 4 * (TILE // rows), chunk, 0)


def proj_kernel(
    meta, nscr, wg, mod, q_gain, k_gain,
    qkv, proj, wk, ws, vec, wc,
):
    zhi, core = meta[1], meta[4]
    for sy in range(16):
        for d in range(4):
            zh = mod4(zhi - d)
            for part in range(3):
                wc[(sy // 4) * 2 + zh // 2, lax.rem(zh, 2) * 4 + sy % 4, :, part * HD : (part + 1) * HD] = (
                    wg[sy, d, part * 48 : (part + 1) * 48, :]
                )
    for r in range(4):
        wk[r] = wc[2 * r + core]
        ws[r] = wc[2 * r + 1 - core]

    acc = jnp.zeros((4 * TILE, WIDTH), F32)
    flat = jnp.zeros((16, WIDTH), F32)
    for g in range(8):
        w_g = wc[g].reshape(WIDTH, WIDTH)
        acc = acc + nn(nscr[g].reshape(4 * TILE, WIDTH), w_g)
        scale_hi, scale_lo = hi_lo(1.0 + mod[1, g])
        shift_hi, shift_lo = hi_lo(mod[0, g])
        four = jnp.concatenate([scale_hi, scale_lo, shift_hi, shift_lo], axis=0)
        lhs = jnp.concatenate([four, jnp.zeros((12, WIDTH), BF)], axis=0)
        flat = flat + nn(lhs, w_g)
    vec[...] = flat
    proj[...] = acc + (flat[2:3] + flat[3:4])
    for t in range(4):
        span = slice(t * TILE, (t + 1) * TILE)
        q = proj[span, 0:HD]
        k = proj[span, HD : 2 * HD]
        q_inv = lax.rsqrt(jnp.mean(q * q, axis=1, keepdims=True) + EPS)
        k_inv = lax.rsqrt(jnp.mean(k * k, axis=1, keepdims=True) + EPS)
        qkv[t, :, 0:HD] = (q * q_inv * q_gain[...]).astype(BF)
        qkv[t, :, HD : 2 * HD] = (k * k_inv * k_gain[...]).astype(BF)
        qkv[t, :, 2 * HD : 3 * HD] = proj[span, 2 * HD : 3 * HD].astype(BF)


def norm_back(raw, gain, grad):
    inv = lax.rsqrt(jnp.mean(raw * raw, axis=1, keepdims=True) + EPS)
    scaled = grad * gain
    dot = jnp.mean(scaled * raw, axis=1, keepdims=True)
    return inv * (scaled - raw * (inv * inv * dot))


def sweep_kernel(
    meta, nb, k0, k1, k2, k3, proj, vec, q_gain, k_gain, *rest
):
    tiles, ups = rest[-2:]
    first_sweep = len(rest) == 8
    probs, out = (rest[5], rest[4]) if first_sweep else (rest[1], rest[2])
    zhi, y = meta[1], meta[2]
    for ref, offset in zip((k0, k1, k2, k3), PLACES):
        yy = mod4(y + offset)
        for z in range(4):
            tiles[z * 4 + yy] = ref[z]
    for i, offset in enumerate(PLACES):
        for z in range(4):
            if first_sweep:
                ups[mod4(zhi - z) * 4 + mod4(y + offset)] = rest[i][z]
            else:
                ups[z * 4 + i] = rest[0][i, z]

    m1_hi, m1_lo = hi_lo(vec[0:1] + vec[1:2])
    m1 = jnp.concatenate([m1_hi, m1_lo, jnp.zeros((14, WIDTH), BF)], axis=0)
    ones = jnp.ones((16, WIDTH), BF)
    s0 = vec[2:3] + vec[3:4]

    def k_of(t):
        return tiles[t, :, HD : 2 * HD]

    def v_of(t):
        return tiles[t, :, 2 * HD : 3 * HD]

    def own(jz, carry):
        j = jz * 4 + y
        near = (nb[1, j], nb[2, j])
        d_k = jnp.zeros((TILE, HD), F32)
        d_v = jnp.zeros((TILE, HD), F32)
        d_q = None
        for slot in range(3):
            if slot == 0:
                i = j
                keys = (j, near[0], near[1])
            else:
                i = near[slot - 1]
                keys = (j, i, nb[1, i] + nb[2, i] - j)
            q = tiles[i, :, 0:HD]
            up = ups[i]
            k_all = jnp.concatenate([k_of(t) for t in keys], axis=0)
            v_all = jnp.concatenate([v_of(t) for t in keys], axis=0)
            if first_sweep:
                expo = jnp.exp(nt(k_all, q))
                prob = expo * (1.0 / jnp.sum(expo, axis=0, keepdims=True))
                probs[jz, slot] = prob
            else:
                prob = probs[jz, slot]
            prob_b = prob.astype(BF)
            dprob = nt(v_all, up)
            delta = jnp.sum(prob_b.astype(F32) * dprob, axis=0, keepdims=True)
            if slot == 0:
                dscore = (prob * (dprob - delta)).astype(BF)
                d_q = tn(dscore, k_all)
                dscore = dscore[0:TILE]
            else:
                dscore = (prob[0:TILE] * (dprob[0:TILE] - delta)).astype(BF)
            d_k = d_k + nn(dscore, q)
            d_v = d_v + nn(prob_b[0:TILE], up)
        start = pl.multiple_of(jz * TILE, TILE)
        raw = proj[pl.ds(start, TILE), :]
        d_q = norm_back(raw[:, 0:HD], q_gain[...], d_q)
        d_k = norm_back(raw[:, HD : 2 * HD], k_gain[...], d_k)
        d_all = jnp.concatenate([d_q, d_k, d_v], axis=1).astype(BF)
        out[pl.ds(start, TILE), :] = d_all
        first = nt(m1, d_all)
        prod_hi, prod_lo = hi_lo(d_all.astype(F32) * (raw - s0))
        second = nt(ones, prod_hi) + nt(ones, prod_lo)
        row = jnp.concatenate(
            [first[0:1] + first[1:2], second[0:1], jnp.zeros((1, TILE), F32)], axis=1
        )
        at = lax.broadcasted_iota(jnp.int32, (8, WIDTH), 0)
        return carry + jnp.where(at == jz, row, 0.0)

    stats = lax.fori_loop(0, 4, own, jnp.zeros((8, WIDTH), F32))
    out[4 * TILE : 4 * TILE + 16, :] = jnp.concatenate(hi_lo(stats), axis=0)


def stats_of(ref, start):
    both = ref[start : start + 16, :].astype(F32)
    return both[0:8] + both[8:16]


def route(meta):
    forward = meta[4] == 0
    return jnp.where(forward, 3, 1), jnp.where(forward, 1, 3)


def feature_kernel(far_only, meta, own, other, wk, wr, *outs):
    zlo = meta[3]
    stats = jnp.concatenate(hi_lo(stats_of(own, 4 * TILE) + stats_of(other, 4 * TILE)), axis=0)
    for offset, o in zip((2,) if far_only else (0, *route(meta)), outs):
        r = mod4(zlo + offset)
        value = nt(own[0 : 4 * TILE, :], wk[r].reshape(WIDTH, WIDTH))
        value = value + nt(other[0 : 4 * TILE, :], wr[r].reshape(WIDTH, WIDTH))
        o[0 : 4 * TILE, :] = value.astype(BF)
        o[4 * TILE : 4 * TILE + 16, :] = stats


def features(far_only, args):
    count = 1 if far_only else 3
    return call(
        functools.partial(feature_kernel, far_only),
        [sds((4 * TILE + 16, WIDTH), BF)] * count,
        args,
        1,
        (),
        2 * 4 * TILE * FEATS * WIDTH * count // 4,
        12,
    )


def add_kernel(a, b, out):
    rows = out.shape[0] - 16
    out[0:rows, :] = (a[0:rows, :].astype(F32) + b[0:rows, :].astype(F32)).astype(BF)
    out[rows : rows + 16, :] = jnp.concatenate(hi_lo(stats_of(a, rows) + stats_of(b, rows)), axis=0)


def window_kernel(meta, a0, a1, a2, *outs):
    zhi = meta[1]
    stats = stats_of(a0, 4 * TILE) + stats_of(a1, 4 * TILE) + stats_of(a2, 4 * TILE)
    at = lax.broadcasted_iota(jnp.int32, (8, WIDTH), 0)
    for d, o in zip((0, 2, *route(meta)), outs):
        t = mod4(zhi + d)
        span = pl.ds(pl.multiple_of(t * TILE, TILE), TILE)
        o[0:TILE, :] = (a0[span, :].astype(F32) + a1[span, :].astype(F32) + a2[span, :].astype(F32)).astype(BF)
        row = jnp.sum(jnp.where(at == t, stats, 0.0), axis=0, keepdims=True)
        o[TILE : TILE + 16, :] = jnp.concatenate(hi_lo(jnp.broadcast_to(row, (8, WIDTH))), axis=0)


def window_piece_kernel(meta, a0, a1, a2, *outs):
    zhi = meta[1]
    places = [mod4(zhi + d) for d in (0, 2, *route(meta))]
    stats = stats_of(a0, 4 * TILE) + stats_of(a1, 4 * TILE) + stats_of(a2, 4 * TILE)
    stats = jnp.concatenate([stats[0:4, 0:TILE], stats[0:4, TILE : 2 * TILE]], axis=0)
    for t in range(4):
        span = slice(t * TILE, (t + 1) * TILE)
        value = a0[span, :].astype(F32) + a1[span, :].astype(F32) + a2[span, :].astype(F32)
        for at, o in zip(places, outs):
            o[span, :] = lane_piece(value, at).astype(BF)
    for at, o in zip(places, outs):
        o[4 * TILE : 4 * TILE + 16, :] = jnp.concatenate(hi_lo(stats * jnp.where(at == 3, 0.0, 1.0)), axis=0)


def term_piece_kernel(meta, a0, a1, a2, packed, mod, sent):
    group = meta[3] * 2 + meta[4]
    stats = stats_of(a0, 4 * TILE)
    for a in (a1, a2):
        stats = stats + stats_of(a, 4 * TILE)
    scale = 1.0 + lane_piece(mod[1, group], meta[1])
    for t in range(4):
        span = slice(t * TILE, (t + 1) * TILE)
        grad = a0[span, :].astype(F32)
        for a in (a1, a2):
            grad = grad + a[span, :].astype(F32)
        value = packed[4 + t] * (grad * scale - column(stats[t : t + 1]) - packed[t] * column(stats[4 + t : 5 + t]))
        sent[t] = value.astype(BF)


def upstream_piece_kernel(meta, ids, coeffs, first, mod, t1, t2, t3, out):
    group = meta[3] * 2 + meta[4]
    after, decay, weight = decays(meta, ids, coeffs)
    gate = lane_piece(mod[2, group], meta[1]) * weight
    for t in range(4):
        later = t1[t].astype(F32) + t2[t].astype(F32) * after[0] + t3[t].astype(F32) * (after[0] * after[1])
        out[t] = (first[mod4(meta[1] - t)].astype(F32) + gate * later).astype(BF)


def column(row):
    return jnp.transpose(jnp.broadcast_to(row * (1.0 / FEATS), (TILE, TILE)))


def term_kernel(meta, a0, a1, a2, packed, mod, term, sent, moments):
    group = meta[3] * 2 + meta[4]
    grad = a0[0:TILE, :].astype(F32)
    stats = stats_of(a0, TILE)
    for a in (a1, a2):
        grad = grad + a[0:TILE, :].astype(F32)
        stats = stats + stats_of(a, TILE)
    first = stats[0:1, 0:TILE]
    second = stats[0:1, TILE : 2 * TILE]
    moments[...] = jnp.concatenate([first, second], axis=0) * (FEATS**-0.5)

    def wide(value):
        return jnp.concatenate([value] * 3, axis=1)

    du = grad * (1.0 + mod[1, group])
    normed = jnp.concatenate([packed[9 + i] for i in range(3)], axis=1)
    value = wide(packed[8]) * (du - wide(column(first)) - normed * wide(column(second)))
    term[...] = value
    sent[...] = value.astype(BF)


def decays(meta, ids, coeffs):
    step = meta[0]
    after = []
    for ahead in (1, 2, 3):
        at = jnp.minimum(step + ahead, 3)
        after.append(jnp.where(step + ahead <= 3, coeffs[0, ids[at]], 1.0))
    return after, coeffs[0, ids[step]], coeffs[1, ids[step]]


def lam_of(meta, ids, coeffs, cot, terms):
    after, decay, weight = decays(meta, ids, coeffs)
    lam = cot[...] * (after[0] * after[1] * after[2])
    for ref, factor in zip(terms, (1.0, after[0], after[0] * after[1])):
        lam = lam + ref[...].astype(F32) * factor
    return lam, decay, weight


def cut_kernel(meta, ids, coeffs, cot_far, mod_far, w_far, o0, o1, o2, o3, cot, mod, w, sems):
    copies = [
        pltpu.make_async_copy(src, dst, sems.at[i])
        for i, (src, dst) in enumerate(((cot_far, cot), (mod_far, mod), (w_far, w)))
    ]
    for copy in copies:
        copy.start()
    for copy in copies:
        copy.wait()
    zhi = meta[1]
    group = meta[3] * 2 + meta[4]
    lam, decay, weight = lam_of(meta, ids, coeffs, cot, ())
    up = mod[2, group] * weight * lam
    for d, o in enumerate((o0, o1, o2, o3)):
        at = mod4(zhi + d)
        for part in range(3):
            o[part * 48 : (part + 1) * 48, :] = lane_piece(w[part].astype(F32), at).astype(BF)
        o[144:272, :] = lane_piece(up, at).astype(BF)


def adjoint_kernel(meta, ids, coeffs, cot, term, t1, t2, t3, out):
    lam, decay, weight = lam_of(meta, ids, coeffs, cot, (t1, t2, t3))
    out[...] = decay * lam + term[...]


def turn(value, axis, offset):
    return lax.ppermute(value, axis, [(i, (i + offset) % 4) for i in range(4)])


def ring4(value, axis):
    return [value] + [turn(value, axis, -offset) for offset in PLACES[1:]]


def hand_on(before, after, axis):
    pairs = []
    for i in range(4):
        pairs.append((2 * i, 2 * ((i - 1) % 4)))
        pairs.append((2 * i + 1, 2 * ((i + 1) % 4) + 1))
    return lax.ppermute(jnp.where(lax.axis_index("core") == 0, after, before), (axis, "core"), pairs)


def relayed(value, axis):
    before, after = turn(value, axis, 1), turn(value, axis, -1)
    return [value, before, after, hand_on(before, after, axis)]


def to_heads(pieces):
    got = [pieces[0]]
    for d in (1, 2, 3):
        pairs = [(i, (i + d) % 4) for i in range(4) if (i + d) % 4 != 3]
        got.append(lax.ppermute(pieces[d], "zhi", pairs))
    return got


def to_earlier(value):
    return [lax.ppermute(value, "step", [(j, j - d) for j in range(d, 4)]) for d in (1, 2, 3)]


def swing(value, axes, count, forward, hops=1, headless=False):
    pairs = []
    for i in range(count):
        for core, step in ((0, forward), (1, -forward)):
            if not headless or (i + hops * step) % count != 3:
                pairs.append((2 * i + core, 2 * ((i + step) % count) + core))
    return lax.ppermute(value, (*axes, "core"), pairs)


def reduced(far, plain, waiting, axes, count, headless=False):
    half_way = swing(far, axes, count, 1, 2, headless)
    got = swing(plain, axes, count, -1, 1, headless)
    (waiting,) = call(add_kernel, [sds(waiting.shape, BF)], (waiting, half_way), 0)
    return got, swing(waiting, axes, count, 1, 1, headless)


def along_z(value, offset):
    return lax.ppermute(value, ("zhi", "zlo"), [(i, (i + offset) % 16) for i in range(16)])


def far_z(value):
    pairs = []
    for i in range(16):
        pairs.append((2 * i, 2 * ((i + 2) % 16)))
        pairs.append((2 * i + 1, 2 * ((i - 2) % 16) + 1))
    return lax.ppermute(value, ("zhi", "zlo", "core"), pairs)


def other_core(value):
    return lax.ppermute(value, "core", [(0, 1), (1, 0)])


def shards(states, modulation, cotangent, w_qkv, q_gain, k_gain, step_ids, coeffs, neighbours):
    zhi = lax.axis_index("zhi")
    meta = jnp.stack([lax.axis_index(a) for a in ("step", "zhi", "y", "zlo", "core")]).astype(jnp.int32)
    coeffs, neighbours = coeffs.T, neighbours.T
    mod = modulation.reshape(3, 8, 1, WIDTH)
    gq = (q_gain / jnp.sqrt(jnp.float32(HD))).reshape(1, HD)
    gk = k_gain.reshape(1, HD)

    pieces = call(
        cut_kernel,
        [sds((272, HD), BF)] * 4,
        (meta, step_ids, coeffs, cotangent, mod, jnp.transpose(w_qkv, (1, 0, 2))),
        3,
        [
            pltpu.VMEM((TILE, WIDTH), F32),
            pltpu.VMEM((3, 8, 1, WIDTH), F32),
            pltpu.VMEM((3, 48, WIDTH), BF),
            pltpu.SemaphoreType.DMA((3,)),
        ],
        grant=12,
        far=3,
    )
    pieces = to_heads(pieces)
    own_rows = jnp.stack([p[0:144] for p in pieces])
    pieces[1], x = lax.optimization_barrier((pieces[1], states[0]))
    own_up = jnp.stack([p[144:272] for p in pieces])

    before, after = turn(x, "zhi", 1), turn(x, "zhi", -1)
    own_rows, before, after = lax.optimization_barrier((own_rows, before, after))
    far = hand_on(before, after, "zhi")
    y_rows = lax.all_gather(own_rows, "y")
    y_rows, far, own_up = lax.optimization_barrier((y_rows, far, own_up))
    wg = lax.all_gather(y_rows, "step").reshape(16, 4, 144, HD)
    x_tiles = jnp.stack([x, before, far, after])
    xa = [x_tiles, along_z(x_tiles, 1), along_z(x_tiles, -1), far_z(x_tiles)]
    up_before, up_after = turn(own_up, "y", 1), turn(own_up, "y", -1)
    up_before, up_after, xa[3] = lax.optimization_barrier((up_before, up_after, xa[3]))
    first_ups = [own_up, up_before, up_after, hand_on(up_before, up_after, "y")]
    xb = [other_core(a) for a in xa]

    tokens = 4 * TILE
    scaled, packed = call(
        norm_kernel,
        [sds((8, 4, TILE, WIDTH), BF), sds((12, TILE, HD), F32)],
        (meta, *xa, *xb, mod),
        1,
        (),
        0,
        12,
    )
    scaled, wg, *first_ups = lax.optimization_barrier((scaled, wg, *first_ups))
    qkv, proj, wk, ws, vec = call(
        proj_kernel,
        [
            sds((4, TILE, WIDTH), BF),
            sds((tokens, WIDTH), F32),
            sds((4, 8, 48, WIDTH), BF),
            sds((4, 8, 48, WIDTH), BF),
            sds((16, WIDTH), F32),
        ],
        (meta, scaled, wg, mod, gq, gk),
        1,
        [pltpu.VMEM((8, 8, 48, WIDTH), BF)],
        2 * tokens * FEATS * WIDTH,
        20,
    )
    all_qkv = relayed(qkv, "y")
    wr = other_core(ws)

    again = first_ups
    for sweep in range(SWEEPS):
        outs = [sds((tokens + 16, WIDTH), BF), sds((4, 3, WIDTH, TILE), F32)]
        dproj, *kept = call(
            sweep_kernel,
            outs[: 2 - sweep],
            (meta, neighbours, *all_qkv, proj, vec, gq, gk, *again),
            2,
            [pltpu.VMEM((16, TILE, WIDTH), BF), pltpu.VMEM((16, TILE, HD), BF)],
            400 * 1000 * 1000,
            12,
        )
        pair = (meta, dproj, other_core(dproj), wk, wr)
        (far,) = features(True, pair)
        here, plain, waiting = features(False, pair)
        near = (here, *reduced(far, plain, waiting, ("zhi", "zlo"), 16))
        if sweep + 1 < SWEEPS:
            own, *others = call(window_piece_kernel, [sds((tokens + 16, HD), BF)] * 4, (meta, *near), 1)
            (sent,) = call(
                term_piece_kernel,
                [sds((4, TILE, HD), BF)],
                (meta, own, *reduced(*others, ("zhi",), 4, True), packed, mod),
                1,
            )
            (up,) = call(
                upstream_piece_kernel,
                [sds((4, TILE, HD), BF)],
                (meta, step_ids, coeffs, first_ups[0], mod, *to_earlier(sent)),
                3,
            )
            again = (lax.all_gather(up, "y"), *kept)
    own, *others = call(window_kernel, [sds((TILE + 16, WIDTH), BF)] * 4, (meta, *near), 1)
    term, sent, moments = call(
        term_kernel,
        [sds((TILE, WIDTH), F32), sds((TILE, WIDTH), BF), sds((2, TILE), F32)],
        (meta, own, *reduced(*others, ("zhi",), 4), packed, mod),
        1,
    )
    (adjoint,) = call(
        adjoint_kernel,
        [sds((TILE, WIDTH), F32)],
        (meta, step_ids, coeffs, cotangent, term, *to_earlier(sent)),
        3,
    )
    return adjoint[None], moments[None]


def solution(mesh):
    fine = Mesh(mesh.devices.reshape(4, 4, 4, 4, 2), ("step", "zhi", "y", "zlo", "core"))
    blk, head = ("zhi", "y"), ("zlo", "core")
    in_specs = (
        P("step", blk, head),
        P("step", None, None),
        P(blk, head),
        P(("step",) + blk, None, head),
        P(),
        P(),
        P(),
        P(),
        P(),
    )
    out_specs = (P("step", blk, head), P("step", None, blk))
    return jax.shard_map(shards, mesh=fine, in_specs=in_specs, out_specs=out_specs, check_vma=False)
```

```python
import functools

import jax
import jax.numpy as jnp
from jax import lax
from jax.experimental import pallas as pl
from jax.experimental.pallas import tpu as pltpu
from jax.sharding import Mesh
from jax.sharding import PartitionSpec as P

HD = 128
TILE = 128
WIDTH = 384
FEATS = 3072
SWEEPS = 2
EPS = 1e-06
BF = jnp.bfloat16
F32 = jnp.float32
MIB = 1024 * 1024
PLACES = (0, -1, 1, 2)

VM = pl.BlockSpec(memory_space=pltpu.VMEM)
SM = pl.BlockSpec(memory_space=pltpu.SMEM)
HBM = pl.BlockSpec(memory_space=pltpu.HBM)


def call(body, outs, args, smem, scratch=(), flops=0, grant=8, far=0, far_outs=0):
    specs = [SM if i < smem else VM for i in range(len(args))]
    specs[smem : smem + far] = [HBM] * far
    moved = sum(a.size * a.dtype.itemsize for a in args) + sum(
        o.size * o.dtype.itemsize for o in outs
    )
    return pl.pallas_call(
        body,
        out_shape=tuple(outs),
        in_specs=specs,
        out_specs=tuple([VM] * (len(outs) - far_outs) + [HBM] * far_outs),
        scratch_shapes=list(scratch),
        compiler_params=pltpu.CompilerParams(vmem_limit_bytes=grant * MIB),
        cost_estimate=pl.CostEstimate(flops=flops, bytes_accessed=moved, transcendentals=0),
    )(*args)


def sds(shape, dtype):
    return jax.ShapeDtypeStruct(shape, dtype)


def nt(a, b):
    return lax.dot_general(a, b, (((1,), (1,)), ((), ())), preferred_element_type=F32)


def tn(a, b):
    return lax.dot_general(a, b, (((0,), (0,)), ((), ())), preferred_element_type=F32)


def nn(a, b):
    return jnp.dot(a, b, preferred_element_type=F32)


def hi_lo(value):
    hi = value.astype(BF)
    return hi, (value - hi.astype(F32)).astype(BF)


def mod4(value):
    return lax.rem(value + 8, 4)


def lane_piece(value, at):
    out = jnp.zeros(value.shape[:-1] + (HD,), value.dtype)
    for i in range(3):
        out = jnp.where(at == i, value[..., i * HD : (i + 1) * HD], out)
    return out


def norm_kernel(
    meta, xa0, xa1, xa2, xa3, xb0, xb1, xb2, xb3, mod,
    scaled, packed,
):
    zhi, zlo, core = meta[1], meta[3], meta[4]
    place = zhi * 4 + zlo
    own_far = jnp.where(core == 0, -2, 2)
    sources = []
    for refs, side, far in (
        ((xa0, xa1, xa2, xa3), core, own_far),
        ((xb0, xb1, xb2, xb3), 1 - core, -own_far),
    ):
        for ref, offset in zip(refs, (0, -1, 1, far)):
            at = lax.rem(place + offset + 16, 16)
            sources.append((ref, at // 4, lax.rem(at, 4) * 2 + side))

    rows = 32

    def chunk(turn, carry):
        t = turn // (TILE // rows)
        start = lax.rem(turn, TILE // rows) * rows
        span = pl.ds(pl.multiple_of(start, rows), rows)

        def load(source):
            ref, z, g = source
            d = mod4(z - t)
            return ref[d, span, :].astype(F32)

        total = jnp.zeros((rows, WIDTH), F32)
        for source in sources:
            total = total + load(source)
        mean = jnp.sum(total, axis=1, keepdims=True) * (1.0 / FEATS)
        square = jnp.zeros((rows, WIDTH), F32)
        for source in sources:
            centred = load(source) - mean
            square = square + centred * centred
        inv = lax.rsqrt(jnp.sum(square, axis=1, keepdims=True) * (1.0 / FEATS) + EPS)
        for source in sources:
            normed = (load(source) - mean) * inv
            scaled[source[2], t, span, :] = (normed * (1.0 + mod[1, source[2]])).astype(BF)
        normed = (load(sources[0]) - mean) * inv
        inv_wide = jnp.broadcast_to(inv, (rows, HD))
        packed[t, span, :] = lane_piece(normed, zhi)
        packed[4 + t, span, :] = inv_wide

        @pl.when(t == zhi)
        def _():
            packed[8, span, :] = inv_wide
            for i in range(3):
                packed[9 + i, span, :] = normed[:, i * HD : (i + 1) * HD]

        return carry

    lax.fori_loop(0, 4 * (TILE // rows), chunk, 0)


def proj_kernel(
    meta, nscr, wg, mod, q_gain, k_gain,
    qk, v, proj, wk, ws, vec, wc,
):
    zhi, core = meta[1], meta[4]
    for sy in range(16):
        for d in range(4):
            zh = mod4(zhi - d)
            for part in range(3):
                wc[(sy // 4) * 2 + zh // 2, lax.rem(zh, 2) * 4 + sy % 4, :, part * HD : (part + 1) * HD] = (
                    wg[sy, d, part * 48 : (part + 1) * 48, :]
                )
    for r in range(4):
        wk[r] = wc[2 * r + core]
        ws[r] = wc[2 * r + 1 - core]

    acc = jnp.zeros((4 * TILE, WIDTH), F32)
    flat = jnp.zeros((16, WIDTH), F32)
    for g in range(8):
        w_g = wc[g].reshape(WIDTH, WIDTH)
        acc = acc + nn(nscr[g].reshape(4 * TILE, WIDTH), w_g)
        scale_hi, scale_lo = hi_lo(1.0 + mod[1, g])
        shift_hi, shift_lo = hi_lo(mod[0, g])
        four = jnp.concatenate([scale_hi, scale_lo, shift_hi, shift_lo], axis=0)
        lhs = jnp.concatenate([four, jnp.zeros((12, WIDTH), BF)], axis=0)
        flat = flat + nn(lhs, w_g)
    vec[...] = flat
    proj[...] = acc + (flat[2:3] + flat[3:4])
    for t in range(4):
        span = slice(t * TILE, (t + 1) * TILE)
        q = proj[span, 0:HD]
        k = proj[span, HD : 2 * HD]
        q_inv = lax.rsqrt(jnp.mean(q * q, axis=1, keepdims=True) + EPS)
        k_inv = lax.rsqrt(jnp.mean(k * k, axis=1, keepdims=True) + EPS)
        qk[t, :, 0:HD] = (q * q_inv * q_gain[...]).astype(BF)
        qk[t, :, HD : 2 * HD] = (k * k_inv * k_gain[...]).astype(BF)
        v[t] = proj[span, 2 * HD : 3 * HD].astype(BF)


def norm_back(raw, gain, grad):
    inv = lax.rsqrt(jnp.mean(raw * raw, axis=1, keepdims=True) + EPS)
    scaled = grad * gain
    dot = jnp.mean(scaled * raw, axis=1, keepdims=True)
    return inv * (scaled - raw * (inv * inv * dot))


def sweep_kernel(
    meta, nb, k0, k1, k2, k3, v0, v1, v2, v3, proj, vec, q_gain, k_gain, *rest
):
    tiles, ups = rest[-2:]
    first_sweep = len(rest) == 8
    probs, out = (rest[5], rest[4]) if first_sweep else (rest[1], rest[2])
    zhi, y = meta[1], meta[2]
    for ref, v_ref, offset in zip((k0, k1, k2, k3), (v0, v1, v2, v3), PLACES):
        yy = mod4(y + offset)
        for z in range(4):
            tiles[z * 4 + yy, :, 0 : 2 * HD] = ref[z]
            tiles[z * 4 + yy, :, 2 * HD : 3 * HD] = v_ref[z]
    for i, offset in enumerate(PLACES):
        for z in range(4):
            if first_sweep:
                ups[mod4(zhi - z) * 4 + mod4(y + offset)] = rest[i][z]
            else:
                ups[z * 4 + i] = rest[0][i, z]

    m1_hi, m1_lo = hi_lo(vec[0:1] + vec[1:2])
    m1 = jnp.concatenate([m1_hi, m1_lo, jnp.zeros((14, WIDTH), BF)], axis=0)
    ones = jnp.ones((16, WIDTH), BF)
    s0 = vec[2:3] + vec[3:4]

    def k_of(t):
        return tiles[t, :, HD : 2 * HD]

    def v_of(t):
        return tiles[t, :, 2 * HD : 3 * HD]

    def own(jz, carry):
        j = jz * 4 + y
        near = (nb[1, j], nb[2, j])
        d_k = jnp.zeros((TILE, HD), F32)
        d_v = jnp.zeros((TILE, HD), F32)
        d_q = None
        for slot in range(3):
            if slot == 0:
                i = j
                keys = (j, near[0], near[1])
            else:
                i = near[slot - 1]
                keys = (j, i, nb[1, i] + nb[2, i] - j)
            q = tiles[i, :, 0:HD]
            up = ups[i]
            k_all = jnp.concatenate([k_of(t) for t in keys], axis=0)
            v_all = jnp.concatenate([v_of(t) for t in keys], axis=0)
            if first_sweep:
                expo = jnp.exp(nt(k_all, q))
                prob = expo * (1.0 / jnp.sum(expo, axis=0, keepdims=True))
                probs[jz, slot] = prob
            else:
                prob = probs[jz, slot]
            prob_b = prob.astype(BF)
            dprob = nt(v_all, up)
            delta = jnp.sum(prob_b.astype(F32) * dprob, axis=0, keepdims=True)
            if slot == 0:
                dscore = (prob * (dprob - delta)).astype(BF)
                d_q = tn(dscore, k_all)
                dscore = dscore[0:TILE]
            else:
                dscore = (prob[0:TILE] * (dprob[0:TILE] - delta)).astype(BF)
            d_k = d_k + nn(dscore, q)
            d_v = d_v + nn(prob_b[0:TILE], up)
        start = pl.multiple_of(jz * TILE, TILE)
        raw = proj[pl.ds(start, TILE), :]
        d_q = norm_back(raw[:, 0:HD], q_gain[...], d_q)
        d_k = norm_back(raw[:, HD : 2 * HD], k_gain[...], d_k)
        d_all = jnp.concatenate([d_q, d_k, d_v], axis=1).astype(BF)
        out[pl.ds(start, TILE), :] = d_all
        first = nt(m1, d_all)
        prod_hi, prod_lo = hi_lo(d_all.astype(F32) * (raw - s0))
        second = nt(ones, prod_hi) + nt(ones, prod_lo)
        row = jnp.concatenate(
            [first[0:1] + first[1:2], second[0:1], jnp.zeros((1, TILE), F32)], axis=1
        )
        at = lax.broadcasted_iota(jnp.int32, (8, WIDTH), 0)
        return carry + jnp.where(at == jz, row, 0.0)

    stats = lax.fori_loop(0, 4, own, jnp.zeros((8, WIDTH), F32))
    out[4 * TILE : 4 * TILE + 16, :] = jnp.concatenate(hi_lo(stats), axis=0)


def stats_of(ref, start):
    both = ref[start : start + 16, :].astype(F32)
    return both[0:8] + both[8:16]


def route(meta):
    forward = meta[4] == 0
    return jnp.where(forward, 3, 1), jnp.where(forward, 1, 3)


def feature_kernel(far_only, meta, own, other, wk, wr, *outs):
    zlo = meta[3]
    stats = jnp.concatenate(hi_lo(stats_of(own, 4 * TILE) + stats_of(other, 4 * TILE)), axis=0)
    for offset, o in zip((2,) if far_only else (0, *route(meta)), outs):
        r = mod4(zlo + offset)
        value = nt(own[0 : 4 * TILE, :], wk[r].reshape(WIDTH, WIDTH))
        value = value + nt(other[0 : 4 * TILE, :], wr[r].reshape(WIDTH, WIDTH))
        o[0 : 4 * TILE, :] = value.astype(BF)
        o[4 * TILE : 4 * TILE + 16, :] = stats


def features(far_only, args):
    count = 1 if far_only else 3
    return call(
        functools.partial(feature_kernel, far_only),
        [sds((4 * TILE + 16, WIDTH), BF)] * count,
        args,
        1,
        (),
        2 * 4 * TILE * FEATS * WIDTH * count // 4,
        12,
    )


def add_kernel(a, b, out):
    rows = out.shape[0] - 16
    out[0:rows, :] = (a[0:rows, :].astype(F32) + b[0:rows, :].astype(F32)).astype(BF)
    out[rows : rows + 16, :] = jnp.concatenate(hi_lo(stats_of(a, rows) + stats_of(b, rows)), axis=0)


def window_kernel(meta, a0, a1, a2, *outs):
    zhi = meta[1]
    stats = stats_of(a0, 4 * TILE) + stats_of(a1, 4 * TILE) + stats_of(a2, 4 * TILE)
    at = lax.broadcasted_iota(jnp.int32, (8, WIDTH), 0)
    for d, o in zip((0, 2, *route(meta)), outs):
        t = mod4(zhi + d)
        span = pl.ds(pl.multiple_of(t * TILE, TILE), TILE)
        o[0:TILE, :] = (a0[span, :].astype(F32) + a1[span, :].astype(F32) + a2[span, :].astype(F32)).astype(BF)
        row = jnp.sum(jnp.where(at == t, stats, 0.0), axis=0, keepdims=True)
        o[TILE : TILE + 16, :] = jnp.concatenate(hi_lo(jnp.broadcast_to(row, (8, WIDTH))), axis=0)


def window_piece_kernel(meta, a0, a1, a2, *outs):
    zhi = meta[1]
    places = [mod4(zhi + d) for d in (0, 2, *route(meta))]
    stats = stats_of(a0, 4 * TILE) + stats_of(a1, 4 * TILE) + stats_of(a2, 4 * TILE)
    stats = jnp.concatenate([stats[0:4, 0:TILE], stats[0:4, TILE : 2 * TILE]], axis=0)
    for t in range(4):
        span = slice(t * TILE, (t + 1) * TILE)
        value = a0[span, :].astype(F32) + a1[span, :].astype(F32) + a2[span, :].astype(F32)
        for at, o in zip(places, outs):
            o[span, :] = lane_piece(value, at).astype(BF)
    for at, o in zip(places, outs):
        o[4 * TILE : 4 * TILE + 16, :] = jnp.concatenate(hi_lo(stats * jnp.where(at == 3, 0.0, 1.0)), axis=0)


def term_piece_kernel(meta, a0, a1, a2, packed, mod, sent):
    group = meta[3] * 2 + meta[4]
    stats = stats_of(a0, 4 * TILE)
    for a in (a1, a2):
        stats = stats + stats_of(a, 4 * TILE)
    scale = 1.0 + lane_piece(mod[1, group], meta[1])
    for t in range(4):
        span = slice(t * TILE, (t + 1) * TILE)
        grad = a0[span, :].astype(F32)
        for a in (a1, a2):
            grad = grad + a[span, :].astype(F32)
        value = packed[4 + t] * (grad * scale - column(stats[t : t + 1]) - packed[t] * column(stats[4 + t : 5 + t]))
        sent[t] = value.astype(BF)


def upstream_piece_kernel(meta, ids, coeffs, first, mod, t1, t2, t3, out):
    group = meta[3] * 2 + meta[4]
    after, decay, weight = decays(meta, ids, coeffs)
    gate = lane_piece(mod[2, group], meta[1]) * weight
    for t in range(4):
        later = t1[t].astype(F32) + t2[t].astype(F32) * after[0] + t3[t].astype(F32) * (after[0] * after[1])
        out[t] = (first[mod4(meta[1] - t)].astype(F32) + gate * later).astype(BF)


def column(row):
    return jnp.transpose(jnp.broadcast_to(row * (1.0 / FEATS), (TILE, TILE)))


def term_kernel(meta, a0, a1, a2, packed, mod, term, sent, moments):
    group = meta[3] * 2 + meta[4]
    grad = a0[0:TILE, :].astype(F32)
    stats = stats_of(a0, TILE)
    for a in (a1, a2):
        grad = grad + a[0:TILE, :].astype(F32)
        stats = stats + stats_of(a, TILE)
    first = stats[0:1, 0:TILE]
    second = stats[0:1, TILE : 2 * TILE]
    moments[...] = jnp.concatenate([first, second], axis=0) * (FEATS**-0.5)

    def wide(value):
        return jnp.concatenate([value] * 3, axis=1)

    du = grad * (1.0 + mod[1, group])
    normed = jnp.concatenate([packed[9 + i] for i in range(3)], axis=1)
    value = wide(packed[8]) * (du - wide(column(first)) - normed * wide(column(second)))
    term[...] = value
    sent[...] = value.astype(BF)


def decays(meta, ids, coeffs):
    step = meta[0]
    after = []
    for ahead in (1, 2, 3):
        at = jnp.minimum(step + ahead, 3)
        after.append(jnp.where(step + ahead <= 3, coeffs[0, ids[at]], 1.0))
    return after, coeffs[0, ids[step]], coeffs[1, ids[step]]


def lam_of(meta, ids, coeffs, cot, terms):
    after, decay, weight = decays(meta, ids, coeffs)
    lam = cot[...] * (after[0] * after[1] * after[2])
    for ref, factor in zip(terms, (1.0, after[0], after[0] * after[1])):
        lam = lam + ref[...].astype(F32) * factor
    return lam, decay, weight


def cut_kernel(meta, ids, coeffs, cot_far, mod_far, w_far, o0, o1, o2, o3, cot, mod, w, sems):
    copies = [
        pltpu.make_async_copy(src, dst, sems.at[i])
        for i, (src, dst) in enumerate(((cot_far, cot), (mod_far, mod), (w_far, w)))
    ]
    for copy in copies:
        copy.start()
    for copy in copies:
        copy.wait()
    zhi = meta[1]
    group = meta[3] * 2 + meta[4]
    lam, decay, weight = lam_of(meta, ids, coeffs, cot, ())
    up = mod[2, group] * weight * lam
    for d, o in enumerate((o0, o1, o2, o3)):
        at = mod4(zhi + d)
        for part in range(3):
            o[part * 48 : (part + 1) * 48, :] = lane_piece(w[part].astype(F32), at).astype(BF)
        o[144:272, :] = lane_piece(up, at).astype(BF)


def adjoint_kernel(meta, ids, coeffs, cot, term, t1, t2, t3, out):
    lam, decay, weight = lam_of(meta, ids, coeffs, cot, (t1, t2, t3))
    out[...] = decay * lam + term[...]


def turn(value, axis, offset):
    return lax.ppermute(value, axis, [(i, (i + offset) % 4) for i in range(4)])


def ring4(value, axis):
    return [value] + [turn(value, axis, -offset) for offset in PLACES[1:]]


def hand_on(before, after, axis):
    pairs = []
    for i in range(4):
        pairs.append((2 * i, 2 * ((i - 1) % 4)))
        pairs.append((2 * i + 1, 2 * ((i + 1) % 4) + 1))
    return lax.ppermute(jnp.where(lax.axis_index("core") == 0, after, before), (axis, "core"), pairs)


def relayed(value, axis):
    before, after = turn(value, axis, 1), turn(value, axis, -1)
    return [value, before, after, hand_on(before, after, axis)]


def to_heads(pieces):
    got = [pieces[0]]
    for d in (1, 2, 3):
        pairs = [(i, (i + d) % 4) for i in range(4) if (i + d) % 4 != 3]
        got.append(lax.ppermute(pieces[d], "zhi", pairs))
    return got


def to_earlier(value):
    return [lax.ppermute(value, "step", [(j, j - d) for j in range(d, 4)]) for d in (1, 2, 3)]


def swing(value, axes, count, forward, hops=1, headless=False):
    pairs = []
    for i in range(count):
        for core, step in ((0, forward), (1, -forward)):
            if not headless or (i + hops * step) % count != 3:
                pairs.append((2 * i + core, 2 * ((i + step) % count) + core))
    return lax.ppermute(value, (*axes, "core"), pairs)


def reduced(far, plain, waiting, axes, count, headless=False):
    half_way = swing(far, axes, count, 1, 2, headless)
    got = swing(plain, axes, count, -1, 1, headless)
    (waiting,) = call(add_kernel, [sds(waiting.shape, BF)], (waiting, half_way), 0)
    return got, swing(waiting, axes, count, 1, 1, headless)


def along_z(value, offset):
    return lax.ppermute(value, ("zhi", "zlo"), [(i, (i + offset) % 16) for i in range(16)])


def far_z(value):
    pairs = []
    for i in range(16):
        pairs.append((2 * i, 2 * ((i + 2) % 16)))
        pairs.append((2 * i + 1, 2 * ((i - 2) % 16) + 1))
    return lax.ppermute(value, ("zhi", "zlo", "core"), pairs)


def other_core(value):
    return lax.ppermute(value, "core", [(0, 1), (1, 0)])


def shards(states, modulation, cotangent, w_qkv, q_gain, k_gain, step_ids, coeffs, neighbours):
    zhi = lax.axis_index("zhi")
    meta = jnp.stack([lax.axis_index(a) for a in ("step", "zhi", "y", "zlo", "core")]).astype(jnp.int32)
    coeffs, neighbours = coeffs.T, neighbours.T
    mod = modulation.reshape(3, 8, 1, WIDTH)
    gq = (q_gain / jnp.sqrt(jnp.float32(HD))).reshape(1, HD)
    gk = k_gain.reshape(1, HD)

    pieces = call(
        cut_kernel,
        [sds((272, HD), BF)] * 4,
        (meta, step_ids, coeffs, cotangent, mod, jnp.transpose(w_qkv, (1, 0, 2))),
        3,
        [
            pltpu.VMEM((TILE, WIDTH), F32),
            pltpu.VMEM((3, 8, 1, WIDTH), F32),
            pltpu.VMEM((3, 48, WIDTH), BF),
            pltpu.SemaphoreType.DMA((3,)),
        ],
        grant=12,
        far=3,
    )
    pieces = to_heads(pieces)
    own_rows = jnp.stack([p[0:144] for p in pieces])
    pieces[1], x = lax.optimization_barrier((pieces[1], states[0]))
    own_up = jnp.stack([p[144:272] for p in pieces])

    before, after = turn(x, "zhi", 1), turn(x, "zhi", -1)
    own_rows, before, after = lax.optimization_barrier((own_rows, before, after))
    far = hand_on(before, after, "zhi")
    y_rows = lax.all_gather(own_rows, "y")
    y_rows, far, own_up = lax.optimization_barrier((y_rows, far, own_up))
    wg = lax.all_gather(y_rows, "step").reshape(16, 4, 144, HD)
    x_tiles = jnp.stack([x, before, far, after])
    xa = [x_tiles, along_z(x_tiles, 1), along_z(x_tiles, -1), far_z(x_tiles)]
    up_before, up_after = turn(own_up, "y", 1), turn(own_up, "y", -1)
    up_before, up_after, xa[3] = lax.optimization_barrier((up_before, up_after, xa[3]))
    first_ups = [own_up, up_before, up_after, hand_on(up_before, up_after, "y")]
    xb = [other_core(a) for a in xa]

    tokens = 4 * TILE
    scaled, packed = call(
        norm_kernel,
        [sds((8, 4, TILE, WIDTH), BF), sds((12, TILE, HD), F32)],
        (meta, *xa, *xb, mod),
        1,
        (),
        0,
        12,
    )
    scaled, wg, *first_ups = lax.optimization_barrier((scaled, wg, *first_ups))
    qk, v, proj, wk, ws, vec = call(
        proj_kernel,
        [
            sds((4, TILE, 2 * HD), BF),
            sds((4, TILE, HD), BF),
            sds((tokens, WIDTH), F32),
            sds((4, 8, 48, WIDTH), BF),
            sds((4, 8, 48, WIDTH), BF),
            sds((16, WIDTH), F32),
        ],
        (meta, scaled, wg, mod, gq, gk),
        1,
        [pltpu.VMEM((8, 8, 48, WIDTH), BF)],
        2 * tokens * FEATS * WIDTH,
        20,
    )
    qk_before, qk_after = turn(qk, "y", 1), turn(qk, "y", -1)
    v_before, v_after = turn(v, "y", 1), turn(v, "y", -1)
    all_qkv = [qk, qk_before, qk_after, hand_on(qk_before, qk_after, "y")]
    all_qkv += [v, v_before, v_after, hand_on(v_before, v_after, "y")]
    wr = other_core(ws)

    again = first_ups
    for sweep in range(SWEEPS):
        outs = [sds((tokens + 16, WIDTH), BF), sds((4, 3, WIDTH, TILE), F32)]
        dproj, *kept = call(
            sweep_kernel,
            outs[: 2 - sweep],
            (meta, neighbours, *all_qkv, proj, vec, gq, gk, *again),
            2,
            [pltpu.VMEM((16, TILE, WIDTH), BF), pltpu.VMEM((16, TILE, HD), BF)],
            400 * 1000 * 1000,
            12,
        )
        pair = (meta, dproj, other_core(dproj), wk, wr)
        (far,) = features(True, pair)
        here, plain, waiting = features(False, pair)
        near = (here, *reduced(far, plain, waiting, ("zhi", "zlo"), 16))
        if sweep + 1 < SWEEPS:
            own, *others = call(window_piece_kernel, [sds((tokens + 16, HD), BF)] * 4, (meta, *near), 1)
            (sent,) = call(
                term_piece_kernel,
                [sds((4, TILE, HD), BF)],
                (meta, own, *reduced(*others, ("zhi",), 4, True), packed, mod),
                1,
            )
            (up,) = call(
                upstream_piece_kernel,
                [sds((4, TILE, HD), BF)],
                (meta, step_ids, coeffs, first_ups[0], mod, *to_earlier(sent)),
                3,
            )
            again = (lax.all_gather(up, "y"), *kept)
    own, *others = call(window_kernel, [sds((TILE + 16, WIDTH), BF)] * 4, (meta, *near), 1)
    term, sent, moments = call(
        term_kernel,
        [sds((TILE, WIDTH), F32), sds((TILE, WIDTH), BF), sds((2, TILE), F32)],
        (meta, own, *reduced(*others, ("zhi",), 4), packed, mod),
        1,
    )
    (adjoint,) = call(
        adjoint_kernel,
        [sds((TILE, WIDTH), F32)],
        (meta, step_ids, coeffs, cotangent, term, *to_earlier(sent)),
        3,
    )
    return adjoint[None], moments[None]


def solution(mesh):
    fine = Mesh(mesh.devices.reshape(4, 4, 4, 4, 2), ("step", "zhi", "y", "zlo", "core"))
    blk, head = ("zhi", "y"), ("zlo", "core")
    in_specs = (
        P("step", blk, head),
        P("step", None, None),
        P(blk, head),
        P(("step",) + blk, None, head),
        P(),
        P(),
        P(),
        P(),
        P(),
    )
    out_specs = (P("step", blk, head), P("step", None, blk))
    return jax.shard_map(shards, mesh=fine, in_specs=in_specs, out_specs=out_specs, check_vma=False)
```

```python
import functools

import jax
import jax.numpy as jnp
from jax import lax
from jax.experimental import pallas as pl
from jax.experimental.pallas import tpu as pltpu
from jax.sharding import Mesh
from jax.sharding import PartitionSpec as P

HD = 128
TILE = 128
WIDTH = 384
FEATS = 3072
SWEEPS = 2
EPS = 1e-06
BF = jnp.bfloat16
F32 = jnp.float32
MIB = 1024 * 1024
PLACES = (0, -1, 1, 2)

VM = pl.BlockSpec(memory_space=pltpu.VMEM)
SM = pl.BlockSpec(memory_space=pltpu.SMEM)
HBM = pl.BlockSpec(memory_space=pltpu.HBM)


def call(body, outs, args, smem, scratch=(), flops=0, grant=8, far=0, far_outs=0):
    specs = [SM if i < smem else VM for i in range(len(args))]
    specs[smem : smem + far] = [HBM] * far
    moved = sum(a.size * a.dtype.itemsize for a in args) + sum(
        o.size * o.dtype.itemsize for o in outs
    )
    return pl.pallas_call(
        body,
        out_shape=tuple(outs),
        in_specs=specs,
        out_specs=tuple([VM] * (len(outs) - far_outs) + [HBM] * far_outs),
        scratch_shapes=list(scratch),
        compiler_params=pltpu.CompilerParams(vmem_limit_bytes=grant * MIB),
        cost_estimate=pl.CostEstimate(flops=flops, bytes_accessed=moved, transcendentals=0),
    )(*args)


def sds(shape, dtype):
    return jax.ShapeDtypeStruct(shape, dtype)


def nt(a, b):
    return lax.dot_general(a, b, (((1,), (1,)), ((), ())), preferred_element_type=F32)


def tn(a, b):
    return lax.dot_general(a, b, (((0,), (0,)), ((), ())), preferred_element_type=F32)


def nn(a, b):
    return jnp.dot(a, b, preferred_element_type=F32)


def hi_lo(value):
    hi = value.astype(BF)
    return hi, (value - hi.astype(F32)).astype(BF)


def mod4(value):
    return lax.rem(value + 8, 4)


def lane_piece(value, at):
    out = jnp.zeros(value.shape[:-1] + (HD,), value.dtype)
    for i in range(3):
        out = jnp.where(at == i, value[..., i * HD : (i + 1) * HD], out)
    return out


def norm_kernel(
    meta, xa0, xa1, xa2, xa3, xb0, xb1, xb2, xb3, mod,
    scaled, packed,
):
    zhi, zlo, core = meta[1], meta[3], meta[4]
    place = zhi * 4 + zlo
    own_far = jnp.where(core == 0, -2, 2)
    sources = []
    for refs, side, far in (
        ((xa0, xa1, xa2, xa3), core, own_far),
        ((xb0, xb1, xb2, xb3), 1 - core, -own_far),
    ):
        for ref, offset in zip(refs, (0, -1, 1, far)):
            at = lax.rem(place + offset + 16, 16)
            sources.append((ref, at // 4, lax.rem(at, 4) * 2 + side))

    rows = 32

    def chunk(turn, carry):
        t = turn // (TILE // rows)
        start = lax.rem(turn, TILE // rows) * rows
        span = pl.ds(pl.multiple_of(start, rows), rows)

        def load(source):
            ref, z, g = source
            d = mod4(z - t)
            return ref[d, span, :].astype(F32)

        total = jnp.zeros((rows, WIDTH), F32)
        for source in sources:
            total = total + load(source)
        mean = jnp.sum(total, axis=1, keepdims=True) * (1.0 / FEATS)
        square = jnp.zeros((rows, WIDTH), F32)
        for source in sources:
            centred = load(source) - mean
            square = square + centred * centred
        inv = lax.rsqrt(jnp.sum(square, axis=1, keepdims=True) * (1.0 / FEATS) + EPS)
        for source in sources:
            normed = (load(source) - mean) * inv
            scaled[source[2], t, span, :] = (normed * (1.0 + mod[1, source[2]])).astype(BF)
        normed = (load(sources[0]) - mean) * inv
        inv_wide = jnp.broadcast_to(inv, (rows, HD))
        packed[t, span, :] = lane_piece(normed, zhi)
        packed[4 + t, span, :] = inv_wide

        @pl.when(t == zhi)
        def _():
            packed[8, span, :] = inv_wide
            for i in range(3):
                packed[9 + i, span, :] = normed[:, i * HD : (i + 1) * HD]

        return carry

    lax.fori_loop(0, 4 * (TILE // rows), chunk, 0)


def proj_kernel(
    meta, nscr, wg, mod, q_gain, k_gain,
    qkv, proj, wk, ws, vec, wc,
):
    zhi, core = meta[1], meta[4]
    for sy in range(16):
        for d in range(4):
            zh = mod4(zhi - d)
            for part in range(3):
                wc[(sy // 4) * 2 + zh // 2, lax.rem(zh, 2) * 4 + sy % 4, :, part * HD : (part + 1) * HD] = (
                    wg[sy, d, part * 48 : (part + 1) * 48, :]
                )
    for r in range(4):
        wk[r] = wc[2 * r + core]
        ws[r] = wc[2 * r + 1 - core]

    acc = jnp.zeros((4 * TILE, WIDTH), F32)
    flat = jnp.zeros((16, WIDTH), F32)
    for g in range(8):
        w_g = wc[g].reshape(WIDTH, WIDTH)
        acc = acc + nn(nscr[g].reshape(4 * TILE, WIDTH), w_g)
        scale_hi, scale_lo = hi_lo(1.0 + mod[1, g])
        shift_hi, shift_lo = hi_lo(mod[0, g])
        four = jnp.concatenate([scale_hi, scale_lo, shift_hi, shift_lo], axis=0)
        lhs = jnp.concatenate([four, jnp.zeros((12, WIDTH), BF)], axis=0)
        flat = flat + nn(lhs, w_g)
    vec[...] = flat
    proj[...] = acc + (flat[2:3] + flat[3:4])
    for t in range(4):
        span = slice(t * TILE, (t + 1) * TILE)
        q = proj[span, 0:HD]
        k = proj[span, HD : 2 * HD]
        q_inv = lax.rsqrt(jnp.mean(q * q, axis=1, keepdims=True) + EPS)
        k_inv = lax.rsqrt(jnp.mean(k * k, axis=1, keepdims=True) + EPS)
        qkv[t, :, 0:HD] = (q * q_inv * q_gain[...]).astype(BF)
        qkv[t, :, HD : 2 * HD] = (k * k_inv * k_gain[...]).astype(BF)
        qkv[t, :, 2 * HD : 3 * HD] = proj[span, 2 * HD : 3 * HD].astype(BF)


def norm_back(raw, gain, grad):
    inv = lax.rsqrt(jnp.mean(raw * raw, axis=1, keepdims=True) + EPS)
    scaled = grad * gain
    dot = jnp.mean(scaled * raw, axis=1, keepdims=True)
    return inv * (scaled - raw * (inv * inv * dot))


def sweep_kernel(
    meta, nb, k0, k1, k2, k3, proj, vec, q_gain, k_gain, *rest
):
    tiles, ups = rest[-2:]
    first_sweep = len(rest) == 8
    probs, out = (rest[5], rest[4]) if first_sweep else (rest[1], rest[2])
    zhi, y = meta[1], meta[2]
    for ref, offset in zip((k0, k1, k2, k3), PLACES):
        yy = mod4(y + offset)
        for z in range(4):
            tiles[z * 4 + yy] = ref[z]
    for i, offset in enumerate(PLACES):
        for z in range(4):
            if first_sweep:
                ups[mod4(zhi - z) * 4 + mod4(y + offset)] = rest[i][z]
            else:
                ups[z * 4 + i] = rest[0][i, z]

    m1_hi, m1_lo = hi_lo(vec[0:1] + vec[1:2])
    m1 = jnp.concatenate([m1_hi, m1_lo, jnp.zeros((14, WIDTH), BF)], axis=0)
    ones = jnp.ones((16, WIDTH), BF)
    s0 = vec[2:3] + vec[3:4]

    def k_of(t):
        return tiles[t, :, HD : 2 * HD]

    def v_of(t):
        return tiles[t, :, 2 * HD : 3 * HD]

    def own(jz, carry):
        j = jz * 4 + y
        near = (nb[1, j], nb[2, j])
        d_k = jnp.zeros((TILE, HD), F32)
        d_v = jnp.zeros((TILE, HD), F32)
        d_q = None
        for slot in range(3):
            if slot == 0:
                i = j
                keys = (j, near[0], near[1])
            else:
                i = near[slot - 1]
                keys = (j, i, nb[1, i] + nb[2, i] - j)
            q = tiles[i, :, 0:HD]
            up = ups[i]
            k_all = jnp.concatenate([k_of(t) for t in keys], axis=0)
            v_all = jnp.concatenate([v_of(t) for t in keys], axis=0)
            if first_sweep:
                expo = jnp.exp(nt(k_all, q))
                prob = expo * (1.0 / jnp.sum(expo, axis=0, keepdims=True))
                probs[jz, slot] = prob
            else:
                prob = probs[jz, slot]
            prob_b = prob.astype(BF)
            dprob = nt(v_all, up)
            delta = jnp.sum(prob_b.astype(F32) * dprob, axis=0, keepdims=True)
            if slot == 0:
                dscore = (prob * (dprob - delta)).astype(BF)
                d_q = tn(dscore, k_all)
                dscore = dscore[0:TILE]
            else:
                dscore = (prob[0:TILE] * (dprob[0:TILE] - delta)).astype(BF)
            d_k = d_k + nn(dscore, q)
            d_v = d_v + nn(prob_b[0:TILE], up)
        start = pl.multiple_of(jz * TILE, TILE)
        raw = proj[pl.ds(start, TILE), :]
        d_q = norm_back(raw[:, 0:HD], q_gain[...], d_q)
        d_k = norm_back(raw[:, HD : 2 * HD], k_gain[...], d_k)
        d_all = jnp.concatenate([d_q, d_k, d_v], axis=1).astype(BF)
        out[pl.ds(start, TILE), :] = d_all
        first = nt(m1, d_all)
        prod_hi, prod_lo = hi_lo(d_all.astype(F32) * (raw - s0))
        second = nt(ones, prod_hi) + nt(ones, prod_lo)
        row = jnp.concatenate(
            [first[0:1] + first[1:2], second[0:1], jnp.zeros((1, TILE), F32)], axis=1
        )
        at = lax.broadcasted_iota(jnp.int32, (8, WIDTH), 0)
        return carry + jnp.where(at == jz, row, 0.0)

    stats = lax.fori_loop(0, 4, own, jnp.zeros((8, WIDTH), F32))
    out[4 * TILE : 4 * TILE + 16, :] = jnp.concatenate(hi_lo(stats), axis=0)


def stats_of(ref, start):
    both = ref[start : start + 16, :].astype(F32)
    return both[0:8] + both[8:16]


def route(meta):
    forward = meta[4] == 0
    return jnp.where(forward, 3, 1), jnp.where(forward, 1, 3)


def feature_kernel(far_only, meta, own, other, wk, wr, *outs):
    zlo = meta[3]
    stats = jnp.concatenate(hi_lo(stats_of(own, 4 * TILE) + stats_of(other, 4 * TILE)), axis=0)
    for offset, o in zip((2,) if far_only else (0, *route(meta)), outs):
        r = mod4(zlo + offset)
        value = nt(own[0 : 4 * TILE, :], wk[r].reshape(WIDTH, WIDTH))
        value = value + nt(other[0 : 4 * TILE, :], wr[r].reshape(WIDTH, WIDTH))
        o[0 : 4 * TILE, :] = value.astype(BF)
        o[4 * TILE : 4 * TILE + 16, :] = stats


def features(far_only, args):
    count = 1 if far_only else 3
    return call(
        functools.partial(feature_kernel, far_only),
        [sds((4 * TILE + 16, WIDTH), BF)] * count,
        args,
        1,
        (),
        2 * 4 * TILE * FEATS * WIDTH * count // 4,
        16,
    )


def add_kernel(a, b, out):
    rows = out.shape[0] - 16
    out[0:rows, :] = (a[0:rows, :].astype(F32) + b[0:rows, :].astype(F32)).astype(BF)
    out[rows : rows + 16, :] = jnp.concatenate(hi_lo(stats_of(a, rows) + stats_of(b, rows)), axis=0)


def window_kernel(meta, a0, a1, a2, *outs):
    zhi = meta[1]
    stats = stats_of(a0, 4 * TILE) + stats_of(a1, 4 * TILE) + stats_of(a2, 4 * TILE)
    at = lax.broadcasted_iota(jnp.int32, (8, WIDTH), 0)
    for d, o in zip((0, 2, *route(meta)), outs):
        t = mod4(zhi + d)
        span = pl.ds(pl.multiple_of(t * TILE, TILE), TILE)
        o[0:TILE, :] = (a0[span, :].astype(F32) + a1[span, :].astype(F32) + a2[span, :].astype(F32)).astype(BF)
        row = jnp.sum(jnp.where(at == t, stats, 0.0), axis=0, keepdims=True)
        o[TILE : TILE + 16, :] = jnp.concatenate(hi_lo(jnp.broadcast_to(row, (8, WIDTH))), axis=0)


def window_piece_kernel(meta, a0, a1, a2, *outs):
    zhi = meta[1]
    places = [mod4(zhi + d) for d in (0, 2, *route(meta))]
    stats = stats_of(a0, 4 * TILE) + stats_of(a1, 4 * TILE) + stats_of(a2, 4 * TILE)
    stats = jnp.concatenate([stats[0:4, 0:TILE], stats[0:4, TILE : 2 * TILE]], axis=0)
    for t in range(4):
        span = slice(t * TILE, (t + 1) * TILE)
        value = a0[span, :].astype(F32) + a1[span, :].astype(F32) + a2[span, :].astype(F32)
        for at, o in zip(places, outs):
            o[span, :] = lane_piece(value, at).astype(BF)
    for at, o in zip(places, outs):
        o[4 * TILE : 4 * TILE + 16, :] = jnp.concatenate(hi_lo(stats * jnp.where(at == 3, 0.0, 1.0)), axis=0)


def term_piece_kernel(meta, a0, a1, a2, packed, mod, sent):
    group = meta[3] * 2 + meta[4]
    stats = stats_of(a0, 4 * TILE)
    for a in (a1, a2):
        stats = stats + stats_of(a, 4 * TILE)
    scale = 1.0 + lane_piece(mod[1, group], meta[1])
    for t in range(4):
        span = slice(t * TILE, (t + 1) * TILE)
        grad = a0[span, :].astype(F32)
        for a in (a1, a2):
            grad = grad + a[span, :].astype(F32)
        value = packed[4 + t] * (grad * scale - column(stats[t : t + 1]) - packed[t] * column(stats[4 + t : 5 + t]))
        sent[t] = value.astype(BF)


def upstream_piece_kernel(meta, ids, coeffs, first, mod, t1, t2, t3, out):
    group = meta[3] * 2 + meta[4]
    after, decay, weight = decays(meta, ids, coeffs)
    gate = lane_piece(mod[2, group], meta[1]) * weight
    for t in range(4):
        later = t1[t].astype(F32) + t2[t].astype(F32) * after[0] + t3[t].astype(F32) * (after[0] * after[1])
        out[t] = (first[mod4(meta[1] - t)].astype(F32) + gate * later).astype(BF)


def column(row):
    return jnp.transpose(jnp.broadcast_to(row * (1.0 / FEATS), (TILE, TILE)))


def term_kernel(meta, a0, a1, a2, packed, mod, term, sent, moments):
    group = meta[3] * 2 + meta[4]
    grad = a0[0:TILE, :].astype(F32)
    stats = stats_of(a0, TILE)
    for a in (a1, a2):
        grad = grad + a[0:TILE, :].astype(F32)
        stats = stats + stats_of(a, TILE)
    first = stats[0:1, 0:TILE]
    second = stats[0:1, TILE : 2 * TILE]
    moments[...] = jnp.concatenate([first, second], axis=0) * (FEATS**-0.5)

    def wide(value):
        return jnp.concatenate([value] * 3, axis=1)

    du = grad * (1.0 + mod[1, group])
    normed = jnp.concatenate([packed[9 + i] for i in range(3)], axis=1)
    value = wide(packed[8]) * (du - wide(column(first)) - normed * wide(column(second)))
    term[...] = value
    sent[...] = value.astype(BF)


def decays(meta, ids, coeffs):
    step = meta[0]
    after = []
    for ahead in (1, 2, 3):
        at = jnp.minimum(step + ahead, 3)
        after.append(jnp.where(step + ahead <= 3, coeffs[0, ids[at]], 1.0))
    return after, coeffs[0, ids[step]], coeffs[1, ids[step]]


def lam_of(meta, ids, coeffs, cot, terms):
    after, decay, weight = decays(meta, ids, coeffs)
    lam = cot[...] * (after[0] * after[1] * after[2])
    for ref, factor in zip(terms, (1.0, after[0], after[0] * after[1])):
        lam = lam + ref[...].astype(F32) * factor
    return lam, decay, weight


def cut_kernel(meta, ids, coeffs, cot_far, mod_far, w_far, o0, o1, o2, o3, cot, mod, w, sems):
    copies = [
        pltpu.make_async_copy(src, dst, sems.at[i])
        for i, (src, dst) in enumerate(((cot_far, cot), (mod_far, mod), (w_far, w)))
    ]
    for copy in copies:
        copy.start()
    for copy in copies:
        copy.wait()
    zhi = meta[1]
    group = meta[3] * 2 + meta[4]
    lam, decay, weight = lam_of(meta, ids, coeffs, cot, ())
    up = mod[2, group] * weight * lam
    for d, o in enumerate((o0, o1, o2, o3)):
        at = mod4(zhi + d)
        for part in range(3):
            o[part * 48 : (part + 1) * 48, :] = lane_piece(w[part].astype(F32), at).astype(BF)
        o[144:272, :] = lane_piece(up, at).astype(BF)


def adjoint_kernel(meta, ids, coeffs, cot, term, t1, t2, t3, out):
    lam, decay, weight = lam_of(meta, ids, coeffs, cot, (t1, t2, t3))
    out[...] = decay * lam + term[...]


def turn(value, axis, offset):
    return lax.ppermute(value, axis, [(i, (i + offset) % 4) for i in range(4)])


def ring4(value, axis):
    return [value] + [turn(value, axis, -offset) for offset in PLACES[1:]]


def hand_on(before, after, axis):
    pairs = []
    for i in range(4):
        pairs.append((2 * i, 2 * ((i - 1) % 4)))
        pairs.append((2 * i + 1, 2 * ((i + 1) % 4) + 1))
    return lax.ppermute(jnp.where(lax.axis_index("core") == 0, after, before), (axis, "core"), pairs)


def relayed(value, axis):
    before, after = turn(value, axis, 1), turn(value, axis, -1)
    return [value, before, after, hand_on(before, after, axis)]


def to_heads(pieces):
    got = [pieces[0]]
    for d in (1, 2, 3):
        pairs = [(i, (i + d) % 4) for i in range(4) if (i + d) % 4 != 3]
        got.append(lax.ppermute(pieces[d], "zhi", pairs))
    return got


def to_earlier(value):
    return [lax.ppermute(value, "step", [(j, j - d) for j in range(d, 4)]) for d in (1, 2, 3)]


def swing(value, axes, count, forward, hops=1, headless=False):
    pairs = []
    for i in range(count):
        for core, step in ((0, forward), (1, -forward)):
            if not headless or (i + hops * step) % count != 3:
                pairs.append((2 * i + core, 2 * ((i + step) % count) + core))
    return lax.ppermute(value, (*axes, "core"), pairs)


def reduced(far, plain, waiting, axes, count, headless=False):
    half_way = swing(far, axes, count, 1, 2, headless)
    got = swing(plain, axes, count, -1, 1, headless)
    (waiting,) = call(add_kernel, [sds(waiting.shape, BF)], (waiting, half_way), 0)
    return got, swing(waiting, axes, count, 1, 1, headless)


def along_z(value, offset):
    return lax.ppermute(value, ("zhi", "zlo"), [(i, (i + offset) % 16) for i in range(16)])


def far_z(value):
    pairs = []
    for i in range(16):
        pairs.append((2 * i, 2 * ((i + 2) % 16)))
        pairs.append((2 * i + 1, 2 * ((i - 2) % 16) + 1))
    return lax.ppermute(value, ("zhi", "zlo", "core"), pairs)


def other_core(value):
    return lax.ppermute(value, "core", [(0, 1), (1, 0)])


def shards(states, modulation, cotangent, w_qkv, q_gain, k_gain, step_ids, coeffs, neighbours):
    zhi = lax.axis_index("zhi")
    meta = jnp.stack([lax.axis_index(a) for a in ("step", "zhi", "y", "zlo", "core")]).astype(jnp.int32)
    coeffs, neighbours = coeffs.T, neighbours.T
    mod = modulation.reshape(3, 8, 1, WIDTH)
    gq = (q_gain / jnp.sqrt(jnp.float32(HD))).reshape(1, HD)
    gk = k_gain.reshape(1, HD)

    pieces = call(
        cut_kernel,
        [sds((272, HD), BF)] * 4,
        (meta, step_ids, coeffs, cotangent, mod, jnp.transpose(w_qkv, (1, 0, 2))),
        3,
        [
            pltpu.VMEM((TILE, WIDTH), F32),
            pltpu.VMEM((3, 8, 1, WIDTH), F32),
            pltpu.VMEM((3, 48, WIDTH), BF),
            pltpu.SemaphoreType.DMA((3,)),
        ],
        grant=12,
        far=3,
    )
    pieces = to_heads(pieces)
    *pieces, x = lax.optimization_barrier((*pieces, states[0]))
    own_rows = jnp.stack([p[0:144] for p in pieces])
    own_up = jnp.stack([p[144:272] for p in pieces])

    before, after = turn(x, "zhi", 1), turn(x, "zhi", -1)
    y_rows = lax.all_gather(own_rows, "y")
    y_rows, before, after, own_up = lax.optimization_barrier((y_rows, before, after, own_up))
    far = hand_on(before, after, "zhi")
    wg = lax.all_gather(y_rows, "step").reshape(16, 4, 144, HD)
    x_tiles = jnp.stack([x, before, far, after])
    xa = [x_tiles, along_z(x_tiles, 1), along_z(x_tiles, -1), far_z(x_tiles)]
    up_before, up_after = turn(own_up, "y", 1), turn(own_up, "y", -1)
    up_before, up_after, xa[3] = lax.optimization_barrier((up_before, up_after, xa[3]))
    first_ups = [own_up, up_before, up_after, hand_on(up_before, up_after, "y")]
    xb = [other_core(a) for a in xa]

    tokens = 4 * TILE
    scaled, packed = call(
        norm_kernel,
        [sds((8, 4, TILE, WIDTH), BF), sds((12, TILE, HD), F32)],
        (meta, *xa, *xb, mod),
        1,
        (),
        0,
        16,
    )
    scaled, wg, *first_ups = lax.optimization_barrier((scaled, wg, *first_ups))
    qkv, proj, wk, ws, vec = call(
        proj_kernel,
        [
            sds((4, TILE, WIDTH), BF),
            sds((tokens, WIDTH), F32),
            sds((4, 8, 48, WIDTH), BF),
            sds((4, 8, 48, WIDTH), BF),
            sds((16, WIDTH), F32),
        ],
        (meta, scaled, wg, mod, gq, gk),
        1,
        [pltpu.VMEM((8, 8, 48, WIDTH), BF)],
        2 * tokens * FEATS * WIDTH,
        24,
    )
    all_qkv = relayed(qkv, "y")
    wr = other_core(ws)

    again = first_ups
    for sweep in range(SWEEPS):
        outs = [sds((tokens + 16, WIDTH), BF), sds((4, 3, WIDTH, TILE), F32)]
        dproj, *kept = call(
            sweep_kernel,
            outs[: 2 - sweep],
            (meta, neighbours, *all_qkv, proj, vec, gq, gk, *again),
            2,
            [pltpu.VMEM((16, TILE, WIDTH), BF), pltpu.VMEM((16, TILE, HD), BF)],
            400 * 1000 * 1000,
            16,
        )
        pair = (meta, dproj, other_core(dproj), wk, wr)
        (far,) = features(True, pair)
        here, plain, waiting = features(False, pair)
        near = (here, *reduced(far, plain, waiting, ("zhi", "zlo"), 16))
        if sweep + 1 < SWEEPS:
            own, *others = call(window_piece_kernel, [sds((tokens + 16, HD), BF)] * 4, (meta, *near), 1)
            (sent,) = call(
                term_piece_kernel,
                [sds((4, TILE, HD), BF)],
                (meta, own, *reduced(*others, ("zhi",), 4, True), packed, mod),
                1,
            )
            (up,) = call(
                upstream_piece_kernel,
                [sds((4, TILE, HD), BF)],
                (meta, step_ids, coeffs, first_ups[0], mod, *to_earlier(sent)),
                3,
            )
            again = (lax.all_gather(up, "y"), *kept)
    own, *others = call(window_kernel, [sds((TILE + 16, WIDTH), BF)] * 4, (meta, *near), 1)
    term, sent, moments = call(
        term_kernel,
        [sds((TILE, WIDTH), F32), sds((TILE, WIDTH), BF), sds((2, TILE), F32)],
        (meta, own, *reduced(*others, ("zhi",), 4), packed, mod),
        1,
    )
    (adjoint,) = call(
        adjoint_kernel,
        [sds((TILE, WIDTH), F32)],
        (meta, step_ids, coeffs, cotangent, term, *to_earlier(sent)),
        3,
    )
    return adjoint[None], moments[None]


def solution(mesh):
    fine = Mesh(mesh.devices.reshape(4, 4, 4, 4, 2), ("step", "zhi", "y", "zlo", "core"))
    blk, head = ("zhi", "y"), ("zlo", "core")
    in_specs = (
        P("step", blk, head),
        P("step", None, None),
        P(blk, head),
        P(("step",) + blk, None, head),
        P(),
        P(),
        P(),
        P(),
        P(),
    )
    out_specs = (P("step", blk, head), P("step", None, blk))
    return jax.shard_map(shards, mesh=fine, in_specs=in_specs, out_specs=out_specs, check_vma=False)
```

```python
import functools

import jax
import jax.numpy as jnp
from jax import lax
from jax.experimental import pallas as pl
from jax.experimental.pallas import tpu as pltpu
from jax.sharding import Mesh
from jax.sharding import PartitionSpec as P

HD = 128
TILE = 128
WIDTH = 384
FEATS = 3072
SWEEPS = 2
EPS = 1e-06
BF = jnp.bfloat16
F32 = jnp.float32
MIB = 1024 * 1024
PLACES = (0, -1, 1, 2)

VM = pl.BlockSpec(memory_space=pltpu.VMEM)
SM = pl.BlockSpec(memory_space=pltpu.SMEM)
HBM = pl.BlockSpec(memory_space=pltpu.HBM)


def call(body, outs, args, smem, scratch=(), flops=0, grant=8, far=0, far_outs=0):
    specs = [SM if i < smem else VM for i in range(len(args))]
    specs[smem : smem + far] = [HBM] * far
    moved = sum(a.size * a.dtype.itemsize for a in args) + sum(
        o.size * o.dtype.itemsize for o in outs
    )
    return pl.pallas_call(
        body,
        out_shape=tuple(outs),
        in_specs=specs,
        out_specs=tuple([VM] * (len(outs) - far_outs) + [HBM] * far_outs),
        scratch_shapes=list(scratch),
        compiler_params=pltpu.CompilerParams(vmem_limit_bytes=grant * MIB),
        cost_estimate=pl.CostEstimate(flops=flops, bytes_accessed=moved, transcendentals=0),
    )(*args)


def sds(shape, dtype):
    return jax.ShapeDtypeStruct(shape, dtype)


def nt(a, b):
    return lax.dot_general(a, b, (((1,), (1,)), ((), ())), preferred_element_type=F32)


def tn(a, b):
    return lax.dot_general(a, b, (((0,), (0,)), ((), ())), preferred_element_type=F32)


def nn(a, b):
    return jnp.dot(a, b, preferred_element_type=F32)


def hi_lo(value):
    hi = value.astype(BF)
    return hi, (value - hi.astype(F32)).astype(BF)


def mod4(value):
    return lax.rem(value + 8, 4)


def lane_piece(value, at):
    out = jnp.zeros(value.shape[:-1] + (HD,), value.dtype)
    for i in range(3):
        out = jnp.where(at == i, value[..., i * HD : (i + 1) * HD], out)
    return out


def norm_kernel(
    meta, xa0, xa1, xa2, xa3, xb0, xb1, xb2, xb3, mod,
    scaled, packed,
):
    zhi, zlo, core = meta[1], meta[3], meta[4]
    place = zhi * 4 + zlo
    own_far = jnp.where(core == 0, -2, 2)
    sources = []
    for refs, side, far in (
        ((xa0, xa1, xa2, xa3), core, own_far),
        ((xb0, xb1, xb2, xb3), 1 - core, -own_far),
    ):
        for ref, offset in zip(refs, (0, -1, 1, far)):
            at = lax.rem(place + offset + 16, 16)
            sources.append((ref, at // 4, lax.rem(at, 4) * 2 + side))

    rows = 32

    def chunk(turn, carry):
        t = turn // (TILE // rows)
        start = lax.rem(turn, TILE // rows) * rows
        span = pl.ds(pl.multiple_of(start, rows), rows)

        def load(source):
            ref, z, g = source
            d = mod4(z - t)
            return ref[d, span, :].astype(F32)

        total = jnp.zeros((rows, WIDTH), F32)
        for source in sources:
            total = total + load(source)
        mean = jnp.sum(total, axis=1, keepdims=True) * (1.0 / FEATS)
        square = jnp.zeros((rows, WIDTH), F32)
        for source in sources:
            centred = load(source) - mean
            square = square + centred * centred
        inv = lax.rsqrt(jnp.sum(square, axis=1, keepdims=True) * (1.0 / FEATS) + EPS)
        for source in sources:
            normed = (load(source) - mean) * inv
            scaled[source[2], t, span, :] = (normed * (1.0 + mod[1, source[2]])).astype(BF)
        normed = (load(sources[0]) - mean) * inv
        inv_wide = jnp.broadcast_to(inv, (rows, HD))
        packed[t, span, :] = lane_piece(normed, zhi)
        packed[4 + t, span, :] = inv_wide

        @pl.when(t == zhi)
        def _():
            packed[8, span, :] = inv_wide
            for i in range(3):
                packed[9 + i, span, :] = normed[:, i * HD : (i + 1) * HD]

        return carry

    lax.fori_loop(0, 4 * (TILE // rows), chunk, 0)


def proj_kernel(
    meta, nscr, wg, mod, q_gain, k_gain,
    qkv, proj, wk, ws, vec, wc,
):
    zhi, core = meta[1], meta[4]
    for sy in range(16):
        for d in range(4):
            zh = mod4(zhi - d)
            for part in range(3):
                wc[(sy // 4) * 2 + zh // 2, lax.rem(zh, 2) * 4 + sy % 4, :, part * HD : (part + 1) * HD] = (
                    wg[sy, d, part * 48 : (part + 1) * 48, :]
                )
    for r in range(4):
        wk[r] = wc[2 * r + core]
        ws[r] = wc[2 * r + 1 - core]

    acc = jnp.zeros((4 * TILE, WIDTH), F32)
    flat = jnp.zeros((16, WIDTH), F32)
    for g in range(8):
        w_g = wc[g].reshape(WIDTH, WIDTH)
        acc = acc + nn(nscr[g].reshape(4 * TILE, WIDTH), w_g)
        scale_hi, scale_lo = hi_lo(1.0 + mod[1, g])
        shift_hi, shift_lo = hi_lo(mod[0, g])
        four = jnp.concatenate([scale_hi, scale_lo, shift_hi, shift_lo], axis=0)
        lhs = jnp.concatenate([four, jnp.zeros((12, WIDTH), BF)], axis=0)
        flat = flat + nn(lhs, w_g)
    vec[...] = flat
    proj[...] = acc + (flat[2:3] + flat[3:4])
    for t in range(4):
        span = slice(t * TILE, (t + 1) * TILE)
        q = proj[span, 0:HD]
        k = proj[span, HD : 2 * HD]
        q_inv = lax.rsqrt(jnp.mean(q * q, axis=1, keepdims=True) + EPS)
        k_inv = lax.rsqrt(jnp.mean(k * k, axis=1, keepdims=True) + EPS)
        qkv[t, :, 0:HD] = (q * q_inv * q_gain[...]).astype(BF)
        qkv[t, :, HD : 2 * HD] = (k * k_inv * k_gain[...]).astype(BF)
        qkv[t, :, 2 * HD : 3 * HD] = proj[span, 2 * HD : 3 * HD].astype(BF)


def norm_back(raw, gain, grad):
    inv = lax.rsqrt(jnp.mean(raw * raw, axis=1, keepdims=True) + EPS)
    scaled = grad * gain
    dot = jnp.mean(scaled * raw, axis=1, keepdims=True)
    return inv * (scaled - raw * (inv * inv * dot))


def sweep_kernel(
    meta, nb, k0, k1, k2, k3, proj, vec, q_gain, k_gain, *rest
):
    tiles, ups = rest[-2:]
    first_sweep = rest[4].shape[-1] == WIDTH
    probs, out = (rest[5], rest[4]) if first_sweep else (rest[4], rest[5])
    zhi, y = meta[1], meta[2]
    for ref, offset in zip((k0, k1, k2, k3), PLACES):
        yy = mod4(y + offset)
        for z in range(4):
            tiles[z * 4 + yy] = ref[z]
    for i, offset in enumerate(PLACES):
        for z in range(4):
            tile = mod4(zhi - z) if first_sweep else z
            ups[tile * 4 + mod4(y + offset)] = rest[i][z]

    m1_hi, m1_lo = hi_lo(vec[0:1] + vec[1:2])
    m1 = jnp.concatenate([m1_hi, m1_lo, jnp.zeros((14, WIDTH), BF)], axis=0)
    ones = jnp.ones((16, WIDTH), BF)
    s0 = vec[2:3] + vec[3:4]

    def k_of(t):
        return tiles[t, :, HD : 2 * HD]

    def v_of(t):
        return tiles[t, :, 2 * HD : 3 * HD]

    def own(jz, carry):
        j = jz * 4 + y
        near = (nb[1, j], nb[2, j])
        d_k = jnp.zeros((TILE, HD), F32)
        d_v = jnp.zeros((TILE, HD), F32)
        d_q = None
        for slot in range(3):
            if slot == 0:
                i = j
                keys = (j, near[0], near[1])
            else:
                i = near[slot - 1]
                keys = (j, i, nb[1, i] + nb[2, i] - j)
            q = tiles[i, :, 0:HD]
            up = ups[i]
            k_all = jnp.concatenate([k_of(t) for t in keys], axis=0)
            v_all = jnp.concatenate([v_of(t) for t in keys], axis=0)
            if first_sweep:
                expo = jnp.exp(nt(k_all, q))
                prob = expo * (1.0 / jnp.sum(expo, axis=0, keepdims=True))
                probs[jz, slot] = prob
            else:
                prob = probs[jz, slot]
            prob_b = prob.astype(BF)
            dprob = nt(v_all, up)
            delta = jnp.sum(prob_b.astype(F32) * dprob, axis=0, keepdims=True)
            if slot == 0:
                dscore = (prob * (dprob - delta)).astype(BF)
                d_q = tn(dscore, k_all)
                dscore = dscore[0:TILE]
            else:
                dscore = (prob[0:TILE] * (dprob[0:TILE] - delta)).astype(BF)
            d_k = d_k + nn(dscore, q)
            d_v = d_v + nn(prob_b[0:TILE], up)
        start = pl.multiple_of(jz * TILE, TILE)
        raw = proj[pl.ds(start, TILE), :]
        d_q = norm_back(raw[:, 0:HD], q_gain[...], d_q)
        d_k = norm_back(raw[:, HD : 2 * HD], k_gain[...], d_k)
        d_all = jnp.concatenate([d_q, d_k, d_v], axis=1).astype(BF)
        out[pl.ds(start, TILE), :] = d_all
        first = nt(m1, d_all)
        prod_hi, prod_lo = hi_lo(d_all.astype(F32) * (raw - s0))
        second = nt(ones, prod_hi) + nt(ones, prod_lo)
        row = jnp.concatenate(
            [first[0:1] + first[1:2], second[0:1], jnp.zeros((1, TILE), F32)], axis=1
        )
        at = lax.broadcasted_iota(jnp.int32, (8, WIDTH), 0)
        return carry + jnp.where(at == jz, row, 0.0)

    stats = lax.fori_loop(0, 4, own, jnp.zeros((8, WIDTH), F32))
    out[4 * TILE : 4 * TILE + 16, :] = jnp.concatenate(hi_lo(stats), axis=0)


def stats_of(ref, start):
    both = ref[start : start + 16, :].astype(F32)
    return both[0:8] + both[8:16]


def route(meta, core):
    forward = meta[4] == core
    return jnp.where(forward, 3, 1), jnp.where(forward, 1, 3)


def feature_kernel(far_only, meta, own, other, wk, wr, *outs):
    zlo = meta[3]
    stats = jnp.concatenate(hi_lo(stats_of(own, 4 * TILE) + stats_of(other, 4 * TILE)), axis=0)
    for offset, o in zip((2,) if far_only else (0, *route(meta, 0)), outs):
        r = mod4(zlo + offset)
        value = nt(own[0 : 4 * TILE, :], wk[r].reshape(WIDTH, WIDTH))
        value = value + nt(other[0 : 4 * TILE, :], wr[r].reshape(WIDTH, WIDTH))
        o[0 : 4 * TILE, :] = value.astype(BF)
        o[4 * TILE : 4 * TILE + 16, :] = stats


def features(far_only, args):
    count = 1 if far_only else 3
    return call(
        functools.partial(feature_kernel, far_only),
        [sds((4 * TILE + 16, WIDTH), BF)] * count,
        args,
        1,
        (),
        2 * 4 * TILE * FEATS * WIDTH * count // 4,
        12,
    )


def add_kernel(a, b, out):
    rows = out.shape[0] - 16
    out[0:rows, :] = (a[0:rows, :].astype(F32) + b[0:rows, :].astype(F32)).astype(BF)
    out[rows : rows + 16, :] = jnp.concatenate(hi_lo(stats_of(a, rows) + stats_of(b, rows)), axis=0)


def window_kernel(meta, a0, a1, a2, *outs):
    zhi = meta[1]
    stats = stats_of(a0, 4 * TILE) + stats_of(a1, 4 * TILE) + stats_of(a2, 4 * TILE)
    at = lax.broadcasted_iota(jnp.int32, (8, WIDTH), 0)
    for d, o in zip((0, 2, *route(meta, 1)), outs):
        t = mod4(zhi + d)
        span = pl.ds(pl.multiple_of(t * TILE, TILE), TILE)
        o[0:TILE, :] = (a0[span, :].astype(F32) + a1[span, :].astype(F32) + a2[span, :].astype(F32)).astype(BF)
        row = jnp.sum(jnp.where(at == t, stats, 0.0), axis=0, keepdims=True)
        o[TILE : TILE + 16, :] = jnp.concatenate(hi_lo(jnp.broadcast_to(row, (8, WIDTH))), axis=0)


def window_piece_kernel(meta, a0, a1, a2, *outs):
    zhi = meta[1]
    places = [mod4(zhi + d) for d in (0, 2, *route(meta, 1))]
    stats = stats_of(a0, 4 * TILE) + stats_of(a1, 4 * TILE) + stats_of(a2, 4 * TILE)
    stats = jnp.concatenate([stats[0:4, 0:TILE], stats[0:4, TILE : 2 * TILE]], axis=0)
    for t in range(4):
        span = slice(t * TILE, (t + 1) * TILE)
        value = a0[span, :].astype(F32) + a1[span, :].astype(F32) + a2[span, :].astype(F32)
        for at, o in zip(places, outs):
            o[span, :] = lane_piece(value, at).astype(BF)
    for at, o in zip(places, outs):
        o[4 * TILE : 4 * TILE + 16, :] = jnp.concatenate(hi_lo(stats * jnp.where(at == 3, 0.0, 1.0)), axis=0)


def term_piece_kernel(meta, a0, a1, a2, packed, mod, sent):
    group = meta[3] * 2 + meta[4]
    stats = stats_of(a0, 4 * TILE)
    for a in (a1, a2):
        stats = stats + stats_of(a, 4 * TILE)
    scale = 1.0 + lane_piece(mod[1, group], meta[1])
    for t in range(4):
        span = slice(t * TILE, (t + 1) * TILE)
        grad = a0[span, :].astype(F32)
        for a in (a1, a2):
            grad = grad + a[span, :].astype(F32)
        value = packed[4 + t] * (grad * scale - column(stats[t : t + 1]) - packed[t] * column(stats[4 + t : 5 + t]))
        sent[t] = value.astype(BF)


def upstream_piece_kernel(meta, ids, coeffs, first, mod, t1, t2, t3, out):
    group = meta[3] * 2 + meta[4]
    after, decay, weight = decays(meta, ids, coeffs)
    gate = lane_piece(mod[2, group], meta[1]) * weight
    for t in range(4):
        later = t1[t].astype(F32) + t2[t].astype(F32) * after[0] + t3[t].astype(F32) * (after[0] * after[1])
        out[t] = (first[mod4(meta[1] - t)].astype(F32) + gate * later).astype(BF)


def column(row):
    return jnp.transpose(jnp.broadcast_to(row * (1.0 / FEATS), (TILE, TILE)))


def term_kernel(meta, a0, a1, a2, packed, mod, term, sent, moments):
    group = meta[3] * 2 + meta[4]
    grad = a0[0:TILE, :].astype(F32)
    stats = stats_of(a0, TILE)
    for a in (a1, a2):
        grad = grad + a[0:TILE, :].astype(F32)
        stats = stats + stats_of(a, TILE)
    first = stats[0:1, 0:TILE]
    second = stats[0:1, TILE : 2 * TILE]
    moments[...] = jnp.concatenate([first, second], axis=0) * (FEATS**-0.5)

    def wide(value):
        return jnp.concatenate([value] * 3, axis=1)

    du = grad * (1.0 + mod[1, group])
    normed = jnp.concatenate([packed[9 + i] for i in range(3)], axis=1)
    value = wide(packed[8]) * (du - wide(column(first)) - normed * wide(column(second)))
    term[...] = value
    sent[...] = value.astype(BF)


def decays(meta, ids, coeffs):
    step = meta[0]
    after = []
    for ahead in (1, 2, 3):
        at = jnp.minimum(step + ahead, 3)
        after.append(jnp.where(step + ahead <= 3, coeffs[0, ids[at]], 1.0))
    return after, coeffs[0, ids[step]], coeffs[1, ids[step]]


def lam_of(meta, ids, coeffs, cot, terms):
    after, decay, weight = decays(meta, ids, coeffs)
    lam = cot[...] * (after[0] * after[1] * after[2])
    for ref, factor in zip(terms, (1.0, after[0], after[0] * after[1])):
        lam = lam + ref[...].astype(F32) * factor
    return lam, decay, weight


def cut_kernel(meta, ids, coeffs, cot_far, mod_far, w_far, o0, o1, o2, o3, cot, mod, w, sems):
    copies = [
        pltpu.make_async_copy(src, dst, sems.at[i])
        for i, (src, dst) in enumerate(((cot_far, cot), (mod_far, mod), (w_far, w)))
    ]
    for copy in copies:
        copy.start()
    for copy in copies:
        copy.wait()
    zhi = meta[1]
    group = meta[3] * 2 + meta[4]
    lam, decay, weight = lam_of(meta, ids, coeffs, cot, ())
    up = mod[2, group] * weight * lam
    for d, o in enumerate((o0, o1, o2, o3)):
        at = mod4(zhi + d)
        for part in range(3):
            o[part * 48 : (part + 1) * 48, :] = lane_piece(w[part].astype(F32), at).astype(BF)
        o[144:272, :] = lane_piece(up, at).astype(BF)


def adjoint_kernel(meta, ids, coeffs, cot, term, t1, t2, t3, out):
    lam, decay, weight = lam_of(meta, ids, coeffs, cot, (t1, t2, t3))
    out[...] = decay * lam + term[...]


def turn(value, axis, offset):
    return lax.ppermute(value, axis, [(i, (i + offset) % 4) for i in range(4)])


def ring4(value, axis):
    return [value] + [turn(value, axis, -offset) for offset in PLACES[1:]]


def hand_on(before, after, axis):
    pairs = []
    for i in range(4):
        pairs.append((2 * i, 2 * ((i - 1) % 4)))
        pairs.append((2 * i + 1, 2 * ((i + 1) % 4) + 1))
    return lax.ppermute(jnp.where(lax.axis_index("core") == 0, after, before), (axis, "core"), pairs)


def relayed(value, axis):
    before, after = turn(value, axis, 1), turn(value, axis, -1)
    return [value, before, after, hand_on(before, after, axis)]


def to_heads(pieces):
    got = [pieces[0]]
    for d in (1, 2, 3):
        pairs = [(i, (i + d) % 4) for i in range(4) if (i + d) % 4 != 3]
        got.append(lax.ppermute(pieces[d], "zhi", pairs))
    return got


def to_earlier(value):
    return [lax.ppermute(value, "step", [(j, j - d) for j in range(d, 4)]) for d in (1, 2, 3)]


def swing(value, axes, count, forward, hops=1, headless=False):
    pairs = []
    for i in range(count):
        for core, step in ((0, forward), (1, -forward)):
            if not headless or (i + hops * step) % count != 3:
                pairs.append((2 * i + core, 2 * ((i + step) % count) + core))
    return lax.ppermute(value, (*axes, "core"), pairs)


def reduced(far, plain, waiting, axes, count, forward, headless=False):
    half_way = swing(far, axes, count, forward, 2, headless)
    got = swing(plain, axes, count, -forward, 1, headless)
    (waiting,) = call(add_kernel, [sds(waiting.shape, BF)], (waiting, half_way), 0)
    return got, swing(waiting, axes, count, forward, 1, headless)


def along_z(value, offset):
    return lax.ppermute(value, ("zhi", "zlo"), [(i, (i + offset) % 16) for i in range(16)])


def far_z(value):
    pairs = []
    for i in range(16):
        pairs.append((2 * i, 2 * ((i + 2) % 16)))
        pairs.append((2 * i + 1, 2 * ((i - 2) % 16) + 1))
    return lax.ppermute(value, ("zhi", "zlo", "core"), pairs)


def other_core(value):
    return lax.ppermute(value, "core", [(0, 1), (1, 0)])


def shards(states, modulation, cotangent, w_qkv, q_gain, k_gain, step_ids, coeffs, neighbours):
    zhi = lax.axis_index("zhi")
    meta = jnp.stack([lax.axis_index(a) for a in ("step", "zhi", "y", "zlo", "core")]).astype(jnp.int32)
    coeffs, neighbours = coeffs.T, neighbours.T
    mod = modulation.reshape(3, 8, 1, WIDTH)
    gq = (q_gain / jnp.sqrt(jnp.float32(HD))).reshape(1, HD)
    gk = k_gain.reshape(1, HD)

    pieces = call(
        cut_kernel,
        [sds((272, HD), BF)] * 4,
        (meta, step_ids, coeffs, cotangent, mod, jnp.transpose(w_qkv, (1, 0, 2))),
        3,
        [
            pltpu.VMEM((TILE, WIDTH), F32),
            pltpu.VMEM((3, 8, 1, WIDTH), F32),
            pltpu.VMEM((3, 48, WIDTH), BF),
            pltpu.SemaphoreType.DMA((3,)),
        ],
        grant=12,
        far=3,
    )
    pieces = to_heads(pieces)
    own_rows = jnp.stack([p[0:144] for p in pieces])
    pieces[1], x = lax.optimization_barrier((pieces[1], states[0]))
    own_up = jnp.stack([p[144:272] for p in pieces])

    before, after = turn(x, "zhi", 1), turn(x, "zhi", -1)
    own_rows, before, after = lax.optimization_barrier((own_rows, before, after))
    far = hand_on(before, after, "zhi")
    y_rows = lax.all_gather(own_rows, "y")
    y_rows, far, own_up = lax.optimization_barrier((y_rows, far, own_up))
    wg = lax.all_gather(y_rows, "step").reshape(16, 4, 144, HD)
    x_tiles = jnp.stack([x, before, far, after])
    xa = [x_tiles, along_z(x_tiles, 1), along_z(x_tiles, -1), far_z(x_tiles)]
    up_before, up_after = turn(own_up, "y", 1), turn(own_up, "y", -1)
    up_before, up_after, xa[3] = lax.optimization_barrier((up_before, up_after, xa[3]))
    first_ups = [own_up, up_before, up_after, hand_on(up_before, up_after, "y")]
    xb = [other_core(a) for a in xa]

    tokens = 4 * TILE
    scaled, packed = call(
        norm_kernel,
        [sds((8, 4, TILE, WIDTH), BF), sds((12, TILE, HD), F32)],
        (meta, *xa, *xb, mod),
        1,
        (),
        0,
        12,
    )
    scaled, wg, *first_ups = lax.optimization_barrier((scaled, wg, *first_ups))
    qkv, proj, wk, ws, vec = call(
        proj_kernel,
        [
            sds((4, TILE, WIDTH), BF),
            sds((tokens, WIDTH), F32),
            sds((4, 8, 48, WIDTH), BF),
            sds((4, 8, 48, WIDTH), BF),
            sds((16, WIDTH), F32),
        ],
        (meta, scaled, wg, mod, gq, gk),
        1,
        [pltpu.VMEM((8, 8, 48, WIDTH), BF)],
        2 * tokens * FEATS * WIDTH,
        20,
    )
    all_qkv = ring4(qkv, "y")
    wr = other_core(ws)

    again = first_ups
    for sweep in range(SWEEPS):
        outs = [sds((tokens + 16, WIDTH), BF), sds((4, 3, WIDTH, TILE), F32)]
        dproj, *kept = call(
            sweep_kernel,
            outs[: 2 - sweep],
            (meta, neighbours, *all_qkv, proj, vec, gq, gk, *again),
            2,
            [pltpu.VMEM((16, TILE, WIDTH), BF), pltpu.VMEM((16, TILE, HD), BF)],
            400 * 1000 * 1000,
            12,
        )
        pair = (meta, dproj, other_core(dproj), wk, wr)
        (far,) = features(True, pair)
        here, plain, waiting = features(False, pair)
        near = (here, *reduced(far, plain, waiting, ("zhi", "zlo"), 16, 1))
        if sweep + 1 < SWEEPS:
            own, *others = call(window_piece_kernel, [sds((tokens + 16, HD), BF)] * 4, (meta, *near), 1)
            (sent,) = call(
                term_piece_kernel,
                [sds((4, TILE, HD), BF)],
                (meta, own, *reduced(*others, ("zhi",), 4, -1, True), packed, mod),
                1,
            )
            (up,) = call(
                upstream_piece_kernel,
                [sds((4, TILE, HD), BF)],
                (meta, step_ids, coeffs, first_ups[0], mod, *to_earlier(sent)),
                3,
            )
            again = (*ring4(up, "y"), *kept)
    own, *others = call(window_kernel, [sds((TILE + 16, WIDTH), BF)] * 4, (meta, *near), 1)
    term, sent, moments = call(
        term_kernel,
        [sds((TILE, WIDTH), F32), sds((TILE, WIDTH), BF), sds((2, TILE), F32)],
        (meta, own, *reduced(*others, ("zhi",), 4, -1), packed, mod),
        1,
    )
    (adjoint,) = call(
        adjoint_kernel,
        [sds((TILE, WIDTH), F32)],
        (meta, step_ids, coeffs, cotangent, term, *to_earlier(sent)),
        3,
    )
    return adjoint[None], moments[None]


def solution(mesh):
    fine = Mesh(mesh.devices.reshape(4, 4, 4, 4, 2), ("step", "zhi", "y", "zlo", "core"))
    blk, head = ("zhi", "y"), ("zlo", "core")
    in_specs = (
        P("step", blk, head),
        P("step", None, None),
        P(blk, head),
        P(("step",) + blk, None, head),
        P(),
        P(),
        P(),
        P(),
        P(),
    )
    out_specs = (P("step", blk, head), P("step", None, blk))
    return jax.shard_map(shards, mesh=fine, in_specs=in_specs, out_specs=out_specs, check_vma=False)
```

```python
import functools

import jax
import jax.numpy as jnp
from jax import lax
from jax.experimental import pallas as pl
from jax.experimental.pallas import tpu as pltpu
from jax.sharding import Mesh
from jax.sharding import PartitionSpec as P

HD = 128
TILE = 128
WIDTH = 384
FEATS = 3072
SWEEPS = 2
EPS = 1e-06
BF = jnp.bfloat16
F32 = jnp.float32
MIB = 1024 * 1024
PLACES = (0, -1, 1, 2)

VM = pl.BlockSpec(memory_space=pltpu.VMEM)
SM = pl.BlockSpec(memory_space=pltpu.SMEM)
HBM = pl.BlockSpec(memory_space=pltpu.HBM)


def call(body, outs, args, smem, scratch=(), flops=0, grant=8, far=0, far_outs=0):
    specs = [SM if i < smem else VM for i in range(len(args))]
    specs[smem : smem + far] = [HBM] * far
    moved = sum(a.size * a.dtype.itemsize for a in args) + sum(
        o.size * o.dtype.itemsize for o in outs
    )
    return pl.pallas_call(
        body,
        out_shape=tuple(outs),
        in_specs=specs,
        out_specs=tuple([VM] * (len(outs) - far_outs) + [HBM] * far_outs),
        scratch_shapes=list(scratch),
        compiler_params=pltpu.CompilerParams(vmem_limit_bytes=grant * MIB),
        cost_estimate=pl.CostEstimate(flops=flops, bytes_accessed=moved, transcendentals=0),
    )(*args)


def sds(shape, dtype):
    return jax.ShapeDtypeStruct(shape, dtype)


def nt(a, b):
    return lax.dot_general(a, b, (((1,), (1,)), ((), ())), preferred_element_type=F32)


def tn(a, b):
    return lax.dot_general(a, b, (((0,), (0,)), ((), ())), preferred_element_type=F32)


def nn(a, b):
    return jnp.dot(a, b, preferred_element_type=F32)


def hi_lo(value):
    hi = value.astype(BF)
    return hi, (value - hi.astype(F32)).astype(BF)


def mod4(value):
    return lax.rem(value + 8, 4)


def lane_piece(value, at):
    out = jnp.zeros(value.shape[:-1] + (HD,), value.dtype)
    for i in range(3):
        out = jnp.where(at == i, value[..., i * HD : (i + 1) * HD], out)
    return out


def norm_kernel(
    meta, xa0, xa1, xa2, xa3, xb0, xb1, xb2, xb3, mod,
    scaled, packed,
):
    zhi, zlo, core = meta[1], meta[3], meta[4]
    place = zhi * 4 + zlo
    own_far = jnp.where(core == 0, -2, 2)
    sources = []
    for refs, side, far in (
        ((xa0, xa1, xa2, xa3), core, own_far),
        ((xb0, xb1, xb2, xb3), 1 - core, -own_far),
    ):
        for ref, offset in zip(refs, (0, -1, 1, far)):
            at = lax.rem(place + offset + 16, 16)
            sources.append((ref, at // 4, lax.rem(at, 4) * 2 + side))

    rows = 32

    def chunk(turn, carry):
        t = turn // (TILE // rows)
        start = lax.rem(turn, TILE // rows) * rows
        span = pl.ds(pl.multiple_of(start, rows), rows)

        def load(source):
            ref, z, g = source
            d = mod4(z - t)
            return ref[d, span, :].astype(F32)

        total = jnp.zeros((rows, WIDTH), F32)
        for source in sources:
            total = total + load(source)
        mean = jnp.sum(total, axis=1, keepdims=True) * (1.0 / FEATS)
        square = jnp.zeros((rows, WIDTH), F32)
        for source in sources:
            centred = load(source) - mean
            square = square + centred * centred
        inv = lax.rsqrt(jnp.sum(square, axis=1, keepdims=True) * (1.0 / FEATS) + EPS)
        for source in sources:
            normed = (load(source) - mean) * inv
            scaled[source[2], t, span, :] = (normed * (1.0 + mod[1, source[2]])).astype(BF)
        normed = (load(sources[0]) - mean) * inv
        inv_wide = jnp.broadcast_to(inv, (rows, HD))
        packed[t, span, :] = lane_piece(normed, zhi)
        packed[4 + t, span, :] = inv_wide

        @pl.when(t == zhi)
        def _():
            packed[8, span, :] = inv_wide
            for i in range(3):
                packed[9 + i, span, :] = normed[:, i * HD : (i + 1) * HD]

        return carry

    lax.fori_loop(0, 4 * (TILE // rows), chunk, 0)


def proj_kernel(
    meta, nscr, wg, mod, q_gain, k_gain,
    qkv, proj, wk, ws, vec, wc,
):
    zhi, core = meta[1], meta[4]
    for sy in range(16):
        for d in range(4):
            zh = mod4(zhi - d)
            for part in range(3):
                wc[(sy // 4) * 2 + zh // 2, lax.rem(zh, 2) * 4 + sy % 4, :, part * HD : (part + 1) * HD] = (
                    wg[sy, d, part * 48 : (part + 1) * 48, :]
                )
    for r in range(4):
        wk[r] = wc[2 * r + core]
        ws[r] = wc[2 * r + 1 - core]

    acc = jnp.zeros((4 * TILE, WIDTH), F32)
    flat = jnp.zeros((16, WIDTH), F32)
    for g in range(8):
        w_g = wc[g].reshape(WIDTH, WIDTH)
        acc = acc + nn(nscr[g].reshape(4 * TILE, WIDTH), w_g)
        scale_hi, scale_lo = hi_lo(1.0 + mod[1, g])
        shift_hi, shift_lo = hi_lo(mod[0, g])
        four = jnp.concatenate([scale_hi, scale_lo, shift_hi, shift_lo], axis=0)
        lhs = jnp.concatenate([four, jnp.zeros((12, WIDTH), BF)], axis=0)
        flat = flat + nn(lhs, w_g)
    vec[...] = flat
    proj[...] = acc + (flat[2:3] + flat[3:4])
    for t in range(4):
        span = slice(t * TILE, (t + 1) * TILE)
        q = proj[span, 0:HD]
        k = proj[span, HD : 2 * HD]
        q_inv = lax.rsqrt(jnp.mean(q * q, axis=1, keepdims=True) + EPS)
        k_inv = lax.rsqrt(jnp.mean(k * k, axis=1, keepdims=True) + EPS)
        qkv[t, :, 0:HD] = (q * q_inv * q_gain[...]).astype(BF)
        qkv[t, :, HD : 2 * HD] = (k * k_inv * k_gain[...]).astype(BF)
        qkv[t, :, 2 * HD : 3 * HD] = proj[span, 2 * HD : 3 * HD].astype(BF)


def norm_back(raw, gain, grad):
    inv = lax.rsqrt(jnp.mean(raw * raw, axis=1, keepdims=True) + EPS)
    scaled = grad * gain
    dot = jnp.mean(scaled * raw, axis=1, keepdims=True)
    return inv * (scaled - raw * (inv * inv * dot))


def sweep_kernel(
    meta, nb, k0, k1, k2, k3, proj, vec, q_gain, k_gain, *rest
):
    tiles, ups = rest[-2:]
    first_sweep = len(rest) == 8
    probs, out = (rest[5], rest[4]) if first_sweep else (rest[1], rest[2])
    zhi, y = meta[1], meta[2]
    for ref, offset in zip((k0, k1, k2, k3), PLACES):
        yy = mod4(y + offset)
        for z in range(4):
            tiles[z * 4 + yy] = ref[z]
    for i, offset in enumerate(PLACES):
        for z in range(4):
            if first_sweep:
                ups[mod4(zhi - z) * 4 + mod4(y + offset)] = rest[i][z]
            else:
                ups[z * 4 + i] = rest[0][i, z]

    m1_hi, m1_lo = hi_lo(vec[0:1] + vec[1:2])
    m1 = jnp.concatenate([m1_hi, m1_lo, jnp.zeros((14, WIDTH), BF)], axis=0)
    ones = jnp.ones((16, WIDTH), BF)
    s0 = vec[2:3] + vec[3:4]

    def k_of(t):
        return tiles[t, :, HD : 2 * HD]

    def v_of(t):
        return tiles[t, :, 2 * HD : 3 * HD]

    def own(jz, carry):
        j = jz * 4 + y
        near = (nb[1, j], nb[2, j])
        d_k = jnp.zeros((TILE, HD), F32)
        d_v = jnp.zeros((TILE, HD), F32)
        d_q = None
        for slot in range(3):
            if slot == 0:
                i = j
                keys = (j, near[0], near[1])
            else:
                i = near[slot - 1]
                keys = (j, i, nb[1, i] + nb[2, i] - j)
            q = tiles[i, :, 0:HD]
            up = ups[i]
            k_all = jnp.concatenate([k_of(t) for t in keys], axis=0)
            v_all = jnp.concatenate([v_of(t) for t in keys], axis=0)
            if first_sweep:
                expo = jnp.exp(nt(k_all, q))
                prob = expo * (1.0 / jnp.sum(expo, axis=0, keepdims=True))
                probs[jz, slot] = prob
            else:
                prob = probs[jz, slot]
            prob_b = prob.astype(BF)
            dprob = nt(v_all, up)
            delta = jnp.sum(prob_b.astype(F32) * dprob, axis=0, keepdims=True)
            if slot == 0:
                dscore = (prob * (dprob - delta)).astype(BF)
                d_q = tn(dscore, k_all)
                dscore = dscore[0:TILE]
            else:
                dscore = (prob[0:TILE] * (dprob[0:TILE] - delta)).astype(BF)
            d_k = d_k + nn(dscore, q)
            d_v = d_v + nn(prob_b[0:TILE], up)
        start = pl.multiple_of(jz * TILE, TILE)
        raw = proj[pl.ds(start, TILE), :]
        d_q = norm_back(raw[:, 0:HD], q_gain[...], d_q)
        d_k = norm_back(raw[:, HD : 2 * HD], k_gain[...], d_k)
        d_all = jnp.concatenate([d_q, d_k, d_v], axis=1).astype(BF)
        out[pl.ds(start, TILE), :] = d_all
        first = nt(m1, d_all)
        prod_hi, prod_lo = hi_lo(d_all.astype(F32) * (raw - s0))
        second = nt(ones, prod_hi) + nt(ones, prod_lo)
        row = jnp.concatenate(
            [first[0:1] + first[1:2], second[0:1], jnp.zeros((1, TILE), F32)], axis=1
        )
        at = lax.broadcasted_iota(jnp.int32, (8, WIDTH), 0)
        return carry + jnp.where(at == jz, row, 0.0)

    stats = lax.fori_loop(0, 4, own, jnp.zeros((8, WIDTH), F32))
    out[4 * TILE : 4 * TILE + 16, :] = jnp.concatenate(hi_lo(stats), axis=0)


def stats_of(ref, start):
    both = ref[start : start + 16, :].astype(F32)
    return both[0:8] + both[8:16]


def route(meta):
    forward = meta[4] == 0
    return jnp.where(forward, 3, 1), jnp.where(forward, 1, 3)


def feature_kernel(far_only, meta, own, other, wk, wr, *outs):
    zlo = meta[3]
    stats = jnp.concatenate(hi_lo(stats_of(own, 4 * TILE) + stats_of(other, 4 * TILE)), axis=0)
    for offset, o in zip((2,) if far_only else (0, *route(meta)), outs):
        r = mod4(zlo + offset)
        value = nt(own[0 : 4 * TILE, :], wk[r].reshape(WIDTH, WIDTH))
        value = value + nt(other[0 : 4 * TILE, :], wr[r].reshape(WIDTH, WIDTH))
        o[0 : 4 * TILE, :] = value.astype(BF)
        o[4 * TILE : 4 * TILE + 16, :] = stats


def features(far_only, args):
    count = 1 if far_only else 3
    return call(
        functools.partial(feature_kernel, far_only),
        [sds((4 * TILE + 16, WIDTH), BF)] * count,
        args,
        1,
        (),
        2 * 4 * TILE * FEATS * WIDTH * count // 4,
        12,
    )


def add_kernel(a, b, out):
    rows = out.shape[0] - 16
    out[0:rows, :] = (a[0:rows, :].astype(F32) + b[0:rows, :].astype(F32)).astype(BF)
    out[rows : rows + 16, :] = jnp.concatenate(hi_lo(stats_of(a, rows) + stats_of(b, rows)), axis=0)


def window_kernel(meta, a0, a1, a2, *outs):
    zhi = meta[1]
    stats = stats_of(a0, 4 * TILE) + stats_of(a1, 4 * TILE) + stats_of(a2, 4 * TILE)
    at = lax.broadcasted_iota(jnp.int32, (8, WIDTH), 0)
    for d, o in zip((0, 2, *route(meta)), outs):
        t = mod4(zhi + d)
        span = pl.ds(pl.multiple_of(t * TILE, TILE), TILE)
        o[0:TILE, :] = (a0[span, :].astype(F32) + a1[span, :].astype(F32) + a2[span, :].astype(F32)).astype(BF)
        row = jnp.sum(jnp.where(at == t, stats, 0.0), axis=0, keepdims=True)
        o[TILE : TILE + 16, :] = jnp.concatenate(hi_lo(jnp.broadcast_to(row, (8, WIDTH))), axis=0)


def window_piece_kernel(meta, a0, a1, a2, *outs):
    zhi = meta[1]
    places = [mod4(zhi + d) for d in (0, 2, *route(meta))]
    stats = stats_of(a0, 4 * TILE) + stats_of(a1, 4 * TILE) + stats_of(a2, 4 * TILE)
    stats = jnp.concatenate([stats[0:4, 0:TILE], stats[0:4, TILE : 2 * TILE]], axis=0)
    for t in range(4):
        span = slice(t * TILE, (t + 1) * TILE)
        value = a0[span, :].astype(F32) + a1[span, :].astype(F32) + a2[span, :].astype(F32)
        for at, o in zip(places, outs):
            o[span, :] = lane_piece(value, at).astype(BF)
    for at, o in zip(places, outs):
        o[4 * TILE : 4 * TILE + 16, :] = jnp.concatenate(hi_lo(stats * jnp.where(at == 3, 0.0, 1.0)), axis=0)


def term_piece_kernel(meta, a0, a1, a2, packed, mod, sent):
    group = meta[3] * 2 + meta[4]
    stats = stats_of(a0, 4 * TILE)
    for a in (a1, a2):
        stats = stats + stats_of(a, 4 * TILE)
    scale = 1.0 + lane_piece(mod[1, group], meta[1])
    for t in range(4):
        span = slice(t * TILE, (t + 1) * TILE)
        grad = a0[span, :].astype(F32)
        for a in (a1, a2):
            grad = grad + a[span, :].astype(F32)
        value = packed[4 + t] * (grad * scale - column(stats[t : t + 1]) - packed[t] * column(stats[4 + t : 5 + t]))
        sent[t] = value.astype(BF)


def upstream_piece_kernel(meta, ids, coeffs, first, mod, t1, t2, t3, out):
    group = meta[3] * 2 + meta[4]
    after, decay, weight = decays(meta, ids, coeffs)
    gate = lane_piece(mod[2, group], meta[1]) * weight
    for t in range(4):
        later = t1[t].astype(F32) + t2[t].astype(F32) * after[0] + t3[t].astype(F32) * (after[0] * after[1])
        out[t] = (first[mod4(meta[1] - t)].astype(F32) + gate * later).astype(BF)


def column(row):
    return jnp.transpose(jnp.broadcast_to(row * (1.0 / FEATS), (TILE, TILE)))


def term_kernel(meta, a0, a1, a2, packed, mod, term, sent, moments):
    group = meta[3] * 2 + meta[4]
    grad = a0[0:TILE, :].astype(F32)
    stats = stats_of(a0, TILE)
    for a in (a1, a2):
        grad = grad + a[0:TILE, :].astype(F32)
        stats = stats + stats_of(a, TILE)
    first = stats[0:1, 0:TILE]
    second = stats[0:1, TILE : 2 * TILE]
    moments[...] = jnp.concatenate([first, second], axis=0) * (FEATS**-0.5)

    def wide(value):
        return jnp.concatenate([value] * 3, axis=1)

    du = grad * (1.0 + mod[1, group])
    normed = jnp.concatenate([packed[9 + i] for i in range(3)], axis=1)
    value = wide(packed[8]) * (du - wide(column(first)) - normed * wide(column(second)))
    term[...] = value
    sent[...] = value.astype(BF)


def decays(meta, ids, coeffs):
    step = meta[0]
    after = []
    for ahead in (1, 2, 3):
        at = jnp.minimum(step + ahead, 3)
        after.append(jnp.where(step + ahead <= 3, coeffs[0, ids[at]], 1.0))
    return after, coeffs[0, ids[step]], coeffs[1, ids[step]]


def lam_of(meta, ids, coeffs, cot, terms):
    after, decay, weight = decays(meta, ids, coeffs)
    lam = cot[...] * (after[0] * after[1] * after[2])
    for ref, factor in zip(terms, (1.0, after[0], after[0] * after[1])):
        lam = lam + ref[...].astype(F32) * factor
    return lam, decay, weight


def cut_kernel(meta, ids, coeffs, cot_far, mod_far, w_far, o0, o1, o2, o3, cot, mod, w, sems):
    copies = [
        pltpu.make_async_copy(src, dst, sems.at[i])
        for i, (src, dst) in enumerate(((cot_far, cot), (mod_far, mod), (w_far, w)))
    ]
    for copy in copies:
        copy.start()
    for copy in copies:
        copy.wait()
    zhi = meta[1]
    group = meta[3] * 2 + meta[4]
    lam, decay, weight = lam_of(meta, ids, coeffs, cot, ())
    up = mod[2, group] * weight * lam
    for d, o in enumerate((o0, o1, o2, o3)):
        at = mod4(zhi + d)
        for part in range(3):
            o[part * 48 : (part + 1) * 48, :] = lane_piece(w[part].astype(F32), at).astype(BF)
        o[144:272, :] = lane_piece(up, at).astype(BF)


def adjoint_kernel(meta, ids, coeffs, cot, term, t1, t2, t3, out):
    lam, decay, weight = lam_of(meta, ids, coeffs, cot, (t1, t2, t3))
    out[...] = decay * lam + term[...]


def turn(value, axis, offset):
    return lax.ppermute(value, axis, [(i, (i + offset) % 4) for i in range(4)])


def ring4(value, axis):
    return [value] + [turn(value, axis, -offset) for offset in PLACES[1:]]


def hand_on(before, after, axis):
    pairs = []
    for i in range(4):
        pairs.append((2 * i, 2 * ((i - 1) % 4)))
        pairs.append((2 * i + 1, 2 * ((i + 1) % 4) + 1))
    return lax.ppermute(jnp.where(lax.axis_index("core") == 0, after, before), (axis, "core"), pairs)


def to_heads(pieces):
    got = [pieces[0]]
    for d in (1, 2, 3):
        pairs = [(i, (i + d) % 4) for i in range(4) if (i + d) % 4 != 3]
        got.append(lax.ppermute(pieces[d], "zhi", pairs))
    return got


def to_earlier(value):
    return [lax.ppermute(value, "step", [(j, j - d) for j in range(d, 4)]) for d in (1, 2, 3)]


def swing(value, axes, count, forward, hops=1, headless=False):
    pairs = []
    for i in range(count):
        for core, step in ((0, forward), (1, -forward)):
            if not headless or (i + hops * step) % count != 3:
                pairs.append((2 * i + core, 2 * ((i + step) % count) + core))
    return lax.ppermute(value, (*axes, "core"), pairs)


def reduced(far, plain, waiting, axes, count, headless=False):
    half_way = swing(far, axes, count, 1, 2, headless)
    got = swing(plain, axes, count, -1, 1, headless)
    (waiting,) = call(add_kernel, [sds(waiting.shape, BF)], (waiting, half_way), 0)
    return got, swing(waiting, axes, count, 1, 1, headless)


def along_z(value, offset):
    return lax.ppermute(value, ("zhi", "zlo"), [(i, (i + offset) % 16) for i in range(16)])


def far_z(value):
    pairs = []
    for i in range(16):
        pairs.append((2 * i, 2 * ((i + 2) % 16)))
        pairs.append((2 * i + 1, 2 * ((i - 2) % 16) + 1))
    return lax.ppermute(value, ("zhi", "zlo", "core"), pairs)


def other_core(value):
    return lax.ppermute(value, "core", [(0, 1), (1, 0)])


def shards(states, modulation, cotangent, w_qkv, q_gain, k_gain, step_ids, coeffs, neighbours):
    zhi = lax.axis_index("zhi")
    meta = jnp.stack([lax.axis_index(a) for a in ("step", "zhi", "y", "zlo", "core")]).astype(jnp.int32)
    coeffs, neighbours = coeffs.T, neighbours.T
    mod = modulation.reshape(3, 8, 1, WIDTH)
    gq = (q_gain / jnp.sqrt(jnp.float32(HD))).reshape(1, HD)
    gk = k_gain.reshape(1, HD)

    pieces = call(
        cut_kernel,
        [sds((272, HD), BF)] * 4,
        (meta, step_ids, coeffs, cotangent, mod, jnp.transpose(w_qkv, (1, 0, 2))),
        3,
        [
            pltpu.VMEM((TILE, WIDTH), F32),
            pltpu.VMEM((3, 8, 1, WIDTH), F32),
            pltpu.VMEM((3, 48, WIDTH), BF),
            pltpu.SemaphoreType.DMA((3,)),
        ],
        grant=12,
        far=3,
    )
    pieces = to_heads(pieces)
    own_rows = jnp.stack([p[0:144] for p in pieces])
    pieces[1], x = lax.optimization_barrier((pieces[1], states[0]))
    own_up = jnp.stack([p[144:272] for p in pieces])

    before, after = turn(x, "zhi", 1), turn(x, "zhi", -1)
    own_rows, before, after = lax.optimization_barrier((own_rows, before, after))
    far = hand_on(before, after, "zhi")
    y_rows = lax.all_gather(own_rows, "y")
    y_rows, far, own_up = lax.optimization_barrier((y_rows, far, own_up))
    wg = lax.all_gather(y_rows, "step").reshape(16, 4, 144, HD)
    x_tiles = jnp.stack([x, before, far, after])
    xa = [x_tiles, along_z(x_tiles, 1), along_z(x_tiles, -1), far_z(x_tiles)]
    first_ups = ring4(own_up, "y")
    *first_ups, xa[3] = lax.optimization_barrier((*first_ups, xa[3]))
    xb = [other_core(a) for a in xa]

    tokens = 4 * TILE
    scaled, packed = call(
        norm_kernel,
        [sds((8, 4, TILE, WIDTH), BF), sds((12, TILE, HD), F32)],
        (meta, *xa, *xb, mod),
        1,
        (),
        0,
        12,
    )
    scaled, wg, *first_ups = lax.optimization_barrier((scaled, wg, *first_ups))
    qkv, proj, wk, ws, vec = call(
        proj_kernel,
        [
            sds((4, TILE, WIDTH), BF),
            sds((tokens, WIDTH), F32),
            sds((4, 8, 48, WIDTH), BF),
            sds((4, 8, 48, WIDTH), BF),
            sds((16, WIDTH), F32),
        ],
        (meta, scaled, wg, mod, gq, gk),
        1,
        [pltpu.VMEM((8, 8, 48, WIDTH), BF)],
        2 * tokens * FEATS * WIDTH,
        20,
    )
    all_qkv = ring4(qkv, "y")
    wr = other_core(ws)

    again = first_ups
    for sweep in range(SWEEPS):
        outs = [sds((tokens + 16, WIDTH), BF), sds((4, 3, WIDTH, TILE), F32)]
        dproj, *kept = call(
            sweep_kernel,
            outs[: 2 - sweep],
            (meta, neighbours, *all_qkv, proj, vec, gq, gk, *again),
            2,
            [pltpu.VMEM((16, TILE, WIDTH), BF), pltpu.VMEM((16, TILE, HD), BF)],
            400 * 1000 * 1000,
            12,
        )
        pair = (meta, dproj, other_core(dproj), wk, wr)
        (far,) = features(True, pair)
        here, plain, waiting = features(False, pair)
        near = (here, *reduced(far, plain, waiting, ("zhi", "zlo"), 16))
        if sweep + 1 < SWEEPS:
            own, *others = call(window_piece_kernel, [sds((tokens + 16, HD), BF)] * 4, (meta, *near), 1)
            (sent,) = call(
                term_piece_kernel,
                [sds((4, TILE, HD), BF)],
                (meta, own, *reduced(*others, ("zhi",), 4, True), packed, mod),
                1,
            )
            (up,) = call(
                upstream_piece_kernel,
                [sds((4, TILE, HD), BF)],
                (meta, step_ids, coeffs, first_ups[0], mod, *to_earlier(sent)),
                3,
            )
            again = (lax.all_gather(up, "y"), *kept)
    own, *others = call(window_kernel, [sds((TILE + 16, WIDTH), BF)] * 4, (meta, *near), 1)
    term, sent, moments = call(
        term_kernel,
        [sds((TILE, WIDTH), F32), sds((TILE, WIDTH), BF), sds((2, TILE), F32)],
        (meta, own, *reduced(*others, ("zhi",), 4), packed, mod),
        1,
    )
    (adjoint,) = call(
        adjoint_kernel,
        [sds((TILE, WIDTH), F32)],
        (meta, step_ids, coeffs, cotangent, term, *to_earlier(sent)),
        3,
    )
    return adjoint[None], moments[None]


def solution(mesh):
    fine = Mesh(mesh.devices.reshape(4, 4, 4, 4, 2), ("step", "zhi", "y", "zlo", "core"))
    blk, head = ("zhi", "y"), ("zlo", "core")
    in_specs = (
        P("step", blk, head),
        P("step", None, None),
        P(blk, head),
        P(("step",) + blk, None, head),
        P(),
        P(),
        P(),
        P(),
        P(),
    )
    out_specs = (P("step", blk, head), P("step", None, blk))
    return jax.shard_map(shards, mesh=fine, in_specs=in_specs, out_specs=out_specs, check_vma=False)
```

```python
import functools

import jax
import jax.numpy as jnp
from jax import lax
from jax.experimental import pallas as pl
from jax.experimental.pallas import tpu as pltpu
from jax.sharding import Mesh
from jax.sharding import PartitionSpec as P

HD = 128
TILE = 128
WIDTH = 384
FEATS = 3072
SWEEPS = 2
EPS = 1e-06
BF = jnp.bfloat16
F32 = jnp.float32
MIB = 1024 * 1024
PLACES = (0, -1, 1, 2)

VM = pl.BlockSpec(memory_space=pltpu.VMEM)
SM = pl.BlockSpec(memory_space=pltpu.SMEM)
HBM = pl.BlockSpec(memory_space=pltpu.HBM)


def call(body, outs, args, smem, scratch=(), flops=0, grant=8, far=0, far_outs=0):
    specs = [SM if i < smem else VM for i in range(len(args))]
    specs[smem : smem + far] = [HBM] * far
    moved = sum(a.size * a.dtype.itemsize for a in args) + sum(
        o.size * o.dtype.itemsize for o in outs
    )
    return pl.pallas_call(
        body,
        out_shape=tuple(outs),
        in_specs=specs,
        out_specs=tuple([VM] * (len(outs) - far_outs) + [HBM] * far_outs),
        scratch_shapes=list(scratch),
        compiler_params=pltpu.CompilerParams(vmem_limit_bytes=grant * MIB),
        cost_estimate=pl.CostEstimate(flops=flops, bytes_accessed=moved, transcendentals=0),
    )(*args)


def sds(shape, dtype):
    return jax.ShapeDtypeStruct(shape, dtype)


def nt(a, b):
    return lax.dot_general(a, b, (((1,), (1,)), ((), ())), preferred_element_type=F32)


def tn(a, b):
    return lax.dot_general(a, b, (((0,), (0,)), ((), ())), preferred_element_type=F32)


def nn(a, b):
    return jnp.dot(a, b, preferred_element_type=F32)


def hi_lo(value):
    hi = value.astype(BF)
    return hi, (value - hi.astype(F32)).astype(BF)


def mod4(value):
    return lax.rem(value + 8, 4)


def lane_piece(value, at):
    out = jnp.zeros(value.shape[:-1] + (HD,), value.dtype)
    for i in range(3):
        out = jnp.where(at == i, value[..., i * HD : (i + 1) * HD], out)
    return out


def norm_kernel(
    meta, xa0, xa1, xa2, xa3, xb0, xb1, xb2, xb3, mod,
    scaled, packed,
):
    zhi, zlo, core = meta[1], meta[3], meta[4]
    place = zhi * 4 + zlo
    own_far = jnp.where(core == 0, -2, 2)
    sources = []
    for refs, side, far in (
        ((xa0, xa1, xa2, xa3), core, own_far),
        ((xb0, xb1, xb2, xb3), 1 - core, -own_far),
    ):
        for ref, offset in zip(refs, (0, -1, 1, far)):
            at = lax.rem(place + offset + 16, 16)
            sources.append((ref, at // 4, lax.rem(at, 4) * 2 + side))

    rows = 32

    def chunk(turn, carry):
        t = turn // (TILE // rows)
        start = lax.rem(turn, TILE // rows) * rows
        span = pl.ds(pl.multiple_of(start, rows), rows)

        def load(source):
            ref, z, g = source
            d = mod4(z - t)
            return ref[d, span, :].astype(F32)

        total = jnp.zeros((rows, WIDTH), F32)
        for source in sources:
            total = total + load(source)
        mean = jnp.sum(total, axis=1, keepdims=True) * (1.0 / FEATS)
        square = jnp.zeros((rows, WIDTH), F32)
        for source in sources:
            centred = load(source) - mean
            square = square + centred * centred
        inv = lax.rsqrt(jnp.sum(square, axis=1, keepdims=True) * (1.0 / FEATS) + EPS)
        for source in sources:
            normed = (load(source) - mean) * inv
            scaled[source[2], t, span, :] = (normed * (1.0 + mod[1, source[2]])).astype(BF)
        normed = (load(sources[0]) - mean) * inv
        inv_wide = jnp.broadcast_to(inv, (rows, HD))
        packed[t, span, :] = lane_piece(normed, zhi)
        packed[4 + t, span, :] = inv_wide

        @pl.when(t == zhi)
        def _():
            packed[8, span, :] = inv_wide
            for i in range(3):
                packed[9 + i, span, :] = normed[:, i * HD : (i + 1) * HD]

        return carry

    lax.fori_loop(0, 4 * (TILE // rows), chunk, 0)


def proj_kernel(
    meta, nscr, wg, mod, q_gain, k_gain,
    qkv, proj, wk, ws, vec, wc,
):
    zhi, core = meta[1], meta[4]
    for sy in range(16):
        for d in range(4):
            zh = mod4(zhi - d)
            for part in range(3):
                wc[(sy // 4) * 2 + zh // 2, lax.rem(zh, 2) * 4 + sy % 4, :, part * HD : (part + 1) * HD] = (
                    wg[sy, d, part * 48 : (part + 1) * 48, :]
                )
    for r in range(4):
        wk[r] = wc[2 * r + core]
        ws[r] = wc[2 * r + 1 - core]

    acc = jnp.zeros((4 * TILE, WIDTH), F32)
    flat = jnp.zeros((16, WIDTH), F32)
    for g in range(8):
        w_g = wc[g].reshape(WIDTH, WIDTH)
        acc = acc + nn(nscr[g].reshape(4 * TILE, WIDTH), w_g)
        scale_hi, scale_lo = hi_lo(1.0 + mod[1, g])
        shift_hi, shift_lo = hi_lo(mod[0, g])
        four = jnp.concatenate([scale_hi, scale_lo, shift_hi, shift_lo], axis=0)
        lhs = jnp.concatenate([four, jnp.zeros((12, WIDTH), BF)], axis=0)
        flat = flat + nn(lhs, w_g)
    vec[...] = flat
    proj[...] = acc + (flat[2:3] + flat[3:4])
    for t in range(4):
        span = slice(t * TILE, (t + 1) * TILE)
        q = proj[span, 0:HD]
        k = proj[span, HD : 2 * HD]
        q_inv = lax.rsqrt(jnp.mean(q * q, axis=1, keepdims=True) + EPS)
        k_inv = lax.rsqrt(jnp.mean(k * k, axis=1, keepdims=True) + EPS)
        qkv[t, :, 0:HD] = (q * q_inv * q_gain[...]).astype(BF)
        qkv[t, :, HD : 2 * HD] = (k * k_inv * k_gain[...]).astype(BF)
        qkv[t, :, 2 * HD : 3 * HD] = proj[span, 2 * HD : 3 * HD].astype(BF)


def norm_back(raw, gain, grad):
    inv = lax.rsqrt(jnp.mean(raw * raw, axis=1, keepdims=True) + EPS)
    scaled = grad * gain
    dot = jnp.mean(scaled * raw, axis=1, keepdims=True)
    return inv * (scaled - raw * (inv * inv * dot))


def sweep_kernel(
    meta, nb, k0, k1, k2, k3, proj, vec, q_gain, k_gain, *rest
):
    tiles, ups = rest[-2:]
    first_sweep = len(rest) == 8
    probs, out = (rest[5], rest[4]) if first_sweep else (rest[1], rest[2])
    zhi, y = meta[1], meta[2]
    for ref, offset in zip((k0, k1, k2, k3), PLACES):
        yy = mod4(y + offset)
        for z in range(4):
            tiles[z * 4 + yy] = ref[z]
    for i, offset in enumerate(PLACES):
        for z in range(4):
            if first_sweep:
                ups[mod4(zhi - z) * 4 + mod4(y + offset)] = rest[i][z]
            else:
                ups[z * 4 + i] = rest[0][i, z]

    m1_hi, m1_lo = hi_lo(vec[0:1] + vec[1:2])
    m1 = jnp.concatenate([m1_hi, m1_lo, jnp.zeros((14, WIDTH), BF)], axis=0)
    ones = jnp.ones((16, WIDTH), BF)
    s0 = vec[2:3] + vec[3:4]

    def k_of(t):
        return tiles[t, :, HD : 2 * HD]

    def v_of(t):
        return tiles[t, :, 2 * HD : 3 * HD]

    def own(jz, carry):
        j = jz * 4 + y
        near = (nb[1, j], nb[2, j])
        d_k = jnp.zeros((TILE, HD), F32)
        d_v = jnp.zeros((TILE, HD), F32)
        d_q = None
        for slot in range(3):
            if slot == 0:
                i = j
                keys = (j, near[0], near[1])
            else:
                i = near[slot - 1]
                keys = (j, i, nb[1, i] + nb[2, i] - j)
            q = tiles[i, :, 0:HD]
            up = ups[i]
            k_all = jnp.concatenate([k_of(t) for t in keys], axis=0)
            v_all = jnp.concatenate([v_of(t) for t in keys], axis=0)
            if first_sweep:
                expo = jnp.exp(nt(k_all, q))
                prob = expo * (1.0 / jnp.sum(expo, axis=0, keepdims=True))
                probs[jz, slot] = prob
            else:
                prob = probs[jz, slot]
            prob_b = prob.astype(BF)
            dprob = nt(v_all, up)
            delta = jnp.sum(prob_b.astype(F32) * dprob, axis=0, keepdims=True)
            if slot == 0:
                dscore = (prob * (dprob - delta)).astype(BF)
                d_q = tn(dscore, k_all)
                dscore = dscore[0:TILE]
            else:
                dscore = (prob[0:TILE] * (dprob[0:TILE] - delta)).astype(BF)
            d_k = d_k + nn(dscore, q)
            d_v = d_v + nn(prob_b[0:TILE], up)
        start = pl.multiple_of(jz * TILE, TILE)
        raw = proj[pl.ds(start, TILE), :]
        d_q = norm_back(raw[:, 0:HD], q_gain[...], d_q)
        d_k = norm_back(raw[:, HD : 2 * HD], k_gain[...], d_k)
        d_all = jnp.concatenate([d_q, d_k, d_v], axis=1).astype(BF)
        out[pl.ds(start, TILE), :] = d_all
        first = nt(m1, d_all)
        prod_hi, prod_lo = hi_lo(d_all.astype(F32) * (raw - s0))
        second = nt(ones, prod_hi) + nt(ones, prod_lo)
        row = jnp.concatenate(
            [first[0:1] + first[1:2], second[0:1], jnp.zeros((1, TILE), F32)], axis=1
        )
        at = lax.broadcasted_iota(jnp.int32, (8, WIDTH), 0)
        return carry + jnp.where(at == jz, row, 0.0)

    stats = lax.fori_loop(0, 4, own, jnp.zeros((8, WIDTH), F32))
    out[4 * TILE : 4 * TILE + 16, :] = jnp.concatenate(hi_lo(stats), axis=0)


def stats_of(ref, start):
    both = ref[start : start + 16, :].astype(F32)
    return both[0:8] + both[8:16]


def route(meta):
    forward = meta[4] == 0
    return jnp.where(forward, 3, 1), jnp.where(forward, 1, 3)


def feature_kernel(far_only, meta, own, other, wk, wr, *outs):
    zlo = meta[3]
    stats = jnp.concatenate(hi_lo(stats_of(own, 4 * TILE) + stats_of(other, 4 * TILE)), axis=0)
    for offset, o in zip((2,) if far_only else (0, *route(meta)), outs):
        r = mod4(zlo + offset)
        value = nt(own[0 : 4 * TILE, :], wk[r].reshape(WIDTH, WIDTH))
        value = value + nt(other[0 : 4 * TILE, :], wr[r].reshape(WIDTH, WIDTH))
        o[0 : 4 * TILE, :] = value.astype(BF)
        o[4 * TILE : 4 * TILE + 16, :] = stats


def features(far_only, args):
    count = 1 if far_only else 3
    return call(
        functools.partial(feature_kernel, far_only),
        [sds((4 * TILE + 16, WIDTH), BF)] * count,
        args,
        1,
        (),
        2 * 4 * TILE * FEATS * WIDTH * count // 4,
        12,
    )


def add_kernel(a, b, out):
    rows = out.shape[0] - 16
    out[0:rows, :] = (a[0:rows, :].astype(F32) + b[0:rows, :].astype(F32)).astype(BF)
    out[rows : rows + 16, :] = jnp.concatenate(hi_lo(stats_of(a, rows) + stats_of(b, rows)), axis=0)


def window_kernel(meta, a0, a1, a2, *outs):
    zhi = meta[1]
    stats = stats_of(a0, 4 * TILE) + stats_of(a1, 4 * TILE) + stats_of(a2, 4 * TILE)
    at = lax.broadcasted_iota(jnp.int32, (8, WIDTH), 0)
    for d, o in zip((0, 2, *route(meta)), outs):
        t = mod4(zhi + d)
        span = pl.ds(pl.multiple_of(t * TILE, TILE), TILE)
        o[0:TILE, :] = (a0[span, :].astype(F32) + a1[span, :].astype(F32) + a2[span, :].astype(F32)).astype(BF)
        row = jnp.sum(jnp.where(at == t, stats, 0.0), axis=0, keepdims=True)
        o[TILE : TILE + 16, :] = jnp.concatenate(hi_lo(jnp.broadcast_to(row, (8, WIDTH))), axis=0)


def window_piece_kernel(meta, a0, a1, a2, *outs):
    zhi = meta[1]
    places = [mod4(zhi + d) for d in (0, 2, *route(meta))]
    stats = stats_of(a0, 4 * TILE) + stats_of(a1, 4 * TILE) + stats_of(a2, 4 * TILE)
    stats = jnp.concatenate([stats[0:4, 0:TILE], stats[0:4, TILE : 2 * TILE]], axis=0)
    for t in range(4):
        span = slice(t * TILE, (t + 1) * TILE)
        value = a0[span, :].astype(F32) + a1[span, :].astype(F32) + a2[span, :].astype(F32)
        for at, o in zip(places, outs):
            o[span, :] = lane_piece(value, at).astype(BF)
    for at, o in zip(places, outs):
        o[4 * TILE : 4 * TILE + 16, :] = jnp.concatenate(hi_lo(stats * jnp.where(at == 3, 0.0, 1.0)), axis=0)


def term_piece_kernel(meta, a0, a1, a2, packed, mod, sent):
    group = meta[3] * 2 + meta[4]
    stats = stats_of(a0, 4 * TILE)
    for a in (a1, a2):
        stats = stats + stats_of(a, 4 * TILE)
    scale = 1.0 + lane_piece(mod[1, group], meta[1])
    for t in range(4):
        span = slice(t * TILE, (t + 1) * TILE)
        grad = a0[span, :].astype(F32)
        for a in (a1, a2):
            grad = grad + a[span, :].astype(F32)
        value = packed[4 + t] * (grad * scale - column(stats[t : t + 1]) - packed[t] * column(stats[4 + t : 5 + t]))
        sent[t] = value.astype(BF)


def upstream_piece_kernel(meta, ids, coeffs, first, mod, t1, t2, t3, out):
    group = meta[3] * 2 + meta[4]
    after, decay, weight = decays(meta, ids, coeffs)
    gate = lane_piece(mod[2, group], meta[1]) * weight
    for t in range(4):
        later = t1[t].astype(F32) + t2[t].astype(F32) * after[0] + t3[t].astype(F32) * (after[0] * after[1])
        out[t] = (first[mod4(meta[1] - t)].astype(F32) + gate * later).astype(BF)


def column(row):
    return jnp.transpose(jnp.broadcast_to(row * (1.0 / FEATS), (TILE, TILE)))


def term_kernel(meta, a0, a1, a2, packed, mod, term, sent, moments):
    group = meta[3] * 2 + meta[4]
    grad = a0[0:TILE, :].astype(F32)
    stats = stats_of(a0, TILE)
    for a in (a1, a2):
        grad = grad + a[0:TILE, :].astype(F32)
        stats = stats + stats_of(a, TILE)
    first = stats[0:1, 0:TILE]
    second = stats[0:1, TILE : 2 * TILE]
    moments[...] = jnp.concatenate([first, second], axis=0) * (FEATS**-0.5)

    def wide(value):
        return jnp.concatenate([value] * 3, axis=1)

    du = grad * (1.0 + mod[1, group])
    normed = jnp.concatenate([packed[9 + i] for i in range(3)], axis=1)
    value = wide(packed[8]) * (du - wide(column(first)) - normed * wide(column(second)))
    term[...] = value
    sent[...] = value.astype(BF)


def decays(meta, ids, coeffs):
    step = meta[0]
    after = []
    for ahead in (1, 2, 3):
        at = jnp.minimum(step + ahead, 3)
        after.append(jnp.where(step + ahead <= 3, coeffs[0, ids[at]], 1.0))
    return after, coeffs[0, ids[step]], coeffs[1, ids[step]]


def lam_of(meta, ids, coeffs, cot, terms):
    after, decay, weight = decays(meta, ids, coeffs)
    lam = cot[...] * (after[0] * after[1] * after[2])
    for ref, factor in zip(terms, (1.0, after[0], after[0] * after[1])):
        lam = lam + ref[...].astype(F32) * factor
    return lam, decay, weight


def cut_kernel(meta, ids, coeffs, cot_far, mod_far, w_far, o0, o1, o2, o3, cot, mod, w, sems):
    copies = [
        pltpu.make_async_copy(src, dst, sems.at[i])
        for i, (src, dst) in enumerate(((cot_far, cot), (mod_far, mod), (w_far, w)))
    ]
    for copy in copies:
        copy.start()
    for copy in copies:
        copy.wait()
    zhi = meta[1]
    group = meta[3] * 2 + meta[4]
    lam, decay, weight = lam_of(meta, ids, coeffs, cot, ())
    up = mod[2, group] * weight * lam
    for d, o in enumerate((o0, o1, o2, o3)):
        at = mod4(zhi + d)
        for part in range(3):
            o[part * 48 : (part + 1) * 48, :] = lane_piece(w[part].astype(F32), at).astype(BF)
        o[144:272, :] = lane_piece(up, at).astype(BF)


def adjoint_kernel(meta, ids, coeffs, cot, term, t1, t2, t3, out):
    lam, decay, weight = lam_of(meta, ids, coeffs, cot, (t1, t2, t3))
    out[...] = decay * lam + term[...]


def turn(value, axis, offset):
    return lax.ppermute(value, axis, [(i, (i + offset) % 4) for i in range(4)])


def ring4(value, axis):
    return [value] + [turn(value, axis, -offset) for offset in PLACES[1:]]


def hand_on(before, after, axis):
    pairs = []
    for i in range(4):
        pairs.append((2 * i, 2 * ((i - 1) % 4)))
        pairs.append((2 * i + 1, 2 * ((i + 1) % 4) + 1))
    return lax.ppermute(jnp.where(lax.axis_index("core") == 0, after, before), (axis, "core"), pairs)


def to_heads(pieces):
    got = [pieces[0]]
    for d in (1, 2, 3):
        pairs = [(i, (i + d) % 4) for i in range(4) if (i + d) % 4 != 3]
        got.append(lax.ppermute(pieces[d], "zhi", pairs))
    return got


def to_earlier(value):
    return [lax.ppermute(value, "step", [(j, j - d) for j in range(d, 4)]) for d in (1, 2, 3)]


def swing(value, axes, count, forward, hops=1, headless=False):
    pairs = []
    for i in range(count):
        for core, step in ((0, forward), (1, -forward)):
            if not headless or (i + hops * step) % count != 3:
                pairs.append((2 * i + core, 2 * ((i + step) % count) + core))
    return lax.ppermute(value, (*axes, "core"), pairs)


def reduced(far, plain, waiting, axes, count, headless=False):
    half_way = swing(far, axes, count, 1, 2, headless)
    got = swing(plain, axes, count, -1, 1, headless)
    (waiting,) = call(add_kernel, [sds(waiting.shape, BF)], (waiting, half_way), 0)
    return got, swing(waiting, axes, count, 1, 1, headless)


def along_z(value, offset):
    return lax.ppermute(value, ("zhi", "zlo"), [(i, (i + offset) % 16) for i in range(16)])


def far_z(value):
    pairs = []
    for i in range(16):
        pairs.append((2 * i, 2 * ((i + 2) % 16)))
        pairs.append((2 * i + 1, 2 * ((i - 2) % 16) + 1))
    return lax.ppermute(value, ("zhi", "zlo", "core"), pairs)


def other_core(value):
    return lax.ppermute(value, "core", [(0, 1), (1, 0)])


def shards(states, modulation, cotangent, w_qkv, q_gain, k_gain, step_ids, coeffs, neighbours):
    zhi = lax.axis_index("zhi")
    meta = jnp.stack([lax.axis_index(a) for a in ("step", "zhi", "y", "zlo", "core")]).astype(jnp.int32)
    coeffs, neighbours = coeffs.T, neighbours.T
    mod = modulation.reshape(3, 8, 1, WIDTH)
    gq = (q_gain / jnp.sqrt(jnp.float32(HD))).reshape(1, HD)
    gk = k_gain.reshape(1, HD)

    pieces = call(
        cut_kernel,
        [sds((272, HD), BF)] * 4,
        (meta, step_ids, coeffs, cotangent, mod, jnp.transpose(w_qkv, (1, 0, 2))),
        3,
        [
            pltpu.VMEM((TILE, WIDTH), F32),
            pltpu.VMEM((3, 8, 1, WIDTH), F32),
            pltpu.VMEM((3, 48, WIDTH), BF),
            pltpu.SemaphoreType.DMA((3,)),
        ],
        grant=12,
        far=3,
    )
    pieces = to_heads(pieces)
    own_rows = jnp.stack([p[0:144] for p in pieces])
    pieces[1], x = lax.optimization_barrier((pieces[1], states[0]))
    own_up = jnp.stack([p[144:272] for p in pieces])

    before, after = turn(x, "zhi", 1), turn(x, "zhi", -1)
    own_rows, before, after = lax.optimization_barrier((own_rows, before, after))
    far = hand_on(before, after, "zhi")
    y_rows = lax.all_gather(own_rows, "y")
    y_rows, far, own_up = lax.optimization_barrier((y_rows, far, own_up))
    wg = lax.all_gather(y_rows, "step").reshape(16, 4, 144, HD)
    x_tiles = jnp.stack([x, before, far, after])
    xa = [x_tiles, along_z(x_tiles, 1), along_z(x_tiles, -1), far_z(x_tiles)]
    up_before, up_after = turn(own_up, "y", 1), turn(own_up, "y", -1)
    up_before, up_after, xa[3] = lax.optimization_barrier((up_before, up_after, xa[3]))
    first_ups = [own_up, up_before, up_after, hand_on(up_before, up_after, "y")]
    xb = [other_core(a) for a in xa]

    tokens = 4 * TILE
    scaled, packed = call(
        norm_kernel,
        [sds((8, 4, TILE, WIDTH), BF), sds((12, TILE, HD), F32)],
        (meta, *xa, *xb, mod),
        1,
        (),
        0,
        12,
    )
    scaled, wg, *first_ups = lax.optimization_barrier((scaled, wg, *first_ups))
    qkv, proj, wk, ws, vec = call(
        proj_kernel,
        [
            sds((4, TILE, WIDTH), BF),
            sds((tokens, WIDTH), F32),
            sds((4, 8, 48, WIDTH), BF),
            sds((4, 8, 48, WIDTH), BF),
            sds((16, WIDTH), F32),
        ],
        (meta, scaled, wg, mod, gq, gk),
        1,
        [pltpu.VMEM((8, 8, 48, WIDTH), BF)],
        2 * tokens * FEATS * WIDTH,
        20,
    )
    all_qkv = ring4(qkv, "y")
    all_qkv[3], ws = lax.optimization_barrier((all_qkv[3], ws))
    wr = other_core(ws)

    again = first_ups
    for sweep in range(SWEEPS):
        outs = [sds((tokens + 16, WIDTH), BF), sds((4, 3, WIDTH, TILE), F32)]
        dproj, *kept = call(
            sweep_kernel,
            outs[: 2 - sweep],
            (meta, neighbours, *all_qkv, proj, vec, gq, gk, *again),
            2,
            [pltpu.VMEM((16, TILE, WIDTH), BF), pltpu.VMEM((16, TILE, HD), BF)],
            400 * 1000 * 1000,
            12,
        )
        pair = (meta, dproj, other_core(dproj), wk, wr)
        (far,) = features(True, pair)
        here, plain, waiting = features(False, pair)
        near = (here, *reduced(far, plain, waiting, ("zhi", "zlo"), 16))
        if sweep + 1 < SWEEPS:
            own, *others = call(window_piece_kernel, [sds((tokens + 16, HD), BF)] * 4, (meta, *near), 1)
            (sent,) = call(
                term_piece_kernel,
                [sds((4, TILE, HD), BF)],
                (meta, own, *reduced(*others, ("zhi",), 4, True), packed, mod),
                1,
            )
            (up,) = call(
                upstream_piece_kernel,
                [sds((4, TILE, HD), BF)],
                (meta, step_ids, coeffs, first_ups[0], mod, *to_earlier(sent)),
                3,
            )
            again = (lax.all_gather(up, "y"), *kept)
    own, *others = call(window_kernel, [sds((TILE + 16, WIDTH), BF)] * 4, (meta, *near), 1)
    term, sent, moments = call(
        term_kernel,
        [sds((TILE, WIDTH), F32), sds((TILE, WIDTH), BF), sds((2, TILE), F32)],
        (meta, own, *reduced(*others, ("zhi",), 4), packed, mod),
        1,
    )
    (adjoint,) = call(
        adjoint_kernel,
        [sds((TILE, WIDTH), F32)],
        (meta, step_ids, coeffs, cotangent, term, *to_earlier(sent)),
        3,
    )
    return adjoint[None], moments[None]


def solution(mesh):
    fine = Mesh(mesh.devices.reshape(4, 4, 4, 4, 2), ("step", "zhi", "y", "zlo", "core"))
    blk, head = ("zhi", "y"), ("zlo", "core")
    in_specs = (
        P("step", blk, head),
        P("step", None, None),
        P(blk, head),
        P(("step",) + blk, None, head),
        P(),
        P(),
        P(),
        P(),
        P(),
    )
    out_specs = (P("step", blk, head), P("step", None, blk))
    return jax.shard_map(shards, mesh=fine, in_specs=in_specs, out_specs=out_specs, check_vma=False)
```
